32 devices in a mesh: wide: 8 (over z, y), narrow: 4 (over x, core).
Axes of the slice: x: 2, y: 2, z: 4, core: 2. Of those that a mesh axis runs over, the one named last changes fastest.
Arguments:
- clean_mel: float32 [16384, 80], P(('wide', 'narrow')), may hold values from -6 to 6
- gauss_noise: float32 [16384, 80], P(('wide', 'narrow')), may hold values from -6 to 6
- flow_time: float32 [32], P(('wide', 'narrow')), may hold values from 0 to 1
- phone_ids: int32 [16384], P(('wide', 'narrow')), may hold values from 0 to 127
- lengths: int32 [32], P(('wide', 'narrow')), may hold values from 32 to 512, as said below
- span_start: int32 [32], P(('wide', 'narrow')), may hold values from 0 to 154, as said below
- span_end: int32 [32], P(('wide', 'narrow')), may hold values from 1 to 512, as said below
- speaker: int32 [32], P(('wide', 'narrow')), may hold values from 0 to 15, as said below
- skip_states: bfloat16 [16384, 1024], P(('wide', 'narrow')), may hold values from -6 to 6
- w_input: float32 [672, 1024], P(None, ('wide', 'narrow')), may hold values from -0.25 to 0.25
- phone_table: float32 [128, 512], P(None, ('wide', 'narrow')), may hold values from -5 to 5
- w_skip: float32 [2048, 1024], P(('wide', 'narrow')), may hold values from -0.125 to 0.125
- w_attend: float32 [1024, 3072], P(('wide', 'narrow')), may hold values from -0.1875 to 0.1875
- w_output: float32 [1024, 1024], P(('wide', 'narrow')), may hold values from -0.375 to 0.375
- w_expand: float32 [1024, 4096], P(('wide', 'narrow')), may hold values from -0.1875 to 0.1875
- w_reduce: float32 [4096, 1024], P(('wide', 'narrow')), may hold values from -0.09375 to 0.09375
- w_head: float32 [1024, 80], P(('wide', 'narrow')), may hold values from -0.1875 to 0.1875
- norm_gains: float32 [3, 1024], P(None, ('wide', 'narrow'))
- moment_input: float32 [672, 1024], P(None, ('wide', 'narrow')), may hold values from -0.0014648438 to 0.0014648438
- moment_table: float32 [128, 512], P(None, ('wide', 'narrow')), may hold values from -6.1035156e-05 to 6.1035156e-05
- moment_skip: float32 [2048, 1024], P(('wide', 'narrow')), may hold values from -0.0014648438 to 0.0014648438
- moment_attend: float32 [1024, 3072], P(('wide', 'narrow')), may hold values from -0.0014648438 to 0.0014648438
- moment_output: float32 [1024, 1024], P(('wide', 'narrow')), may hold values from -0.0014648438 to 0.0014648438
- moment_expand: float32 [1024, 4096], P(('wide', 'narrow')), may hold values from -0.0014648438 to 0.0014648438
- moment_reduce: float32 [4096, 1024], P(('wide', 'narrow')), may hold values from -0.0014648438 to 0.0014648438
- moment_head: float32 [1024, 80], P(('wide', 'narrow')), may hold values from -0.0014648438 to 0.0014648438
- moment_gains: float32 [3, 1024], P(None, ('wide', 'narrow')), may hold values from -0.005859375 to 0.005859375
- square_input: float32 [672, 1024], P(None, ('wide', 'narrow')), may hold values from 6.4438304e-08 to 2.5775321e-07
- square_table: float32 [128, 512], P(None, ('wide', 'narrow')), may hold values from 9.205472e-11 to 3.758901e-10
- square_skip: float32 [2048, 1024], P(('wide', 'narrow')), may hold values from 6.4438304e-08 to 2.5775321e-07
- square_attend: float32 [1024, 3072], P(('wide', 'narrow')), may hold values from 6.4438304e-08 to 2.5775321e-07
- square_output: float32 [1024, 1024], P(('wide', 'narrow')), may hold values from 6.4438304e-08 to 2.5775321e-07
- square_expand: float32 [1024, 4096], P(('wide', 'narrow')), may hold values from 6.4438304e-08 to 2.5775321e-07
- square_reduce: float32 [4096, 1024], P(('wide', 'narrow')), may hold values from 6.4438304e-08 to 2.5775321e-07
- square_head: float32 [1024, 80], P(('wide', 'narrow')), may hold values from 6.4438304e-08 to 2.5775321e-07
- square_gains: float32 [3, 1024], P(None, ('wide', 'narrow')), may hold values from 1.0310129e-06 to 4.1240514e-06
Outputs:
- loss_value: float32 [], replicated
- grad_norm: float32 [], replicated
- next_w_input: float32 [672, 1024], P(None, ('wide', 'narrow'))
- next_phone_table: float32 [128, 512], P(None, ('wide', 'narrow'))
- next_w_skip: float32 [2048, 1024], P(('wide', 'narrow'))
- next_w_attend: float32 [1024, 3072], P(('wide', 'narrow'))
- next_w_output: float32 [1024, 1024], P(('wide', 'narrow'))
- next_w_expand: float32 [1024, 4096], P(('wide', 'narrow'))
- next_w_reduce: float32 [4096, 1024], P(('wide', 'narrow'))
- next_w_head: float32 [1024, 80], P(('wide', 'narrow'))
- next_norm_gains: float32 [3, 1024], P(None, ('wide', 'narrow'))
- next_moment_input: float32 [672, 1024], P(None, ('wide', 'narrow'))
- next_moment_table: float32 [128, 512], P(None, ('wide', 'narrow'))
- next_moment_skip: float32 [2048, 1024], P(('wide', 'narrow'))
- next_moment_attend: float32 [1024, 3072], P(('wide', 'narrow'))
- next_moment_output: float32 [1024, 1024], P(('wide', 'narrow'))
- next_moment_expand: float32 [1024, 4096], P(('wide', 'narrow'))
- next_moment_reduce: float32 [4096, 1024], P(('wide', 'narrow'))
- next_moment_head: float32 [1024, 80], P(('wide', 'narrow'))
- next_moment_gains: float32 [3, 1024], P(None, ('wide', 'narrow'))
- next_square_input: float32 [672, 1024], P(None, ('wide', 'narrow'))
- next_square_table: float32 [128, 512], P(None, ('wide', 'narrow'))
- next_square_skip: float32 [2048, 1024], P(('wide', 'narrow'))
- next_square_attend: float32 [1024, 3072], P(('wide', 'narrow'))
- next_square_output: float32 [1024, 1024], P(('wide', 'narrow'))
- next_square_expand: float32 [1024, 4096], P(('wide', 'narrow'))
- next_square_reduce: float32 [4096, 1024], P(('wide', 'narrow'))
- next_square_head: float32 [1024, 80], P(('wide', 'narrow'))
- next_square_gains: float32 [3, 1024], P(None, ('wide', 'narrow'))
The draws below stay inside these ranges and needn't reach their ends.
Inputs may be any that keep to these rules, and one draw needn't show every extreme that they name: `lengths`: utterance u's length; exactly one utterance has 512 frames. span_start < span_end <= lengths; a span covers 70 to 100 percent of its utterance (rounded down, at least one frame). `span_end`: the end of each span; one span ends at 512. Some speaker group has no utterance.
All inputs are finite; a program needn't handle non-finite values.
Results may differ from the reference program's by a relative error of at most 0.012.
The reference program's roundings to bfloat16 on the way count: a program that leaves them out, or rounds other values in their place, can miss the bound.
Values may be sent and summed in bfloat16 or wider, within the bound.
No kernel may reach another device: no remote copies, remote signals or barrier semaphores. Data moves between devices by JAX's collectives and lax.ppermute only.
A program may use at most 256 MiB of HBM per device.

```python
import math
from functools import partial
import jax
import jax.numpy as jnp
from jax import lax

D = 1024
FF = 4096
HD = 64
MEL = 80
PD = 512
PHONES = 128
FRAMES = 512
SPK = 16
STEP = 10
IN_W = 672
UTTS = 32
FRAMES_ALL = 16384
PARAMS = 15518720
N_WIDE = 8
N_NARROW = 4


def utterance_plan(key):
    total = N_WIDE * N_NARROW
    index = jnp.arange(total)
    wide_pos = index // N_NARROW
    narrow_pos = index % N_NARROW
    wide_span = max(N_WIDE - 1, 1)
    narrow_span = max(N_NARROW - 1, 1)
    base = FRAMES * (wide_span + 2 * wide_pos) * (narrow_span + 2 * narrow_pos) // (9 * wide_span * narrow_span)
    keys = jax.random.split(key, 3)
    jitter = jax.random.randint(keys[0], (total,), 0, FRAMES // 8 + 1)
    lengths = jnp.maximum(base - jitter, max(FRAMES // 16, 4))
    lengths = jnp.where(index == total - 1, FRAMES, lengths).astype(jnp.int32)
    percent = jax.random.randint(keys[1], (total,), 70, 101)
    percent = jnp.where(index == total - 1, 70, percent)
    cover = jnp.maximum(lengths * percent // 100, 1)
    start = jax.random.randint(keys[2], (total,), 0, lengths - cover + 1)
    start = jnp.where(index == 0, 0, start)
    start = jnp.where(index == total - 1, FRAMES - cover, start).astype(jnp.int32)
    return (lengths, start, (start + cover).astype(jnp.int32))


def draw_lengths(key, part):
    plan = utterance_plan(key)
    return plan[0]


def draw_span_start(key, part):
    plan = utterance_plan(key)
    return plan[1]


def draw_span_end(key, part):
    plan = utterance_plan(key)
    return plan[2]


def draw_norm_gains(key, part):
    key = jax.random.fold_in(key, 14)
    ramp = jnp.arange(D, dtype=jnp.float32) / max(D - 1, 1)
    spread = jnp.clip(jax.random.normal(key, (3, D), jnp.float32), -3.0, 3.0)
    return (0.6 + 1.2 * ramp)[None, :] * (1.0 + 0.1 * spread)


def draw_speaker(key, part):
    key = jax.random.fold_in(key, 15)
    keys = jax.random.split(key, 2)
    total = N_WIDE * N_NARROW
    index = jnp.arange(total)
    missing = jax.random.randint(keys[0], (), 1, SPK - 1)
    groups = jax.random.randint(keys[1], (total,), 0, SPK - 1)
    groups = groups + (groups >= missing).astype(jnp.int32)
    groups = jnp.where(index == 0, 0, groups)
    groups = jnp.where(index == total - 1, SPK - 1, groups)
    return groups.astype(jnp.int32)


def place_ends(array, key, low, high):
    spot = [jax.random.randint(jax.random.fold_in(key, axis), (), 0, length) for axis, length in enumerate(array.shape)]
    longest = array.shape.index(max(array.shape))
    next_to = spot[:longest] + [(spot[longest] + 1) % array.shape[longest]] + spot[longest + 1:]
    return array.at[tuple(spot)].set(low).at[tuple(next_to)].set(high)


def steps_of(key, shape, shards, low, top_value):
    loudness = 1.0
    for dim, parts in shards:
        heights = jax.random.uniform(jax.random.fold_in(jax.random.fold_in(key, 6), dim), (parts,), jnp.float32, low / len(shards), top_value / len(shards))
        loudness = loudness * jnp.repeat(jnp.exp(heights), shape[dim] // parts).reshape((-1,) + (1,) * (len(shape) - 1 - dim))
    return loudness


def normal_values(own_key, extent, scale, limit, cuts=(), kind=jnp.bfloat16):
    gain = steps_of(own_key, extent, cuts, -0.22, 0.18) if cuts else 1.0
    entries = jax.random.normal(own_key, extent, jnp.float32) * scale * gain
    return jnp.minimum(jnp.maximum(entries, -limit), limit).astype(kind)


def setup_inputs(seed: int = 0) -> dict:
    key_of = jax.random.split(jax.random.key(seed), 37)
    clean_mel = normal_values(key_of[0], (FRAMES_ALL, MEL), 1.0, 6.0, ((0, 32),), jnp.float32)
    gauss_noise = normal_values(key_of[1], (FRAMES_ALL, MEL), 1.0, 6.0, ((0, 32),), jnp.float32)
    flow_time = jnp.clip(1.0 * jax.random.uniform(key_of[2], (UTTS,), jnp.float32) ** steps_of(key_of[2], (UTTS,), ((0, 32),), -0.2, 0.2), 0.0, 1.0)
    phone_ids = place_ends(jax.random.randint(key_of[3], (FRAMES_ALL,), 0, PHONES), jax.random.fold_in(key_of[3], 1), 0, PHONES - 1).astype(jnp.int32)
    lengths = draw_lengths(jax.random.fold_in(key_of[36], 71), 0)
    span_start = draw_span_start(jax.random.fold_in(key_of[36], 71), 0)
    span_end = draw_span_end(jax.random.fold_in(key_of[36], 71), 0)
    speaker = draw_speaker(jax.random.fold_in(key_of[36], 71), 0)
    skip_states = normal_values(key_of[8], (FRAMES_ALL, D), 1.0, 6.0, ((0, 32),))
    w_input = normal_values(key_of[9], (IN_W, D), IN_W ** -0.5, 0.25, ((1, 32),), jnp.float32)
    phone_table = normal_values(key_of[10], (PHONES, PD), 1.0, 5.0, ((1, 32),), jnp.float32)
    w_skip = normal_values(key_of[11], (2 * D, D), (2 * D) ** -0.5, 0.125, ((0, 32),), jnp.float32)
    w_attend = normal_values(key_of[12], (D, 3 * D), D ** -0.5, 0.1875, ((0, 32),), jnp.float32)
    w_output = normal_values(key_of[13], (D, D), (D // 4) ** -0.5, 0.375, ((0, 32),), jnp.float32)
    w_expand = normal_values(key_of[14], (D, FF), D ** -0.5, 0.1875, ((0, 32),), jnp.float32)
    w_reduce = normal_values(key_of[15], (FF, D), FF ** -0.5, 0.09375, ((0, 32),), jnp.float32)
    w_head = normal_values(key_of[16], (D, MEL), D ** -0.5, 0.1875, ((0, 32),), jnp.float32)
    norm_gains = draw_norm_gains(jax.random.fold_in(key_of[36], 71), 0)
    moment_input = normal_values(key_of[18], (IN_W, D), (PARAMS ** -0.5), 0.0014648438, ((1, 32),), jnp.float32)
    moment_table = normal_values(key_of[19], (PHONES, PD), (0.35 * D ** 0.5 * (IN_W * PHONES * PARAMS) ** -0.5), 6.103515625e-05, ((1, 32),), jnp.float32)
    moment_skip = normal_values(key_of[20], (2 * D, D), (PARAMS ** -0.5), 0.0014648438, ((0, 32),), jnp.float32)
    moment_attend = normal_values(key_of[21], (D, 3 * D), (PARAMS ** -0.5), 0.0014648438, ((0, 32),), jnp.float32)
    moment_output = normal_values(key_of[22], (D, D), (PARAMS ** -0.5), 0.0014648438, ((0, 32),), jnp.float32)
    moment_expand = normal_values(key_of[23], (D, FF), (PARAMS ** -0.5), 0.0014648438, ((0, 32),), jnp.float32)
    moment_reduce = normal_values(key_of[24], (FF, D), (PARAMS ** -0.5), 0.0014648438, ((0, 32),), jnp.float32)
    moment_head = normal_values(key_of[25], (D, MEL), (PARAMS ** -0.5), 0.0014648438, ((0, 32),), jnp.float32)
    moment_gains = normal_values(key_of[26], (3, D), (4 * PARAMS ** -0.5), 0.005859375, ((1, 32),), jnp.float32)
    square_input = jnp.clip(6.443830358193736e-08 + 1.9331491074581209e-07 * jax.random.uniform(key_of[27], (IN_W, D), jnp.float32) ** steps_of(key_of[27], (IN_W, D), ((1, 32),), -0.2, 0.2), 6.443830358193736e-08, 2.5775321432774945e-07)
    square_table = jnp.clip(9.205471801498888e-11 + 2.8383537881149223e-10 * jax.random.uniform(key_of[28], (PHONES, PD), jnp.float32) ** steps_of(key_of[28], (PHONES, PD), ((1, 32),), -0.2, 0.2), 9.205471801498888e-11, 3.758900968264811e-10)
    square_skip = jnp.clip(6.443830358193736e-08 + 1.9331491074581209e-07 * jax.random.uniform(key_of[29], (2 * D, D), jnp.float32) ** steps_of(key_of[29], (2 * D, D), ((0, 32),), -0.2, 0.2), 6.443830358193736e-08, 2.5775321432774945e-07)
    square_attend = jnp.clip(6.443830358193736e-08 + 1.9331491074581209e-07 * jax.random.uniform(key_of[30], (D, 3 * D), jnp.float32) ** steps_of(key_of[30], (D, 3 * D), ((0, 32),), -0.2, 0.2), 6.443830358193736e-08, 2.5775321432774945e-07)
    square_output = jnp.clip(6.443830358193736e-08 + 1.9331491074581209e-07 * jax.random.uniform(key_of[31], (D, D), jnp.float32) ** steps_of(key_of[31], (D, D), ((0, 32),), -0.2, 0.2), 6.443830358193736e-08, 2.5775321432774945e-07)
    square_expand = jnp.clip(6.443830358193736e-08 + 1.9331491074581209e-07 * jax.random.uniform(key_of[32], (D, FF), jnp.float32) ** steps_of(key_of[32], (D, FF), ((0, 32),), -0.2, 0.2), 6.443830358193736e-08, 2.5775321432774945e-07)
    square_reduce = jnp.clip(6.443830358193736e-08 + 1.9331491074581209e-07 * jax.random.uniform(key_of[33], (FF, D), jnp.float32) ** steps_of(key_of[33], (FF, D), ((0, 32),), -0.2, 0.2), 6.443830358193736e-08, 2.5775321432774945e-07)
    square_head = jnp.clip(6.443830358193736e-08 + 1.9331491074581209e-07 * jax.random.uniform(key_of[34], (D, MEL), jnp.float32) ** steps_of(key_of[34], (D, MEL), ((0, 32),), -0.2, 0.2), 6.443830358193736e-08, 2.5775321432774945e-07)
    square_gains = jnp.clip(1.0310128573109978e-06 + 3.0930385719329934e-06 * jax.random.uniform(key_of[35], (3, D), jnp.float32) ** steps_of(key_of[35], (3, D), ((1, 32),), -0.2, 0.2), 1.0310128573109978e-06, 4.124051429243991e-06)
    return {"clean_mel": clean_mel, "gauss_noise": gauss_noise, "flow_time": flow_time, "phone_ids": phone_ids, "lengths": lengths, "span_start": span_start, "span_end": span_end, "speaker": speaker, "skip_states": skip_states, "w_input": w_input, "phone_table": phone_table, "w_skip": w_skip, "w_attend": w_attend, "w_output": w_output, "w_expand": w_expand, "w_reduce": w_reduce, "w_head": w_head, "norm_gains": norm_gains, "moment_input": moment_input, "moment_table": moment_table, "moment_skip": moment_skip, "moment_attend": moment_attend, "moment_output": moment_output, "moment_expand": moment_expand, "moment_reduce": moment_reduce, "moment_head": moment_head, "moment_gains": moment_gains, "square_input": square_input, "square_table": square_table, "square_skip": square_skip, "square_attend": square_attend, "square_output": square_output, "square_expand": square_expand, "square_reduce": square_reduce, "square_head": square_head, "square_gains": square_gains}


@jax.custom_vjp
def low(v):
    return lax.optimization_barrier(v.astype(jnp.bfloat16)).astype(jnp.float32)

@jax.custom_vjp
def low_back(v):
    return v

def low_keep(v):
    return (low(v), None)

def low_pass(kept, grad):
    return (grad,)

def back_keep(v):
    return (v, None)

def back_low(kept, grad):
    return (low(grad),)
low.defvjp(low_keep, low_pass)
low_back.defvjp(back_keep, back_low)
SIGMA = 1e-05
NORM_EPS = 1e-05
LEARN_RATE = 0.01
GAIN_RATE = 0.3
BETA_ONE = 0.5
BETA_TWO = 0.5
DECAY = 0.01
ADAM_EPS = 1e-08
MASKED = -1000000000.0

def dense(left, right):
    return jnp.dot(left, right, precision=lax.Precision.HIGHEST, preferred_element_type=jnp.float32)

def time_features(flow, width):
    half = width // 2
    freqs = jnp.exp(-math.log(10000.0) * jnp.arange(half, dtype=jnp.float32) / half)
    angle = 1000.0 * flow * freqs
    return jnp.concatenate([jnp.sin(angle), jnp.cos(angle)])

def normalize(x):
    centered = x - lax.optimization_barrier(jnp.mean(x, -1, keepdims=True))
    return centered * lax.rsqrt(lax.optimization_barrier(jnp.mean(centered * centered, -1, keepdims=True)) + NORM_EPS)

def head_slopes(heads):
    return 2.0 ** (-8.0 * (jnp.arange(heads, dtype=jnp.float32) + 1.0) / heads)

def utterance_sums(weights, clean_mel, gauss_noise, flow, phone_ids, length, start, finish, skip, speaker_hot):
    w_input, phone_table, w_skip, w_attend, w_output, w_expand, w_reduce, w_head, norm_gains = weights
    frames = clean_mel.shape[0]
    width = w_skip.shape[1]
    heads = width // HD
    position = jnp.arange(frames)
    frame_valid = (position < length).astype(jnp.float32)
    frame_inside = ((position >= start) & (position < finish)).astype(jnp.float32) * frame_valid
    noisy_mel = (1.0 - (1.0 - SIGMA) * flow) * gauss_noise + flow * clean_mel
    context = clean_mel * (frame_valid - frame_inside)[:, None]
    target = clean_mel - (1.0 - SIGMA) * gauss_noise
    features = low(low_back(jnp.concatenate([noisy_mel, context, phone_table[phone_ids]], 1)))
    start_state = dense(features, w_input) + time_features(flow, width)[None, :]
    joined = low(jnp.concatenate([low_back(start_state), skip], 1))
    stream = low_back(dense(joined, w_skip))
    attn_in = low(normalize(stream) * norm_gains[0])
    packed = low(low_back(dense(attn_in, w_attend)))
    query = packed[:, :width].reshape(frames, heads, HD)
    keys = packed[:, width:2 * width].reshape(frames, heads, HD)
    values = packed[:, 2 * width:].reshape(frames, heads, HD)
    dist = jnp.abs(position[:, None] - position[None, :]).astype(jnp.float32)
    scores = jnp.einsum('qhd,khd->hqk', query, keys, precision=lax.Precision.HIGHEST) * HD ** (-0.5)
    scores = scores - head_slopes(heads)[:, None, None] * dist[None]
    scores = low_back(jnp.where(frame_valid[None, None, :] > 0, scores, MASKED))
    attn_probs = low(jax.nn.softmax(scores, axis=-1))
    mixed = jnp.einsum('hqk,khd->qhd', attn_probs, values, precision=lax.Precision.HIGHEST)
    mixed = low(low_back(mixed.reshape(frames, width)))
    stream_mid = stream + low_back(dense(mixed, w_output))
    ffn_in = low(normalize(stream_mid) * norm_gains[1])
    hidden = low_back(dense(ffn_in, w_expand))
    activated = low(jax.nn.gelu(hidden, approximate=False))
    stream_out = stream_mid + low_back(dense(activated, w_reduce))
    head_in = low(normalize(stream_out) * norm_gains[2])
    prediction = low_back(dense(head_in, w_head))
    error = prediction - target
    frame_error = lax.optimization_barrier(jnp.sum(error * error, 1)) * frame_inside
    return jnp.sum(frame_error) * speaker_hot

def group_sums(weights, pieces):
    return lax.optimization_barrier(jnp.sum(jax.vmap(partial(utterance_sums, weights))(*pieces), 0))

def objective(masters, pieces, counts):
    rounded = tuple((low(w) for w in masters))
    step_fn = jax.checkpoint(group_sums)

    def add_group(carry, piece):
        return (carry + step_fn(rounded, piece), None)
    sums, unused = lax.scan(add_group, jnp.zeros((SPK,), jnp.float32), pieces)
    return jnp.mean(sums / jnp.maximum(counts, 1.0))

def adam_step(master, grad, moment, square, rate):
    moment = BETA_ONE * moment + (1.0 - BETA_ONE) * grad
    square = BETA_TWO * square + (1.0 - BETA_TWO) * grad * grad
    moment_hat = moment / (1.0 - BETA_ONE ** STEP)
    square_hat = square / (1.0 - BETA_TWO ** STEP)
    master = master - rate * (moment_hat / (jnp.sqrt(square_hat) + ADAM_EPS) + DECAY * master)
    return (master, moment, square)

def reference(clean_mel, gauss_noise, flow_time, phone_ids, lengths, span_start, span_end, speaker, skip_states, w_input, phone_table, w_skip, w_attend, w_output, w_expand, w_reduce, w_head, norm_gains, moment_input, moment_table, moment_skip, moment_attend, moment_output, moment_expand, moment_reduce, moment_head, moment_gains, square_input, square_table, square_skip, square_attend, square_output, square_expand, square_reduce, square_head, square_gains):
    masters = (w_input, phone_table, w_skip, w_attend, w_output, w_expand, w_reduce, w_head, norm_gains)
    moments = (moment_input, moment_table, moment_skip, moment_attend, moment_output, moment_expand, moment_reduce, moment_head, moment_gains)
    squares = (square_input, square_table, square_skip, square_attend, square_output, square_expand, square_reduce, square_head, square_gains)
    rates = (LEARN_RATE, GAIN_RATE, LEARN_RATE, LEARN_RATE, LEARN_RATE, LEARN_RATE, LEARN_RATE, LEARN_RATE, GAIN_RATE)
    utts = lengths.shape[0]
    frames = clean_mel.shape[0] // utts
    group = math.gcd(utts, max(1, 4096 // frames))
    blocks = utts // group
    speaker_hot = (speaker[:, None] == jnp.arange(SPK)[None, :]).astype(jnp.float32)
    counts = lax.optimization_barrier(jnp.sum(speaker_hot * (span_end - span_start).astype(jnp.float32)[:, None], 0))

    def frame_view(x):
        return x.reshape((blocks, group, frames) + x.shape[1:])

    def utt_view(x):
        return x.reshape((blocks, group) + x.shape[1:])
    pieces = (frame_view(clean_mel), frame_view(gauss_noise), utt_view(flow_time), frame_view(phone_ids), utt_view(lengths), utt_view(span_start), utt_view(span_end), frame_view(skip_states.astype(jnp.float32)), utt_view(speaker_hot))
    loss_value, pullback = jax.vjp(partial(objective, pieces=pieces, counts=counts), masters)
    grads = pullback(jnp.ones((), loss_value.dtype))[0]
    total = sum((jnp.sum(g * g) for g in grads))
    grad_norm = jnp.sqrt(total)
    clip = jnp.minimum(1.0, 1.0 / (grad_norm + 1e-06))
    results = [adam_step(w, g * clip, m, s, r) for w, g, m, s, r in zip(masters, grads, moments, squares, rates)]
    next_weights = tuple((r[0] for r in results))
    next_moments = tuple((r[1] for r in results))
    next_squares = tuple((r[2] for r in results))
    return (loss_value, grad_norm) + next_weights + next_moments + next_squares
```

```python
from functools import partial
import math

import jax
import jax.numpy as jnp
from jax import lax
from jax.experimental import pallas as pl
from jax.experimental.pallas import tpu as pltpu
from jax.sharding import PartitionSpec as P

HD = 64
SPK = 16
STEP = 10


SIGMA = 1e-05
NORM_EPS = 1e-05
LEARN_RATE = 0.01
GAIN_RATE = 0.3
BETA_ONE = 0.5
BETA_TWO = 0.5
DECAY = 0.01
ADAM_EPS = 1e-08
MASKED = -1000000000.0
VMEM = 48 * 1024 * 1024


def as_low(x):
    return x.astype(jnp.bfloat16)


def matmul(left, right):
    return jnp.dot(left, right, preferred_element_type=jnp.float32)


def contract_rows(left, right):
    return lax.dot_general(
        left, right, (((0,), (0,)), ((), ())), preferred_element_type=jnp.float32
    )


def contract_cols(left, right):
    return lax.dot_general(
        left, right, (((1,), (1,)), ((), ())), preferred_element_type=jnp.float32
    )


def time_features(flow, width):
    half = width // 2
    freqs = jnp.exp(-math.log(10000.0) * jnp.arange(half, dtype=jnp.float32) / half)
    angle = 1000.0 * flow * freqs
    return jnp.concatenate([jnp.sin(angle), jnp.cos(angle)])


def normalize(x):
    centered = x - jnp.mean(x, -1, keepdims=True)
    inverse = lax.rsqrt(jnp.mean(centered * centered, -1, keepdims=True) + NORM_EPS)
    return (centered * inverse, inverse)


def normalize_back(grad, normed, inverse):
    return inverse * (
        grad
        - jnp.mean(grad, -1, keepdims=True)
        - normed * jnp.mean(grad * normed, -1, keepdims=True)
    )


def head_slopes(heads):
    return 2.0 ** (-8.0 * (jnp.arange(heads, dtype=jnp.float32) + 1.0) / heads)


def attention_scores(query, keys, frame_valid):
    frames, heads = (query.shape[0], query.shape[1])
    position = jnp.arange(frames)
    dist = jnp.abs(position[:, None] - position[None, :]).astype(jnp.float32)
    scores = jnp.einsum("qhd,khd->hqk", query, keys, preferred_element_type=jnp.float32) * HD ** (
        -0.5
    )
    scores = scores - head_slopes(heads)[:, None, None] * dist[None]
    return jnp.where(frame_valid[None, None, :] > 0, scores, MASKED)


def adam_step(master, grad, moment, square, rate):
    moment = BETA_ONE * moment + (1.0 - BETA_ONE) * grad
    square = BETA_TWO * square + (1.0 - BETA_TWO) * grad * grad
    moment_hat = moment / (1.0 - BETA_ONE**STEP)
    square_hat = square / (1.0 - BETA_TWO**STEP)
    master = master - rate * (moment_hat / (jnp.sqrt(square_hat) + ADAM_EPS) + DECAY * master)
    return (master, moment, square)


AXES = ("wide", "narrow")


def grid_sizes(wide, narrow):
    low = 1
    while (2 * low) * (2 * low) <= wide:
        low *= 2
    return (wide // low, low, narrow // 2, 2)


class Grid:
    def __init__(self, mesh):
        self.sizes = grid_sizes(mesh.shape["wide"], mesh.shape["narrow"])
        self.total = mesh.shape["wide"] * mesh.shape["narrow"]

    def coords(self, index):
        out = []
        for size in reversed(self.sizes):
            out.append(index % size)
            index = index // size
        return out[::-1]

    def index(self, coords):
        index = 0
        for size, value in zip(self.sizes, coords):
            index = index * size + value
        return index

    def mixed(self):
        return self.sizes[1] == self.sizes[2]

    def axis(self, role, core):
        if role == "z":
            return 0
        if role == "core":
            return 3
        if self.mixed():
            return (2, 1)[core] if role == "far" else (1, 2)[core]
        return 2 if role == "far" else 1

    def size(self, role):
        return self.sizes[self.axis(role, 0)]

    def pairs(self, role, step):
        out = []
        for source in range(self.total):
            coords = self.coords(source)
            axis = self.axis(role, coords[3])
            coords[axis] = (coords[axis] + step) % self.sizes[axis]
            out.append((source, self.index(coords)))
        return out

    def owners(self, core_step, direction):
        me = self.coords(lax.axis_index(AXES))
        core = (me[3] + core_step) % 2
        far, near, deep = (self.size(r) for r in ("far", "near", "z"))
        f, n, k = jnp.meshgrid(jnp.arange(far), jnp.arange(near), jnp.arange(deep), indexing="ij")
        z = (me[0] + direction * k) % self.sizes[0]
        if self.mixed():
            y = jnp.where(core == 0, me[1] + direction * n, me[1] + direction * f) % self.sizes[1]
            x = jnp.where(core == 0, me[2] + direction * f, me[2] + direction * n) % self.sizes[2]
        else:
            y = (me[1] + direction * n) % self.sizes[1]
            x = (me[2] + direction * f) % self.sizes[2]
        return self.index((z, y, x, core)).reshape(-1).astype(jnp.int32)


def shift(grid, x, role, step):
    return lax.ppermute(x, AXES, grid.pairs(role, step))


def tied(x, *others):
    return lax.optimization_barrier((x,) + others)[0]


def spread(grid, x, role):
    return [x] + [shift(grid, x, role, step) for step in range(1, grid.size(role))]


def gather(grid, x, after):
    if after is not None:
        x = tied(x, after)
    deep = jnp.stack(spread(grid, x, "z"))
    near = jnp.concatenate(spread(grid, deep, "near"))
    far = jnp.concatenate(spread(grid, near, "far"))
    other = shift(grid, far, "core", 1)
    return far, other, deep


def place_kernel(rows, own_ref, other_ref, far_ref, core_ref, *refs):
    outs, sem = refs[:-1], refs[-1]
    copies = []
    for idx, source in ((own_ref, far_ref), (other_ref, core_ref)):
        for i in range(source.shape[0]):
            start = 0
            for out, count in zip(outs, rows):
                copy = pltpu.make_async_copy(
                    source.at[i, pl.ds(start, count)], out.at[idx[i]], sem
                )
                copy.start()
                copies.append(copy)
                start += count
    for copy in copies:
        copy.wait()


def place(rows, own, other, far, core):
    total = 2 * far.shape[0]
    width = far.shape[2]
    return pl.pallas_call(
        partial(place_kernel, rows),
        out_shape=[jax.ShapeDtypeStruct((total, r, width), far.dtype) for r in rows],
        in_specs=[pl.BlockSpec(memory_space=pltpu.SMEM)] * 2 + [pl.BlockSpec(memory_space=pl.ANY)] * 2,
        out_specs=[pl.BlockSpec(memory_space=pltpu.VMEM)] * len(rows),
        scratch_shapes=[pltpu.SemaphoreType.DMA],
        compiler_params=pltpu.CompilerParams(vmem_limit_bytes=VMEM),
        cost_estimate=pl.CostEstimate(
            flops=0, transcendentals=0, bytes_accessed=4 * total * sum(rows) * width
        ),
        name="place",
    )(own, other, far, core)


def pick_kernel(rows, idx_ref, *refs):
    out = refs[-1]
    start = 0
    for ref, count in zip(refs[:-1], rows):
        out[0, start : start + count] = ref[0]
        start += count


def pick(parts, idx):
    rows = [p.shape[1] for p in parts]
    width = parts[0].shape[2]
    count = idx.shape[0]
    return pl.pallas_call(
        partial(pick_kernel, rows),
        grid_spec=pltpu.PrefetchScalarGridSpec(
            num_scalar_prefetch=1,
            grid=(count,),
            in_specs=[pl.BlockSpec((1, r, width), lambda i, idx: (idx[i], 0, 0)) for r in rows],
            out_specs=pl.BlockSpec((1, sum(rows), width), lambda i, idx: (i, 0, 0)),
        ),
        out_shape=jax.ShapeDtypeStruct((count, sum(rows), width), parts[0].dtype),
        cost_estimate=pl.CostEstimate(
            flops=0, transcendentals=0, bytes_accessed=4 * count * sum(rows) * width
        ),
        name="pick",
    )(idx, *parts)


def fold_kernel(rows, far, idx_ref, *refs):
    outs = refs[-far:]
    came = refs[-2 * far : -far]
    start = 0
    for w, count in enumerate(rows):
        for f in range(far):
            part = refs[w * far + f]
            total = part[0].astype(jnp.float32) + came[f][0, start : start + count].astype(jnp.float32)
            outs[f][0, start : start + count] = total.astype(outs[f].dtype)
        start += count


def fold(parts, came, idx, far):
    rows = [p.shape[1] for p in parts]
    width = parts[0].shape[2]
    count = idx.shape[0] // far
    height = sum(rows)

    def part_map(f, i, idx):
        return (idx[f * count + i], 0, 0)

    def came_map(f, i, idx):
        return (f * count + i, 0, 0)

    return pl.pallas_call(
        partial(fold_kernel, rows, far),
        grid_spec=pltpu.PrefetchScalarGridSpec(
            num_scalar_prefetch=1,
            grid=(count,),
            in_specs=[
                pl.BlockSpec((1, r, width), partial(part_map, f)) for r in rows for f in range(far)
            ]
            + [pl.BlockSpec((1, height, width), partial(came_map, f)) for f in range(far)],
            out_specs=[pl.BlockSpec((1, height, width), lambda i, idx: (i, 0, 0))] * far,
        ),
        out_shape=[jax.ShapeDtypeStruct((count, height, width), jnp.bfloat16)] * far,
        compiler_params=pltpu.CompilerParams(vmem_limit_bytes=VMEM),
        cost_estimate=pl.CostEstimate(
            flops=0, transcendentals=0, bytes_accessed=6 * far * count * height * width
        ),
        name="fold",
    )(idx, *[p for p in parts for _ in range(far)], *[came] * far)


def scatter(grid, parts, mine, theirs, after):
    sent = pick(parts, theirs)
    if after is not None:
        sent = tied(sent, after)
    came = shift(grid, sent, "core", 1)
    far, near, deep = (grid.size(r) for r in ("far", "near", "z"))
    legs = fold(parts, came, mine, far)
    moved = [shift(grid, legs[f], "far", f) for f in range(1, far)]
    legs = [
        as_low(
            sum(leg[n * deep : (n + 1) * deep].astype(jnp.float32) for leg in [legs[0]] + moved)
        )
        for n in range(near)
    ]
    first = moved[0] if moved else None
    moved = [shift(grid, legs[n], "near", n) for n in range(1, near)]
    legs = [sum(leg[k].astype(jnp.float32) for leg in [legs[0]] + moved) for k in range(deep)]
    moved = [shift(grid, as_low(legs[k]), "z", k) for k in range(1, deep)]
    return sum((m.astype(jnp.float32) for m in moved), legs[0]), first


def all_sum(grid, x):
    step = 1
    while step < grid.total:
        x = x + lax.ppermute(x, AXES, [(i, i ^ step) for i in range(grid.total)])
        step *= 2
    return x


def shards(
    grid,
    fast,
    clean_mel,
    gauss_noise,
    flow_time,
    phone_ids,
    lengths,
    span_start,
    span_end,
    speaker,
    skip_states,
    w_input,
    phone_table,
    w_skip,
    w_attend,
    w_output,
    w_expand,
    w_reduce,
    w_head,
    norm_gains,
    moment_input,
    moment_table,
    moment_skip,
    moment_attend,
    moment_output,
    moment_expand,
    moment_reduce,
    moment_head,
    moment_gains,
    square_input,
    square_table,
    square_skip,
    square_attend,
    square_output,
    square_expand,
    square_reduce,
    square_head,
    square_gains,
):
    masters = (w_input, phone_table, w_skip, w_attend, w_output, w_expand, w_reduce, w_head, norm_gains)
    moments = (
        moment_input, moment_table, moment_skip, moment_attend, moment_output,
        moment_expand, moment_reduce, moment_head, moment_gains,
    )
    squares = (
        square_input, square_table, square_skip, square_attend, square_output,
        square_expand, square_reduce, square_head, square_gains,
    )
    rates = (LEARN_RATE, GAIN_RATE) + (LEARN_RATE,) * 6 + (GAIN_RATE,)
    frames, mel_bins = clean_mel.shape
    width = w_skip.shape[1]
    heads = width // HD
    devices = grid.total
    unit = width // devices
    inputs = w_input.shape[0]
    phones = phone_table.shape[0]
    phone_width = phone_table.shape[1] * devices
    table_lanes = phone_table.shape[0] * phone_table.shape[1] // unit
    at_table = inputs
    at_head = at_table + table_lanes
    at_gain = at_head + mel_bins
    at_count = at_gain + 3
    position = jnp.arange(frames)
    frame_valid = (position < lengths[0]).astype(jnp.float32)
    frame_inside = ((position >= span_start[0]) & (position < span_end[0])).astype(
        jnp.float32
    ) * frame_valid
    speaker_hot = (speaker[0] == jnp.arange(SPK)).astype(jnp.float32)
    count = jnp.sum(frame_inside)
    count_high = jnp.floor(count / 16.0)
    tally = jnp.stack([speaker[0].astype(jnp.float32), count_high, count - 16.0 * count_high])

    small = jnp.concatenate(
        [
            w_input.T,
            phone_table.T.reshape(unit, table_lanes),
            w_head,
            norm_gains.T,
            jnp.broadcast_to(tally[None, :], (unit, 3)),
            jnp.zeros((unit, width - at_count - 3), jnp.float32),
        ],
        1,
    )

    def blocks(x):
        return [as_low(x[:, j : j + width]) for j in range(0, x.shape[1], width)]

    attend_rows = blocks(w_attend)
    expand_rows = blocks(w_expand)
    half = len(expand_rows) // 2
    stages = [
        [as_low(small), as_low(w_skip)],
        attend_rows,
        [as_low(w_output)] + expand_rows[:half],
        expand_rows[half:],
        [as_low(w_reduce)],
    ]
    if fast:
        own, other = grid.owners(0, -1), grid.owners(1, -1)
    fulls = []
    after = None
    for stage in stages:
        rows = [w.shape[0] for w in stage]
        load = jnp.concatenate(stage, 0)
        if fast:
            far, core, after = gather(grid, load, after)
            full = place(rows, own, other, far, core)
        else:
            whole = lax.all_gather(load, AXES, axis=0, tiled=False)
            ends = [sum(rows[:j]) for j in range(len(rows) + 1)]
            full = [whole[:, a:b] for a, b in zip(ends, ends[1:])]
        fulls.append([f.reshape(-1, width) for f in full])
    small_full, skip_full = fulls[0]
    attend_full = fulls[1]
    output_full = fulls[2][0]
    expand_full = fulls[2][1:] + fulls[3]
    reduce_full = fulls[4][0]
    input_turned = small_full[:, :inputs]
    table_full = small_full[:, at_table:at_head].reshape(phone_width, phones).T
    head_full = small_full[:, at_head:at_gain]
    gains_wide = small_full[:, at_gain:at_count].astype(jnp.float32).T
    tallies = small_full.reshape(devices, unit, width)[:, 0, at_count : at_count + 3].astype(
        jnp.float32
    )
    counts = jnp.sum(
        (tallies[:, :1] == jnp.arange(SPK, dtype=jnp.float32)[None, :])
        * (16.0 * tallies[:, 1:2] + tallies[:, 2:3]),
        0,
    )

    flow = flow_time[0]
    noisy_mel = (1.0 - (1.0 - SIGMA) * flow) * gauss_noise + flow * clean_mel
    context = clean_mel * (frame_valid - frame_inside)[:, None]
    target = clean_mel - (1.0 - SIGMA) * gauss_noise
    phone_hot = as_low(phone_ids[:, None] == jnp.arange(phones)[None, :])
    embedded = as_low(matmul(phone_hot, table_full))
    features = jnp.concatenate([as_low(noisy_mel), as_low(context), embedded], 1)
    start_state = contract_cols(features, input_turned) + time_features(flow, width)[None, :]
    joined = jnp.concatenate([as_low(start_state), skip_states], 1)
    stream = matmul(joined, skip_full)
    normed_one, inverse_one = normalize(stream)
    attn_in = as_low(normed_one * gains_wide[0])
    query, keys, values = [
        as_low(matmul(attn_in, w)).reshape(frames, heads, HD) for w in attend_full
    ]
    scores = attention_scores(query, keys, frame_valid)
    top_score = jnp.max(scores, -1, keepdims=True)
    expo = jnp.exp(scores - top_score)
    exp_total = jnp.sum(expo, -1, keepdims=True)
    log_total = top_score + jnp.log(exp_total)
    attn_probs = as_low(expo / exp_total)
    mixed = as_low(
        jnp.einsum("hqk,khd->qhd", attn_probs, values, preferred_element_type=jnp.float32).reshape(
            frames, width
        )
    )
    stream_mid = stream + matmul(mixed, output_full)
    normed_two, inverse_two = normalize(stream_mid)
    ffn_in = as_low(normed_two * gains_wide[1])
    hidden = [matmul(ffn_in, w) for w in expand_full]
    activated = [as_low(jax.nn.gelu(h, approximate=False)) for h in hidden]
    stream_out = stream_mid + matmul(jnp.concatenate(activated, 1), reduce_full)
    normed_three, inverse_three = normalize(stream_out)
    head_in = as_low(normed_three * gains_wide[2])
    prediction = matmul(head_in, head_full)
    error = prediction - target
    frame_error = jnp.sum(error * error, 1) * frame_inside
    local_sum = speaker_hot * jnp.sum(frame_error)
    share = jnp.sum(speaker_hot / jnp.maximum(counts, 1.0)) / SPK
    d_prediction = as_low(2.0 * share * error * frame_inside[:, None])
    grad_head = contract_rows(head_in, d_prediction)
    d_head_in = contract_cols(d_prediction, head_full)
    grad_gain_three = jnp.sum(d_head_in * normed_three, 0)
    d_stream_out = normalize_back(d_head_in * gains_wide[2], normed_three, inverse_three)
    d_branch = as_low(d_stream_out)
    if fast:
        mine, theirs = grid.owners(0, 1), grid.owners(1, 1)
    chain = [None]

    def send(parts):
        rows = [p.shape[0] // devices for p in parts]
        if fast:
            low_parts = [as_low(p).reshape(devices, r, width) for p, r in zip(parts, rows)]
            total, chain[0] = scatter(grid, low_parts, mine, theirs, chain[0])
        else:
            parts = [p.reshape(devices, r, width) for p, r in zip(parts, rows)]
            total = lax.psum_scatter(jnp.concatenate(parts, 1), AXES, scatter_dimension=0)
        ends = [sum(rows[:j]) for j in range(len(rows) + 1)]
        return [total[a:b] for a, b in zip(ends, ends[1:])]

    (share_reduce,) = send([jnp.concatenate([contract_rows(a, d_branch) for a in activated], 0)])
    count_wide = len(activated)
    d_hidden = []
    for j in range(count_wide):
        d_activated = contract_cols(d_branch, reduce_full[j * width : (j + 1) * width])
        gelu_pull = jax.vjp(partial(jax.nn.gelu, approximate=False), hidden[j])[1]
        d_hidden.append(as_low(gelu_pull(d_activated)[0]))
    share_expand = send([contract_rows(ffn_in, d) for d in d_hidden])
    d_ffn_in = sum(contract_cols(d, w) for d, w in zip(d_hidden, expand_full))
    grad_gain_two = jnp.sum(d_ffn_in * normed_two, 0)
    d_stream_mid = d_stream_out + normalize_back(d_ffn_in * gains_wide[1], normed_two, inverse_two)
    d_out = as_low(d_stream_mid)
    grad_output = contract_rows(mixed, d_out)
    d_mixed = as_low(contract_cols(d_out, output_full)).reshape(frames, heads, HD)
    probs_full = jnp.exp(attention_scores(query, keys, frame_valid) - log_total)
    d_probs = jnp.einsum("qhd,khd->hqk", d_mixed, values, preferred_element_type=jnp.float32)
    d_values = jnp.einsum("hqk,qhd->khd", attn_probs, d_mixed, preferred_element_type=jnp.float32)
    row_dot = jnp.sum(d_probs * probs_full, -1, keepdims=True)
    d_scores = as_low(probs_full * (d_probs - row_dot))
    d_query = jnp.einsum(
        "hqk,khd->qhd", d_scores, keys, preferred_element_type=jnp.float32
    ) * HD ** (-0.5)
    d_keys = jnp.einsum(
        "hqk,qhd->khd", d_scores, query, preferred_element_type=jnp.float32
    ) * HD ** (-0.5)
    d_packed = [as_low(d.reshape(frames, width)) for d in (d_query, d_keys, d_values)]
    share_output, *share_attend = send([grad_output] + [contract_rows(attn_in, d) for d in d_packed])
    d_attn_in = sum(contract_cols(d, w) for d, w in zip(d_packed, attend_full))
    grad_gain_one = jnp.sum(d_attn_in * normed_one, 0)
    d_stream = d_stream_mid + normalize_back(d_attn_in * gains_wide[0], normed_one, inverse_one)
    d_joined_in = as_low(d_stream)
    grad_skip = contract_rows(joined, d_joined_in)
    d_start = as_low(contract_cols(d_joined_in, skip_full[:width]))
    grad_input = contract_rows(d_start, features)
    d_phones = as_low(matmul(d_start, input_turned[:, 2 * mel_bins :]))
    grad_table = contract_rows(d_phones, phone_hot)
    grad_small = jnp.concatenate(
        [
            grad_input,
            grad_table.reshape(width, table_lanes),
            grad_head,
            jnp.stack([grad_gain_one, grad_gain_two, grad_gain_three], 1),
            jnp.zeros((width, width - at_count), jnp.float32),
        ],
        1,
    )
    share_skip, share_small = send([grad_skip, grad_small])
    shares = (
        share_small[:, :inputs].T,
        share_small[:, at_table:at_head].reshape(phone_width // devices, phones).T,
        share_skip,
        jnp.concatenate(share_attend, 1),
        share_output,
        jnp.concatenate(share_expand, 1),
        share_reduce,
        share_small[:, at_head:at_gain],
        share_small[:, at_gain:at_count].T,
    )
    local_square = sum((jnp.sum(g * g) for g in shares))
    totals = all_sum(grid, jnp.concatenate([local_sum, local_square[None]]))
    sums, total_square = totals[:SPK], totals[SPK]
    loss_value = jnp.mean(sums / jnp.maximum(counts, 1.0))
    grad_norm = jnp.sqrt(total_square)
    clip = jnp.minimum(1.0, 1.0 / (grad_norm + 1e-06))
    results = [
        adam_step(w, g * clip, m, s, r)
        for w, g, m, s, r in zip(masters, shares, moments, squares, rates)
    ]
    next_weights = tuple((r[0] for r in results))
    next_moments = tuple((r[1] for r in results))
    next_squares = tuple((r[2] for r in results))
    return (loss_value, grad_norm) + next_weights + next_moments + next_squares


def solution(mesh):
    grid = Grid(mesh)
    in_specs = (
        P(("wide", "narrow"), None),
        P(("wide", "narrow"), None),
        P(("wide", "narrow")),
        P(("wide", "narrow")),
        P(("wide", "narrow")),
        P(("wide", "narrow")),
        P(("wide", "narrow")),
        P(("wide", "narrow")),
        P(("wide", "narrow"), None),
        P(None, ("wide", "narrow")),
        P(None, ("wide", "narrow")),
        P(("wide", "narrow"), None),
        P(("wide", "narrow"), None),
        P(("wide", "narrow"), None),
        P(("wide", "narrow"), None),
        P(("wide", "narrow"), None),
        P(("wide", "narrow"), None),
        P(None, ("wide", "narrow")),
        P(None, ("wide", "narrow")),
        P(None, ("wide", "narrow")),
        P(("wide", "narrow"), None),
        P(("wide", "narrow"), None),
        P(("wide", "narrow"), None),
        P(("wide", "narrow"), None),
        P(("wide", "narrow"), None),
        P(("wide", "narrow"), None),
        P(None, ("wide", "narrow")),
        P(None, ("wide", "narrow")),
        P(None, ("wide", "narrow")),
        P(("wide", "narrow"), None),
        P(("wide", "narrow"), None),
        P(("wide", "narrow"), None),
        P(("wide", "narrow"), None),
        P(("wide", "narrow"), None),
        P(("wide", "narrow"), None),
        P(None, ("wide", "narrow")),
    )
    out_specs = (
        P(),
        P(),
        P(None, ("wide", "narrow")),
        P(None, ("wide", "narrow")),
        P(("wide", "narrow"), None),
        P(("wide", "narrow"), None),
        P(("wide", "narrow"), None),
        P(("wide", "narrow"), None),
        P(("wide", "narrow"), None),
        P(("wide", "narrow"), None),
        P(None, ("wide", "narrow")),
        P(None, ("wide", "narrow")),
        P(None, ("wide", "narrow")),
        P(("wide", "narrow"), None),
        P(("wide", "narrow"), None),
        P(("wide", "narrow"), None),
        P(("wide", "narrow"), None),
        P(("wide", "narrow"), None),
        P(("wide", "narrow"), None),
        P(None, ("wide", "narrow")),
        P(None, ("wide", "narrow")),
        P(None, ("wide", "narrow")),
        P(("wide", "narrow"), None),
        P(("wide", "narrow"), None),
        P(("wide", "narrow"), None),
        P(("wide", "narrow"), None),
        P(("wide", "narrow"), None),
        P(("wide", "narrow"), None),
        P(None, ("wide", "narrow")),
    )

    def body(*args):
        unit = args[11].shape[1] // grid.total
        return shards(grid, unit % 32 == 0, *args)

    return jax.shard_map(body, mesh=mesh, in_specs=in_specs, out_specs=out_specs, check_vma=False)
```

```python
from functools import partial
import math

import jax
import jax.numpy as jnp
from jax import lax
from jax.experimental import pallas as pl
from jax.experimental.pallas import tpu as pltpu
from jax.sharding import PartitionSpec as P

HD = 64
SPK = 16
STEP = 10


SIGMA = 1e-05
NORM_EPS = 1e-05
LEARN_RATE = 0.01
GAIN_RATE = 0.3
BETA_ONE = 0.5
BETA_TWO = 0.5
DECAY = 0.01
ADAM_EPS = 1e-08
FAR_AWAY = -1e30
VMEM = 56 * 1024 * 1024
TABLE_AT = 768
HEAD_AT = 896


def as_low(x):
    return x.astype(jnp.bfloat16)


def contract_rows(left, right):
    return lax.dot_general(
        left, right, (((0,), (0,)), ((), ())), preferred_element_type=jnp.float32
    )


def time_features(flow, width):
    half = width // 2
    freqs = jnp.exp(-math.log(10000.0) * jnp.arange(half, dtype=jnp.float32) / half)
    angle = 1000.0 * flow * freqs
    return jnp.concatenate([jnp.sin(angle), jnp.cos(angle)])


def normalize(x):
    centered = x - jnp.mean(x, -1, keepdims=True)
    inverse = lax.rsqrt(jnp.mean(centered * centered, -1, keepdims=True) + NORM_EPS)
    return (centered * inverse, inverse)


def normalize_back(grad, normed, inverse):
    return inverse * (
        grad
        - jnp.mean(grad, -1, keepdims=True)
        - normed * jnp.mean(grad * normed, -1, keepdims=True)
    )


def head_slopes(heads):
    return 2.0 ** (-8.0 * (jnp.arange(heads, dtype=jnp.float32) + 1.0) / heads)


def adam_step(master, grad, moment, square, rate):
    moment = BETA_ONE * moment + (1.0 - BETA_ONE) * grad
    square = BETA_TWO * square + (1.0 - BETA_TWO) * grad * grad
    moment_hat = moment / (1.0 - BETA_ONE**STEP)
    square_hat = square / (1.0 - BETA_TWO**STEP)
    master = master - rate * (moment_hat / (jnp.sqrt(square_hat) + ADAM_EPS) + DECAY * master)
    return (master, moment, square)


AXES = ("wide", "narrow")


def grid_sizes(wide, narrow):
    low = 1
    while (2 * low) * (2 * low) <= wide:
        low *= 2
    return (wide // low, low, narrow // 2, 2)


class Grid:
    def __init__(self, mesh):
        self.sizes = grid_sizes(mesh.shape["wide"], mesh.shape["narrow"])
        self.total = mesh.shape["wide"] * mesh.shape["narrow"]

    def coords(self, index):
        out = []
        for size in reversed(self.sizes):
            out.append(index % size)
            index = index // size
        return out[::-1]

    def index(self, coords):
        index = 0
        for size, value in zip(self.sizes, coords):
            index = index * size + value
        return index

    def mixed(self):
        return self.sizes[1] == self.sizes[2]

    def axis(self, role, core):
        if role == "z":
            return 0
        if role == "core":
            return 3
        if self.mixed():
            return (2, 1)[core] if role == "far" else (1, 2)[core]
        return 2 if role == "far" else 1

    def size(self, role):
        return self.sizes[self.axis(role, 0)]

    def pairs(self, role, step):
        out = []
        for source in range(self.total):
            coords = self.coords(source)
            axis = self.axis(role, coords[3])
            coords[axis] = (coords[axis] + step) % self.sizes[axis]
            out.append((source, self.index(coords)))
        return out

    def lines(self):
        deep = self.total // self.sizes[0]
        return [[z * deep + rest for z in range(self.sizes[0])] for rest in range(deep)]

    def owners(self, core_step, direction):
        me = self.coords(lax.axis_index(AXES))
        core = (me[3] + core_step) % 2
        far, near, deep = (self.size(r) for r in ("far", "near", "z"))
        f, n, z = jnp.meshgrid(jnp.arange(far), jnp.arange(near), jnp.arange(deep), indexing="ij")
        if self.mixed():
            y = jnp.where(core == 0, me[1] + direction * n, me[1] + direction * f) % self.sizes[1]
            x = jnp.where(core == 0, me[2] + direction * f, me[2] + direction * n) % self.sizes[2]
        else:
            y = (me[1] + direction * n) % self.sizes[1]
            x = (me[2] + direction * f) % self.sizes[2]
        return self.index((z, y, x, core)).reshape(-1).astype(jnp.int32)


def shift(grid, x, role, step):
    return lax.ppermute(x, AXES, grid.pairs(role, step))


def tied(x, *others):
    return lax.optimization_barrier((x,) + others)[0]


def swap_deep(grid, x):
    return lax.all_to_all(x, AXES, 0, 0, axis_index_groups=grid.lines())


def join(*xs):
    return lax.optimization_barrier(xs)


def spread(grid, x, role):
    return [x] + [shift(grid, x, role, step) for step in range(1, grid.size(role))]


def all_sum(grid, x):
    step = 1
    while step < grid.total:
        x = x + lax.ppermute(x, AXES, [(i, i ^ step) for i in range(grid.total)])
        step *= 2
    return x


def dot_nn(a, b):
    return lax.dot_general(a, b, (((1,), (0,)), ((), ())), preferred_element_type=jnp.float32)


def dot_nt(a, b):
    return lax.dot_general(a, b, (((1,), (1,)), ((), ())), preferred_element_type=jnp.float32)


def dot_tn(a, b):
    return lax.dot_general(a, b, (((0,), (0,)), ((), ())), preferred_element_type=jnp.float32)


def params():
    return pltpu.CompilerParams(vmem_limit_bytes=VMEM)


def key_bias(length, frames):
    key = lax.broadcasted_iota(jnp.int32, (frames, frames), 0)
    query = lax.broadcasted_iota(jnp.int32, (frames, frames), 1)
    dist = -jnp.abs(key - query).astype(jnp.float32)
    return jnp.where(key < length, dist, FAR_AWAY)


def attend_kernel(length_ref, slope_ref, packed_ref, mixed_ref, lse_ref, bias_ref):
    step = pl.program_id(0)
    q_ref, k_ref, v_ref = (packed_ref.at[j] for j in range(3))
    frames = q_ref.shape[0]

    @pl.when(step == 0)
    def _():
        bias_ref[...] = key_bias(length_ref[0], frames)

    parts = []
    for h in range(2):
        lanes = slice(h * HD, (h + 1) * HD)
        scores = dot_nt(k_ref[:, lanes], q_ref[:, lanes] * jnp.bfloat16(HD**-0.5))
        scores = scores + slope_ref[2 * step + h] * bias_ref[...]
        top = jnp.max(scores, 0, keepdims=True)
        expo = jnp.exp(scores - top)
        total = jnp.sum(expo, 0, keepdims=True)
        lse_ref[0, h : h + 1] = top + jnp.log(total)
        probs = as_low(expo * (1.0 / total))
        parts.append(dot_tn(v_ref[:, lanes], probs))
    mixed_ref[...] = as_low(jnp.concatenate(parts, 0).T)


def attend(length, slopes, packed):
    _, frames, width = packed.shape
    pairs = width // (2 * HD)
    block = pl.BlockSpec((frames, 2 * HD), lambda i: (0, i))
    return pl.pallas_call(
        attend_kernel,
        grid=(pairs,),
        in_specs=[pl.BlockSpec(memory_space=pltpu.SMEM)] * 2
        + [pl.BlockSpec((3, frames, 2 * HD), lambda i: (0, 0, i))],
        out_specs=[block, pl.BlockSpec((1, 2, frames), lambda i: (i, 0, 0))],
        out_shape=[
            jax.ShapeDtypeStruct((frames, width), jnp.bfloat16),
            jax.ShapeDtypeStruct((pairs, 2, frames), jnp.float32),
        ],
        scratch_shapes=[pltpu.VMEM((frames, frames), jnp.float32)],
        compiler_params=params(),
        name="attend",
    )(length, slopes, packed)


def attend_back_kernel(length_ref, slope_ref, packed_ref, d_ref, lse_ref, out_ref, bias_ref):
    step = pl.program_id(0)
    q_ref, k_ref, v_ref = (packed_ref.at[j] for j in range(3))
    frames = q_ref.shape[0]

    @pl.when(step == 0)
    def _():
        bias_ref[...] = key_bias(length_ref[0], frames)

    d_query, d_keys, d_values = [], [], []
    for h in range(2):
        lanes = slice(h * HD, (h + 1) * HD)
        query = q_ref[:, lanes] * jnp.bfloat16(HD**-0.5)
        keys, values, d_mixed = k_ref[:, lanes], v_ref[:, lanes], d_ref[:, lanes]
        scores = dot_nt(keys, query) + slope_ref[2 * step + h] * bias_ref[...]
        probs = jnp.exp(scores - lse_ref[0, h : h + 1])
        d_probs = dot_nt(values, d_mixed)
        row_dot = jnp.sum(d_probs * probs, 0, keepdims=True)
        d_scores = as_low(probs * (d_probs - row_dot))
        d_values.append(dot_nn(as_low(probs), d_mixed))
        d_keys.append(dot_nn(d_scores, query))
        d_query.append(dot_tn(keys, d_scores))
    out_ref[0] = as_low((jnp.concatenate(d_query, 0) * HD**-0.5).T)
    out_ref[1] = as_low(jnp.concatenate(d_keys, 1))
    out_ref[2] = as_low(jnp.concatenate(d_values, 1))


def attend_back(length, slopes, packed, d_mixed, lse):
    _, frames, width = packed.shape
    pairs = width // (2 * HD)
    stacked = pl.BlockSpec((3, frames, 2 * HD), lambda i: (0, 0, i))
    return pl.pallas_call(
        attend_back_kernel,
        grid=(pairs,),
        in_specs=[pl.BlockSpec(memory_space=pltpu.SMEM)] * 2
        + [stacked, pl.BlockSpec((frames, 2 * HD), lambda i: (0, i))]
        + [pl.BlockSpec((1, 2, frames), lambda i: (i, 0, 0))],
        out_specs=stacked,
        out_shape=jax.ShapeDtypeStruct((3, frames, width), jnp.bfloat16),
        scratch_shapes=[pltpu.VMEM((frames, frames), jnp.float32)],
        compiler_params=params(),
        name="attend_back",
    )(length, slopes, packed, d_mixed, lse)


def gelu_both(x):
    z = jnp.abs(x) * (0.5**0.5)
    bell = jnp.exp(-z * z)
    t = 1.0 / (1.0 + 0.3275911 * z)
    poly = t * (0.254829592 + t * (-0.284496736 + t * (1.421413741 + t * (-1.453152027 + t * 1.061405429))))
    tail = 0.5 * poly * bell
    share = jnp.where(x >= 0, 1.0 - tail, tail)
    return x * share, share + x * bell * (0.5 / math.pi) ** 0.5


def expand_kernel(x_ref, w_ref, act_ref, turned_ref, slope_ref):
    hidden = dot_nn(x_ref[...], w_ref[0])
    act, slope = gelu_both(hidden)
    act = as_low(act)
    act_ref[...] = act
    turned_ref[...] = act.T
    slope_ref[...] = as_low(slope)


def expand(x, w, tile=1024):
    frames, width = x.shape
    count, _, wide = w.shape
    per = wide // tile
    total = count * wide
    return pl.pallas_call(
        expand_kernel,
        grid=(count * per,),
        in_specs=[
            pl.BlockSpec((frames, width), lambda i: (0, 0)),
            pl.BlockSpec((1, width, tile), lambda i: (i // per, 0, i % per)),
        ],
        out_specs=[
            pl.BlockSpec((frames, tile), lambda i: (0, i)),
            pl.BlockSpec((tile, frames), lambda i: (i, 0)),
            pl.BlockSpec((frames, tile), lambda i: (0, i)),
        ],
        out_shape=[
            jax.ShapeDtypeStruct((frames, total), jnp.bfloat16),
            jax.ShapeDtypeStruct((total, frames), jnp.bfloat16),
            jax.ShapeDtypeStruct((frames, total), jnp.bfloat16),
        ],
        compiler_params=params(),
        name="expand",
    )(x, w)


def front_kernel(
    small_ref, table_ref, skip_ref, states_ref, hot_ref, mel_ref, time_ref, gain_ref,
    embed_ref, stream_ref, start_ref, normed_ref, turned_ref,
):
    phones = embed_ref.shape[1]
    width = stream_ref.shape[1]
    embedded = as_low(dot_nt(hot_ref[...], table_ref[...]))
    embed_ref[...] = embedded
    start = dot_nt(embedded, small_ref[:, :phones])
    start = start + dot_nt(mel_ref[...], small_ref[:, phones:TABLE_AT]) + time_ref[...]
    start = as_low(start)
    start_ref[...] = start.T
    stream = dot_nn(start, skip_ref[:width]) + dot_nn(states_ref[...], skip_ref[width:])
    stream_ref[...] = stream
    normed = as_low(normalize(stream)[0] * gain_ref[...])
    normed_ref[...] = normed
    turned_ref[...] = normed.T


def front(small, table, skip, states, hot, mel, time, gain):
    frames, width = states.shape
    phones = table.shape[0]
    f32, low = jnp.float32, jnp.bfloat16
    return pl.pallas_call(
        front_kernel,
        out_shape=[
            jax.ShapeDtypeStruct((frames, phones), low),
            jax.ShapeDtypeStruct((frames, width), f32),
            jax.ShapeDtypeStruct((width, frames), low),
            jax.ShapeDtypeStruct((frames, width), low),
            jax.ShapeDtypeStruct((width, frames), low),
        ],
        compiler_params=params(),
        name="front",
    )(small, table, skip, states, hot, mel, time, gain)


def pack_kernel(x_ref, w_ref, out_ref):
    out_ref[0] = as_low(dot_nn(x_ref[...], w_ref[0]))


def pack(x, w):
    frames, width = x.shape
    return pl.pallas_call(
        pack_kernel,
        grid=(w.shape[0],),
        in_specs=[
            pl.BlockSpec((frames, width), lambda i: (0, 0)),
            pl.BlockSpec((1, width, width), lambda i: (i, 0, 0)),
        ],
        out_specs=pl.BlockSpec((1, frames, width), lambda i: (i, 0, 0)),
        out_shape=jax.ShapeDtypeStruct((w.shape[0], frames, width), jnp.bfloat16),
        compiler_params=params(),
        name="pack",
    )(x, w)


def mid_kernel(mixed_ref, w_ref, stream_ref, gain_ref, mid_ref, in_ref, turned_ref, mixed_turned_ref):
    mixed = mixed_ref[...]
    mid = stream_ref[...] + dot_nn(mixed, w_ref[...])
    mid_ref[...] = mid
    normed = as_low(normalize(mid)[0] * gain_ref[...])
    in_ref[...] = normed
    turned_ref[...] = normed.T
    mixed_turned_ref[...] = mixed.T


def mid_step(mixed, w, stream, gain):
    frames, width = stream.shape
    low = jnp.bfloat16
    return pl.pallas_call(
        mid_kernel,
        out_shape=[
            jax.ShapeDtypeStruct((frames, width), jnp.float32),
            jax.ShapeDtypeStruct((frames, width), low),
            jax.ShapeDtypeStruct((width, frames), low),
            jax.ShapeDtypeStruct((width, frames), low),
        ],
        compiler_params=params(),
        name="mid",
    )(mixed, w, stream, gain)


def head_kernel(
    share_ref, act_ref, w_ref, mid_ref, head_ref, target_ref, inside_ref, gain_ref,
    d_ref, low_ref, grad_ref, gain_grad_ref, error_ref, total_ref,
):
    step = pl.program_id(0)
    part = dot_nn(act_ref[...], w_ref[...])

    @pl.when(step == 0)
    def _():
        total_ref[...] = mid_ref[...] + part

    @pl.when(step > 0)
    def _():
        total_ref[...] += part

    @pl.when(step == pl.num_programs(0) - 1)
    def _():
        bins = target_ref.shape[1]
        normed, inverse = normalize(total_ref[...])
        gain = gain_ref[...]
        head_in = as_low(normed * gain)
        head = head_ref[:, :bins]
        inside = inside_ref[...]
        error = dot_nn(head_in, head) - target_ref[...]
        error_ref[...] = jnp.sum(jnp.sum(error * error, 1, keepdims=True) * inside, 0, keepdims=True)
        d_prediction = as_low((2.0 * share_ref[0]) * error * inside)
        grad_ref[...] = dot_tn(head_in, d_prediction)
        d_head_in = dot_nt(d_prediction, head)
        gain_grad_ref[...] = jnp.sum(d_head_in * normed, 0, keepdims=True)
        d_stream = normalize_back(d_head_in * gain, normed, inverse)
        d_ref[...] = d_stream
        low_ref[...] = as_low(d_stream)


def head_step(share, act, w, mid, head, target, inside, gain, tile=1024):
    frames, width = mid.shape
    bins = target.shape[1]
    whole = lambda *shape: pl.BlockSpec(shape, lambda i: (0,) * len(shape))
    return pl.pallas_call(
        head_kernel,
        grid=(act.shape[1] // tile,),
        in_specs=[
            pl.BlockSpec(memory_space=pltpu.SMEM),
            pl.BlockSpec((frames, tile), lambda i: (0, i)),
            pl.BlockSpec((tile, width), lambda i: (i, 0)),
            whole(frames, width), whole(*head.shape), whole(frames, bins), whole(frames, 1), whole(1, width),
        ],
        out_specs=[
            whole(frames, width), whole(frames, width), whole(width, bins), whole(1, width), whole(1, 1),
        ],
        out_shape=[
            jax.ShapeDtypeStruct((frames, width), jnp.float32),
            jax.ShapeDtypeStruct((frames, width), jnp.bfloat16),
            jax.ShapeDtypeStruct((width, bins), jnp.float32),
            jax.ShapeDtypeStruct((1, width), jnp.float32),
            jax.ShapeDtypeStruct((1, 1), jnp.float32),
        ],
        scratch_shapes=[pltpu.VMEM((frames, width), jnp.float32)],
        compiler_params=params(),
        name="head",
    )(share, act, w, mid, head, target, inside, gain)


def ffn_back_kernel(
    low_ref, d_ref, down_ref, slope_ref, up_ref, mid_ref, gain_ref,
    out_ref, out_low_ref, gain_grad_ref, hidden_ref, total_ref,
):
    step = pl.program_id(0)
    d_hidden = as_low(dot_nt(low_ref[...], down_ref[...]) * slope_ref[...].astype(jnp.float32))
    hidden_ref[0] = d_hidden
    part = dot_nt(d_hidden, up_ref[0])

    @pl.when(step == 0)
    def _():
        total_ref[...] = part

    @pl.when(step > 0)
    def _():
        total_ref[...] += part

    @pl.when(step == pl.num_programs(0) - 1)
    def _():
        normed, inverse = normalize(mid_ref[...])
        grad = total_ref[...]
        gain_grad_ref[...] = jnp.sum(grad * normed, 0, keepdims=True)
        out = d_ref[...] + normalize_back(grad * gain_ref[...], normed, inverse)
        out_ref[...] = out
        out_low_ref[...] = as_low(out)


def ffn_back(low, d, down, slope, up, mid, gain):
    frames, width = mid.shape
    count = up.shape[0]
    whole = lambda *shape: pl.BlockSpec(shape, lambda i: (0,) * len(shape))
    return pl.pallas_call(
        ffn_back_kernel,
        grid=(count,),
        in_specs=[
            whole(frames, width), whole(frames, width),
            pl.BlockSpec((width, width), lambda i: (i, 0)),
            pl.BlockSpec((frames, width), lambda i: (0, i)),
            pl.BlockSpec((1, width, width), lambda i: (i, 0, 0)),
            whole(frames, width), whole(1, width),
        ],
        out_specs=[whole(frames, width), whole(frames, width), whole(1, width)]
        + [pl.BlockSpec((1, frames, width), lambda i: (i, 0, 0))],
        out_shape=[
            jax.ShapeDtypeStruct((frames, width), jnp.float32),
            jax.ShapeDtypeStruct((frames, width), jnp.bfloat16),
            jax.ShapeDtypeStruct((1, width), jnp.float32),
        ]
        + [jax.ShapeDtypeStruct((count, frames, width), jnp.bfloat16)],
        scratch_shapes=[pltpu.VMEM((frames, width), jnp.float32)],
        compiler_params=params(),
        name="ffn_back",
    )(low, d, down, slope, up, mid, gain)


def pack_back_kernel(packed_ref, w_ref, d_ref, stream_ref, gain_ref, low_ref, gain_grad_ref):
    grad = sum(dot_nt(packed_ref[j], w_ref[j]) for j in range(w_ref.shape[0]))
    normed, inverse = normalize(stream_ref[...])
    gain_grad_ref[...] = jnp.sum(grad * normed, 0, keepdims=True)
    low_ref[...] = as_low(d_ref[...] + normalize_back(grad * gain_ref[...], normed, inverse))


def pack_back(packed, w, d, stream, gain):
    frames, width = stream.shape
    return pl.pallas_call(
        pack_back_kernel,
        out_shape=[
            jax.ShapeDtypeStruct((frames, width), jnp.bfloat16),
            jax.ShapeDtypeStruct((1, width), jnp.float32),
        ],
        compiler_params=params(),
        name="pack_back",
    )(packed, w, d, stream, gain)


def tail_kernel(d_ref, skip_ref, small_ref, embed_ref, mel_ref, hot_ref, main_ref, table_ref):
    phones = embed_ref.shape[1]
    d_start = as_low(dot_nt(d_ref[...], skip_ref[...]))
    d_phones = as_low(dot_nn(d_start, small_ref[:, :phones]))
    main_ref[:, :phones] = as_low(dot_tn(d_start, embed_ref[...]))
    main_ref[:, phones:] = as_low(dot_tn(d_start, mel_ref[...]))
    table_ref[...] = as_low(dot_tn(d_phones, hot_ref[...]))


def tail(d, skip, small, embed, mel, hot):
    width = d.shape[1]
    phones = embed.shape[1]
    whole = lambda x: pl.BlockSpec(x.shape, lambda i: (0, 0))
    return pl.pallas_call(
        tail_kernel,
        grid=(1,),
        in_specs=[whole(d), pl.BlockSpec((width, width), lambda i: (0, 0))]
        + [whole(x) for x in (small, embed, mel, hot)],
        out_specs=[
            pl.BlockSpec((width, TABLE_AT), lambda i: (0, 0)),
            pl.BlockSpec((phones, hot.shape[1]), lambda i: (0, 0)),
        ],
        out_shape=[
            jax.ShapeDtypeStruct((width, TABLE_AT), jnp.bfloat16),
            jax.ShapeDtypeStruct((phones, hot.shape[1]), jnp.bfloat16),
        ],
        compiler_params=params(),
        name="tail",
    )(d, skip, small, embed, mel, hot)


def grads_kernel(plan, count, rows, legs, came_too, idx_ref, *refs):
    refs, picked_ref, sems = refs[:-2], refs[-2], refs[-1]
    outs = refs[len(refs) - legs :]
    came_ref = refs[len(refs) - legs - 1] if came_too else None
    step = pl.program_id(0)
    each = count // legs

    def copies(c):
        lefts, rights, stride, offset = plan[c]
        if rights is None:
            return []
        slot = c % 2
        return [
            pltpu.make_async_copy(
                refs[left].at[pl.ds(pl.multiple_of(idx_ref[i] * stride + offset, rows), rows)],
                picked_ref.at[slot, side, pl.ds(i * rows, rows)],
                sems.at[slot],
            )
            for side, left in enumerate(lefts)
            for i in range(count)
        ]

    def chunk(c):
        lefts, rights, _, _ = plan[c]
        if c == 0:
            for copy in copies(0):
                copy.start()
        if c + 1 < len(plan):
            for copy in copies(c + 1):
                copy.start()
        for copy in copies(c):
            copy.wait()
        if rights is None:
            main, table, edge = (refs[r] for r in lefts)
            thick = table.shape[0] // (main.shape[0] // rows)
            blocks = []
            for i in range(count):
                start = pl.multiple_of(idx_ref[i] * rows, rows)
                short = pl.multiple_of(idx_ref[i] * thick, thick)
                lead = table[pl.ds(short, thick)]
                rest = jnp.zeros((rows - thick, lead.shape[1]), lead.dtype)
                middle = jnp.concatenate([lead, rest], 0) if thick < rows else lead
                block = [main[pl.ds(start, rows)], middle, edge[pl.ds(start, rows)]]
                blocks.append(jnp.concatenate(block, 1).astype(jnp.float32))
            total = jnp.stack(blocks)
            if came_too:
                total = total + came_ref[...].astype(jnp.float32)
        else:
            wide = outs[0].shape[2]
            total = sum(
                dot_nn(picked_ref[c % 2, side], refs[r][0] if len(refs[r].shape) == 3 else refs[r][...])
                for side, r in enumerate(rights)
            )
            total = total.reshape(count, rows, wide)
        for f in range(legs):
            outs[f][...] = as_low(total[f * each : (f + 1) * each])

    for c in range(len(plan)):
        pl.when(step == c)(partial(chunk, c))


def grads(plan, arrays, idx, frames, rows, width, legs, came=None):
    count = idx.shape[0]
    picked = [j for entry in plan if entry[1] is not None for j in entry[0]]

    def spec(j, x):
        if j in picked:
            return pl.BlockSpec(memory_space=pl.ANY)
        if len(x.shape) == 3:
            first = min(c for c, entry in enumerate(plan) if entry[1] is not None and j in entry[1])
            return pl.BlockSpec((1,) + x.shape[1:], lambda i: (jnp.maximum(i - first, 0), 0, 0))
        return pl.BlockSpec(x.shape, lambda i, n=len(x.shape): (0,) * n)

    specs = [spec(j, x) for j, x in enumerate(arrays)]
    if came is not None:
        specs.append(pl.BlockSpec((count, rows, width), lambda i: (0, 0, 0)))
        arrays = list(arrays) + [came]
    return pl.pallas_call(
        partial(grads_kernel, plan, count, rows, legs, came is not None),
        grid=(len(plan),),
        in_specs=[pl.BlockSpec(memory_space=pltpu.SMEM)] + specs,
        out_specs=[pl.BlockSpec((count // legs, rows, width), lambda i: (0, i, 0))] * legs,
        out_shape=[jax.ShapeDtypeStruct((count // legs, rows * len(plan), width), jnp.bfloat16)] * legs,
        scratch_shapes=[
            pltpu.VMEM((2, 2, count * rows, frames), jnp.bfloat16),
            pltpu.SemaphoreType.DMA((2,)),
        ],
        compiler_params=params(),
        name="grads",
    )(idx, *arrays)


def fold_kernel(legs, *refs):
    ins, outs = refs[:-legs], refs[-legs:]
    took = len(ins) // legs
    for j in range(legs):
        total = ins[j * took][...].astype(jnp.float32)
        for ref in ins[j * took + 1 : (j + 1) * took]:
            total = total + ref[...].astype(jnp.float32)
        outs[j][...] = as_low(total)


def fold(parts, legs):
    count, rows, width = parts[0].shape
    each = count // legs
    tile = rows // 2
    return pl.pallas_call(
        partial(fold_kernel, legs),
        grid=(rows // tile,),
        in_specs=[
            pl.BlockSpec((each, tile, width), lambda i, j=j: (j, i, 0)) for j in range(legs) for _ in parts
        ],
        out_specs=[pl.BlockSpec((each, tile, width), lambda i: (0, i, 0))] * legs,
        out_shape=[jax.ShapeDtypeStruct((each, rows, width), jnp.bfloat16)] * legs,
        compiler_params=params(),
        name="fold",
    )(*[p for _ in range(legs) for p in parts])


def stack_kernel(*refs):
    ins, out, sem = refs[:-2], refs[-2], refs[-1]
    copies = [pltpu.make_async_copy(ref, out.at[i], sem) for i, ref in enumerate(ins)]
    for copy in copies:
        copy.start()
    for copy in copies:
        copy.wait()


def stack(parts):
    return pl.pallas_call(
        stack_kernel,
        in_specs=[pl.BlockSpec(memory_space=pl.ANY)] * len(parts),
        out_specs=pl.BlockSpec(memory_space=pltpu.VMEM),
        out_shape=jax.ShapeDtypeStruct((len(parts),) + parts[0].shape, parts[0].dtype),
        scratch_shapes=[pltpu.SemaphoreType.DMA],
        compiler_params=params(),
        name="stack",
    )(*parts)


def place_kernel(layout, sources, count, *refs):
    idx_refs, sources_refs = refs[:2], refs[2 : 2 + sources]
    outs, sem = refs[2 + sources : -1], refs[-1]
    copies = []
    for s, source in enumerate(sources_refs):
        idx_ref = idx_refs[s // (sources // 2)]
        first = (s % (sources // 2)) * count
        for i in range(count):
            owner = idx_ref[first + i]
            start = 0
            for (out, block), rows in layout:
                ref = outs[out]
                goal = ref.at[owner] if block is None else ref.at[block, owner]
                copy = pltpu.make_async_copy(source.at[i, pl.ds(start, rows)], goal, sem)
                copy.start()
                copies.append(copy)
                start += rows
    for copy in copies:
        copy.wait()


def place(layout, shapes, own, other, pieces):
    width = pieces[0].shape[2]
    return pl.pallas_call(
        partial(place_kernel, layout, len(pieces), pieces[0].shape[0]),
        in_specs=[pl.BlockSpec(memory_space=pltpu.SMEM)] * 2
        + [pl.BlockSpec(memory_space=pl.ANY)] * len(pieces),
        out_specs=[pl.BlockSpec(memory_space=pltpu.VMEM)] * len(shapes),
        out_shape=[jax.ShapeDtypeStruct(s, jnp.bfloat16) for s in shapes],
        scratch_shapes=[pltpu.SemaphoreType.DMA],
        compiler_params=params(),
        name="place",
    )(own, other, *pieces)


def shards(
    grid,
    fast,
    clean_mel,
    gauss_noise,
    flow_time,
    phone_ids,
    lengths,
    span_start,
    span_end,
    speaker,
    skip_states,
    w_input,
    phone_table,
    w_skip,
    w_attend,
    w_output,
    w_expand,
    w_reduce,
    w_head,
    norm_gains,
    moment_input,
    moment_table,
    moment_skip,
    moment_attend,
    moment_output,
    moment_expand,
    moment_reduce,
    moment_head,
    moment_gains,
    square_input,
    square_table,
    square_skip,
    square_attend,
    square_output,
    square_expand,
    square_reduce,
    square_head,
    square_gains,
):
    masters = (w_input, phone_table, w_skip, w_attend, w_output, w_expand, w_reduce, w_head, norm_gains)
    moments = (
        moment_input, moment_table, moment_skip, moment_attend, moment_output,
        moment_expand, moment_reduce, moment_head, moment_gains,
    )
    squares = (
        square_input, square_table, square_skip, square_attend, square_output,
        square_expand, square_reduce, square_head, square_gains,
    )
    rates = (LEARN_RATE, GAIN_RATE) + (LEARN_RATE,) * 6 + (GAIN_RATE,)
    frames, mel_bins = clean_mel.shape
    width = w_skip.shape[1]
    heads = width // HD
    devices = grid.total
    unit = width // devices
    inputs = w_input.shape[0]
    phones = phone_table.shape[0]
    phone_wide = phone_table.shape[1]
    phone_width = phone_wide * devices
    mel_lanes = TABLE_AT - phone_width
    at_gain = HEAD_AT + mel_bins
    at_count = at_gain + 3
    position = jnp.arange(frames)
    frame_valid = (position < lengths[0]).astype(jnp.float32)
    frame_inside = ((position >= span_start[0]) & (position < span_end[0])).astype(
        jnp.float32
    ) * frame_valid
    speaker_hot = (speaker[0] == jnp.arange(SPK)).astype(jnp.float32)
    count = jnp.sum(frame_inside)
    count_high = jnp.floor(count / 16.0)
    tally = jnp.stack([speaker[0].astype(jnp.float32), count_high, count - 16.0 * count_high])

    low_input = as_low(w_input)
    small = jnp.concatenate(
        [
            low_input[2 * mel_bins :].T,
            low_input[: 2 * mel_bins].T,
            jnp.zeros((unit, TABLE_AT - inputs), jnp.bfloat16),
            jnp.pad(as_low(phone_table).T, ((0, unit - phone_wide), (0, 0))),
            as_low(w_head),
            as_low(norm_gains).T,
            jnp.broadcast_to(as_low(tally)[None, :], (unit, 3)),
            jnp.zeros((unit, width - at_count - 3), jnp.bfloat16),
        ],
        1,
    )

    def blocks(x):
        return [as_low(x[:, j : j + width]) for j in range(0, x.shape[1], width)]

    attend_blocks, expand_blocks = blocks(w_attend), blocks(w_expand)
    packs, wides = len(attend_blocks), len(expand_blocks)
    stages = [
        [("small", None, small), ("skip", None, as_low(w_skip))],
        [("attend", j, w) for j, w in enumerate(attend_blocks)],
        [("output", None, as_low(w_output))] + [("expand", j, w) for j, w in enumerate(expand_blocks)],
        [("reduce", None, as_low(w_reduce))],
    ]
    counts_of = {"attend": packs, "expand": wides}
    if fast:
        own, other = grid.owners(0, -1), grid.owners(1, -1)

    def named(stage):
        return list(dict.fromkeys(name for name, _, _ in stage))

    def load(stage):
        return jnp.concatenate([w for _, _, w in stage], 0)

    def along(x, role, *after):
        return spread(grid, tied(x, *after) if after else x, role)

    def deepen(x, *after):
        x = tied(x, *after) if after else x
        return swap_deep(grid, jnp.broadcast_to(x[None], (grid.size("z"),) + x.shape))

    def plane(moved):
        return stack(moved).reshape((-1,) + moved[0].shape[1:])

    def settle(stage, pieces, own, other):
        pieces = pieces + [shift(grid, p, "core", 1) for p in pieces]
        names = named(stage)
        shapes, layout = [], []
        for name in names:
            rows = [w.shape[0] for n, _, w in stage if n == name][0]
            lead = (counts_of[name],) if name in counts_of else ()
            shapes.append(lead + (devices, rows, width))
        for name, block, w in stage:
            layout.append(((names.index(name), block), w.shape[0]))
        return dict(zip(names, place(layout, shapes, own, other, pieces)))

    def gather_whole(stage):
        full = {name: [] for name in named(stage)}
        rows = lax.all_gather(load(stage), AXES, axis=0, tiled=False)
        start = 0
        for name, _, w in stage:
            full[name].append(rows[:, start : start + w.shape[0]])
            start += w.shape[0]
        return {n: jnp.stack(p) if n in counts_of else p[0] for n, p in full.items()}

    loads = [load(stage) for stage in stages]
    if fast:
        deep_0 = deepen(loads[0])
        near_0, deep_1 = join(along(deep_0, "near"), deepen(loads[1], deep_0))
        near_0 = plane(near_0)
        far_0, near_1, deep_2 = join(
            along(near_0, "far"), along(deep_1, "near", near_0), deepen(loads[2], near_0)
        )
        near_1 = plane(near_1)
        far_1, near_2 = along(near_1, "far"), along(deep_2, "near", near_1)
        deep_3 = deepen(loads[3], near_1)
        far_0 = [tied(p, near_1) for p in far_0]
        whole = settle(stages[0], far_0, own, other)
    else:
        whole = gather_whole(stages[0])
    small_full = whole["small"].reshape(width, width)
    skip_full = whole["skip"].reshape(-1, width)
    table_turned = whole["small"][:, :phone_wide, TABLE_AT:HEAD_AT].reshape(phone_width, phones)
    head_block = small_full[:, HEAD_AT:]
    gains_wide = head_block[:, mel_bins : mel_bins + 3].astype(jnp.float32).T
    tallies = whole["small"][:, 0, at_count : at_count + 3].astype(jnp.float32)
    counts = jnp.sum(
        (tallies[:, :1] == jnp.arange(SPK, dtype=jnp.float32)[None, :])
        * (16.0 * tallies[:, 1:2] + tallies[:, 2:3]),
        0,
    )
    share = jnp.sum(speaker_hot / jnp.maximum(counts, 1.0)) / SPK

    flow = flow_time[0]
    noisy_mel = (1.0 - (1.0 - SIGMA) * flow) * gauss_noise + flow * clean_mel
    context = clean_mel * (frame_valid - frame_inside)[:, None]
    target = clean_mel - (1.0 - SIGMA) * gauss_noise
    mel = jnp.concatenate([as_low(noisy_mel), as_low(context)], 1)
    mel = jnp.pad(mel, ((0, 0), (0, mel_lanes - mel.shape[1])))
    phone_hot = as_low(phone_ids[:, None] == jnp.arange(phones)[None, :])
    slopes = head_slopes(heads)
    states_turned = skip_states.T

    embedded, stream, start_turned, attn_in, attn_turned = front(
        small_full, table_turned, skip_full, skip_states, phone_hot, mel,
        time_features(flow, width)[None, :], gains_wide[0:1],
    )
    if fast:
        far_1, near_2, deep_3, embedded, stream, start_turned, attn_in, attn_turned = join(
            far_1, near_2, deep_3, embedded, stream, start_turned, attn_in, attn_turned
        )
        near_2 = plane(near_2)
        far_2, near_3 = along(near_2, "far"), along(deep_3, "near", near_2)
        far_1 = [tied(p, near_2) for p in far_1]
        whole.update(settle(stages[1], far_1, own, other))
    else:
        whole.update(gather_whole(stages[1]))
    attend_full = whole["attend"].reshape(packs, width, width)
    packed = pack(attn_in, attend_full)
    mixed, lse = attend(lengths, slopes, packed)
    if fast:
        far_2, near_3, packed, mixed, lse = join(far_2, near_3, packed, mixed, lse)
        near_3 = plane(near_3)
        far_3 = along(near_3, "far")
        far_2 = [tied(p, near_3) for p in far_2]
        whole.update(settle(stages[2], far_2, own, other))
    else:
        whole.update(gather_whole(stages[2]))
    output_full = whole["output"].reshape(width, width)
    expand_full = whole["expand"].reshape(wides, width, width)
    stream_mid, ffn_in, ffn_turned, mixed_turned = mid_step(
        mixed, output_full, stream, gains_wide[1:2]
    )
    activated, act_turned, gelu_slope = expand(ffn_in, expand_full)
    if fast:
        far_3, stream_mid, ffn_turned, mixed_turned, activated, act_turned, gelu_slope = join(
            far_3, stream_mid, ffn_turned, mixed_turned, activated, act_turned, gelu_slope
        )
        whole.update(settle(stages[3], far_3, own, other))
    else:
        whole.update(gather_whole(stages[3]))
    reduce_full = whole["reduce"].reshape(-1, width)
    d_stream_out, d_branch, grad_head, grad_gain_three, error_sum = head_step(
        share[None], activated, reduce_full, stream_mid, head_block, target,
        frame_inside[:, None], gains_wide[2:3],
    )
    if fast:
        mine, theirs = grid.owners(0, 1), grid.owners(1, 1)
    far, near, deep = (grid.size(r) for r in ("far", "near", "z"))

    def sibling(x):
        return shift(grid, x, "core", 1)

    def both(*arrays):
        return [y for x in arrays for y in (x, sibling(x))]

    def sums(plan, arrays, *others, **options):
        first = [tied(arrays[0], *others)] if others else arrays[:1]
        return grads(plan, first + arrays[1:], mine, frames, unit, width, far, **options)

    def hops(legs, role, *others):
        sent = [tied(leg, *others) if others else leg for leg in legs[1:]]
        return [shift(grid, leg, role, j + 1) for j, leg in enumerate(sent)]

    def dense(pairs):
        parts = []
        for turned, right, stride, offset in pairs:
            if right is None:
                part = turned.reshape(devices, unit, width)
            else:
                turned = turned.reshape(devices, stride, frames)[:, offset : offset + unit]
                part = dot_nn(turned.reshape(width, frames), right).reshape(devices, unit, width)
            parts.append(part)
        return lax.psum_scatter(jnp.concatenate(parts, 1), AXES, scatter_dimension=0)

    offsets = [j * unit for j in range(wides)]
    if fast:
        plan = [((0, 1), (2, 3), wides * unit, o) for o in offsets]
        legs_0 = sums(plan, both(act_turned, d_branch))
        moved_0 = hops(legs_0, "far")
        d_branch_next = tied(d_branch, legs_0[0])
    else:
        share_reduce = dense([(act_turned, d_branch, wides * unit, o) for o in offsets])
        d_branch_next = d_branch
    d_stream_mid, d_out, grad_gain_two, d_hidden = ffn_back(
        d_branch_next, d_stream_out, reduce_full, gelu_slope, expand_full, stream_mid, gains_wide[1:2]
    )
    if fast:
        turned = both(ffn_turned, mixed_turned, attn_turned)
        moved_0, turned, d_stream_mid, d_out, d_hidden = join(
            moved_0, turned, d_stream_mid, d_out, d_hidden
        )
        legs_0 = fold([legs_0[0]] + moved_0, near)
        moved_0 = hops(legs_0, "near")
        d_out, d_hidden = tied(d_out, legs_0[0]), tied(d_hidden, legs_0[0])
    d_mixed = as_low(dot_nt(d_out, output_full))
    if fast:
        plan = [((0, 1), (2, 3), unit, 0) for j in range(wides)]
        legs_1 = sums(plan, turned[:2] + both(d_hidden), d_mixed)
        d_outs = both(d_out)
        moved_0, legs_1, d_mixed, d_outs = join(moved_0, legs_1, d_mixed, d_outs)
        (sums_0,) = fold([legs_0[0]] + moved_0, 1)
        d_mixed = tied(d_mixed, sums_0)
        moved_1 = hops(legs_1, "far", sums_0)
        sums_0 = swap_deep(grid, sums_0)
    else:
        share_expand = dense([(ffn_turned, d, unit, 0) for d in d_hidden])
    d_packed = attend_back(lengths, slopes, packed, d_mixed, lse)
    if fast:
        moved_1, sums_0, d_packed = join(moved_1, sums_0, d_packed)
        legs_1 = fold([legs_1[0]] + moved_1, near)
        moved_1 = hops(legs_1, "near")
        d_packed = tied(d_packed, legs_1[0])
    d_joined_in, grad_gain_one = pack_back(
        d_packed, attend_full, d_stream_mid, stream, gains_wide[0:1]
    )
    joined_turned = jnp.concatenate([start_turned, states_turned], 0)
    if fast:
        plan = [((0, 1), (2, 3), unit, 0)] + [((4, 5), (6, 7), unit, 0) for j in range(packs)]
        legs_2 = sums(plan, turned[2:4] + d_outs + turned[4:] + both(d_packed), d_joined_in)
        joined = both(joined_turned)
        moved_1, legs_2, joined, d_joined_in = join(moved_1, legs_2, joined, d_joined_in)
        (sums_1,) = fold([legs_1[0]] + moved_1, 1)
        d_joined_in = tied(d_joined_in, sums_1)
        moved_2 = hops(legs_2, "far", sums_1)
        sums_1 = swap_deep(grid, sums_1)
    else:
        share_attend = dense(
            [(mixed_turned, d_out, unit, 0)] + [(attn_turned, d, unit, 0) for d in d_packed]
        )
    main, table = tail(d_joined_in, skip_full, small_full, embedded, mel, phone_hot)
    gain_grads = jnp.concatenate([grad_gain_one, grad_gain_two, grad_gain_three], 0).T
    edge = jnp.pad(
        jnp.concatenate([as_low(grad_head), as_low(gain_grads)], 1),
        ((0, 0), (0, width - at_count)),
    )
    if fast:
        small_grads = [main, table, edge]
        (sent,) = grads([((0, 1, 2), None, 0, 0)], small_grads, theirs, frames, unit, width, 1)
        plan = [((0, 1), (2, 3), 2 * unit, o) for o in offsets[:2]] + [((4, 5, 6), None, 0, 0)]
        legs_3 = sums(plan, joined + both(d_joined_in) + small_grads, sent, came=sibling(sent))
        moved_2, sums_1, legs_3 = join(moved_2, sums_1, legs_3)
        legs_2 = fold([legs_2[0]] + moved_2, near)
        moved_2 = hops(legs_2, "near")
        moved_3 = hops(legs_3, "far", legs_2[0])
        moved_2, moved_3 = join(moved_2, moved_3)
        (sums_2,) = fold([legs_2[0]] + moved_2, 1)
        legs_3 = fold([legs_3[0], tied(moved_3[0], sums_2)] + moved_3[1:], near)
        moved_3 = hops(legs_3, "near")
        sums_2 = swap_deep(grid, sums_2)
        (sums_3,) = fold([legs_3[0]] + moved_3, 1)
        sums_3 = swap_deep(grid, sums_3)
        share_reduce, share_expand, share_attend, share_last = [
            jnp.sum(x.astype(jnp.float32), 0) for x in (sums_0, sums_1, sums_2, sums_3)
        ]
    else:
        table = table.reshape(devices, phone_wide, phones)
        table = jnp.pad(table, ((0, 0), (0, unit - phone_wide), (0, 0))).reshape(width, phones)
        small_grads = jnp.concatenate([main, table, edge], 1).astype(jnp.float32)
        share_last = dense(
            [(joined_turned, d_joined_in, 2 * unit, o) for o in offsets[:2]]
            + [(small_grads, None, 0, 0)]
        )

    def columns(rows):
        return jnp.concatenate([rows[j : j + unit] for j in range(0, rows.shape[0], unit)], 1)

    share_small = share_last[2 * unit :]
    shares = (
        jnp.concatenate([share_small[:, phone_width:inputs], share_small[:, :phone_width]], 1).T,
        share_small[:phone_wide, TABLE_AT:HEAD_AT].T,
        share_last[: 2 * unit],
        columns(share_attend[unit:]),
        share_attend[:unit],
        columns(share_expand),
        share_reduce,
        share_small[:, HEAD_AT:at_gain],
        share_small[:, at_gain:at_count].T,
    )
    local_square = sum((jnp.sum(g * g) for g in shares))
    totals = all_sum(grid, jnp.concatenate([speaker_hot * error_sum[0, 0], local_square[None]]))
    sums, total_square = totals[:SPK], totals[SPK]
    loss_value = jnp.mean(sums / jnp.maximum(counts, 1.0))
    grad_norm = jnp.sqrt(total_square)
    clip = jnp.minimum(1.0, 1.0 / (grad_norm + 1e-06))
    results = [
        adam_step(w, g * clip, m, s, r)
        for w, g, m, s, r in zip(masters, shares, moments, squares, rates)
    ]
    next_weights = tuple((r[0] for r in results))
    next_moments = tuple((r[1] for r in results))
    next_squares = tuple((r[2] for r in results))
    return (loss_value, grad_norm) + next_weights + next_moments + next_squares


def solution(mesh):
    grid = Grid(mesh)
    in_specs = (
        P(("wide", "narrow"), None),
        P(("wide", "narrow"), None),
        P(("wide", "narrow")),
        P(("wide", "narrow")),
        P(("wide", "narrow")),
        P(("wide", "narrow")),
        P(("wide", "narrow")),
        P(("wide", "narrow")),
        P(("wide", "narrow"), None),
        P(None, ("wide", "narrow")),
        P(None, ("wide", "narrow")),
        P(("wide", "narrow"), None),
        P(("wide", "narrow"), None),
        P(("wide", "narrow"), None),
        P(("wide", "narrow"), None),
        P(("wide", "narrow"), None),
        P(("wide", "narrow"), None),
        P(None, ("wide", "narrow")),
        P(None, ("wide", "narrow")),
        P(None, ("wide", "narrow")),
        P(("wide", "narrow"), None),
        P(("wide", "narrow"), None),
        P(("wide", "narrow"), None),
        P(("wide", "narrow"), None),
        P(("wide", "narrow"), None),
        P(("wide", "narrow"), None),
        P(None, ("wide", "narrow")),
        P(None, ("wide", "narrow")),
        P(None, ("wide", "narrow")),
        P(("wide", "narrow"), None),
        P(("wide", "narrow"), None),
        P(("wide", "narrow"), None),
        P(("wide", "narrow"), None),
        P(("wide", "narrow"), None),
        P(("wide", "narrow"), None),
        P(None, ("wide", "narrow")),
    )
    out_specs = (
        P(),
        P(),
        P(None, ("wide", "narrow")),
        P(None, ("wide", "narrow")),
        P(("wide", "narrow"), None),
        P(("wide", "narrow"), None),
        P(("wide", "narrow"), None),
        P(("wide", "narrow"), None),
        P(("wide", "narrow"), None),
        P(("wide", "narrow"), None),
        P(None, ("wide", "narrow")),
        P(None, ("wide", "narrow")),
        P(None, ("wide", "narrow")),
        P(("wide", "narrow"), None),
        P(("wide", "narrow"), None),
        P(("wide", "narrow"), None),
        P(("wide", "narrow"), None),
        P(("wide", "narrow"), None),
        P(("wide", "narrow"), None),
        P(None, ("wide", "narrow")),
        P(None, ("wide", "narrow")),
        P(None, ("wide", "narrow")),
        P(("wide", "narrow"), None),
        P(("wide", "narrow"), None),
        P(("wide", "narrow"), None),
        P(("wide", "narrow"), None),
        P(("wide", "narrow"), None),
        P(("wide", "narrow"), None),
        P(None, ("wide", "narrow")),
    )

    def body(*args):
        unit = args[11].shape[1] // grid.total
        return shards(grid, unit % 32 == 0, *args)

    return jax.shard_map(body, mesh=mesh, in_specs=in_specs, out_specs=out_specs, check_vma=False)
```

```python
from functools import partial
import math

import jax
import jax.numpy as jnp
from jax import lax
from jax.experimental import pallas as pl
from jax.experimental.pallas import tpu as pltpu
from jax.sharding import PartitionSpec as P

HD = 64
SPK = 16
STEP = 10


SIGMA = 1e-05
NORM_EPS = 1e-05
LEARN_RATE = 0.01
GAIN_RATE = 0.3
BETA_ONE = 0.5
BETA_TWO = 0.5
DECAY = 0.01
ADAM_EPS = 1e-08
FAR_AWAY = -1e30
VMEM = 62 * 1024 * 1024
TABLE_AT = 768
HEAD_AT = 896
BANDS = 32


def as_low(x):
    return x.astype(jnp.bfloat16)


def contract_rows(left, right):
    return lax.dot_general(
        left, right, (((0,), (0,)), ((), ())), preferred_element_type=jnp.float32
    )


def time_features(flow, width):
    half = width // 2
    freqs = jnp.exp(-math.log(10000.0) * jnp.arange(half, dtype=jnp.float32) / half)
    angle = 1000.0 * flow * freqs
    return jnp.concatenate([jnp.sin(angle), jnp.cos(angle)])


def normalize(x):
    centered = x - jnp.mean(x, -1, keepdims=True)
    inverse = lax.rsqrt(jnp.mean(centered * centered, -1, keepdims=True) + NORM_EPS)
    return (centered * inverse, inverse)


def normalize_back(grad, normed, inverse):
    return inverse * (
        grad
        - jnp.mean(grad, -1, keepdims=True)
        - normed * jnp.mean(grad * normed, -1, keepdims=True)
    )


def head_slopes(heads):
    return 2.0 ** (-8.0 * (jnp.arange(heads, dtype=jnp.float32) + 1.0) / heads)


def adam_step(master, grad, moment, square, rate):
    moment = BETA_ONE * moment + (1.0 - BETA_ONE) * grad
    square = BETA_TWO * square + (1.0 - BETA_TWO) * grad * grad
    moment_hat = moment / (1.0 - BETA_ONE**STEP)
    square_hat = square / (1.0 - BETA_TWO**STEP)
    master = master - rate * (moment_hat / (jnp.sqrt(square_hat) + ADAM_EPS) + DECAY * master)
    return (master, moment, square)


AXES = ("wide", "narrow")


def grid_sizes(wide, narrow):
    low = 1
    while (2 * low) * (2 * low) <= wide:
        low *= 2
    return (wide // low, low, narrow // 2, 2)


class Grid:
    def __init__(self, mesh):
        self.sizes = grid_sizes(mesh.shape["wide"], mesh.shape["narrow"])
        self.total = mesh.shape["wide"] * mesh.shape["narrow"]

    def coords(self, index):
        out = []
        for size in reversed(self.sizes):
            out.append(index % size)
            index = index // size
        return out[::-1]

    def index(self, coords):
        index = 0
        for size, value in zip(self.sizes, coords):
            index = index * size + value
        return index

    def mixed(self):
        return self.sizes[1] == self.sizes[2]

    def axis(self, role, core):
        if role == "z":
            return 0
        if role == "core":
            return 3
        if self.mixed():
            return (2, 1)[core] if role == "far" else (1, 2)[core]
        return 2 if role == "far" else 1

    def size(self, role):
        return self.sizes[self.axis(role, 0)]

    def pairs(self, role, step):
        out = []
        for source in range(self.total):
            coords = self.coords(source)
            axis = self.axis(role, coords[3])
            coords[axis] = (coords[axis] + step) % self.sizes[axis]
            out.append((source, self.index(coords)))
        return out

    def lines(self):
        deep = self.total // self.sizes[0]
        return [[z * deep + rest for z in range(self.sizes[0])] for rest in range(deep)]

    def owners(self, core_step, direction, deep_first=False):
        me = self.coords(lax.axis_index(AXES))
        core = (me[3] + core_step) % 2
        far, near, deep = (self.size(r) for r in ("far", "near", "z"))
        f, n, z = jnp.meshgrid(jnp.arange(far), jnp.arange(near), jnp.arange(deep), indexing="ij")
        if deep_first:
            f, n, z = (t.swapaxes(1, 2) for t in (f, n, z))
        if self.mixed():
            y = jnp.where(core == 0, me[1] + direction * n, me[1] + direction * f) % self.sizes[1]
            x = jnp.where(core == 0, me[2] + direction * f, me[2] + direction * n) % self.sizes[2]
        else:
            y = (me[1] + direction * n) % self.sizes[1]
            x = (me[2] + direction * f) % self.sizes[2]
        return self.index((z, y, x, core)).reshape(-1).astype(jnp.int32)


def shift(grid, x, role, step):
    return lax.ppermute(x, AXES, grid.pairs(role, step))


def tied(x, *others):
    return lax.optimization_barrier((x,) + others)[0]


def swap_deep(grid, x):
    return lax.all_to_all(x, AXES, 0, 0, axis_index_groups=grid.lines())


def join(*xs):
    return lax.optimization_barrier(xs)


def spread(grid, x, role):
    return [x] + [shift(grid, x, role, step) for step in range(1, grid.size(role))]


def all_sum(grid, x):
    return jnp.sum(lax.all_to_all(jnp.broadcast_to(x[None], (grid.total,) + x.shape), AXES, 0, 0), 0)


def dot_nn(a, b):
    return lax.dot_general(a, b, (((1,), (0,)), ((), ())), preferred_element_type=jnp.float32)


def dot_nt(a, b):
    return lax.dot_general(a, b, (((1,), (1,)), ((), ())), preferred_element_type=jnp.float32)


def dot_tn(a, b):
    return lax.dot_general(a, b, (((0,), (0,)), ((), ())), preferred_element_type=jnp.float32)


def params():
    return pltpu.CompilerParams(vmem_limit_bytes=VMEM)


def key_bias(length, frames):
    key = lax.broadcasted_iota(jnp.int32, (frames, frames), 0)
    query = lax.broadcasted_iota(jnp.int32, (frames, frames), 1)
    dist = -jnp.abs(key - query).astype(jnp.float32)
    return jnp.where(key < length, dist, FAR_AWAY)


def attend_kernel(length_ref, slope_ref, packed_ref, mixed_ref, lse_ref, bias_ref):
    step = pl.program_id(0)
    q_ref, k_ref, v_ref = (packed_ref.at[j] for j in range(3))
    frames = q_ref.shape[0]

    @pl.when(step == 0)
    def _():
        bias_ref[...] = key_bias(length_ref[0], frames)

    parts = []
    for h in range(2):
        lanes = slice(h * HD, (h + 1) * HD)
        scores = dot_nt(k_ref[:, lanes], q_ref[:, lanes] * jnp.bfloat16(HD**-0.5))
        scores = scores + slope_ref[2 * step + h] * bias_ref[...]
        top = jnp.max(scores, 0, keepdims=True)
        expo = jnp.exp(scores - top)
        total = jnp.sum(expo, 0, keepdims=True)
        lse_ref[0, h : h + 1] = top + jnp.log(total)
        probs = as_low(expo * (1.0 / total))
        parts.append(dot_tn(v_ref[:, lanes], probs))
    mixed_ref[...] = as_low(jnp.concatenate(parts, 0).T)


def attend(length, slopes, packed):
    _, frames, width = packed.shape
    pairs = width // (2 * HD)
    block = pl.BlockSpec((frames, 2 * HD), lambda i: (0, i))
    return pl.pallas_call(
        attend_kernel,
        grid=(pairs,),
        in_specs=[pl.BlockSpec(memory_space=pltpu.SMEM)] * 2
        + [pl.BlockSpec((3, frames, 2 * HD), lambda i: (0, 0, i))],
        out_specs=[block, pl.BlockSpec((1, 2, frames), lambda i: (i, 0, 0))],
        out_shape=[
            jax.ShapeDtypeStruct((frames, width), jnp.bfloat16),
            jax.ShapeDtypeStruct((pairs, 2, frames), jnp.float32),
        ],
        scratch_shapes=[pltpu.VMEM((frames, frames), jnp.float32)],
        compiler_params=params(),
        name="attend",
    )(length, slopes, packed)


def attend_back_kernel(
    length_ref, slope_ref, packed_ref, d_ref, lse_ref, dq_ref, dk_ref, dv_ref, bias_ref
):
    step = pl.program_id(0)
    q_ref, k_ref, v_ref = (packed_ref.at[j] for j in range(3))
    frames = q_ref.shape[0]

    @pl.when(step == 0)
    def _():
        bias_ref[...] = key_bias(length_ref[0], frames)

    d_query, d_keys, d_values = [], [], []
    for h in range(2):
        lanes = slice(h * HD, (h + 1) * HD)
        query = q_ref[:, lanes] * jnp.bfloat16(HD**-0.5)
        keys, values, d_mixed = k_ref[:, lanes], v_ref[:, lanes], d_ref[:, lanes]
        scores = dot_nt(keys, query) + slope_ref[2 * step + h] * bias_ref[...]
        probs = jnp.exp(scores - lse_ref[0, h : h + 1])
        d_probs = dot_nt(values, d_mixed)
        row_dot = jnp.sum(d_probs * probs, 0, keepdims=True)
        d_scores = as_low(probs * (d_probs - row_dot))
        d_values.append(dot_nn(as_low(probs), d_mixed))
        d_keys.append(dot_nn(d_scores, query))
        d_query.append(dot_tn(keys, d_scores))
    dq_ref[...] = as_low((jnp.concatenate(d_query, 0) * HD**-0.5).T)
    dk_ref[...] = as_low(jnp.concatenate(d_keys, 1))
    dv_ref[...] = as_low(jnp.concatenate(d_values, 1))


def attend_back(length, slopes, packed, d_mixed, lse):
    _, frames, width = packed.shape
    pairs = width // (2 * HD)
    stacked = pl.BlockSpec((3, frames, 2 * HD), lambda i: (0, 0, i))
    return pl.pallas_call(
        attend_back_kernel,
        grid=(pairs,),
        in_specs=[pl.BlockSpec(memory_space=pltpu.SMEM)] * 2
        + [stacked, pl.BlockSpec((frames, 2 * HD), lambda i: (0, i))]
        + [pl.BlockSpec((1, 2, frames), lambda i: (i, 0, 0))],
        out_specs=[pl.BlockSpec((frames, 2 * HD), lambda i: (0, i))] * 3,
        out_shape=[jax.ShapeDtypeStruct((frames, width), jnp.bfloat16)] * 3,
        scratch_shapes=[pltpu.VMEM((frames, frames), jnp.float32)],
        compiler_params=params(),
        name="attend_back",
    )(length, slopes, packed, d_mixed, lse)


def gelu_both(x):
    z = jnp.abs(x) * (0.5**0.5)
    bell = jnp.exp(-z * z)
    t = 1.0 / (1.0 + 0.3275911 * z)
    poly = t * (0.254829592 + t * (-0.284496736 + t * (1.421413741 + t * (-1.453152027 + t * 1.061405429))))
    tail = 0.5 * poly * bell
    share = jnp.where(x >= 0, 1.0 - tail, tail)
    return x * share, share + x * bell * (0.5 / math.pi) ** 0.5


def expand_kernel(count, blocks, own_ref, other_ref, *refs):
    sources = refs[:count]
    x_ref, w_out, act_ref, turned_ref, slope_ref, w_ref, sems, out_sems = refs[count:]
    step = pl.program_id(0)
    width = x_ref.shape[1]
    unit = width // sum(source.shape[0] for source in sources)

    def copies(j):
        entry = (w_ref.at[j], (j + 1) * unit, unit, None, sems.at[j])
        return landing((own_ref, other_ref), sources, [entry])

    def kept(j):
        return pltpu.make_async_copy(w_ref.at[j], w_out.at[j], out_sems.at[j])

    def chunk(j):
        if j == 0:
            for n in range(blocks):
                begin(copies(n))
        finish(copies(j))
        kept(j).start()
        hidden = dot_nn(x_ref[...], w_ref[j])
        act, slope = gelu_both(hidden)
        act = as_low(act)
        act_ref[...] = act
        turned_ref[...] = act.T
        slope_ref[...] = as_low(slope)
        if j == blocks - 1:
            for n in range(blocks):
                kept(n).wait()

    for j in range(blocks):
        pl.when(step == j)(partial(chunk, j))


def expand(own, other, pieces, x, blocks):
    frames, width = x.shape
    total = blocks * width
    return pl.pallas_call(
        partial(expand_kernel, len(pieces), blocks),
        grid=(blocks,),
        in_specs=piece_specs(pieces) + [pl.BlockSpec((frames, width), lambda i: (0, 0))],
        out_specs=[
            pl.BlockSpec(memory_space=pl.ANY),
            pl.BlockSpec((frames, width), lambda i: (0, i)),
            pl.BlockSpec((width, frames), lambda i: (i, 0)),
            pl.BlockSpec((frames, width), lambda i: (0, i)),
        ],
        out_shape=[
            jax.ShapeDtypeStruct((blocks, width, width), jnp.bfloat16),
            jax.ShapeDtypeStruct((frames, total), jnp.bfloat16),
            jax.ShapeDtypeStruct((total, frames), jnp.bfloat16),
            jax.ShapeDtypeStruct((frames, total), jnp.bfloat16),
        ],
        scratch_shapes=[
            pltpu.VMEM((blocks, width, width), jnp.bfloat16),
            pltpu.SemaphoreType.DMA((blocks,)),
            pltpu.SemaphoreType.DMA((blocks,)),
        ],
        compiler_params=params(),
        name="expand",
    )(own, other, *pieces, x)


def landing(idx_refs, sources, entries):
    half = len(sources) // 2
    copies = []
    for s, source in enumerate(sources):
        idx_ref = idx_refs[s // half]
        count = source.shape[0]
        for i in range(count):
            band = idx_ref[(s % half) * count + i]
            for goal, start, rows, lane, sem in entries:
                part = source.at[i, pl.ds(start, rows)]
                if lane is not None:
                    part = source.at[i, pl.ds(start, rows), pl.ds(lane, goal.shape[-1])]
                place = goal.at[pl.ds(pl.multiple_of(band * rows, rows), rows)]
                copies.append(pltpu.make_async_copy(part, place, sem))
    return copies


def begin(copies):
    for copy in copies:
        copy.start()


def finish(copies):
    for copy in copies:
        copy.wait()


def piece_specs(pieces):
    smem = pl.BlockSpec(memory_space=pltpu.SMEM)
    return [smem, smem] + [pl.BlockSpec(memory_space=pl.ANY)] * len(pieces)


def gain_row(edge_ref, at):
    return edge_ref[at : at + 1].astype(jnp.float32)


def front_kernel(
    at_gain, count, phone_rows, own_ref, other_ref, *refs
):
    sources = refs[:count]
    states_ref, states_turned_ref, hot_ref, mel_ref, time_ref = refs[count : count + 5]
    (
        small_out, skip_out, embed_ref, stream_ref, joined_ref, normed_ref, turned_ref, edge_ref,
        small_ref, skip_ref, table_ref, sems, out_sems,
    ) = refs[count + 5 :]
    width = stream_ref.shape[1]
    bands = sum(source.shape[0] for source in sources)
    unit = width // bands
    idx = (own_ref, other_ref)
    first = landing(
        idx, sources,
        [(small_ref, 0, unit, None, sems.at[0]), (table_ref, 0, phone_rows, TABLE_AT, sems.at[0])],
    )
    second = landing(idx, sources, [(skip_ref, unit, 2 * unit, None, sems.at[1])])
    begin(first)
    begin(second)
    phones = embed_ref.shape[1]
    joined_ref[width:] = states_turned_ref[...]
    finish(first)
    small_copy = pltpu.make_async_copy(small_ref, small_out, out_sems.at[0])
    small_copy.start()
    edge_ref[...] = small_ref[:, HEAD_AT:].T
    embedded = as_low(dot_nt(hot_ref[...], table_ref[...]))
    embed_ref[...] = embedded
    start = dot_nt(embedded, small_ref[:, :phones])
    start = start + dot_nt(mel_ref[...], small_ref[:, phones:TABLE_AT]) + time_ref[...]
    start = as_low(start)
    joined_ref[:width] = start.T
    finish(second)
    skip_copy = pltpu.make_async_copy(skip_ref, skip_out, out_sems.at[1])
    skip_copy.start()
    stream = dot_nn(start, skip_ref[:width]) + dot_nn(states_ref[...], skip_ref[width:])
    stream_ref[...] = stream
    normed = as_low(normalize(stream)[0] * gain_row(edge_ref, at_gain))
    normed_ref[...] = normed
    turned_ref[...] = normed.T
    small_copy.wait()
    skip_copy.wait()


def front(own, other, pieces, states, states_turned, hot, mel, time, phones, at_gain):
    frames, width = states.shape
    f32, low = jnp.float32, jnp.bfloat16
    bands = sum(p.shape[0] for p in pieces)
    vmem, anywhere = pl.BlockSpec(memory_space=pltpu.VMEM), pl.BlockSpec(memory_space=pl.ANY)
    return pl.pallas_call(
        partial(front_kernel, at_gain, len(pieces), phones // bands),
        in_specs=piece_specs(pieces) + [vmem] * 5,
        out_specs=[anywhere] * 2 + [vmem] * 6,
        out_shape=[
            jax.ShapeDtypeStruct((width, width), low),
            jax.ShapeDtypeStruct((2 * width, width), low),
            jax.ShapeDtypeStruct((frames, phones), low),
            jax.ShapeDtypeStruct((frames, width), f32),
            jax.ShapeDtypeStruct((2 * width, frames), low),
            jax.ShapeDtypeStruct((frames, width), low),
            jax.ShapeDtypeStruct((width, frames), low),
            jax.ShapeDtypeStruct((width - HEAD_AT, width), low),
        ],
        scratch_shapes=[
            pltpu.VMEM((width, width), low),
            pltpu.VMEM((2 * width, width), low),
            pltpu.VMEM((phones, hot.shape[1]), low),
            pltpu.SemaphoreType.DMA((2,)),
            pltpu.SemaphoreType.DMA((2,)),
        ],
        compiler_params=params(),
        name="front",
    )(own, other, *pieces, states, states_turned, hot, mel, time)


def pack_kernel(count, blocks, own_ref, other_ref, *refs):
    sources = refs[:count]
    x_ref, w_out, out_ref, w_ref, sems, out_sems = refs[count:]
    step = pl.program_id(0)
    width = x_ref.shape[1]
    unit = width // sum(source.shape[0] for source in sources)

    def copies(j):
        entry = (w_ref.at[j], j * unit, unit, None, sems.at[j])
        return landing((own_ref, other_ref), sources, [entry])

    def kept(j):
        return pltpu.make_async_copy(w_ref.at[j], w_out.at[j], out_sems.at[j])

    def chunk(j):
        if j == 0:
            for n in range(blocks):
                begin(copies(n))
        finish(copies(j))
        kept(j).start()
        out_ref[0] = as_low(dot_nn(x_ref[...], w_ref[j]))
        if j == blocks - 1:
            for n in range(blocks):
                kept(n).wait()

    for j in range(blocks):
        pl.when(step == j)(partial(chunk, j))


def pack(own, other, pieces, x, blocks):
    frames, width = x.shape
    return pl.pallas_call(
        partial(pack_kernel, len(pieces), blocks),
        grid=(blocks,),
        in_specs=piece_specs(pieces) + [pl.BlockSpec((frames, width), lambda i: (0, 0))],
        out_specs=[
            pl.BlockSpec(memory_space=pl.ANY),
            pl.BlockSpec((1, frames, width), lambda i: (i, 0, 0)),
        ],
        out_shape=[
            jax.ShapeDtypeStruct((blocks, width, width), jnp.bfloat16),
            jax.ShapeDtypeStruct((blocks, frames, width), jnp.bfloat16),
        ],
        scratch_shapes=[
            pltpu.VMEM((blocks, width, width), jnp.bfloat16),
            pltpu.SemaphoreType.DMA((blocks,)),
            pltpu.SemaphoreType.DMA((blocks,)),
        ],
        compiler_params=params(),
        name="pack",
    )(own, other, *pieces, x)


def mid_kernel(at_gain, count, own_ref, other_ref, *refs):
    sources = refs[:count]
    (
        mixed_ref, stream_ref, edge_ref, w_out, mid_ref, in_ref, turned_ref, mixed_turned_ref,
        w_ref, sem, out_sem,
    ) = refs[count:]
    width = stream_ref.shape[1]
    unit = width // sum(source.shape[0] for source in sources)
    copies = landing((own_ref, other_ref), sources, [(w_ref, 0, unit, None, sem)])
    begin(copies)
    mixed = mixed_ref[...]
    mixed_turned_ref[...] = mixed.T
    finish(copies)
    kept = pltpu.make_async_copy(w_ref, w_out, out_sem)
    kept.start()
    mid = stream_ref[...] + dot_nn(mixed, w_ref[...])
    mid_ref[...] = mid
    normed = as_low(normalize(mid)[0] * gain_row(edge_ref, at_gain))
    in_ref[...] = normed
    turned_ref[...] = normed.T
    kept.wait()


def mid_step(own, other, pieces, mixed, stream, edge, at_gain):
    frames, width = stream.shape
    low = jnp.bfloat16
    vmem = pl.BlockSpec(memory_space=pltpu.VMEM)
    return pl.pallas_call(
        partial(mid_kernel, at_gain, len(pieces)),
        in_specs=piece_specs(pieces) + [vmem] * 3,
        out_specs=[pl.BlockSpec(memory_space=pl.ANY)] + [vmem] * 4,
        out_shape=[
            jax.ShapeDtypeStruct((width, width), low),
            jax.ShapeDtypeStruct((frames, width), jnp.float32),
            jax.ShapeDtypeStruct((frames, width), low),
            jax.ShapeDtypeStruct((width, frames), low),
            jax.ShapeDtypeStruct((width, frames), low),
        ],
        scratch_shapes=[
            pltpu.VMEM((width, width), low),
            pltpu.SemaphoreType.DMA,
            pltpu.SemaphoreType.DMA,
        ],
        compiler_params=params(),
        name="mid",
    )(own, other, *pieces, mixed, stream, edge)


def head_kernel(at_gain, count, share_ref, own_ref, other_ref, *refs):
    sources = refs[:count]
    (
        act_ref, mid_ref, edge_ref, target_ref, inside_ref,
        w_out, d_ref, low_ref, grad_ref, gain_grad_ref, error_ref,
        total_ref, w_ref, sem, out_sem,
    ) = refs[count:]
    step = pl.program_id(0)
    tile = act_ref.shape[1]
    rows = w_ref.shape[0] // sum(source.shape[0] for source in sources)
    kept = pltpu.make_async_copy(w_ref, w_out, out_sem)

    @pl.when(step == 0)
    def _():
        copies = landing((own_ref, other_ref), sources, [(w_ref, 0, rows, None, sem)])
        begin(copies)
        finish(copies)
        kept.start()

    part = dot_nn(act_ref[...], w_ref[pl.ds(pl.multiple_of(step * tile, tile), tile)])

    @pl.when(step == 0)
    def _():
        total_ref[...] = mid_ref[...] + part

    @pl.when(step > 0)
    def _():
        total_ref[...] += part

    @pl.when(step == pl.num_programs(0) - 1)
    def _():
        bins = target_ref.shape[1]
        normed, inverse = normalize(total_ref[...])
        gain = gain_row(edge_ref, at_gain)
        head_in = as_low(normed * gain)
        head = edge_ref[:bins]
        inside = inside_ref[...]
        error = dot_nt(head_in, head) - target_ref[...]
        error_ref[...] = jnp.sum(jnp.sum(error * error, 1, keepdims=True) * inside, 0, keepdims=True)
        d_prediction = as_low((2.0 * share_ref[0]) * error * inside)
        grad_ref[...] = dot_tn(head_in, d_prediction)
        d_head_in = dot_nn(d_prediction, head)
        gain_grad_ref[...] = jnp.sum(d_head_in * normed, 0, keepdims=True)
        d_stream = normalize_back(d_head_in * gain, normed, inverse)
        d_ref[...] = d_stream
        low_ref[...] = as_low(d_stream)
        kept.wait()


def head_step(share, own, other, pieces, act, mid, edge, target, inside, at_gain, tile=1024):
    frames, width = mid.shape
    bins = target.shape[1]
    total = act.shape[1]
    whole = lambda *shape: pl.BlockSpec(shape, lambda i: (0,) * len(shape))
    return pl.pallas_call(
        partial(head_kernel, at_gain, len(pieces)),
        grid=(total // tile,),
        in_specs=[pl.BlockSpec(memory_space=pltpu.SMEM)]
        + piece_specs(pieces)
        + [
            pl.BlockSpec((frames, tile), lambda i: (0, i)),
            whole(frames, width), whole(*edge.shape), whole(frames, bins), whole(frames, 1),
        ],
        out_specs=[
            pl.BlockSpec(memory_space=pl.ANY),
            whole(frames, width), whole(frames, width), whole(width, bins), whole(1, width), whole(1, 1),
        ],
        out_shape=[
            jax.ShapeDtypeStruct((total, width), jnp.bfloat16),
            jax.ShapeDtypeStruct((frames, width), jnp.float32),
            jax.ShapeDtypeStruct((frames, width), jnp.bfloat16),
            jax.ShapeDtypeStruct((width, bins), jnp.float32),
            jax.ShapeDtypeStruct((1, width), jnp.float32),
            jax.ShapeDtypeStruct((1, 1), jnp.float32),
        ],
        scratch_shapes=[
            pltpu.VMEM((frames, width), jnp.float32),
            pltpu.VMEM((total, width), jnp.bfloat16),
            pltpu.SemaphoreType.DMA,
            pltpu.SemaphoreType.DMA,
        ],
        compiler_params=params(),
        name="head",
    )(share, own, other, *pieces, act, mid, edge, target, inside)


def ffn_back_kernel(
    at_gain, low_ref, d_ref, down_ref, slope_ref, up_ref, mid_ref, edge_ref,
    out_ref, out_low_ref, gain_grad_ref, *refs,
):
    hidden_refs, total_ref = refs[:-1], refs[-1]
    step = pl.program_id(0)
    d_hidden = as_low(dot_nt(low_ref[...], down_ref[...]) * slope_ref[...].astype(jnp.float32))
    for j, ref in enumerate(hidden_refs):

        @pl.when(step == j)
        def _(ref=ref):
            ref[...] = d_hidden

    part = dot_nt(d_hidden, up_ref[0])

    @pl.when(step == 0)
    def _():
        total_ref[...] = part

    @pl.when(step > 0)
    def _():
        total_ref[...] += part

    @pl.when(step == pl.num_programs(0) - 1)
    def _():
        normed, inverse = normalize(mid_ref[...])
        grad = total_ref[...]
        gain_grad_ref[...] = jnp.sum(grad * normed, 0, keepdims=True)
        out = d_ref[...] + normalize_back(grad * gain_row(edge_ref, at_gain), normed, inverse)
        out_ref[...] = out
        out_low_ref[...] = as_low(out)


def ffn_back(low, d, down, slope, up, mid, edge, at_gain):
    frames, width = mid.shape
    count = up.shape[0]
    whole = lambda *shape: pl.BlockSpec(shape, lambda i: (0,) * len(shape))
    return pl.pallas_call(
        partial(ffn_back_kernel, at_gain),
        grid=(count,),
        in_specs=[
            whole(frames, width), whole(frames, width),
            pl.BlockSpec((width, width), lambda i: (i, 0)),
            pl.BlockSpec((frames, width), lambda i: (0, i)),
            pl.BlockSpec((1, width, width), lambda i: (i, 0, 0)),
            whole(frames, width), whole(*edge.shape),
        ],
        out_specs=[whole(frames, width), whole(frames, width), whole(1, width)]
        + [whole(frames, width)] * count,
        out_shape=[
            jax.ShapeDtypeStruct((frames, width), jnp.float32),
            jax.ShapeDtypeStruct((frames, width), jnp.bfloat16),
            jax.ShapeDtypeStruct((1, width), jnp.float32),
        ]
        + [jax.ShapeDtypeStruct((frames, width), jnp.bfloat16)] * count,
        scratch_shapes=[pltpu.VMEM((frames, width), jnp.float32)],
        compiler_params=params(),
        name="ffn_back",
    )(low, d, down, slope, up, mid, edge)


def pack_back_kernel(at_gain, blocks, *refs):
    w_ref, d_ref, stream_ref, edge_ref, low_ref, gain_grad_ref, total_ref = refs[blocks:]
    step = pl.program_id(0)

    def chunk(j):
        part = dot_nt(refs[j][...], w_ref[0])
        total_ref[...] = part if j == 0 else total_ref[...] + part

    for j in range(blocks):
        pl.when(step == j)(partial(chunk, j))

    @pl.when(step == pl.num_programs(0) - 1)
    def _():
        grad = total_ref[...]
        normed, inverse = normalize(stream_ref[...])
        gain_grad_ref[...] = jnp.sum(grad * normed, 0, keepdims=True)
        gain = gain_row(edge_ref, at_gain)
        low_ref[...] = as_low(d_ref[...] + normalize_back(grad * gain, normed, inverse))


def pack_back(packed, w, d, stream, edge, at_gain):
    frames, width = stream.shape
    whole = lambda *shape: pl.BlockSpec(shape, lambda i: (0,) * len(shape))
    return pl.pallas_call(
        partial(pack_back_kernel, at_gain, w.shape[0]),
        grid=(w.shape[0],),
        in_specs=[whole(frames, width)] * w.shape[0]
        + [
            pl.BlockSpec((1, width, width), lambda i: (i, 0, 0)),
            whole(frames, width), whole(frames, width), whole(*edge.shape),
        ],
        out_specs=[whole(frames, width), whole(1, width)],
        out_shape=[
            jax.ShapeDtypeStruct((frames, width), jnp.bfloat16),
            jax.ShapeDtypeStruct((1, width), jnp.float32),
        ],
        scratch_shapes=[pltpu.VMEM((frames, width), jnp.float32)],
        compiler_params=params(),
        name="pack_back",
    )(*packed, w, d, stream, edge)


def tail_kernel(
    at_gain, d_ref, skip_ref, small_ref, embed_ref, mel_ref, hot_ref, head_ref, one_ref, two_ref, three_ref,
    main_ref, table_ref, edge_ref,
):
    phones = embed_ref.shape[1]
    d_start = as_low(dot_nt(d_ref[...], skip_ref[...]))
    d_phones = as_low(dot_nn(d_start, small_ref[:, :phones]))
    main_ref[:, :phones] = as_low(dot_tn(d_start, embed_ref[...]))
    main_ref[:, phones:] = as_low(dot_tn(d_start, mel_ref[...]))
    table_ref[...] = as_low(dot_tn(d_phones, hot_ref[...]))
    edge = head_ref[...]
    lanes = edge.shape[1]
    edge = jnp.pad(edge, ((0, 0), (0, edge_ref.shape[1] - lanes)))
    lane = lax.broadcasted_iota(jnp.int32, edge.shape, 1)
    for j, ref in enumerate((one_ref, two_ref, three_ref)):
        column = jnp.broadcast_to(ref[...], (8, edge.shape[0])).T[:, :1]
        edge = jnp.where(lane == at_gain + j, column, edge)
    edge_ref[...] = as_low(edge)


def tail(d, skip, small, embed, mel, hot, head, gains, at_gain):
    width = d.shape[1]
    phones = embed.shape[1]
    whole = lambda x: pl.BlockSpec(x.shape, lambda i: (0, 0))
    arrays = (small, embed, mel, hot, head, *gains)
    shapes = [(width, TABLE_AT), (phones, hot.shape[1]), (width, width - HEAD_AT)]
    return pl.pallas_call(
        partial(tail_kernel, at_gain),
        grid=(1,),
        in_specs=[whole(d), pl.BlockSpec((width, width), lambda i: (0, 0))] + [whole(x) for x in arrays],
        out_specs=[pl.BlockSpec(s, lambda i: (0, 0)) for s in shapes],
        out_shape=[jax.ShapeDtypeStruct(s, jnp.bfloat16) for s in shapes],
        compiler_params=params(),
        name="tail",
    )(d, skip, *arrays)


def grads_kernel(plan, count, rows, legs, came_too, idx_ref, *refs):
    refs, picked_ref, right_ref, sems = refs[:-3], refs[-3], refs[-2], refs[-1]
    outs = refs[len(refs) - legs :]
    came_ref = refs[len(refs) - legs - 1] if came_too else None
    step = pl.program_id(0)
    each = count // legs

    def copies(c):
        lefts, rights, stride, offset = plan[c]
        if rights is None:
            return []
        slot = c % 2
        return [
            pltpu.make_async_copy(
                refs[left].at[pl.ds(pl.multiple_of(idx_ref[i] * stride + offset, rows), rows)],
                picked_ref.at[slot, side, pl.ds(i * rows, rows)],
                sems.at[slot],
            )
            for side, left in enumerate(lefts)
            for i in range(count)
        ] + [
            pltpu.make_async_copy(refs[right], right_ref.at[slot, side], sems.at[slot])
            for side, right in enumerate(rights)
        ]

    def chunk(c):
        lefts, rights, _, _ = plan[c]
        if c == 0:
            for copy in copies(0):
                copy.start()
        if c + 1 < len(plan):
            for copy in copies(c + 1):
                copy.start()
        for copy in copies(c):
            copy.wait()
        if rights is None:
            main, table, edge = (refs[r] for r in lefts)
            thick = table.shape[0] // (main.shape[0] // rows)
            blocks = []
            for i in range(count):
                start = pl.multiple_of(idx_ref[i] * rows, rows)
                short = pl.multiple_of(idx_ref[i] * thick, thick)
                lead = table[pl.ds(short, thick)]
                rest = jnp.zeros((rows - thick, lead.shape[1]), lead.dtype)
                middle = jnp.concatenate([lead, rest], 0) if thick < rows else lead
                block = [main[pl.ds(start, rows)], middle, edge[pl.ds(start, rows)]]
                blocks.append(jnp.concatenate(block, 1).astype(jnp.float32))
            total = jnp.stack(blocks)
            if came_too:
                total = total + came_ref[...].astype(jnp.float32)
        else:
            wide = outs[0].shape[2]
            total = sum(dot_nn(picked_ref[c % 2, side], right_ref[c % 2, side]) for side in range(len(rights)))
            total = total.reshape(count, rows, wide)
        for f in range(legs):
            outs[f][...] = as_low(total[f * each : (f + 1) * each])

    for c in range(len(plan)):
        pl.when(step == c)(partial(chunk, c))


def grads(plan, arrays, idx, frames, rows, width, legs, came=None):
    count = idx.shape[0]
    copied = [j for entry in plan if entry[1] is not None for j in entry[0] + entry[1]]

    def spec(j, x):
        if j in copied:
            return pl.BlockSpec(memory_space=pl.ANY)
        return pl.BlockSpec(x.shape, lambda i, n=len(x.shape): (0,) * n)

    specs = [spec(j, x) for j, x in enumerate(arrays)]
    if came is not None:
        specs.append(pl.BlockSpec((count, rows, width), lambda i: (0, 0, 0)))
        arrays = list(arrays) + [came]
    return pl.pallas_call(
        partial(grads_kernel, plan, count, rows, legs, came is not None),
        grid=(len(plan),),
        in_specs=[pl.BlockSpec(memory_space=pltpu.SMEM)] + specs,
        out_specs=[pl.BlockSpec((count // legs, rows, width), lambda i: (0, i, 0))] * legs,
        out_shape=[jax.ShapeDtypeStruct((count // legs, rows * len(plan), width), jnp.bfloat16)] * legs,
        scratch_shapes=[
            pltpu.VMEM((2, 2, count * rows, frames), jnp.bfloat16),
            pltpu.VMEM((2, 2, frames, width), jnp.bfloat16),
            pltpu.SemaphoreType.DMA((2,)),
        ],
        compiler_params=params(),
        name="grads",
    )(idx, *arrays)


def fold_kernel(legs, *refs):
    ins, outs = refs[:-legs], refs[-legs:]
    took = len(ins) // legs
    for j in range(legs):
        total = ins[j * took][...].astype(jnp.float32)
        for ref in ins[j * took + 1 : (j + 1) * took]:
            total = total + ref[...].astype(jnp.float32)
        outs[j][...] = as_low(total)


def fold(parts, legs):
    count, rows, width = parts[0].shape
    each = count // legs
    tile = rows // 2
    return pl.pallas_call(
        partial(fold_kernel, legs),
        grid=(rows // tile,),
        in_specs=[
            pl.BlockSpec((each, tile, width), lambda i, j=j: (j, i, 0)) for j in range(legs) for _ in parts
        ],
        out_specs=[pl.BlockSpec((each, tile, width), lambda i: (0, i, 0))] * legs,
        out_shape=[jax.ShapeDtypeStruct((each, rows, width), jnp.bfloat16)] * legs,
        compiler_params=params(),
        name="fold",
    )(*[p for _ in range(legs) for p in parts])


def stack_kernel(*refs):
    ins, out, sem = refs[:-2], refs[-2], refs[-1]
    copies = [pltpu.make_async_copy(ref, out.at[i], sem) for i, ref in enumerate(ins)]
    for copy in copies:
        copy.start()
    for copy in copies:
        copy.wait()


def stack(parts):
    return pl.pallas_call(
        stack_kernel,
        in_specs=[pl.BlockSpec(memory_space=pl.ANY)] * len(parts),
        out_specs=pl.BlockSpec(memory_space=pltpu.VMEM),
        out_shape=jax.ShapeDtypeStruct((len(parts),) + parts[0].shape, parts[0].dtype),
        scratch_shapes=[pltpu.SemaphoreType.DMA],
        compiler_params=params(),
        name="stack",
    )(*parts)


def update(grad, rate, master_ref, moment_ref, square_ref, clip):
    return adam_step(master_ref[...], grad * clip, moment_ref[...], square_ref[...], rate)


def adam_kernel(at, clip_ref, *refs):
    phone_rows, phone_width, inputs, at_gain = at
    small, skip, attend, output, expand, reduce = refs[:6]
    masters, moments, squares = refs[6:15], refs[15:24], refs[24:33]
    outs = refs[33:]
    unit = small.shape[0]
    clip = clip_ref[0]
    mel_lanes = inputs - phone_width
    lanes = [small[:, phone_width : phone_width + mel_lanes], small[:, :phone_width]]
    edge = small[:, HEAD_AT:]
    turned_edge = edge.T
    bins = masters[7].shape[1]

    def columns(ref, first):
        blocks = [ref[j : j + unit] for j in range(first, ref.shape[0], unit)]
        return jnp.concatenate(blocks, 1)

    grads_of = [
        jnp.concatenate(lanes, 1),
        small[:phone_rows, TABLE_AT:HEAD_AT],
        skip[...],
        columns(attend, unit),
        attend[:unit],
        columns(expand, 0),
        reduce[...],
        edge[:, :bins],
        turned_edge[at_gain : at_gain + 3],
    ]
    for j, grad in enumerate(grads_of):
        rate = GAIN_RATE if j in (1, 8) else LEARN_RATE
        after = update(grad, rate, masters[j], moments[j], squares[j], clip)
        for n, value in enumerate(after):
            outs[9 * n + j][...] = value


def adam(clip, shares, masters, moments, squares, at):
    turned = lambda group: [x.T if j < 2 else x for j, x in enumerate(group)]
    masters, moments, squares = turned(masters), turned(moments), turned(squares)
    vmem = pl.BlockSpec(memory_space=pltpu.VMEM)
    arrays = [*shares, *masters, *moments, *squares]
    results = pl.pallas_call(
        partial(adam_kernel, at),
        in_specs=[pl.BlockSpec(memory_space=pltpu.SMEM)] + [vmem] * len(arrays),
        out_specs=[vmem] * 27,
        out_shape=[jax.ShapeDtypeStruct(x.shape, jnp.float32) for x in (*masters, *moments, *squares)],
        compiler_params=params(),
        name="adam",
    )(clip, *arrays)
    return [y for n in range(3) for y in turned(results[9 * n : 9 * n + 9])]


def shards(
    grid,
    fast,
    clean_mel,
    gauss_noise,
    flow_time,
    phone_ids,
    lengths,
    span_start,
    span_end,
    speaker,
    skip_states,
    w_input,
    phone_table,
    w_skip,
    w_attend,
    w_output,
    w_expand,
    w_reduce,
    w_head,
    norm_gains,
    moment_input,
    moment_table,
    moment_skip,
    moment_attend,
    moment_output,
    moment_expand,
    moment_reduce,
    moment_head,
    moment_gains,
    square_input,
    square_table,
    square_skip,
    square_attend,
    square_output,
    square_expand,
    square_reduce,
    square_head,
    square_gains,
):
    masters = (w_input, phone_table, w_skip, w_attend, w_output, w_expand, w_reduce, w_head, norm_gains)
    moments = (
        moment_input, moment_table, moment_skip, moment_attend, moment_output,
        moment_expand, moment_reduce, moment_head, moment_gains,
    )
    squares = (
        square_input, square_table, square_skip, square_attend, square_output,
        square_expand, square_reduce, square_head, square_gains,
    )
    frames, mel_bins = clean_mel.shape
    width = w_skip.shape[1]
    heads = width // HD
    devices = grid.total
    unit = width // devices
    inputs = w_input.shape[0]
    phones = phone_table.shape[0]
    phone_wide = phone_table.shape[1]
    phone_width = phone_wide * devices
    mel_lanes = TABLE_AT - phone_width
    at_gain = HEAD_AT + mel_bins
    at_count = at_gain + 3
    position = jnp.arange(frames)
    frame_valid = (position < lengths[0]).astype(jnp.float32)
    frame_inside = ((position >= span_start[0]) & (position < span_end[0])).astype(
        jnp.float32
    ) * frame_valid
    speaker_hot = (speaker[0] == jnp.arange(SPK)).astype(jnp.float32)
    count = jnp.sum(frame_inside)
    count_high = jnp.floor(count / 16.0)
    tally = jnp.stack([speaker[0].astype(jnp.float32), count_high, count - 16.0 * count_high])

    low_input = as_low(w_input)
    small = jnp.concatenate(
        [
            low_input[2 * mel_bins :].T,
            low_input[: 2 * mel_bins].T,
            jnp.zeros((unit, TABLE_AT - inputs), jnp.bfloat16),
            jnp.pad(as_low(phone_table).T, ((0, unit - phone_wide), (0, 0))),
            as_low(w_head),
            as_low(norm_gains).T,
            jnp.broadcast_to(as_low(tally)[None, :], (unit, 3)),
            jnp.zeros((unit, width - at_count - 3), jnp.bfloat16),
        ],
        1,
    )

    def blocks(x):
        return [as_low(x[:, j : j + width]) for j in range(0, x.shape[1], width)]

    attend_blocks, expand_blocks = blocks(w_attend), blocks(w_expand)
    packs, wides = len(attend_blocks), len(expand_blocks)
    stages = [
        [("small", None, small), ("skip", None, as_low(w_skip))],
        [("attend", j, w) for j, w in enumerate(attend_blocks)],
        [("output", None, as_low(w_output))] + [("expand", j, w) for j, w in enumerate(expand_blocks)],
        [("reduce", None, as_low(w_reduce))],
    ]
    if fast:
        own, other = grid.owners(0, -1), grid.owners(1, -1)
        own_turned, other_turned = grid.owners(0, -1, True), grid.owners(1, -1, True)
        mine, theirs = grid.owners(0, 1), grid.owners(1, 1)

    def load(stage):
        return jnp.concatenate([w for _, _, w in stage], 0)

    def sibling(x):
        return shift(grid, x, "core", 1)

    def along(x, role, *after):
        return spread(grid, tied(x, *after) if after else x, role)

    def deepen(x, *after):
        x = tied(x, *after) if after else x
        return swap_deep(grid, jnp.broadcast_to(x[None], (grid.size("z"),) + x.shape))

    def plane(moved):
        return stack(moved).reshape((-1,) + moved[0].shape[1:])

    def gather_whole(stage):
        rows = lax.all_gather(load(stage), AXES, axis=0, tiled=False)
        parts, start = [], 0
        for name, _, w in stage:
            part = rows[:, start : start + w.shape[0]]
            start += w.shape[0]
            if name == "small":
                table = part[:, :phone_wide, TABLE_AT:HEAD_AT].reshape(BANDS, -1, phones)
                table = jnp.pad(table, ((0, 0), (0, width // BANDS - table.shape[1]), (0, 0)))
                part = part.reshape(BANDS, -1, width)
                part = jnp.concatenate([part[..., :TABLE_AT], table, part[..., HEAD_AT:]], 2)
            parts.append(part.reshape(BANDS, -1, width))
        rows = jnp.concatenate(parts, 1)
        return [rows[: BANDS // 2], rows[BANDS // 2 :]]

    flow = flow_time[0]
    noisy_mel = (1.0 - (1.0 - SIGMA) * flow) * gauss_noise + flow * clean_mel
    context = clean_mel * (frame_valid - frame_inside)[:, None]
    target = clean_mel - (1.0 - SIGMA) * gauss_noise
    mel = jnp.concatenate([as_low(noisy_mel), as_low(context)], 1)
    mel = jnp.pad(mel, ((0, 0), (0, mel_lanes - mel.shape[1])))
    phone_hot = as_low(phone_ids[:, None] == jnp.arange(phones)[None, :])
    slopes = head_slopes(heads)
    times = time_features(flow, width)[None, :]
    inside = frame_inside[:, None]
    states_turned = skip_states.T
    loads = [load(stage) for stage in stages]
    if fast:
        deep_0, near_2 = join(deepen(loads[0]), along(loads[2], "near"))
        pair_2 = stack(near_2)
        near_0, deep_1, target, mel, phone_hot, slopes, times, inside, states_turned = join(
            along(deep_0, "near"), deepen(loads[1], deep_0),
            target, mel, phone_hot, slopes, times, inside, states_turned,
        )
        near_0 = plane(near_0)
        deep_2 = deepen(pair_2, near_0)
        far_0, core_0, near_1, own, other, own_turned, other_turned, mine, theirs = join(
            along(near_0, "far")[1], sibling(near_0), along(deep_1, "near", near_0),
            own, other, own_turned, other_turned, mine, theirs,
        )
        near_1 = plane(near_1)
        far_0 = tied(far_0, near_1)
        pieces_0 = [near_0, far_0, core_0, sibling(far_0)]
        far_1 = along(near_1, "far")[1]
        core_1 = sibling(near_1)
    else:
        own, other = jnp.arange(BANDS // 2), jnp.arange(BANDS // 2, BANDS)
        own_turned, other_turned = own, other
        pieces_0 = gather_whole(stages[0])
    small_full, skip_full, embedded, stream, joined_turned, attn_in, attn_turned, edges = front(
        own, other, pieces_0, skip_states, states_turned, phone_hot, mel, times, phone_width, mel_bins
    )
    tallies = edges[at_count - HEAD_AT : at_count - HEAD_AT + 3].reshape(3, devices, unit)
    tallies = tallies[:, :, 0].astype(jnp.float32)
    counts = jnp.sum(
        (tallies[0][:, None] == jnp.arange(SPK, dtype=jnp.float32)[None, :])
        * (16.0 * tallies[1] + tallies[2])[:, None],
        0,
    )
    share = jnp.sum(speaker_hot / jnp.maximum(counts, 1.0)) / SPK

    if fast:
        far_1, core_1, deep_2, embedded, stream, attn_in, attn_turned, edges = join(
            far_1, core_1, deep_2, embedded, stream, attn_in, attn_turned, edges
        )
        near_2 = deep_2.reshape((-1,) + deep_2.shape[2:])
        pieces_1 = [near_1, far_1, core_1, sibling(far_1)]
        far_2 = along(near_2, "far")[1]
        core_2 = sibling(near_2)
        deep_3 = deepen(loads[3], near_2)
    else:
        pieces_1 = gather_whole(stages[1])
    attend_full, packed = pack(own, other, pieces_1, attn_in, packs)
    mixed, lse = attend(lengths, slopes, packed)
    if fast:
        far_2, deep_3, core_2, packed, mixed, lse, share, joined_turned = join(
            far_2, deep_3, core_2, packed, mixed, lse, share, joined_turned
        )
        near_3 = along(deep_3, "near")
        pieces_2 = [near_2, far_2, core_2, sibling(far_2)]
    else:
        pieces_2 = gather_whole(stages[2])
    output_full, stream_mid, ffn_in, ffn_turned, mixed_turned = mid_step(
        own_turned, other_turned, pieces_2, mixed, stream, edges, mel_bins + 1
    )
    if fast:
        near_3 = plane([near_3[0], tied(near_3[1], ffn_in)] + near_3[2:])
        far_3 = along(near_3, "far")[1]
        core_3 = sibling(near_3)
    expand_full, activated, act_turned, gelu_slope = expand(
        own_turned, other_turned, pieces_2, ffn_in, wides
    )
    if fast:
        far_3, core_3, stream_mid, ffn_turned, mixed_turned, activated, act_turned, gelu_slope = join(
            far_3, core_3, stream_mid, ffn_turned, mixed_turned, activated, act_turned, gelu_slope
        )
        pieces_3 = [near_3, far_3, core_3, sibling(far_3)]
    else:
        pieces_3 = gather_whole(stages[3])
    reduce_full, d_stream_out, d_branch, grad_head, grad_gain_three, error_sum = head_step(
        share[None], own, other, pieces_3, activated, stream_mid, edges, target, inside, mel_bins + 2
    )
    far, near, deep = (grid.size(r) for r in ("far", "near", "z"))

    def both(*arrays):
        return [y for x in arrays for y in (x, sibling(x))]

    def sums(plan, arrays, *others, **options):
        first = [tied(arrays[0], *others)] if others else arrays[:1]
        return grads(plan, first + arrays[1:], mine, frames, unit, width, far, **options)

    def hops(legs, role, *others):
        sent = [tied(leg, *others) if others else leg for leg in legs[1:]]
        return [shift(grid, leg, role, j + 1) for j, leg in enumerate(sent)]

    def dense(pairs):
        parts = []
        for turned, right, stride, offset in pairs:
            if right is None:
                part = turned.reshape(devices, unit, width)
            else:
                turned = turned.reshape(devices, stride, frames)[:, offset : offset + unit]
                part = dot_nn(turned.reshape(width, frames), right).reshape(devices, unit, width)
            parts.append(part)
        return lax.psum_scatter(jnp.concatenate(parts, 1), AXES, scatter_dimension=0)

    offsets = [j * unit for j in range(wides)]
    if fast:
        plan = [((0, 1), (2, 3), wides * unit, o) for o in offsets]
        legs_0 = sums(plan, both(tied(act_turned, pieces_3[3]), d_branch))
        moved_0 = hops(legs_0, "far")
        d_branch_next = tied(d_branch, legs_0[0])
    else:
        share_reduce = dense([(act_turned, d_branch, wides * unit, o) for o in offsets])
        d_branch_next = d_branch
    d_stream_mid, d_out, grad_gain_two, *d_hidden = ffn_back(
        d_branch_next, d_stream_out, reduce_full, gelu_slope, expand_full, stream_mid, edges, mel_bins + 1
    )
    d_mixed = as_low(dot_nt(d_out, output_full))
    if fast:
        turned = both(ffn_turned)
        d_hiddens = both(*d_hidden)
        moved_0, turned, d_hiddens, d_stream_mid, d_out, d_mixed = join(
            moved_0, turned, d_hiddens, d_stream_mid, d_out, d_mixed
        )
        legs_0 = fold([legs_0[0]] + moved_0, near)
        moved_0 = hops(legs_0, "near")
        plan = [((0, 1), (2 + 2 * j, 3 + 2 * j), unit, 0) for j in range(wides)]
        legs_1 = sums(plan, turned + d_hiddens, legs_0[0])
        turned = both(tied(mixed_turned, legs_0[0]), attn_turned, d_out)
        moved_0, legs_1, turned, d_mixed = join(moved_0, legs_1, turned, d_mixed)
        (sums_0,) = fold([legs_0[0]] + moved_0, 1)
        d_mixed = tied(d_mixed, sums_0)
        moved_1 = hops(legs_1, "far", sums_0)
        sums_0 = swap_deep(grid, sums_0)
    else:
        share_expand = dense([(ffn_turned, d, unit, 0) for d in d_hidden])
    d_packed = attend_back(lengths, slopes, packed, d_mixed, lse)
    d_joined_in, grad_gain_one = pack_back(
        d_packed, attend_full, d_stream_mid, stream, edges, mel_bins
    )
    if fast:
        d_packs = both(*d_packed)
        moved_1, sums_0, d_packs, d_joined_in = join(moved_1, sums_0, d_packs, d_joined_in)
        legs_1 = fold([legs_1[0]] + moved_1, near)
        moved_1 = hops(legs_1, "near")
        plan = [((0, 1), (4, 5), unit, 0)]
        plan = plan + [((2, 3), (6 + 2 * j, 7 + 2 * j), unit, 0) for j in range(packs)]
        legs_2 = sums(plan, turned + d_packs, legs_1[0])
        joined = both(tied(joined_turned, legs_1[0]), tied(d_joined_in, legs_1[0]))
        moved_1, legs_2, joined, d_joined_in = join(moved_1, legs_2, joined, d_joined_in)
        (sums_1,) = fold([legs_1[0]] + moved_1, 1)
        d_joined_in = tied(d_joined_in, sums_1)
        moved_2 = hops(legs_2, "far", sums_1)
        sums_1 = swap_deep(grid, sums_1)
    else:
        share_attend = dense(
            [(mixed_turned, d_out, unit, 0)] + [(attn_turned, d, unit, 0) for d in d_packed]
        )
        share_skip = dense([(joined_turned, d_joined_in, 2 * unit, o) for o in offsets[:2]])
    gain_grads = [grad_gain_one, grad_gain_two, grad_gain_three]
    small_grads = tail(
        d_joined_in, skip_full, small_full, embedded, mel, phone_hot, grad_head, gain_grads, mel_bins
    )
    if fast:
        plan = [((0, 1, 2), None, 0, 0)]
        small_grads = list(small_grads)
        (sent,) = grads(plan, small_grads, theirs, frames, unit, width, 1)
        plan_skip = [((0, 1), (2, 3), 2 * unit, o) for o in offsets[:2]]
        legs_3 = sums(plan_skip, joined, sent)
        legs_4 = grads(plan, small_grads, mine, frames, unit, width, far, sibling(sent))
        moved_2, legs_3, legs_4 = join(moved_2, legs_3, legs_4)
        legs_2 = fold([legs_2[0]] + moved_2, near)
        moved_2 = hops(legs_2, "near")
        moved_3 = hops(legs_3, "far", legs_2[0])
        moved_2, moved_3, sums_1 = join(moved_2, moved_3, sums_1)
        (sums_2,) = fold([legs_2[0]] + moved_2, 1)
        legs_3 = fold([legs_3[0], tied(moved_3[0], sums_2)] + moved_3[1:], near)
        sums_2 = swap_deep(grid, sums_2)
        moved_3 = hops(legs_3, "near")
        moved_4 = hops(legs_4, "far", legs_3[0])
        moved_3, moved_4, sums_2 = join(moved_3, moved_4, sums_2)
        (sums_3,) = fold([legs_3[0]] + moved_3, 1)
        legs_4 = fold([legs_4[0], tied(moved_4[0], sums_3)] + moved_4[1:], near)
        moved_4 = hops(legs_4, "near")
        sums_3 = swap_deep(grid, sums_3)
        moved_4, sums_3 = join(moved_4, sums_3)
        (sums_4,) = fold([legs_4[0]] + moved_4, 1)
        sums_4 = swap_deep(grid, sums_4)
        share_reduce, share_expand, share_attend, share_skip, share_small = [
            jnp.sum(x.astype(jnp.float32), 0) for x in (sums_0, sums_1, sums_2, sums_3, sums_4)
        ]
    else:
        main, table, edge = small_grads
        table = table.reshape(devices, phone_wide, phones)
        table = jnp.pad(table, ((0, 0), (0, unit - phone_wide), (0, 0))).reshape(width, phones)
        small_grads = jnp.concatenate([main, table, edge], 1).astype(jnp.float32)
        share_small = dense([(small_grads, None, 0, 0)])

    shares = (share_small, share_skip, share_attend, share_expand, share_reduce)
    local_square = sum((jnp.sum(g * g) for g in shares))
    totals = all_sum(grid, jnp.concatenate([speaker_hot * error_sum[0, 0], local_square[None]]))
    sums, total_square = totals[:SPK], totals[SPK]
    loss_value = jnp.mean(sums / jnp.maximum(counts, 1.0))
    grad_norm = jnp.sqrt(total_square)
    clip = jnp.minimum(1.0, 1.0 / (grad_norm + 1e-06))
    shares = (share_small, share_skip, share_attend, share_attend, share_expand, share_reduce)
    at = (phone_wide, phone_width, inputs, mel_bins)
    results = adam(clip[None], shares, masters, moments, squares, at)
    return (loss_value, grad_norm, *results)


def solution(mesh):
    grid = Grid(mesh)
    in_specs = (
        P(("wide", "narrow"), None),
        P(("wide", "narrow"), None),
        P(("wide", "narrow")),
        P(("wide", "narrow")),
        P(("wide", "narrow")),
        P(("wide", "narrow")),
        P(("wide", "narrow")),
        P(("wide", "narrow")),
        P(("wide", "narrow"), None),
        P(None, ("wide", "narrow")),
        P(None, ("wide", "narrow")),
        P(("wide", "narrow"), None),
        P(("wide", "narrow"), None),
        P(("wide", "narrow"), None),
        P(("wide", "narrow"), None),
        P(("wide", "narrow"), None),
        P(("wide", "narrow"), None),
        P(None, ("wide", "narrow")),
        P(None, ("wide", "narrow")),
        P(None, ("wide", "narrow")),
        P(("wide", "narrow"), None),
        P(("wide", "narrow"), None),
        P(("wide", "narrow"), None),
        P(("wide", "narrow"), None),
        P(("wide", "narrow"), None),
        P(("wide", "narrow"), None),
        P(None, ("wide", "narrow")),
        P(None, ("wide", "narrow")),
        P(None, ("wide", "narrow")),
        P(("wide", "narrow"), None),
        P(("wide", "narrow"), None),
        P(("wide", "narrow"), None),
        P(("wide", "narrow"), None),
        P(("wide", "narrow"), None),
        P(("wide", "narrow"), None),
        P(None, ("wide", "narrow")),
    )
    out_specs = (
        P(),
        P(),
        P(None, ("wide", "narrow")),
        P(None, ("wide", "narrow")),
        P(("wide", "narrow"), None),
        P(("wide", "narrow"), None),
        P(("wide", "narrow"), None),
        P(("wide", "narrow"), None),
        P(("wide", "narrow"), None),
        P(("wide", "narrow"), None),
        P(None, ("wide", "narrow")),
        P(None, ("wide", "narrow")),
        P(None, ("wide", "narrow")),
        P(("wide", "narrow"), None),
        P(("wide", "narrow"), None),
        P(("wide", "narrow"), None),
        P(("wide", "narrow"), None),
        P(("wide", "narrow"), None),
        P(("wide", "narrow"), None),
        P(None, ("wide", "narrow")),
        P(None, ("wide", "narrow")),
        P(None, ("wide", "narrow")),
        P(("wide", "narrow"), None),
        P(("wide", "narrow"), None),
        P(("wide", "narrow"), None),
        P(("wide", "narrow"), None),
        P(("wide", "narrow"), None),
        P(("wide", "narrow"), None),
        P(None, ("wide", "narrow")),
    )

    def body(*args):
        unit = args[11].shape[1] // grid.total
        return shards(grid, unit % 32 == 0, *args)

    return jax.shard_map(body, mesh=mesh, in_specs=in_specs, out_specs=out_specs, check_vma=False)
```

```python
from functools import partial
import math

import jax
import jax.numpy as jnp
from jax import lax
from jax.experimental import pallas as pl
from jax.experimental.pallas import tpu as pltpu
from jax.sharding import PartitionSpec as P

HD = 64
SPK = 16
STEP = 10


SIGMA = 1e-05
NORM_EPS = 1e-05
LEARN_RATE = 0.01
GAIN_RATE = 0.3
BETA_ONE = 0.5
BETA_TWO = 0.5
DECAY = 0.01
ADAM_EPS = 1e-08
FAR_AWAY = -1e30
VMEM = 64 * 1024 * 1024
TABLE_AT = 768
HEAD_AT = 896
BANDS = 32
HEADS_AT_ONCE = 4


def as_low(x):
    return x.astype(jnp.bfloat16)


def contract_rows(left, right):
    return lax.dot_general(
        left, right, (((0,), (0,)), ((), ())), preferred_element_type=jnp.float32
    )


def time_features(flow, width):
    half = width // 2
    freqs = jnp.exp(-math.log(10000.0) * jnp.arange(half, dtype=jnp.float32) / half)
    angle = 1000.0 * flow * freqs
    return jnp.concatenate([jnp.sin(angle), jnp.cos(angle)])


def normalize(x):
    centered = x - jnp.mean(x, -1, keepdims=True)
    inverse = lax.rsqrt(jnp.mean(centered * centered, -1, keepdims=True) + NORM_EPS)
    return (centered * inverse, inverse)


def normalize_back(grad, normed, inverse):
    return inverse * (
        grad
        - jnp.mean(grad, -1, keepdims=True)
        - normed * jnp.mean(grad * normed, -1, keepdims=True)
    )


def head_slopes(heads):
    return 2.0 ** (-8.0 * (jnp.arange(heads, dtype=jnp.float32) + 1.0) / heads)


def adam_step(master, grad, moment, square, rate):
    moment = BETA_ONE * moment + (1.0 - BETA_ONE) * grad
    square = BETA_TWO * square + (1.0 - BETA_TWO) * grad * grad
    moment_hat = moment / (1.0 - BETA_ONE**STEP)
    square_hat = square / (1.0 - BETA_TWO**STEP)
    master = master - rate * (moment_hat / (jnp.sqrt(square_hat) + ADAM_EPS) + DECAY * master)
    return (master, moment, square)


AXES = ("wide", "narrow")


def grid_sizes(wide, narrow):
    low = 1
    while (2 * low) * (2 * low) <= wide:
        low *= 2
    return (wide // low, low, narrow // 2, 2)


class Grid:
    def __init__(self, mesh):
        self.sizes = grid_sizes(mesh.shape["wide"], mesh.shape["narrow"])
        self.total = mesh.shape["wide"] * mesh.shape["narrow"]

    def coords(self, index):
        out = []
        for size in reversed(self.sizes):
            out.append(index % size)
            index = index // size
        return out[::-1]

    def index(self, coords):
        index = 0
        for size, value in zip(self.sizes, coords):
            index = index * size + value
        return index

    def mixed(self):
        return self.sizes[1] == self.sizes[2]

    def axis(self, role, core):
        if role == "z":
            return 0
        if role == "core":
            return 3
        if self.mixed():
            return (2, 1)[core] if role == "far" else (1, 2)[core]
        return 2 if role == "far" else 1

    def size(self, role):
        return self.sizes[self.axis(role, 0)]

    def pairs(self, role, step):
        out = []
        for source in range(self.total):
            coords = self.coords(source)
            axis = self.axis(role, coords[3])
            coords[axis] = (coords[axis] + step) % self.sizes[axis]
            out.append((source, self.index(coords)))
        return out

    def lines(self):
        deep = self.total // self.sizes[0]
        return [[z * deep + rest for z in range(self.sizes[0])] for rest in range(deep)]

    def owners(self, core_step, direction, deep_first=False):
        me = self.coords(lax.axis_index(AXES))
        core = (me[3] + core_step) % 2
        far, near, deep = (self.size(r) for r in ("far", "near", "z"))
        f, n, z = jnp.meshgrid(jnp.arange(far), jnp.arange(near), jnp.arange(deep), indexing="ij")
        if deep_first:
            f, n, z = (t.swapaxes(1, 2) for t in (f, n, z))
        if self.mixed():
            y = jnp.where(core == 0, me[1] + direction * n, me[1] + direction * f) % self.sizes[1]
            x = jnp.where(core == 0, me[2] + direction * f, me[2] + direction * n) % self.sizes[2]
        else:
            y = (me[1] + direction * n) % self.sizes[1]
            x = (me[2] + direction * f) % self.sizes[2]
        return self.index((z, y, x, core)).reshape(-1).astype(jnp.int32)


def shift(grid, x, role, step):
    return lax.ppermute(x, AXES, grid.pairs(role, step))


def tied(x, *others):
    return lax.optimization_barrier((x,) + others)[0]


def swap_deep(grid, x):
    return lax.all_to_all(x, AXES, 0, 0, axis_index_groups=grid.lines())


def join(*xs):
    return lax.optimization_barrier(xs)


def spread(grid, x, role):
    return [x] + [shift(grid, x, role, step) for step in range(1, grid.size(role))]


def all_sum(grid, x):
    return jnp.sum(lax.all_to_all(jnp.broadcast_to(x[None], (grid.total,) + x.shape), AXES, 0, 0), 0)


def dot_nn(a, b):
    return lax.dot_general(a, b, (((1,), (0,)), ((), ())), preferred_element_type=jnp.float32)


def dot_nt(a, b):
    return lax.dot_general(a, b, (((1,), (1,)), ((), ())), preferred_element_type=jnp.float32)


def dot_tn(a, b):
    return lax.dot_general(a, b, (((0,), (0,)), ((), ())), preferred_element_type=jnp.float32)


def params():
    return pltpu.CompilerParams(vmem_limit_bytes=VMEM)


def key_bias(length, frames):
    key = lax.broadcasted_iota(jnp.int32, (frames, frames), 0)
    query = lax.broadcasted_iota(jnp.int32, (frames, frames), 1)
    dist = -jnp.abs(key - query).astype(jnp.float32)
    return jnp.where(key < length, dist, FAR_AWAY)


def attend_kernel(length_ref, slope_ref, packed_ref, mixed_ref, lse_ref, bias_ref):
    step = pl.program_id(0)
    q_ref, k_ref, v_ref = (packed_ref.at[j] for j in range(3))
    frames, lanes_here = mixed_ref.shape
    here = lanes_here // HD

    @pl.when(step == 0)
    def _():
        bias_ref[...] = key_bias(length_ref[0], frames)

    parts = []
    for h in range(here):
        lanes = slice(h * HD, (h + 1) * HD)
        scores = dot_nt(k_ref[:, lanes], q_ref[:, lanes] * jnp.bfloat16(HD**-0.5))
        scores = scores + slope_ref[here * step + h] * bias_ref[...]
        top = jnp.max(scores, 0, keepdims=True)
        expo = jnp.exp(scores - top)
        total = jnp.sum(expo, 0, keepdims=True)
        lse_ref[0, h : h + 1] = top + jnp.log(total)
        probs = as_low(expo * (1.0 / total))
        parts.append(dot_tn(v_ref[:, lanes], probs))
    mixed_ref[...] = as_low(jnp.concatenate(parts, 0).T)


def attend(length, slopes, packed):
    _, frames, width = packed.shape
    steps = width // (HEADS_AT_ONCE * HD)
    block = pl.BlockSpec((frames, HEADS_AT_ONCE * HD), lambda i: (0, i))
    return pl.pallas_call(
        attend_kernel,
        grid=(steps,),
        in_specs=[pl.BlockSpec(memory_space=pltpu.SMEM)] * 2
        + [pl.BlockSpec((3, frames, HEADS_AT_ONCE * HD), lambda i: (0, 0, i))],
        out_specs=[block, pl.BlockSpec((1, HEADS_AT_ONCE, frames), lambda i: (i, 0, 0))],
        out_shape=[
            jax.ShapeDtypeStruct((frames, width), jnp.bfloat16),
            jax.ShapeDtypeStruct((steps, HEADS_AT_ONCE, frames), jnp.float32),
        ],
        scratch_shapes=[pltpu.VMEM((frames, frames), jnp.float32)],
        compiler_params=params(),
        name="attend",
    )(length, slopes, packed)


def attend_back_kernel(
    length_ref, slope_ref, packed_ref, d_out_ref, w_ref, lse_ref, dq_ref, dk_ref, dv_ref, bias_ref
):
    step = pl.program_id(0)
    q_ref, k_ref, v_ref = (packed_ref.at[j] for j in range(3))
    frames, lanes_here = dq_ref.shape
    here = lanes_here // HD

    @pl.when(step == 0)
    def _():
        bias_ref[...] = key_bias(length_ref[0], frames)

    d_mixed_here = as_low(dot_nt(d_out_ref[...], w_ref[...]))
    d_query, d_keys, d_values = [], [], []
    for h in range(here):
        lanes = slice(h * HD, (h + 1) * HD)
        query = q_ref[:, lanes] * jnp.bfloat16(HD**-0.5)
        keys, values, d_mixed = k_ref[:, lanes], v_ref[:, lanes], d_mixed_here[:, lanes]
        scores = dot_nt(keys, query) + slope_ref[here * step + h] * bias_ref[...]
        probs = jnp.exp(scores - lse_ref[0, h : h + 1])
        d_probs = dot_nt(values, d_mixed)
        row_dot = jnp.sum(d_probs * probs, 0, keepdims=True)
        d_scores = as_low(probs * (d_probs - row_dot))
        d_values.append(dot_nn(as_low(probs), d_mixed))
        d_keys.append(dot_nn(d_scores, query))
        d_query.append(dot_tn(keys, d_scores))
    dq_ref[...] = as_low((jnp.concatenate(d_query, 0) * HD**-0.5).T)
    dk_ref[...] = as_low(jnp.concatenate(d_keys, 1))
    dv_ref[...] = as_low(jnp.concatenate(d_values, 1))


def attend_back(length, slopes, packed, d_out, w, lse):
    _, frames, width = packed.shape
    wide = HEADS_AT_ONCE * HD
    block = pl.BlockSpec((frames, wide), lambda i: (0, i))
    return pl.pallas_call(
        attend_back_kernel,
        grid=(width // wide,),
        in_specs=[pl.BlockSpec(memory_space=pltpu.SMEM)] * 2
        + [
            pl.BlockSpec((3, frames, wide), lambda i: (0, 0, i)),
            pl.BlockSpec((frames, width), lambda i: (0, 0)),
            pl.BlockSpec((wide, width), lambda i: (i, 0)),
            pl.BlockSpec((1, HEADS_AT_ONCE, frames), lambda i: (i, 0, 0)),
        ],
        out_specs=[block] * 3,
        out_shape=[jax.ShapeDtypeStruct((frames, width), jnp.bfloat16)] * 3,
        scratch_shapes=[pltpu.VMEM((frames, frames), jnp.float32)],
        compiler_params=params(),
        name="attend_back",
    )(length, slopes, packed, d_out, w, lse)


def gelu_both(x):
    z = jnp.abs(x) * (0.5**0.5)
    bell = jnp.exp(-z * z)
    t = 1.0 / (1.0 + 0.3275911 * z)
    poly = t * (0.254829592 + t * (-0.284496736 + t * (1.421413741 + t * (-1.453152027 + t * 1.061405429))))
    tail = 0.5 * poly * bell
    share = jnp.where(x >= 0, 1.0 - tail, tail)
    return x * share, share + x * bell * (0.5 / math.pi) ** 0.5


def expand_kernel(count, blocks, own_ref, other_ref, *refs):
    sources = refs[:count]
    x_ref, w_out, act_ref, turned_ref, slope_ref, w_ref, sems, out_sems = refs[count:]
    step = pl.program_id(0)
    width = x_ref.shape[1]
    unit = width // sum(source.shape[0] for source in sources)

    def copies(j):
        entry = (w_ref.at[j], (j + 1) * unit, unit, None, sems.at[j])
        return landing((own_ref, other_ref), sources, [entry])

    def kept(j):
        return pltpu.make_async_copy(w_ref.at[j], w_out.at[j], out_sems.at[j])

    def chunk(j):
        if j == 0:
            for n in range(blocks):
                begin(copies(n))
        finish(copies(j))
        kept(j).start()
        hidden = dot_nn(x_ref[...], w_ref[j])
        act, slope = gelu_both(hidden)
        act = as_low(act)
        act_ref[...] = act
        turned_ref[...] = act.T
        slope_ref[...] = as_low(slope)
        if j == blocks - 1:
            for n in range(blocks):
                kept(n).wait()

    for j in range(blocks):
        pl.when(step == j)(partial(chunk, j))


def expand(own, other, pieces, x, blocks):
    frames, width = x.shape
    total = blocks * width
    return pl.pallas_call(
        partial(expand_kernel, len(pieces), blocks),
        grid=(blocks,),
        in_specs=piece_specs(pieces) + [pl.BlockSpec((frames, width), lambda i: (0, 0))],
        out_specs=[
            pl.BlockSpec(memory_space=pl.ANY),
            pl.BlockSpec((frames, width), lambda i: (0, i)),
            pl.BlockSpec((width, frames), lambda i: (i, 0)),
            pl.BlockSpec((frames, width), lambda i: (0, i)),
        ],
        out_shape=[
            jax.ShapeDtypeStruct((blocks, width, width), jnp.bfloat16),
            jax.ShapeDtypeStruct((frames, total), jnp.bfloat16),
            jax.ShapeDtypeStruct((total, frames), jnp.bfloat16),
            jax.ShapeDtypeStruct((frames, total), jnp.bfloat16),
        ],
        scratch_shapes=[
            pltpu.VMEM((blocks, width, width), jnp.bfloat16),
            pltpu.SemaphoreType.DMA((blocks,)),
            pltpu.SemaphoreType.DMA((blocks,)),
        ],
        compiler_params=params(),
        name="expand",
    )(own, other, *pieces, x)


def landing(idx_refs, sources, entries):
    half = len(sources) // 2
    copies = []
    for s, source in enumerate(sources):
        idx_ref = idx_refs[s // half]
        count = source.shape[0]
        for i in range(count):
            band = idx_ref[(s % half) * count + i]
            for goal, start, rows, lane, sem in entries:
                part = source.at[i, pl.ds(start, rows)]
                if lane is not None:
                    part = source.at[i, pl.ds(start, rows), pl.ds(lane, goal.shape[-1])]
                place = goal.at[pl.ds(pl.multiple_of(band * rows, rows), rows)]
                copies.append(pltpu.make_async_copy(part, place, sem))
    return copies


def begin(copies):
    for copy in copies:
        copy.start()


def finish(copies):
    for copy in copies:
        copy.wait()


def piece_specs(pieces):
    smem = pl.BlockSpec(memory_space=pltpu.SMEM)
    return [smem, smem] + [pl.BlockSpec(memory_space=pl.ANY)] * len(pieces)


def gain_row(edge_ref, at):
    return edge_ref[at : at + 1].astype(jnp.float32)


def front_kernel(
    at_gain, count, phone_rows, own_ref, other_ref, *refs
):
    sources = refs[:count]
    states_ref, states_turned_ref, hot_ref, mel_ref, time_ref = refs[count : count + 5]
    (
        small_out, skip_out, embed_ref, stream_ref, joined_ref, normed_ref, turned_ref, edge_ref,
        small_ref, skip_ref, table_ref, sems, out_sems,
    ) = refs[count + 5 :]
    width = stream_ref.shape[1]
    bands = sum(source.shape[0] for source in sources)
    unit = width // bands
    idx = (own_ref, other_ref)
    first = landing(
        idx, sources,
        [(small_ref, 0, unit, None, sems.at[0]), (table_ref, 0, phone_rows, TABLE_AT, sems.at[0])],
    )
    second = landing(idx, sources, [(skip_ref, unit, 2 * unit, None, sems.at[1])])
    begin(first)
    begin(second)
    phones = embed_ref.shape[1]
    joined_ref[width:] = states_turned_ref[...]
    finish(first)
    small_copy = pltpu.make_async_copy(small_ref, small_out, out_sems.at[0])
    small_copy.start()
    edge_ref[...] = small_ref[:, HEAD_AT:].T
    embedded = as_low(dot_nt(hot_ref[...], table_ref[...]))
    embed_ref[...] = embedded
    start = dot_nt(embedded, small_ref[:, :phones])
    start = start + dot_nt(mel_ref[...], small_ref[:, phones:TABLE_AT]) + time_ref[...]
    start = as_low(start)
    joined_ref[:width] = start.T
    finish(second)
    skip_copy = pltpu.make_async_copy(skip_ref, skip_out, out_sems.at[1])
    skip_copy.start()
    stream = dot_nn(start, skip_ref[:width]) + dot_nn(states_ref[...], skip_ref[width:])
    stream_ref[...] = stream
    normed = as_low(normalize(stream)[0] * gain_row(edge_ref, at_gain))
    normed_ref[...] = normed
    turned_ref[...] = normed.T
    small_copy.wait()
    skip_copy.wait()


def front(own, other, pieces, states, states_turned, hot, mel, time, phones, at_gain):
    frames, width = states.shape
    f32, low = jnp.float32, jnp.bfloat16
    bands = sum(p.shape[0] for p in pieces)
    vmem, anywhere = pl.BlockSpec(memory_space=pltpu.VMEM), pl.BlockSpec(memory_space=pl.ANY)
    return pl.pallas_call(
        partial(front_kernel, at_gain, len(pieces), phones // bands),
        in_specs=piece_specs(pieces) + [vmem] * 5,
        out_specs=[anywhere] * 2 + [vmem] * 6,
        out_shape=[
            jax.ShapeDtypeStruct((width, width), low),
            jax.ShapeDtypeStruct((2 * width, width), low),
            jax.ShapeDtypeStruct((frames, phones), low),
            jax.ShapeDtypeStruct((frames, width), f32),
            jax.ShapeDtypeStruct((2 * width, frames), low),
            jax.ShapeDtypeStruct((frames, width), low),
            jax.ShapeDtypeStruct((width, frames), low),
            jax.ShapeDtypeStruct((width - HEAD_AT, width), low),
        ],
        scratch_shapes=[
            pltpu.VMEM((width, width), low),
            pltpu.VMEM((2 * width, width), low),
            pltpu.VMEM((phones, hot.shape[1]), low),
            pltpu.SemaphoreType.DMA((2,)),
            pltpu.SemaphoreType.DMA((2,)),
        ],
        compiler_params=params(),
        name="front",
    )(own, other, *pieces, states, states_turned, hot, mel, time)


def pack_kernel(count, blocks, own_ref, other_ref, *refs):
    sources = refs[:count]
    x_ref, w_out, out_ref, w_ref, sems, out_sems = refs[count:]
    step = pl.program_id(0)
    width = x_ref.shape[1]
    unit = width // sum(source.shape[0] for source in sources)

    def copies(j):
        entry = (w_ref.at[j], j * unit, unit, None, sems.at[j])
        return landing((own_ref, other_ref), sources, [entry])

    def kept(j):
        return pltpu.make_async_copy(w_ref.at[j], w_out.at[j], out_sems.at[j])

    def chunk(j):
        if j == 0:
            for n in range(blocks):
                begin(copies(n))
        finish(copies(j))
        kept(j).start()
        out_ref[0] = as_low(dot_nn(x_ref[...], w_ref[j]))
        if j == blocks - 1:
            for n in range(blocks):
                kept(n).wait()

    for j in range(blocks):
        pl.when(step == j)(partial(chunk, j))


def pack(own, other, pieces, x, blocks):
    frames, width = x.shape
    return pl.pallas_call(
        partial(pack_kernel, len(pieces), blocks),
        grid=(blocks,),
        in_specs=piece_specs(pieces) + [pl.BlockSpec((frames, width), lambda i: (0, 0))],
        out_specs=[
            pl.BlockSpec(memory_space=pl.ANY),
            pl.BlockSpec((1, frames, width), lambda i: (i, 0, 0)),
        ],
        out_shape=[
            jax.ShapeDtypeStruct((blocks, width, width), jnp.bfloat16),
            jax.ShapeDtypeStruct((blocks, frames, width), jnp.bfloat16),
        ],
        scratch_shapes=[
            pltpu.VMEM((blocks, width, width), jnp.bfloat16),
            pltpu.SemaphoreType.DMA((blocks,)),
            pltpu.SemaphoreType.DMA((blocks,)),
        ],
        compiler_params=params(),
        name="pack",
    )(own, other, *pieces, x)


def mid_kernel(at_gain, count, own_ref, other_ref, *refs):
    sources = refs[:count]
    (
        mixed_ref, stream_ref, edge_ref, w_out, mid_ref, in_ref, turned_ref, mixed_turned_ref,
        w_ref, sem, out_sem,
    ) = refs[count:]
    width = stream_ref.shape[1]
    unit = width // sum(source.shape[0] for source in sources)
    copies = landing((own_ref, other_ref), sources, [(w_ref, 0, unit, None, sem)])
    begin(copies)
    mixed = mixed_ref[...]
    mixed_turned_ref[...] = mixed.T
    finish(copies)
    kept = pltpu.make_async_copy(w_ref, w_out, out_sem)
    kept.start()
    mid = stream_ref[...] + dot_nn(mixed, w_ref[...])
    mid_ref[...] = mid
    normed = as_low(normalize(mid)[0] * gain_row(edge_ref, at_gain))
    in_ref[...] = normed
    turned_ref[...] = normed.T
    kept.wait()


def mid_step(own, other, pieces, mixed, stream, edge, at_gain):
    frames, width = stream.shape
    low = jnp.bfloat16
    vmem = pl.BlockSpec(memory_space=pltpu.VMEM)
    return pl.pallas_call(
        partial(mid_kernel, at_gain, len(pieces)),
        in_specs=piece_specs(pieces) + [vmem] * 3,
        out_specs=[pl.BlockSpec(memory_space=pl.ANY)] + [vmem] * 4,
        out_shape=[
            jax.ShapeDtypeStruct((width, width), low),
            jax.ShapeDtypeStruct((frames, width), jnp.float32),
            jax.ShapeDtypeStruct((frames, width), low),
            jax.ShapeDtypeStruct((width, frames), low),
            jax.ShapeDtypeStruct((width, frames), low),
        ],
        scratch_shapes=[
            pltpu.VMEM((width, width), low),
            pltpu.SemaphoreType.DMA,
            pltpu.SemaphoreType.DMA,
        ],
        compiler_params=params(),
        name="mid",
    )(own, other, *pieces, mixed, stream, edge)


def head_kernel(at_gain, count, share_ref, own_ref, other_ref, *refs):
    sources = refs[:count]
    (
        act_ref, mid_ref, edge_ref, target_ref, inside_ref,
        w_out, d_ref, low_ref, grad_ref, gain_grad_ref, error_ref,
        total_ref, w_ref, sem, out_sem,
    ) = refs[count:]
    step = pl.program_id(0)
    tile = act_ref.shape[1]
    rows = w_ref.shape[0] // sum(source.shape[0] for source in sources)
    kept = pltpu.make_async_copy(w_ref, w_out, out_sem)

    @pl.when(step == 0)
    def _():
        copies = landing((own_ref, other_ref), sources, [(w_ref, 0, rows, None, sem)])
        begin(copies)
        finish(copies)
        kept.start()

    part = dot_nn(act_ref[...], w_ref[pl.ds(pl.multiple_of(step * tile, tile), tile)])

    @pl.when(step == 0)
    def _():
        total_ref[...] = mid_ref[...] + part

    @pl.when(step > 0)
    def _():
        total_ref[...] += part

    @pl.when(step == pl.num_programs(0) - 1)
    def _():
        bins = target_ref.shape[1]
        normed, inverse = normalize(total_ref[...])
        gain = gain_row(edge_ref, at_gain)
        head_in = as_low(normed * gain)
        head = edge_ref[:bins]
        inside = inside_ref[...]
        error = dot_nt(head_in, head) - target_ref[...]
        error_ref[...] = jnp.sum(jnp.sum(error * error, 1, keepdims=True) * inside, 0, keepdims=True)
        d_prediction = as_low((2.0 * share_ref[0]) * error * inside)
        grad_ref[...] = dot_tn(head_in, d_prediction)
        d_head_in = dot_nn(d_prediction, head)
        gain_grad_ref[...] = jnp.sum(d_head_in * normed, 0, keepdims=True)
        d_stream = normalize_back(d_head_in * gain, normed, inverse)
        d_ref[...] = d_stream
        low_ref[...] = as_low(d_stream)
        kept.wait()


def head_step(share, own, other, pieces, act, mid, edge, target, inside, at_gain, tile=1024):
    frames, width = mid.shape
    bins = target.shape[1]
    total = act.shape[1]
    whole = lambda *shape: pl.BlockSpec(shape, lambda i: (0,) * len(shape))
    return pl.pallas_call(
        partial(head_kernel, at_gain, len(pieces)),
        grid=(total // tile,),
        in_specs=[pl.BlockSpec(memory_space=pltpu.SMEM)]
        + piece_specs(pieces)
        + [
            pl.BlockSpec((frames, tile), lambda i: (0, i)),
            whole(frames, width), whole(*edge.shape), whole(frames, bins), whole(frames, 1),
        ],
        out_specs=[
            pl.BlockSpec(memory_space=pl.ANY),
            whole(frames, width), whole(frames, width), whole(width, bins), whole(1, width), whole(1, 1),
        ],
        out_shape=[
            jax.ShapeDtypeStruct((total, width), jnp.bfloat16),
            jax.ShapeDtypeStruct((frames, width), jnp.float32),
            jax.ShapeDtypeStruct((frames, width), jnp.bfloat16),
            jax.ShapeDtypeStruct((width, bins), jnp.float32),
            jax.ShapeDtypeStruct((1, width), jnp.float32),
            jax.ShapeDtypeStruct((1, 1), jnp.float32),
        ],
        scratch_shapes=[
            pltpu.VMEM((frames, width), jnp.float32),
            pltpu.VMEM((total, width), jnp.bfloat16),
            pltpu.SemaphoreType.DMA,
            pltpu.SemaphoreType.DMA,
        ],
        compiler_params=params(),
        name="head",
    )(share, own, other, *pieces, act, mid, edge, target, inside)


def ffn_back_kernel(
    at_gain, low_ref, d_ref, down_ref, slope_ref, up_ref, mid_ref, edge_ref,
    out_ref, out_low_ref, gain_grad_ref, *refs,
):
    hidden_refs, total_ref = refs[:-1], refs[-1]
    step = pl.program_id(0)
    d_hidden = as_low(dot_nt(low_ref[...], down_ref[...]) * slope_ref[...].astype(jnp.float32))
    for j, ref in enumerate(hidden_refs):

        @pl.when(step == j)
        def _(ref=ref):
            ref[...] = d_hidden

    part = dot_nt(d_hidden, up_ref[0])

    @pl.when(step == 0)
    def _():
        total_ref[...] = part

    @pl.when(step > 0)
    def _():
        total_ref[...] += part

    @pl.when(step == pl.num_programs(0) - 1)
    def _():
        normed, inverse = normalize(mid_ref[...])
        grad = total_ref[...]
        gain_grad_ref[...] = jnp.sum(grad * normed, 0, keepdims=True)
        out = d_ref[...] + normalize_back(grad * gain_row(edge_ref, at_gain), normed, inverse)
        out_ref[...] = out
        out_low_ref[...] = as_low(out)


def ffn_back(low, d, down, slope, up, mid, edge, at_gain):
    frames, width = mid.shape
    count = up.shape[0]
    whole = lambda *shape: pl.BlockSpec(shape, lambda i: (0,) * len(shape))
    return pl.pallas_call(
        partial(ffn_back_kernel, at_gain),
        grid=(count,),
        in_specs=[
            whole(frames, width), whole(frames, width),
            pl.BlockSpec((width, width), lambda i: (i, 0)),
            pl.BlockSpec((frames, width), lambda i: (0, i)),
            pl.BlockSpec((1, width, width), lambda i: (i, 0, 0)),
            whole(frames, width), whole(*edge.shape),
        ],
        out_specs=[whole(frames, width), whole(frames, width), whole(1, width)]
        + [whole(frames, width)] * count,
        out_shape=[
            jax.ShapeDtypeStruct((frames, width), jnp.float32),
            jax.ShapeDtypeStruct((frames, width), jnp.bfloat16),
            jax.ShapeDtypeStruct((1, width), jnp.float32),
        ]
        + [jax.ShapeDtypeStruct((frames, width), jnp.bfloat16)] * count,
        scratch_shapes=[pltpu.VMEM((frames, width), jnp.float32)],
        compiler_params=params(),
        name="ffn_back",
    )(low, d, down, slope, up, mid, edge)


def pack_back_kernel(at_gain, blocks, *refs):
    w_ref, d_ref, stream_ref, edge_ref, low_ref, gain_grad_ref, total_ref = refs[blocks:]
    step = pl.program_id(0)

    def chunk(j):
        part = dot_nt(refs[j][...], w_ref[0])
        total_ref[...] = part if j == 0 else total_ref[...] + part

    for j in range(blocks):
        pl.when(step == j)(partial(chunk, j))

    @pl.when(step == pl.num_programs(0) - 1)
    def _():
        grad = total_ref[...]
        normed, inverse = normalize(stream_ref[...])
        gain_grad_ref[...] = jnp.sum(grad * normed, 0, keepdims=True)
        gain = gain_row(edge_ref, at_gain)
        low_ref[...] = as_low(d_ref[...] + normalize_back(grad * gain, normed, inverse))


def pack_back(packed, w, d, stream, edge, at_gain):
    frames, width = stream.shape
    whole = lambda *shape: pl.BlockSpec(shape, lambda i: (0,) * len(shape))
    return pl.pallas_call(
        partial(pack_back_kernel, at_gain, w.shape[0]),
        grid=(w.shape[0],),
        in_specs=[whole(frames, width)] * w.shape[0]
        + [
            pl.BlockSpec((1, width, width), lambda i: (i, 0, 0)),
            whole(frames, width), whole(frames, width), whole(*edge.shape),
        ],
        out_specs=[whole(frames, width), whole(1, width)],
        out_shape=[
            jax.ShapeDtypeStruct((frames, width), jnp.bfloat16),
            jax.ShapeDtypeStruct((1, width), jnp.float32),
        ],
        scratch_shapes=[pltpu.VMEM((frames, width), jnp.float32)],
        compiler_params=params(),
        name="pack_back",
    )(*packed, w, d, stream, edge)


def tail_kernel(
    at_gain, d_ref, skip_ref, small_ref, embed_ref, mel_ref, hot_ref, head_ref, one_ref, two_ref, three_ref,
    main_ref, table_ref, edge_ref,
):
    phones = embed_ref.shape[1]
    d_start = as_low(dot_nt(d_ref[...], skip_ref[...]))
    d_phones = as_low(dot_nn(d_start, small_ref[:, :phones]))
    main_ref[:, :phones] = as_low(dot_tn(d_start, embed_ref[...]))
    main_ref[:, phones:] = as_low(dot_tn(d_start, mel_ref[...]))
    table_ref[...] = as_low(dot_tn(d_phones, hot_ref[...]))
    edge = head_ref[...]
    lanes = edge.shape[1]
    edge = jnp.pad(edge, ((0, 0), (0, edge_ref.shape[1] - lanes)))
    lane = lax.broadcasted_iota(jnp.int32, edge.shape, 1)
    for j, ref in enumerate((one_ref, two_ref, three_ref)):
        column = jnp.broadcast_to(ref[...], (8, edge.shape[0])).T[:, :1]
        edge = jnp.where(lane == at_gain + j, column, edge)
    edge_ref[...] = as_low(edge)


def tail(d, skip, small, embed, mel, hot, head, gains, at_gain):
    width = d.shape[1]
    phones = embed.shape[1]
    whole = lambda x: pl.BlockSpec(x.shape, lambda i: (0, 0))
    arrays = (small, embed, mel, hot, head, *gains)
    shapes = [(width, TABLE_AT), (phones, hot.shape[1]), (width, width - HEAD_AT)]
    return pl.pallas_call(
        partial(tail_kernel, at_gain),
        grid=(1,),
        in_specs=[whole(d), pl.BlockSpec((width, width), lambda i: (0, 0))] + [whole(x) for x in arrays],
        out_specs=[pl.BlockSpec(s, lambda i: (0, 0)) for s in shapes],
        out_shape=[jax.ShapeDtypeStruct(s, jnp.bfloat16) for s in shapes],
        compiler_params=params(),
        name="tail",
    )(d, skip, *arrays)


def grads_kernel(plan, count, rows, legs, came_too, idx_ref, *refs):
    refs, picked_ref, right_ref, sems = refs[:-3], refs[-3], refs[-2], refs[-1]
    outs = refs[len(refs) - legs :]
    came_ref = refs[len(refs) - legs - 1] if came_too else None
    step = pl.program_id(0)
    each = count // legs

    def copies(c):
        lefts, rights, stride, offset = plan[c]
        if rights is None:
            return []
        slot = c % 2
        return [
            pltpu.make_async_copy(
                refs[left].at[pl.ds(pl.multiple_of(idx_ref[i] * stride + offset, rows), rows)],
                picked_ref.at[slot, side, pl.ds(i * rows, rows)],
                sems.at[slot],
            )
            for side, left in enumerate(lefts)
            for i in range(count)
        ] + [
            pltpu.make_async_copy(refs[right], right_ref.at[slot, side], sems.at[slot])
            for side, right in enumerate(rights)
        ]

    def chunk(c):
        lefts, rights, _, _ = plan[c]
        if c == 0:
            for copy in copies(0):
                copy.start()
        if c + 1 < len(plan):
            for copy in copies(c + 1):
                copy.start()
        for copy in copies(c):
            copy.wait()
        if rights is None:
            main, table, edge = (refs[r] for r in lefts)
            thick = table.shape[0] // (main.shape[0] // rows)
            blocks = []
            for i in range(count):
                start = pl.multiple_of(idx_ref[i] * rows, rows)
                short = pl.multiple_of(idx_ref[i] * thick, thick)
                lead = table[pl.ds(short, thick)]
                rest = jnp.zeros((rows - thick, lead.shape[1]), lead.dtype)
                middle = jnp.concatenate([lead, rest], 0) if thick < rows else lead
                block = [main[pl.ds(start, rows)], middle, edge[pl.ds(start, rows)]]
                blocks.append(jnp.concatenate(block, 1).astype(jnp.float32))
            total = jnp.stack(blocks)
            if came_too:
                total = total + came_ref[...].astype(jnp.float32)
        else:
            wide = outs[0].shape[2]
            total = sum(dot_nn(picked_ref[c % 2, side], right_ref[c % 2, side]) for side in range(len(rights)))
            total = total.reshape(count, rows, wide)
        for f in range(legs):
            outs[f][...] = as_low(total[f * each : (f + 1) * each])

    for c in range(len(plan)):
        pl.when(step == c)(partial(chunk, c))


def grads(plan, arrays, idx, frames, rows, width, legs, came=None):
    count = idx.shape[0]
    copied = [j for entry in plan if entry[1] is not None for j in entry[0] + entry[1]]

    def spec(j, x):
        if j in copied:
            return pl.BlockSpec(memory_space=pltpu.HBM)
        return pl.BlockSpec(x.shape, lambda i, n=len(x.shape): (0,) * n)

    specs = [spec(j, x) for j, x in enumerate(arrays)]
    if came is not None:
        specs.append(pl.BlockSpec((count, rows, width), lambda i: (0, 0, 0)))
        arrays = list(arrays) + [came]
    return pl.pallas_call(
        partial(grads_kernel, plan, count, rows, legs, came is not None),
        grid=(len(plan),),
        in_specs=[pl.BlockSpec(memory_space=pltpu.SMEM)] + specs,
        out_specs=[pl.BlockSpec((count // legs, rows, width), lambda i: (0, i, 0))] * legs,
        out_shape=[jax.ShapeDtypeStruct((count // legs, rows * len(plan), width), jnp.bfloat16)] * legs,
        scratch_shapes=[
            pltpu.VMEM((2, 2, count * rows, frames), jnp.bfloat16),
            pltpu.VMEM((2, 2, frames, width), jnp.bfloat16),
            pltpu.SemaphoreType.DMA((2,)),
        ],
        compiler_params=params(),
        name="grads",
    )(idx, *arrays)


def fold_kernel(legs, *refs):
    ins, outs = refs[:-legs], refs[-legs:]
    took = len(ins) // legs
    for j in range(legs):
        total = ins[j * took][...].astype(jnp.float32)
        for ref in ins[j * took + 1 : (j + 1) * took]:
            total = total + ref[...].astype(jnp.float32)
        outs[j][...] = as_low(total)


def fold(parts, legs):
    count, rows, width = parts[0].shape
    each = count // legs
    tile = rows // 2
    return pl.pallas_call(
        partial(fold_kernel, legs),
        grid=(rows // tile,),
        in_specs=[
            pl.BlockSpec((each, tile, width), lambda i, j=j: (j, i, 0)) for j in range(legs) for _ in parts
        ],
        out_specs=[pl.BlockSpec((each, tile, width), lambda i: (0, i, 0))] * legs,
        out_shape=[jax.ShapeDtypeStruct((each, rows, width), jnp.bfloat16)] * legs,
        compiler_params=params(),
        name="fold",
    )(*[p for _ in range(legs) for p in parts])


def stack_kernel(*refs):
    ins, out, sem = refs[:-2], refs[-2], refs[-1]
    copies = [pltpu.make_async_copy(ref, out.at[i], sem) for i, ref in enumerate(ins)]
    for copy in copies:
        copy.start()
    for copy in copies:
        copy.wait()


def stack(parts):
    return pl.pallas_call(
        stack_kernel,
        in_specs=[pl.BlockSpec(memory_space=pl.ANY)] * len(parts),
        out_specs=pl.BlockSpec(memory_space=pltpu.VMEM),
        out_shape=jax.ShapeDtypeStruct((len(parts),) + parts[0].shape, parts[0].dtype),
        scratch_shapes=[pltpu.SemaphoreType.DMA],
        compiler_params=params(),
        name="stack",
    )(*parts)


def update(grad, rate, master_ref, moment_ref, square_ref, clip):
    return adam_step(master_ref[...], grad * clip, moment_ref[...], square_ref[...], rate)


def adam_kernel(at, clip_ref, *refs):
    phone_rows, phone_width, inputs, at_gain = at
    last, attend, expand, reduce = refs[:4]
    masters, moments, squares = refs[4:13], refs[13:22], refs[22:31]
    outs = refs[31:]
    unit = last.shape[0] // 3
    small = last[2 * unit :]
    clip = clip_ref[0]
    mel_lanes = inputs - phone_width
    lanes = [small[:, phone_width : phone_width + mel_lanes], small[:, :phone_width]]
    edge = small[:, HEAD_AT:]
    turned_edge = edge.T
    bins = masters[7].shape[1]

    def columns(ref, first):
        blocks = [ref[j : j + unit] for j in range(first, ref.shape[0], unit)]
        return jnp.concatenate(blocks, 1)

    grads_of = [
        jnp.concatenate(lanes, 1),
        small[:phone_rows, TABLE_AT:HEAD_AT],
        last[: 2 * unit],
        columns(attend, unit),
        attend[:unit],
        columns(expand, 0),
        reduce[...],
        edge[:, :bins],
        turned_edge[at_gain : at_gain + 3],
    ]
    for j, grad in enumerate(grads_of):
        rate = GAIN_RATE if j in (1, 8) else LEARN_RATE
        after = update(grad, rate, masters[j], moments[j], squares[j], clip)
        for n, value in enumerate(after):
            outs[9 * n + j][...] = value


def adam(clip, shares, masters, moments, squares, at):
    turned = lambda group: [x.T if j < 2 else x for j, x in enumerate(group)]
    masters, moments, squares = turned(masters), turned(moments), turned(squares)
    vmem = pl.BlockSpec(memory_space=pltpu.VMEM)
    arrays = [*shares, *masters, *moments, *squares]
    results = pl.pallas_call(
        partial(adam_kernel, at),
        in_specs=[pl.BlockSpec(memory_space=pltpu.SMEM)] + [vmem] * len(arrays),
        out_specs=[vmem] * 27,
        out_shape=[jax.ShapeDtypeStruct(x.shape, jnp.float32) for x in (*masters, *moments, *squares)],
        compiler_params=params(),
        name="adam",
    )(clip, *arrays)
    return [y for n in range(3) for y in turned(results[9 * n : 9 * n + 9])]


def prepare_kernel(at_mel, at_count, frames, facts_ref, input_ref, table_ref, head_ref, gains_ref, skip_ref, out_ref):
    unit, inputs = input_ref.shape
    phones = inputs - at_mel
    turned = as_low(input_ref[...])
    out_ref[0, :unit, :phones] = turned[:, at_mel:]
    out_ref[0, :unit, phones:TABLE_AT] = jnp.pad(turned[:, :at_mel], ((0, 0), (0, TABLE_AT - inputs)))
    table = as_low(table_ref[...])
    rest = jnp.zeros((unit - table.shape[0], table.shape[1]), jnp.bfloat16)
    out_ref[0, :unit, TABLE_AT:HEAD_AT] = jnp.concatenate([table, rest], 0)
    bins = head_ref.shape[1]
    edge = jnp.pad(head_ref[...], ((0, 0), (0, out_ref.shape[2] - HEAD_AT - bins)))
    lane = lax.broadcasted_iota(jnp.int32, edge.shape, 1)
    spot = (gains_ref.shape[0], edge.shape[1])
    row = lax.broadcasted_iota(jnp.int32, spot, 0)
    here = lax.broadcasted_iota(jnp.int32, spot, 1) == row + bins
    edge = as_low(edge).astype(jnp.float32) + dot_tn(as_low(gains_ref[...]), as_low(here))
    end = jnp.minimum(jnp.minimum(facts_ref[2], facts_ref[3]), frames)
    count = jnp.maximum(end - jnp.maximum(facts_ref[1], 0), 0)
    for j, fact in enumerate((facts_ref[0], lax.div(count, 16), lax.rem(count, 16))):
        edge = jnp.where(lane == at_count - HEAD_AT + j, fact.astype(jnp.float32), edge)
    out_ref[0, :unit, HEAD_AT:] = as_low(edge)
    out_ref[0, unit:] = as_low(skip_ref[...])
    for z in range(1, out_ref.shape[0]):
        out_ref[z] = out_ref[0]


def prepare(facts, turned, table, head, gains, skip, deep, frames, at_mel, at_count):
    vmem = pl.BlockSpec(memory_space=pltpu.VMEM)
    rows, width = turned.shape[0] + skip.shape[0], skip.shape[1]
    return pl.pallas_call(
        partial(prepare_kernel, at_mel, at_count, frames),
        in_specs=[pl.BlockSpec(memory_space=pltpu.SMEM)] + [vmem] * 5,
        out_specs=vmem,
        out_shape=jax.ShapeDtypeStruct((deep, rows, width), jnp.bfloat16),
        compiler_params=params(),
        name="prepare",
    )(facts, turned, table, head, gains, skip)


def shards(
    grid,
    fast,
    clean_mel,
    gauss_noise,
    flow_time,
    phone_ids,
    lengths,
    span_start,
    span_end,
    speaker,
    skip_states,
    w_input,
    phone_table,
    w_skip,
    w_attend,
    w_output,
    w_expand,
    w_reduce,
    w_head,
    norm_gains,
    moment_input,
    moment_table,
    moment_skip,
    moment_attend,
    moment_output,
    moment_expand,
    moment_reduce,
    moment_head,
    moment_gains,
    square_input,
    square_table,
    square_skip,
    square_attend,
    square_output,
    square_expand,
    square_reduce,
    square_head,
    square_gains,
):
    masters = (w_input, phone_table, w_skip, w_attend, w_output, w_expand, w_reduce, w_head, norm_gains)
    moments = (
        moment_input, moment_table, moment_skip, moment_attend, moment_output,
        moment_expand, moment_reduce, moment_head, moment_gains,
    )
    squares = (
        square_input, square_table, square_skip, square_attend, square_output,
        square_expand, square_reduce, square_head, square_gains,
    )
    frames, mel_bins = clean_mel.shape
    width = w_skip.shape[1]
    heads = width // HD
    devices = grid.total
    unit = width // devices
    inputs = w_input.shape[0]
    phones = phone_table.shape[0]
    phone_wide = phone_table.shape[1]
    phone_width = phone_wide * devices
    mel_lanes = TABLE_AT - phone_width
    at_gain = HEAD_AT + mel_bins
    at_count = at_gain + 3
    position = jnp.arange(frames)
    frame_valid = (position < lengths[0]).astype(jnp.float32)
    frame_inside = ((position >= span_start[0]) & (position < span_end[0])).astype(
        jnp.float32
    ) * frame_valid
    speaker_hot = (speaker[0] == jnp.arange(SPK)).astype(jnp.float32)
    count = jnp.sum(frame_inside)
    count_high = jnp.floor(count / 16.0)
    tally = jnp.stack([speaker[0].astype(jnp.float32), count_high, count - 16.0 * count_high])

    low_input = as_low(w_input)
    small = jnp.concatenate(
        [
            low_input[2 * mel_bins :].T,
            low_input[: 2 * mel_bins].T,
            jnp.zeros((unit, TABLE_AT - inputs), jnp.bfloat16),
            jnp.pad(as_low(phone_table).T, ((0, unit - phone_wide), (0, 0))),
            as_low(w_head),
            as_low(norm_gains).T,
            jnp.broadcast_to(as_low(tally)[None, :], (unit, 3)),
            jnp.zeros((unit, width - at_count - 3), jnp.bfloat16),
        ],
        1,
    )

    def blocks(x):
        return [as_low(x[:, j : j + width]) for j in range(0, x.shape[1], width)]

    attend_blocks, expand_blocks = blocks(w_attend), blocks(w_expand)
    packs, wides = len(attend_blocks), len(expand_blocks)
    stages = [
        [("small", None, small), ("skip", None, as_low(w_skip))],
        [("attend", j, w) for j, w in enumerate(attend_blocks)],
        [("output", None, as_low(w_output))] + [("expand", j, w) for j, w in enumerate(expand_blocks)],
        [("reduce", None, as_low(w_reduce))],
    ]
    if fast:
        own, other = grid.owners(0, -1), grid.owners(1, -1)
        own_turned, other_turned = grid.owners(0, -1, True), grid.owners(1, -1, True)
        mine, theirs = grid.owners(0, 1), grid.owners(1, 1)

    def load(stage):
        return jnp.concatenate([w for _, _, w in stage], 0)

    def sibling(x):
        return shift(grid, x, "core", 1)

    def along(x, role, *after):
        return spread(grid, tied(x, *after) if after else x, role)

    def copies(x):
        return jnp.broadcast_to(x[None], (grid.size("z"),) + x.shape)

    def deepen(x, *after):
        return swap_deep(grid, tied(x, *after) if after else x)

    def plane(moved):
        return stack(moved).reshape((-1,) + moved[0].shape[1:])

    def gather_whole(stage):
        rows = lax.all_gather(load(stage), AXES, axis=0, tiled=False)
        parts, start = [], 0
        for name, _, w in stage:
            part = rows[:, start : start + w.shape[0]]
            start += w.shape[0]
            if name == "small":
                table = part[:, :phone_wide, TABLE_AT:HEAD_AT].reshape(BANDS, -1, phones)
                table = jnp.pad(table, ((0, 0), (0, width // BANDS - table.shape[1]), (0, 0)))
                part = part.reshape(BANDS, -1, width)
                part = jnp.concatenate([part[..., :TABLE_AT], table, part[..., HEAD_AT:]], 2)
            parts.append(part.reshape(BANDS, -1, width))
        rows = jnp.concatenate(parts, 1)
        return [rows[: BANDS // 2], rows[BANDS // 2 :]]

    flow = flow_time[0]
    noisy_mel = (1.0 - (1.0 - SIGMA) * flow) * gauss_noise + flow * clean_mel
    context = clean_mel * (frame_valid - frame_inside)[:, None]
    target = clean_mel - (1.0 - SIGMA) * gauss_noise
    mel = jnp.concatenate([as_low(noisy_mel), as_low(context)], 1)
    mel = jnp.pad(mel, ((0, 0), (0, mel_lanes - mel.shape[1])))
    phone_hot = as_low(phone_ids[:, None] == jnp.arange(phones)[None, :])
    slopes = head_slopes(heads)
    times = time_features(flow, width)[None, :]
    inside = frame_inside[:, None]
    states_turned = skip_states.T
    loads = [load(stage) for stage in stages]
    if fast:
        if unit % 16 == 0 and inputs % 16 == 0:
            first = prepare(
                jnp.stack([speaker[0], span_start[0], span_end[0], lengths[0]]), w_input.T, phone_table.T,
                w_head, norm_gains, w_skip, grid.size("z"), frames, 2 * mel_bins, at_count,
            )
        else:
            first = copies(loads[0])
        deep_0, near_2, load_1, load_3 = join(
            deepen(first), along(loads[2], "near"), copies(loads[1]), copies(loads[3])
        )
        pair_2 = copies(stack(near_2))
        near_0, deep_1, pair_2, target, mel, phone_hot, slopes, times, inside, states_turned = join(
            along(deep_0, "near", pair_2), deepen(load_1, deep_0), pair_2,
            target, mel, phone_hot, slopes, times, inside, states_turned,
        )
        near_0 = plane(near_0)
        deep_2 = deepen(pair_2, near_0)
        far_0, core_0, near_1, own, other, own_turned, other_turned, mine, theirs = join(
            along(near_0, "far")[1], sibling(near_0), along(deep_1, "near", near_0),
            own, other, own_turned, other_turned, mine, theirs,
        )
        near_1 = plane(near_1)
        far_0 = tied(far_0, near_1)
        pieces_0 = [near_0, far_0, core_0, sibling(far_0)]
        far_1 = along(near_1, "far")[1]
        core_1 = sibling(near_1)
    else:
        own, other = jnp.arange(BANDS // 2), jnp.arange(BANDS // 2, BANDS)
        own_turned, other_turned = own, other
        pieces_0 = gather_whole(stages[0])
    small_full, skip_full, embedded, stream, joined_turned, attn_in, attn_turned, edges = front(
        own, other, pieces_0, skip_states, states_turned, phone_hot, mel, times, phone_width, mel_bins
    )
    tallies = edges[at_count - HEAD_AT : at_count - HEAD_AT + 3].reshape(3, devices, unit)
    tallies = tallies[:, :, 0].astype(jnp.float32)
    counts = jnp.sum(
        (tallies[0][:, None] == jnp.arange(SPK, dtype=jnp.float32)[None, :])
        * (16.0 * tallies[1] + tallies[2])[:, None],
        0,
    )
    share = jnp.sum(speaker_hot / jnp.maximum(counts, 1.0)) / SPK

    if fast:
        far_1, core_1, deep_2, embedded, stream, attn_in, attn_turned, edges, share, counts = join(
            far_1, core_1, deep_2, embedded, stream, attn_in, attn_turned, edges, share, counts
        )
        near_2 = deep_2.reshape((-1,) + deep_2.shape[2:])
        pieces_1 = [near_1, far_1, core_1, sibling(far_1)]
        far_2 = along(near_2, "far")[1]
        core_2 = sibling(near_2)
        deep_3 = deepen(load_3, near_2)
    else:
        pieces_1 = gather_whole(stages[1])
    attend_full, packed = pack(own, other, pieces_1, attn_in, packs)
    mixed, lse = attend(lengths, slopes, packed)
    if fast:
        far_2, deep_3, core_2, packed, mixed, lse, joined_turned = join(
            far_2, deep_3, core_2, packed, mixed, lse, joined_turned
        )
        near_3 = along(deep_3, "near")
        pieces_2 = [near_2, far_2, core_2, sibling(far_2)]
    else:
        pieces_2 = gather_whole(stages[2])
    output_full, stream_mid, ffn_in, ffn_turned, mixed_turned = mid_step(
        own_turned, other_turned, pieces_2, mixed, stream, edges, mel_bins + 1
    )
    if fast:
        near_3 = plane([near_3[0], tied(near_3[1], ffn_in)] + near_3[2:])
        far_3 = along(near_3, "far")[1]
        core_3 = sibling(near_3)
    expand_full, activated, act_turned, gelu_slope = expand(
        own_turned, other_turned, pieces_2, ffn_in, wides
    )
    if fast:
        far_3, core_3, stream_mid, ffn_turned, mixed_turned, activated, act_turned, gelu_slope = join(
            far_3, core_3, stream_mid, ffn_turned, mixed_turned, activated, act_turned, gelu_slope
        )
        pieces_3 = [near_3, far_3, core_3, sibling(far_3)]
    else:
        pieces_3 = gather_whole(stages[3])
    reduce_full, d_stream_out, d_branch, grad_head, grad_gain_three, error_sum = head_step(
        share[None], own, other, pieces_3, activated, stream_mid, edges, target, inside, mel_bins + 2
    )
    far, near, deep = (grid.size(r) for r in ("far", "near", "z"))

    def both(*arrays):
        return [y for x in arrays for y in (x, sibling(x))]

    def sums(plan, arrays, *others, **options):
        first = [tied(arrays[0], *others)] if others else arrays[:1]
        return grads(plan, first + arrays[1:], mine, frames, unit, width, far, **options)

    def hops(legs, role, *others):
        sent = [tied(leg, *others) if others else leg for leg in legs[1:]]
        return [shift(grid, leg, role, j + 1) for j, leg in enumerate(sent)]

    def dense(pairs):
        parts = []
        for turned, right, stride, offset in pairs:
            if right is None:
                part = turned.reshape(devices, unit, width)
            else:
                turned = turned.reshape(devices, stride, frames)[:, offset : offset + unit]
                part = dot_nn(turned.reshape(width, frames), right).reshape(devices, unit, width)
            parts.append(part)
        return lax.psum_scatter(jnp.concatenate(parts, 1), AXES, scatter_dimension=0)

    offsets = [j * unit for j in range(wides)]
    if fast:
        plan = [((0, 1), (2, 3), wides * unit, o) for o in offsets]
        legs_0 = sums(plan, both(tied(act_turned, pieces_3[3]), d_branch))
        moved_0 = hops(legs_0, "far")
        d_branch_next = tied(d_branch, legs_0[0])
    else:
        share_reduce = dense([(act_turned, d_branch, wides * unit, o) for o in offsets])
        d_branch_next = d_branch
    d_stream_mid, d_out, grad_gain_two, *d_hidden = ffn_back(
        d_branch_next, d_stream_out, reduce_full, gelu_slope, expand_full, stream_mid, edges, mel_bins + 1
    )
    if fast:
        turned = both(ffn_turned)
        d_hiddens = both(*d_hidden)
        moved_0, turned, d_hiddens, d_stream_mid, d_out = join(
            moved_0, turned, d_hiddens, d_stream_mid, d_out
        )
        legs_0 = fold([legs_0[0]] + moved_0, near)
        moved_0 = hops(legs_0, "near")
        plan = [((0, 1), (2 + 2 * j, 3 + 2 * j), unit, 0) for j in range(wides)]
        legs_1 = sums(plan, turned + d_hiddens, legs_0[0])
        turned = both(tied(mixed_turned, legs_0[0]), attn_turned, d_out)
        moved_0, legs_1, turned, d_out = join(moved_0, legs_1, turned, d_out)
        (sums_0,) = fold([legs_0[0]] + moved_0, 1)
        d_out = tied(d_out, sums_0)
        moved_1 = hops(legs_1, "far", sums_0)
        sums_0 = swap_deep(grid, sums_0)
    else:
        share_expand = dense([(ffn_turned, d, unit, 0) for d in d_hidden])
    d_packed = attend_back(lengths, slopes, packed, d_out, output_full, lse)
    d_joined_in, grad_gain_one = pack_back(
        d_packed, attend_full, d_stream_mid, stream, edges, mel_bins
    )
    if fast:
        d_packs = both(*d_packed)
        moved_1, sums_0, d_packs, d_joined_in = join(moved_1, sums_0, d_packs, d_joined_in)
        legs_1 = fold([legs_1[0]] + moved_1, near)
        moved_1 = hops(legs_1, "near")
        plan = [((0, 1), (4, 5), unit, 0)]
        plan = plan + [((2, 3), (6 + 2 * j, 7 + 2 * j), unit, 0) for j in range(packs)]
        legs_2 = sums(plan, turned + d_packs, legs_1[0])
        joined = both(tied(joined_turned, legs_1[0]), tied(d_joined_in, legs_1[0]))
        moved_1, legs_2, joined, d_joined_in = join(moved_1, legs_2, joined, d_joined_in)
        (sums_1,) = fold([legs_1[0]] + moved_1, 1)
        d_joined_in = tied(d_joined_in, sums_1)
        moved_2 = hops(legs_2, "far", sums_1)
        sums_1 = swap_deep(grid, sums_1)
    else:
        share_attend = dense(
            [(mixed_turned, d_out, unit, 0)] + [(attn_turned, d, unit, 0) for d in d_packed]
        )
    gain_grads = [grad_gain_one, grad_gain_two, grad_gain_three]
    small_grads = tail(
        d_joined_in, skip_full, small_full, embedded, mel, phone_hot, grad_head, gain_grads, mel_bins
    )
    if fast:
        small_grads = list(small_grads)
        (sent,) = grads([((0, 1, 2), None, 0, 0)], small_grads, theirs, frames, unit, width, 1)
        plan = [((0, 1), (2, 3), 2 * unit, o) for o in offsets[:2]] + [((4, 5, 6), None, 0, 0)]
        legs_3 = sums(plan, joined + small_grads, sent, came=sibling(sent))
        moved_2, legs_3 = join(moved_2, legs_3)
        legs_2 = fold([legs_2[0]] + moved_2, near)
        moved_3 = hops(legs_3, "far", legs_2[0])
        moved_2, sums_1 = join(hops(legs_2, "near"), sums_1)
        (sums_2,) = fold([legs_2[0]] + moved_2, 1)
        moved_3 = [tied(moved_3[0], sums_2)] + moved_3[1:]
        legs_3 = fold([legs_3[0]] + moved_3, near)
        moved_3, sums_2 = join(hops(legs_3, "near"), swap_deep(grid, sums_2))
        (sums_3,) = fold([legs_3[0]] + moved_3, 1)
        sums_3 = swap_deep(grid, sums_3)
        share_reduce, share_expand, share_attend, share_last = [
            jnp.sum(x.astype(jnp.float32), 0) for x in (sums_0, sums_1, sums_2, sums_3)
        ]
    else:
        main, table, edge = small_grads
        table = table.reshape(devices, phone_wide, phones)
        table = jnp.pad(table, ((0, 0), (0, unit - phone_wide), (0, 0))).reshape(width, phones)
        small_grads = jnp.concatenate([main, table, edge], 1).astype(jnp.float32)
        share_last = dense(
            [(joined_turned, d_joined_in, 2 * unit, o) for o in offsets[:2]]
            + [(small_grads, None, 0, 0)]
        )

    shares = (share_last, share_attend, share_expand, share_reduce)
    local_square = sum((jnp.sum(g * g) for g in shares))
    totals = all_sum(grid, jnp.concatenate([speaker_hot * error_sum[0, 0], local_square[None]]))
    sums, total_square = totals[:SPK], totals[SPK]
    loss_value = jnp.mean(sums / jnp.maximum(counts, 1.0))
    grad_norm = jnp.sqrt(total_square)
    clip = jnp.minimum(1.0, 1.0 / (grad_norm + 1e-06))
    at = (phone_wide, phone_width, inputs, mel_bins)
    results = adam(clip[None], shares, masters, moments, squares, at)
    return (loss_value, grad_norm, *results)


def solution(mesh):
    grid = Grid(mesh)
    in_specs = (
        P(("wide", "narrow"), None),
        P(("wide", "narrow"), None),
        P(("wide", "narrow")),
        P(("wide", "narrow")),
        P(("wide", "narrow")),
        P(("wide", "narrow")),
        P(("wide", "narrow")),
        P(("wide", "narrow")),
        P(("wide", "narrow"), None),
        P(None, ("wide", "narrow")),
        P(None, ("wide", "narrow")),
        P(("wide", "narrow"), None),
        P(("wide", "narrow"), None),
        P(("wide", "narrow"), None),
        P(("wide", "narrow"), None),
        P(("wide", "narrow"), None),
        P(("wide", "narrow"), None),
        P(None, ("wide", "narrow")),
        P(None, ("wide", "narrow")),
        P(None, ("wide", "narrow")),
        P(("wide", "narrow"), None),
        P(("wide", "narrow"), None),
        P(("wide", "narrow"), None),
        P(("wide", "narrow"), None),
        P(("wide", "narrow"), None),
        P(("wide", "narrow"), None),
        P(None, ("wide", "narrow")),
        P(None, ("wide", "narrow")),
        P(None, ("wide", "narrow")),
        P(("wide", "narrow"), None),
        P(("wide", "narrow"), None),
        P(("wide", "narrow"), None),
        P(("wide", "narrow"), None),
        P(("wide", "narrow"), None),
        P(("wide", "narrow"), None),
        P(None, ("wide", "narrow")),
    )
    out_specs = (
        P(),
        P(),
        P(None, ("wide", "narrow")),
        P(None, ("wide", "narrow")),
        P(("wide", "narrow"), None),
        P(("wide", "narrow"), None),
        P(("wide", "narrow"), None),
        P(("wide", "narrow"), None),
        P(("wide", "narrow"), None),
        P(("wide", "narrow"), None),
        P(None, ("wide", "narrow")),
        P(None, ("wide", "narrow")),
        P(None, ("wide", "narrow")),
        P(("wide", "narrow"), None),
        P(("wide", "narrow"), None),
        P(("wide", "narrow"), None),
        P(("wide", "narrow"), None),
        P(("wide", "narrow"), None),
        P(("wide", "narrow"), None),
        P(None, ("wide", "narrow")),
        P(None, ("wide", "narrow")),
        P(None, ("wide", "narrow")),
        P(("wide", "narrow"), None),
        P(("wide", "narrow"), None),
        P(("wide", "narrow"), None),
        P(("wide", "narrow"), None),
        P(("wide", "narrow"), None),
        P(("wide", "narrow"), None),
        P(None, ("wide", "narrow")),
    )

    def body(*args):
        unit = args[11].shape[1] // grid.total
        return shards(grid, unit % 32 == 0, *args)

    return jax.shard_map(body, mesh=mesh, in_specs=in_specs, out_specs=out_specs, check_vma=False)
```

```python
from functools import partial
import math

import jax
import jax.numpy as jnp
from jax import lax
from jax.experimental import pallas as pl
from jax.experimental.pallas import tpu as pltpu
from jax.sharding import PartitionSpec as P

HD = 64
SPK = 16
STEP = 10


SIGMA = 1e-05
NORM_EPS = 1e-05
LEARN_RATE = 0.01
GAIN_RATE = 0.3
BETA_ONE = 0.5
BETA_TWO = 0.5
DECAY = 0.01
ADAM_EPS = 1e-08
FAR_AWAY = -1e30
VMEM = 64 * 1024 * 1024
TABLE_AT = 768
HEAD_AT = 896
BANDS = 32
HEADS_AT_ONCE = 4


def as_low(x):
    return x.astype(jnp.bfloat16)


def contract_rows(left, right):
    return lax.dot_general(
        left, right, (((0,), (0,)), ((), ())), preferred_element_type=jnp.float32
    )


def time_features(flow, width):
    half = width // 2
    freqs = jnp.exp(-math.log(10000.0) * jnp.arange(half, dtype=jnp.float32) / half)
    angle = 1000.0 * flow * freqs
    return jnp.concatenate([jnp.sin(angle), jnp.cos(angle)])


def normalize(x):
    centered = x - jnp.mean(x, -1, keepdims=True)
    inverse = lax.rsqrt(jnp.mean(centered * centered, -1, keepdims=True) + NORM_EPS)
    return (centered * inverse, inverse)


def normalize_back(grad, normed, inverse):
    return inverse * (
        grad
        - jnp.mean(grad, -1, keepdims=True)
        - normed * jnp.mean(grad * normed, -1, keepdims=True)
    )


def head_slopes(heads):
    return 2.0 ** (-8.0 * (jnp.arange(heads, dtype=jnp.float32) + 1.0) / heads)


def adam_step(master, grad, moment, square, rate):
    moment = BETA_ONE * moment + (1.0 - BETA_ONE) * grad
    square = BETA_TWO * square + (1.0 - BETA_TWO) * grad * grad
    moment_hat = moment / (1.0 - BETA_ONE**STEP)
    square_hat = square / (1.0 - BETA_TWO**STEP)
    master = master - rate * (moment_hat / (jnp.sqrt(square_hat) + ADAM_EPS) + DECAY * master)
    return (master, moment, square)


AXES = ("wide", "narrow")


def grid_sizes(wide, narrow):
    low = 1
    while (2 * low) * (2 * low) <= wide:
        low *= 2
    return (wide // low, low, narrow // 2, 2)


class Grid:
    def __init__(self, mesh):
        self.sizes = grid_sizes(mesh.shape["wide"], mesh.shape["narrow"])
        self.total = mesh.shape["wide"] * mesh.shape["narrow"]

    def coords(self, index):
        out = []
        for size in reversed(self.sizes):
            out.append(index % size)
            index = index // size
        return out[::-1]

    def index(self, coords):
        index = 0
        for size, value in zip(self.sizes, coords):
            index = index * size + value
        return index

    def mixed(self):
        return self.sizes[1] == self.sizes[2]

    def axis(self, role, core):
        if role == "z":
            return 0
        if role == "core":
            return 3
        if self.mixed():
            return (2, 1)[core] if role == "far" else (1, 2)[core]
        return 2 if role == "far" else 1

    def size(self, role):
        return self.sizes[self.axis(role, 0)]

    def pairs(self, role, step):
        out = []
        for source in range(self.total):
            coords = self.coords(source)
            axis = self.axis(role, coords[3])
            coords[axis] = (coords[axis] + step) % self.sizes[axis]
            out.append((source, self.index(coords)))
        return out

    def lines(self):
        deep = self.total // self.sizes[0]
        return [[z * deep + rest for z in range(self.sizes[0])] for rest in range(deep)]

    def owners(self, core_step, direction, deep_first=False):
        me = self.coords(lax.axis_index(AXES))
        core = (me[3] + core_step) % 2
        far, near, deep = (self.size(r) for r in ("far", "near", "z"))
        f, n, z = jnp.meshgrid(jnp.arange(far), jnp.arange(near), jnp.arange(deep), indexing="ij")
        if deep_first:
            f, n, z = (t.swapaxes(1, 2) for t in (f, n, z))
        if self.mixed():
            y = jnp.where(core == 0, me[1] + direction * n, me[1] + direction * f) % self.sizes[1]
            x = jnp.where(core == 0, me[2] + direction * f, me[2] + direction * n) % self.sizes[2]
        else:
            y = (me[1] + direction * n) % self.sizes[1]
            x = (me[2] + direction * f) % self.sizes[2]
        return self.index((z, y, x, core)).reshape(-1).astype(jnp.int32)


def shift(grid, x, role, step):
    return lax.ppermute(x, AXES, grid.pairs(role, step))


def tied(x, *others):
    return lax.optimization_barrier((x,) + others)[0]


def swap_deep(grid, x):
    return lax.all_to_all(x, AXES, 0, 0, axis_index_groups=grid.lines())


def join(*xs):
    return lax.optimization_barrier(xs)


def spread(grid, x, role):
    return [x] + [shift(grid, x, role, step) for step in range(1, grid.size(role))]


def all_sum(grid, x):
    return jnp.sum(lax.all_to_all(jnp.broadcast_to(x[None], (grid.total,) + x.shape), AXES, 0, 0), 0)


def dot_nn(a, b):
    return lax.dot_general(a, b, (((1,), (0,)), ((), ())), preferred_element_type=jnp.float32)


def dot_nt(a, b):
    return lax.dot_general(a, b, (((1,), (1,)), ((), ())), preferred_element_type=jnp.float32)


def dot_tn(a, b):
    return lax.dot_general(a, b, (((0,), (0,)), ((), ())), preferred_element_type=jnp.float32)


def params():
    return pltpu.CompilerParams(vmem_limit_bytes=VMEM)


def key_bias(length, frames):
    key = lax.broadcasted_iota(jnp.int32, (frames, frames), 0)
    query = lax.broadcasted_iota(jnp.int32, (frames, frames), 1)
    dist = -jnp.abs(key - query).astype(jnp.float32)
    return jnp.where(key < length, dist, FAR_AWAY)


def attend_kernel(length_ref, slope_ref, packed_ref, mixed_ref, lse_ref, bias_ref):
    step = pl.program_id(0)
    q_ref, k_ref, v_ref = (packed_ref.at[j] for j in range(3))
    frames, lanes_here = mixed_ref.shape
    here = lanes_here // HD

    @pl.when(step == 0)
    def _():
        bias_ref[...] = key_bias(length_ref[0], frames)

    parts = []
    for h in range(here):
        lanes = slice(h * HD, (h + 1) * HD)
        scores = dot_nt(k_ref[:, lanes], q_ref[:, lanes] * jnp.bfloat16(HD**-0.5))
        scores = scores + slope_ref[here * step + h] * bias_ref[...]
        top = jnp.max(scores, 0, keepdims=True)
        expo = jnp.exp(scores - top)
        total = jnp.sum(expo, 0, keepdims=True)
        lse_ref[0, h : h + 1] = top + jnp.log(total)
        probs = as_low(expo * (1.0 / total))
        parts.append(dot_tn(v_ref[:, lanes], probs))
    mixed_ref[...] = as_low(jnp.concatenate(parts, 0).T)


def attend(length, slopes, packed):
    _, frames, width = packed.shape
    steps = width // (HEADS_AT_ONCE * HD)
    block = pl.BlockSpec((frames, HEADS_AT_ONCE * HD), lambda i: (0, i))
    return pl.pallas_call(
        attend_kernel,
        grid=(steps,),
        in_specs=[pl.BlockSpec(memory_space=pltpu.SMEM)] * 2
        + [pl.BlockSpec((3, frames, HEADS_AT_ONCE * HD), lambda i: (0, 0, i))],
        out_specs=[block, pl.BlockSpec((1, HEADS_AT_ONCE, frames), lambda i: (i, 0, 0))],
        out_shape=[
            jax.ShapeDtypeStruct((frames, width), jnp.bfloat16),
            jax.ShapeDtypeStruct((steps, HEADS_AT_ONCE, frames), jnp.float32),
        ],
        scratch_shapes=[pltpu.VMEM((frames, frames), jnp.float32)],
        compiler_params=params(),
        name="attend",
    )(length, slopes, packed)


def attend_back_kernel(
    length_ref, slope_ref, packed_ref, d_out_ref, w_ref, lse_ref, dq_ref, dk_ref, dv_ref, bias_ref
):
    step = pl.program_id(0)
    q_ref, k_ref, v_ref = (packed_ref.at[j] for j in range(3))
    frames, lanes_here = dq_ref.shape
    here = lanes_here // HD

    @pl.when(step == 0)
    def _():
        bias_ref[...] = key_bias(length_ref[0], frames)

    d_mixed_here = as_low(dot_nt(d_out_ref[...], w_ref[...]))
    d_query, d_keys, d_values = [], [], []
    for h in range(here):
        lanes = slice(h * HD, (h + 1) * HD)
        query = q_ref[:, lanes] * jnp.bfloat16(HD**-0.5)
        keys, values, d_mixed = k_ref[:, lanes], v_ref[:, lanes], d_mixed_here[:, lanes]
        scores = dot_nt(keys, query) + slope_ref[here * step + h] * bias_ref[...]
        probs = jnp.exp(scores - lse_ref[0, h : h + 1])
        d_probs = dot_nt(values, d_mixed)
        row_dot = jnp.sum(d_probs * probs, 0, keepdims=True)
        d_scores = as_low(probs * (d_probs - row_dot))
        d_values.append(dot_nn(as_low(probs), d_mixed))
        d_keys.append(dot_nn(d_scores, query))
        d_query.append(dot_tn(keys, d_scores))
    dq_ref[...] = as_low((jnp.concatenate(d_query, 0) * HD**-0.5).T)
    dk_ref[...] = as_low(jnp.concatenate(d_keys, 1))
    dv_ref[...] = as_low(jnp.concatenate(d_values, 1))


def attend_back(length, slopes, packed, d_out, w, lse):
    _, frames, width = packed.shape
    wide = HEADS_AT_ONCE * HD
    block = pl.BlockSpec((frames, wide), lambda i: (0, i))
    return pl.pallas_call(
        attend_back_kernel,
        grid=(width // wide,),
        in_specs=[pl.BlockSpec(memory_space=pltpu.SMEM)] * 2
        + [
            pl.BlockSpec((3, frames, wide), lambda i: (0, 0, i)),
            pl.BlockSpec((frames, width), lambda i: (0, 0)),
            pl.BlockSpec((wide, width), lambda i: (i, 0)),
            pl.BlockSpec((1, HEADS_AT_ONCE, frames), lambda i: (i, 0, 0)),
        ],
        out_specs=[block] * 3,
        out_shape=[jax.ShapeDtypeStruct((frames, width), jnp.bfloat16)] * 3,
        scratch_shapes=[pltpu.VMEM((frames, frames), jnp.float32)],
        compiler_params=params(),
        name="attend_back",
    )(length, slopes, packed, d_out, w, lse)


def gelu_both(x):
    z = jnp.abs(x) * (0.5**0.5)
    bell = jnp.exp(-z * z)
    t = 1.0 / (1.0 + 0.3275911 * z)
    poly = t * (0.254829592 + t * (-0.284496736 + t * (1.421413741 + t * (-1.453152027 + t * 1.061405429))))
    tail = 0.5 * poly * bell
    share = jnp.where(x >= 0, 1.0 - tail, tail)
    return x * share, share + x * bell * (0.5 / math.pi) ** 0.5


def expand_kernel(count, blocks, own_ref, other_ref, *refs):
    sources = refs[:count]
    x_ref, w_out, act_ref, turned_ref, slope_ref, w_ref, sems, out_sems = refs[count:]
    step = pl.program_id(0)
    width = x_ref.shape[1]
    unit = width // sum(source.shape[0] for source in sources)

    def copies(j):
        entry = (w_ref.at[j], (j + 1) * unit, unit, None, sems.at[j])
        return landing((own_ref, other_ref), sources, [entry])

    def kept(j):
        return pltpu.make_async_copy(w_ref.at[j], w_out.at[j], out_sems.at[j])

    def chunk(j):
        if j == 0:
            for n in range(blocks):
                begin(copies(n))
        finish(copies(j))
        kept(j).start()
        hidden = dot_nn(x_ref[...], w_ref[j])
        act, slope = gelu_both(hidden)
        act = as_low(act)
        act_ref[...] = act
        turned_ref[...] = act.T
        slope_ref[...] = as_low(slope)
        if j == blocks - 1:
            for n in range(blocks):
                kept(n).wait()

    for j in range(blocks):
        pl.when(step == j)(partial(chunk, j))


def expand(own, other, pieces, x, blocks):
    frames, width = x.shape
    total = blocks * width
    return pl.pallas_call(
        partial(expand_kernel, len(pieces), blocks),
        grid=(blocks,),
        in_specs=piece_specs(pieces) + [pl.BlockSpec((frames, width), lambda i: (0, 0))],
        out_specs=[
            pl.BlockSpec(memory_space=pl.ANY),
            pl.BlockSpec((frames, width), lambda i: (0, i)),
            pl.BlockSpec((width, frames), lambda i: (i, 0)),
            pl.BlockSpec((frames, width), lambda i: (0, i)),
        ],
        out_shape=[
            jax.ShapeDtypeStruct((blocks, width, width), jnp.bfloat16),
            jax.ShapeDtypeStruct((frames, total), jnp.bfloat16),
            jax.ShapeDtypeStruct((total, frames), jnp.bfloat16),
            jax.ShapeDtypeStruct((frames, total), jnp.bfloat16),
        ],
        scratch_shapes=[
            pltpu.VMEM((blocks, width, width), jnp.bfloat16),
            pltpu.SemaphoreType.DMA((blocks,)),
            pltpu.SemaphoreType.DMA((blocks,)),
        ],
        compiler_params=params(),
        name="expand",
    )(own, other, *pieces, x)


def landing(idx_refs, sources, entries):
    half = len(sources) // 2
    copies = []
    for s, source in enumerate(sources):
        idx_ref = idx_refs[s // half]
        count = source.shape[0]
        for i in range(count):
            band = idx_ref[(s % half) * count + i]
            for goal, start, rows, lane, sem in entries:
                part = source.at[i, pl.ds(start, rows)]
                if lane is not None:
                    part = source.at[i, pl.ds(start, rows), pl.ds(lane, goal.shape[-1])]
                place = goal.at[pl.ds(pl.multiple_of(band * rows, rows), rows)]
                copies.append(pltpu.make_async_copy(part, place, sem(band) if callable(sem) else sem))
    return copies


def begin(copies):
    for copy in copies:
        copy.start()


def finish(copies):
    for copy in copies:
        copy.wait()


def piece_specs(pieces):
    smem = pl.BlockSpec(memory_space=pltpu.SMEM)
    return [smem, smem] + [pl.BlockSpec(memory_space=pl.ANY)] * len(pieces)


def gain_row(edge_ref, at):
    return edge_ref[at : at + 1].astype(jnp.float32)


def front_kernel(
    at_gain, at_count, spacing, count, phone_rows, speaker_ref, own_ref, other_ref, *refs
):
    sources = refs[:count]
    states_ref, states_turned_ref, hot_ref, mel_ref, time_ref = refs[count : count + 5]
    (
        small_out, skip_out, embed_ref, stream_ref, joined_ref, normed_ref, turned_ref, edge_ref, share_ref,
        small_ref, skip_ref, table_ref, sems, out_sems,
    ) = refs[count + 5 :]
    width = stream_ref.shape[1]
    bands = sum(source.shape[0] for source in sources)
    unit = width // bands
    idx = (own_ref, other_ref)
    first = landing(
        idx, sources,
        [(small_ref, 0, unit, None, sems.at[0]), (table_ref, 0, phone_rows, TABLE_AT, sems.at[0])],
    )
    second = landing(idx, sources, [(skip_ref, unit, 2 * unit, None, sems.at[1])])
    begin(first)
    begin(second)
    phones = embed_ref.shape[1]
    joined_ref[width:] = states_turned_ref[...]
    finish(first)
    small_copy = pltpu.make_async_copy(small_ref, small_out, out_sems.at[0])
    small_copy.start()
    edge_ref[...] = small_ref[:, HEAD_AT:].T
    facts = edge_ref[at_count - HEAD_AT : at_count - HEAD_AT + 3].astype(jnp.float32)
    lane = lax.broadcasted_iota(jnp.int32, (1, width), 1)
    hit = (facts[:1] == speaker_ref[0].astype(jnp.float32)) & (lax.rem(lane, spacing) == 0)
    masked = jnp.sum(jnp.where(hit, 16.0 * facts[1:2] + facts[2:3], 0.0), 1, keepdims=True)
    share_ref[...] = (1.0 / SPK) / jnp.maximum(masked, 1.0)
    embedded = as_low(dot_nt(hot_ref[...], table_ref[...]))
    embed_ref[...] = embedded
    start = dot_nt(embedded, small_ref[:, :phones])
    start = start + dot_nt(mel_ref[...], small_ref[:, phones:TABLE_AT]) + time_ref[...]
    start = as_low(start)
    joined_ref[:width] = start.T
    finish(second)
    skip_copy = pltpu.make_async_copy(skip_ref, skip_out, out_sems.at[1])
    skip_copy.start()
    stream = dot_nn(start, skip_ref[:width]) + dot_nn(states_ref[...], skip_ref[width:])
    stream_ref[...] = stream
    normed = as_low(normalize(stream)[0] * gain_row(edge_ref, at_gain))
    normed_ref[...] = normed
    turned_ref[...] = normed.T
    small_copy.wait()
    skip_copy.wait()


def front(speaker, own, other, pieces, states, states_turned, hot, mel, time, phones, at_gain, at_count, spacing):
    frames, width = states.shape
    f32, low = jnp.float32, jnp.bfloat16
    bands = sum(p.shape[0] for p in pieces)
    vmem, anywhere = pl.BlockSpec(memory_space=pltpu.VMEM), pl.BlockSpec(memory_space=pl.ANY)
    return pl.pallas_call(
        partial(front_kernel, at_gain, at_count, spacing, len(pieces), phones // bands),
        in_specs=[pl.BlockSpec(memory_space=pltpu.SMEM)] + piece_specs(pieces) + [vmem] * 5,
        out_specs=[anywhere] * 2 + [vmem] * 7,
        out_shape=[
            jax.ShapeDtypeStruct((width, width), low),
            jax.ShapeDtypeStruct((2 * width, width), low),
            jax.ShapeDtypeStruct((frames, phones), low),
            jax.ShapeDtypeStruct((frames, width), f32),
            jax.ShapeDtypeStruct((2 * width, frames), low),
            jax.ShapeDtypeStruct((frames, width), low),
            jax.ShapeDtypeStruct((width, frames), low),
            jax.ShapeDtypeStruct((width - HEAD_AT, width), low),
            jax.ShapeDtypeStruct((1, 1), f32),
        ],
        scratch_shapes=[
            pltpu.VMEM((width, width), low),
            pltpu.VMEM((2 * width, width), low),
            pltpu.VMEM((phones, hot.shape[1]), low),
            pltpu.SemaphoreType.DMA((2,)),
            pltpu.SemaphoreType.DMA((2,)),
        ],
        compiler_params=params(),
        name="front",
    )(speaker, own, other, *pieces, states, states_turned, hot, mel, time)


def pack_kernel(count, blocks, own_ref, other_ref, *refs):
    sources = refs[:count]
    x_ref, w_out, out_ref, w_ref, sems, out_sems = refs[count:]
    step = pl.program_id(0)
    width = x_ref.shape[1]
    unit = width // sum(source.shape[0] for source in sources)

    def copies(j):
        entry = (w_ref.at[j], (3 + j) * unit, unit, None, sems.at[j])
        return landing((own_ref, other_ref), sources, [entry])

    def kept(j):
        return pltpu.make_async_copy(w_ref.at[j], w_out.at[j], out_sems.at[j])

    def chunk(j):
        if j == 0:
            for n in range(blocks):
                begin(copies(n))
        finish(copies(j))
        kept(j).start()
        out_ref[0] = as_low(dot_nn(x_ref[...], w_ref[j]))
        if j == blocks - 1:
            for n in range(blocks):
                kept(n).wait()

    for j in range(blocks):
        pl.when(step == j)(partial(chunk, j))


def pack(own, other, pieces, x, blocks):
    frames, width = x.shape
    return pl.pallas_call(
        partial(pack_kernel, len(pieces), blocks),
        grid=(blocks,),
        in_specs=piece_specs(pieces) + [pl.BlockSpec((frames, width), lambda i: (0, 0))],
        out_specs=[
            pl.BlockSpec(memory_space=pl.ANY),
            pl.BlockSpec((1, frames, width), lambda i: (i, 0, 0)),
        ],
        out_shape=[
            jax.ShapeDtypeStruct((blocks, width, width), jnp.bfloat16),
            jax.ShapeDtypeStruct((blocks, frames, width), jnp.bfloat16),
        ],
        scratch_shapes=[
            pltpu.VMEM((blocks, width, width), jnp.bfloat16),
            pltpu.SemaphoreType.DMA((blocks,)),
            pltpu.SemaphoreType.DMA((blocks,)),
        ],
        compiler_params=params(),
        name="pack",
    )(own, other, *pieces, x)


def mid_kernel(at_gain, count, own_ref, other_ref, *refs):
    sources = refs[:count]
    (
        mixed_ref, stream_ref, edge_ref, w_out, mid_ref, in_ref, turned_ref, mixed_turned_ref,
        w_ref, sem, out_sem,
    ) = refs[count:]
    width = stream_ref.shape[1]
    unit = width // sum(source.shape[0] for source in sources)
    copies = landing((own_ref, other_ref), sources, [(w_ref, 0, unit, None, sem)])
    begin(copies)
    mixed = mixed_ref[...]
    mixed_turned_ref[...] = mixed.T
    finish(copies)
    kept = pltpu.make_async_copy(w_ref, w_out, out_sem)
    kept.start()
    mid = stream_ref[...] + dot_nn(mixed, w_ref[...])
    mid_ref[...] = mid
    normed = as_low(normalize(mid)[0] * gain_row(edge_ref, at_gain))
    in_ref[...] = normed
    turned_ref[...] = normed.T
    kept.wait()


def mid_step(own, other, pieces, mixed, stream, edge, at_gain):
    frames, width = stream.shape
    low = jnp.bfloat16
    vmem = pl.BlockSpec(memory_space=pltpu.VMEM)
    return pl.pallas_call(
        partial(mid_kernel, at_gain, len(pieces)),
        in_specs=piece_specs(pieces) + [vmem] * 3,
        out_specs=[pl.BlockSpec(memory_space=pl.ANY)] + [vmem] * 4,
        out_shape=[
            jax.ShapeDtypeStruct((width, width), low),
            jax.ShapeDtypeStruct((frames, width), jnp.float32),
            jax.ShapeDtypeStruct((frames, width), low),
            jax.ShapeDtypeStruct((width, frames), low),
            jax.ShapeDtypeStruct((width, frames), low),
        ],
        scratch_shapes=[
            pltpu.VMEM((width, width), low),
            pltpu.SemaphoreType.DMA,
            pltpu.SemaphoreType.DMA,
        ],
        compiler_params=params(),
        name="mid",
    )(own, other, *pieces, mixed, stream, edge)


def head_kernel(at_gain, count, share_ref, own_ref, other_ref, *refs):
    sources = refs[:count]
    (
        act_ref, mid_ref, edge_ref, target_ref, inside_ref,
        w_out, d_ref, low_ref, grad_ref, gain_grad_ref, error_ref,
        total_ref, w_ref, sem, out_sem,
    ) = refs[count:]
    step = pl.program_id(0)
    tile = act_ref.shape[1]
    rows = w_ref.shape[0] // sum(source.shape[0] for source in sources)
    kept = pltpu.make_async_copy(w_ref, w_out, out_sem)
    each = tile // rows

    @pl.when(step == 0)
    def _():
        by_step = lambda band: sem.at[lax.div(band, each)]
        begin(landing((own_ref, other_ref), sources, [(w_ref, 0, rows, None, by_step)]))

    for _ in range(each):
        pltpu.make_async_copy(sources[0].at[0, pl.ds(0, rows)], w_ref.at[pl.ds(0, rows)], sem.at[step]).wait()

    @pl.when(step == pl.num_programs(0) - 1)
    def _():
        kept.start()

    part = dot_nn(act_ref[...], w_ref[pl.ds(pl.multiple_of(step * tile, tile), tile)])

    @pl.when(step == 0)
    def _():
        total_ref[...] = mid_ref[...] + part

    @pl.when(step > 0)
    def _():
        total_ref[...] += part

    @pl.when(step == pl.num_programs(0) - 1)
    def _():
        bins = target_ref.shape[1]
        normed, inverse = normalize(total_ref[...])
        gain = gain_row(edge_ref, at_gain)
        head_in = as_low(normed * gain)
        head = edge_ref[:bins]
        inside = inside_ref[...]
        error = dot_nt(head_in, head) - target_ref[...]
        error_ref[...] = jnp.sum(jnp.sum(error * error, 1, keepdims=True) * inside, 0, keepdims=True)
        d_prediction = as_low((2.0 * share_ref[...]) * error * inside)
        grad_ref[...] = dot_tn(head_in, d_prediction)
        d_head_in = dot_nn(d_prediction, head)
        gain_grad_ref[...] = jnp.sum(d_head_in * normed, 0, keepdims=True)
        d_stream = normalize_back(d_head_in * gain, normed, inverse)
        d_ref[...] = d_stream
        low_ref[...] = as_low(d_stream)
        kept.wait()


def head_step(share, own, other, pieces, act, mid, edge, target, inside, at_gain, tile=1024):
    frames, width = mid.shape
    bins = target.shape[1]
    total = act.shape[1]
    whole = lambda *shape: pl.BlockSpec(shape, lambda i: (0,) * len(shape))
    return pl.pallas_call(
        partial(head_kernel, at_gain, len(pieces)),
        grid=(total // tile,),
        in_specs=[whole(1, 1)]
        + piece_specs(pieces)
        + [
            pl.BlockSpec((frames, tile), lambda i: (0, i)),
            whole(frames, width), whole(*edge.shape), whole(frames, bins), whole(frames, 1),
        ],
        out_specs=[
            pl.BlockSpec(memory_space=pl.ANY),
            whole(frames, width), whole(frames, width), whole(width, bins), whole(1, width), whole(1, 1),
        ],
        out_shape=[
            jax.ShapeDtypeStruct((total, width), jnp.bfloat16),
            jax.ShapeDtypeStruct((frames, width), jnp.float32),
            jax.ShapeDtypeStruct((frames, width), jnp.bfloat16),
            jax.ShapeDtypeStruct((width, bins), jnp.float32),
            jax.ShapeDtypeStruct((1, width), jnp.float32),
            jax.ShapeDtypeStruct((1, 1), jnp.float32),
        ],
        scratch_shapes=[
            pltpu.VMEM((frames, width), jnp.float32),
            pltpu.VMEM((total, width), jnp.bfloat16),
            pltpu.SemaphoreType.DMA((total // tile,)),
            pltpu.SemaphoreType.DMA,
        ],
        compiler_params=params(),
        name="head",
    )(share, own, other, *pieces, act, mid, edge, target, inside)


def ffn_back_kernel(
    at_gain, low_ref, d_ref, down_ref, slope_ref, up_ref, mid_ref, edge_ref,
    out_ref, out_low_ref, gain_grad_ref, *refs,
):
    hidden_refs, total_ref = refs[:-1], refs[-1]
    step = pl.program_id(0)
    d_hidden = as_low(dot_nt(low_ref[...], down_ref[...]) * slope_ref[...].astype(jnp.float32))
    for j, ref in enumerate(hidden_refs):

        @pl.when(step == j)
        def _(ref=ref):
            ref[...] = d_hidden

    part = dot_nt(d_hidden, up_ref[0])

    @pl.when(step == 0)
    def _():
        total_ref[...] = part

    @pl.when(step > 0)
    def _():
        total_ref[...] += part

    @pl.when(step == pl.num_programs(0) - 1)
    def _():
        normed, inverse = normalize(mid_ref[...])
        grad = total_ref[...]
        gain_grad_ref[...] = jnp.sum(grad * normed, 0, keepdims=True)
        out = d_ref[...] + normalize_back(grad * gain_row(edge_ref, at_gain), normed, inverse)
        out_ref[...] = out
        out_low_ref[...] = as_low(out)


def ffn_back(low, d, down, slope, up, mid, edge, at_gain):
    frames, width = mid.shape
    count = up.shape[0]
    whole = lambda *shape: pl.BlockSpec(shape, lambda i: (0,) * len(shape))
    return pl.pallas_call(
        partial(ffn_back_kernel, at_gain),
        grid=(count,),
        in_specs=[
            whole(frames, width), whole(frames, width),
            pl.BlockSpec((width, width), lambda i: (i, 0)),
            pl.BlockSpec((frames, width), lambda i: (0, i)),
            pl.BlockSpec((1, width, width), lambda i: (i, 0, 0)),
            whole(frames, width), whole(*edge.shape),
        ],
        out_specs=[whole(frames, width), whole(frames, width), whole(1, width)]
        + [whole(frames, width)] * count,
        out_shape=[
            jax.ShapeDtypeStruct((frames, width), jnp.float32),
            jax.ShapeDtypeStruct((frames, width), jnp.bfloat16),
            jax.ShapeDtypeStruct((1, width), jnp.float32),
        ]
        + [jax.ShapeDtypeStruct((frames, width), jnp.bfloat16)] * count,
        scratch_shapes=[pltpu.VMEM((frames, width), jnp.float32)],
        compiler_params=params(),
        name="ffn_back",
    )(low, d, down, slope, up, mid, edge)


def pack_back_kernel(at_gain, blocks, *refs):
    w_ref, d_ref, stream_ref, edge_ref, low_ref, gain_grad_ref, total_ref = refs[blocks:]
    step = pl.program_id(0)

    def chunk(j):
        part = dot_nt(refs[j][...], w_ref[0])
        total_ref[...] = part if j == 0 else total_ref[...] + part

    for j in range(blocks):
        pl.when(step == j)(partial(chunk, j))

    @pl.when(step == pl.num_programs(0) - 1)
    def _():
        grad = total_ref[...]
        normed, inverse = normalize(stream_ref[...])
        gain_grad_ref[...] = jnp.sum(grad * normed, 0, keepdims=True)
        gain = gain_row(edge_ref, at_gain)
        low_ref[...] = as_low(d_ref[...] + normalize_back(grad * gain, normed, inverse))


def pack_back(packed, w, d, stream, edge, at_gain):
    frames, width = stream.shape
    whole = lambda *shape: pl.BlockSpec(shape, lambda i: (0,) * len(shape))
    return pl.pallas_call(
        partial(pack_back_kernel, at_gain, w.shape[0]),
        grid=(w.shape[0],),
        in_specs=[whole(frames, width)] * w.shape[0]
        + [
            pl.BlockSpec((1, width, width), lambda i: (i, 0, 0)),
            whole(frames, width), whole(frames, width), whole(*edge.shape),
        ],
        out_specs=[whole(frames, width), whole(1, width)],
        out_shape=[
            jax.ShapeDtypeStruct((frames, width), jnp.bfloat16),
            jax.ShapeDtypeStruct((1, width), jnp.float32),
        ],
        scratch_shapes=[pltpu.VMEM((frames, width), jnp.float32)],
        compiler_params=params(),
        name="pack_back",
    )(*packed, w, d, stream, edge)


def tail_kernel(
    at_gain, d_ref, skip_ref, small_ref, embed_ref, mel_ref, hot_ref, head_ref, one_ref, two_ref, three_ref,
    main_ref, table_ref, edge_ref,
):
    phones = embed_ref.shape[1]
    d_start = as_low(dot_nt(d_ref[...], skip_ref[...]))
    d_phones = as_low(dot_nn(d_start, small_ref[:, :phones]))
    main_ref[:, :phones] = as_low(dot_tn(d_start, embed_ref[...]))
    main_ref[:, phones:] = as_low(dot_tn(d_start, mel_ref[...]))
    table_ref[...] = as_low(dot_tn(d_phones, hot_ref[...]))
    edge = head_ref[...]
    lanes = edge.shape[1]
    edge = jnp.pad(edge, ((0, 0), (0, edge_ref.shape[1] - lanes)))
    lane = lax.broadcasted_iota(jnp.int32, edge.shape, 1)
    for j, ref in enumerate((one_ref, two_ref, three_ref)):
        column = jnp.broadcast_to(ref[...], (8, edge.shape[0])).T[:, :1]
        edge = jnp.where(lane == at_gain + j, column, edge)
    edge_ref[...] = as_low(edge)


def tail(d, skip, small, embed, mel, hot, head, gains, at_gain):
    width = d.shape[1]
    phones = embed.shape[1]
    whole = lambda x: pl.BlockSpec(x.shape, lambda i: (0, 0))
    arrays = (small, embed, mel, hot, head, *gains)
    shapes = [(width, TABLE_AT), (phones, hot.shape[1]), (width, width - HEAD_AT)]
    return pl.pallas_call(
        partial(tail_kernel, at_gain),
        grid=(1,),
        in_specs=[whole(d), pl.BlockSpec((width, width), lambda i: (0, 0))] + [whole(x) for x in arrays],
        out_specs=[pl.BlockSpec(s, lambda i: (0, 0)) for s in shapes],
        out_shape=[jax.ShapeDtypeStruct(s, jnp.bfloat16) for s in shapes],
        compiler_params=params(),
        name="tail",
    )(d, skip, *arrays)


def grads_kernel(plan, count, rows, legs, came_too, idx_ref, *refs):
    refs, picked_ref, right_ref, sems = refs[:-3], refs[-3], refs[-2], refs[-1]
    frames = right_ref.shape[1] // 2
    outs = refs[len(refs) - legs :]
    came_ref = refs[len(refs) - legs - 1] if came_too else None
    step = pl.program_id(0)
    each = count // legs

    def copies(c):
        lefts, rights, stride, offset = plan[c]
        if rights is None:
            return []
        slot = c % 2
        return [
            pltpu.make_async_copy(
                refs[left].at[pl.ds(pl.multiple_of(idx_ref[i] * stride + offset, rows), rows)],
                picked_ref.at[slot, pl.ds(i * rows, rows), pl.ds(side * frames, frames)],
                sems.at[slot],
            )
            for side, left in enumerate(lefts)
            for i in range(count)
        ] + [
            pltpu.make_async_copy(refs[right], right_ref.at[slot, pl.ds(side * frames, frames)], sems.at[slot])
            for side, right in enumerate(rights)
        ]

    def chunk(c):
        lefts, rights, _, _ = plan[c]
        if c == 0:
            for copy in copies(0):
                copy.start()
        if c + 1 < len(plan):
            for copy in copies(c + 1):
                copy.start()
        for copy in copies(c):
            copy.wait()
        if rights is None:
            main, table, edge = (refs[r] for r in lefts)
            thick = table.shape[0] // (main.shape[0] // rows)
            blocks = []
            for i in range(count):
                start = pl.multiple_of(idx_ref[i] * rows, rows)
                short = pl.multiple_of(idx_ref[i] * thick, thick)
                lead = table[pl.ds(short, thick)]
                rest = jnp.zeros((rows - thick, lead.shape[1]), lead.dtype)
                middle = jnp.concatenate([lead, rest], 0) if thick < rows else lead
                block = [main[pl.ds(start, rows)], middle, edge[pl.ds(start, rows)]]
                blocks.append(jnp.concatenate(block, 1).astype(jnp.float32))
            total = jnp.stack(blocks)
            if came_too:
                total = total + came_ref[...].astype(jnp.float32)
        else:
            wide = outs[0].shape[2]
            total = dot_nn(picked_ref[c % 2], right_ref[c % 2])
            total = total.reshape(count, rows, wide)
        for f in range(legs):
            outs[f][...] = as_low(total[f * each : (f + 1) * each])

    for c in range(len(plan)):
        pl.when(step == c)(partial(chunk, c))


def grads(plan, arrays, idx, frames, rows, width, legs, came=None):
    count = idx.shape[0]
    copied = [j for entry in plan if entry[1] is not None for j in entry[0] + entry[1]]

    def spec(j, x):
        if j in copied:
            return pl.BlockSpec(memory_space=pltpu.HBM)
        return pl.BlockSpec(x.shape, lambda i, n=len(x.shape): (0,) * n)

    specs = [spec(j, x) for j, x in enumerate(arrays)]
    if came is not None:
        specs.append(pl.BlockSpec((count, rows, width), lambda i: (0, 0, 0)))
        arrays = list(arrays) + [came]
    return pl.pallas_call(
        partial(grads_kernel, plan, count, rows, legs, came is not None),
        grid=(len(plan),),
        in_specs=[pl.BlockSpec(memory_space=pltpu.SMEM)] + specs,
        out_specs=[pl.BlockSpec((count // legs, rows, width), lambda i: (0, i, 0))] * legs,
        out_shape=[jax.ShapeDtypeStruct((count // legs, rows * len(plan), width), jnp.bfloat16)] * legs,
        scratch_shapes=[
            pltpu.VMEM((2, count * rows, 2 * frames), jnp.bfloat16),
            pltpu.VMEM((2, 2 * frames, width), jnp.bfloat16),
            pltpu.SemaphoreType.DMA((2,)),
        ],
        compiler_params=params(),
        name="grads",
    )(idx, *arrays)


def fold_kernel(legs, *refs):
    ins, outs = refs[:-legs], refs[-legs:]
    took = len(ins) // legs
    for j in range(legs):
        total = ins[j * took][...].astype(jnp.float32)
        for ref in ins[j * took + 1 : (j + 1) * took]:
            total = total + ref[...].astype(jnp.float32)
        outs[j][...] = as_low(total)


def fold(parts, legs):
    count, rows, width = parts[0].shape
    each = count // legs
    tile = rows // 2
    return pl.pallas_call(
        partial(fold_kernel, legs),
        grid=(rows // tile,),
        in_specs=[
            pl.BlockSpec((each, tile, width), lambda i, j=j: (j, i, 0)) for j in range(legs) for _ in parts
        ],
        out_specs=[pl.BlockSpec((each, tile, width), lambda i: (0, i, 0))] * legs,
        out_shape=[jax.ShapeDtypeStruct((each, rows, width), jnp.bfloat16)] * legs,
        compiler_params=params(),
        name="fold",
    )(*[p for _ in range(legs) for p in parts])


def stack_kernel(*refs):
    ins, out, sem = refs[:-2], refs[-2], refs[-1]
    copies = [
        pltpu.make_async_copy(ref, out.at[n, i], sem) for n in range(out.shape[0]) for i, ref in enumerate(ins)
    ]
    for copy in copies:
        copy.start()
    for copy in copies:
        copy.wait()


def stack(parts, times):
    return pl.pallas_call(
        stack_kernel,
        in_specs=[pl.BlockSpec(memory_space=pl.ANY)] * len(parts),
        out_specs=pl.BlockSpec(memory_space=pltpu.VMEM),
        out_shape=jax.ShapeDtypeStruct((times, len(parts)) + parts[0].shape, parts[0].dtype),
        scratch_shapes=[pltpu.SemaphoreType.DMA],
        compiler_params=params(),
        name="stack",
    )(*parts)


def update(grad, rate, master_ref, moment_ref, square_ref, clip):
    return adam_step(master_ref[...], grad * clip, moment_ref[...], square_ref[...], rate)


def adam_kernel(at, clip_ref, *refs):
    phone_rows, phone_width, inputs, at_gain = at
    last, attend, expand, reduce = refs[:4]
    masters, moments, squares = refs[4:13], refs[13:22], refs[22:31]
    outs = refs[31:]
    unit = last.shape[0] // 3
    small = last[2 * unit :]
    clip = clip_ref[0]
    mel_lanes = inputs - phone_width
    lanes = [small[:, phone_width : phone_width + mel_lanes], small[:, :phone_width]]
    edge = small[:, HEAD_AT:]
    turned_edge = edge.T
    bins = masters[7].shape[1]

    def columns(ref, first):
        blocks = [ref[j : j + unit] for j in range(first, ref.shape[0], unit)]
        return jnp.concatenate(blocks, 1)

    grads_of = [
        jnp.concatenate(lanes, 1),
        small[:phone_rows, TABLE_AT:HEAD_AT],
        last[: 2 * unit],
        columns(attend, unit),
        attend[:unit],
        columns(expand, 0),
        reduce[...],
        edge[:, :bins],
        turned_edge[at_gain : at_gain + 3],
    ]
    for j, grad in enumerate(grads_of):
        rate = GAIN_RATE if j in (1, 8) else LEARN_RATE
        after = update(grad, rate, masters[j], moments[j], squares[j], clip)
        for n, value in enumerate(after):
            outs[9 * n + j][...] = value


def adam(clip, shares, masters, moments, squares, at):
    turned = lambda group: [x.T if j < 2 else x for j, x in enumerate(group)]
    masters, moments, squares = turned(masters), turned(moments), turned(squares)
    vmem = pl.BlockSpec(memory_space=pltpu.VMEM)
    arrays = [*shares, *masters, *moments, *squares]
    results = pl.pallas_call(
        partial(adam_kernel, at),
        in_specs=[pl.BlockSpec(memory_space=pltpu.SMEM)] + [vmem] * len(arrays),
        out_specs=[vmem] * 27,
        out_shape=[jax.ShapeDtypeStruct(x.shape, jnp.float32) for x in (*masters, *moments, *squares)],
        compiler_params=params(),
        name="adam",
    )(clip, *arrays)
    return [y for n in range(3) for y in turned(results[9 * n : 9 * n + 9])]


def prepare_kernel(
    at_mel, at_count, frames,
    facts_ref, input_ref, table_ref, head_ref, gains_ref, skip_ref, attend_ref, out_ref,
):
    unit, inputs = input_ref.shape
    phones = inputs - at_mel
    turned = as_low(input_ref[...])
    out_ref[0, :unit, :phones] = turned[:, at_mel:]
    out_ref[0, :unit, phones:TABLE_AT] = jnp.pad(turned[:, :at_mel], ((0, 0), (0, TABLE_AT - inputs)))
    table = as_low(table_ref[...])
    rest = jnp.zeros((unit - table.shape[0], table.shape[1]), jnp.bfloat16)
    out_ref[0, :unit, TABLE_AT:HEAD_AT] = jnp.concatenate([table, rest], 0)
    bins = head_ref.shape[1]
    edge = jnp.pad(head_ref[...], ((0, 0), (0, out_ref.shape[2] - HEAD_AT - bins)))
    lane = lax.broadcasted_iota(jnp.int32, edge.shape, 1)
    spot = (gains_ref.shape[0], edge.shape[1])
    row = lax.broadcasted_iota(jnp.int32, spot, 0)
    here = lax.broadcasted_iota(jnp.int32, spot, 1) == row + bins
    edge = as_low(edge).astype(jnp.float32) + dot_tn(as_low(gains_ref[...]), as_low(here))
    end = jnp.minimum(jnp.minimum(facts_ref[2], facts_ref[3]), frames)
    count = jnp.maximum(end - jnp.maximum(facts_ref[1], 0), 0)
    for j, fact in enumerate((facts_ref[0], lax.div(count, 16), lax.rem(count, 16))):
        edge = jnp.where(lane == at_count - HEAD_AT + j, fact.astype(jnp.float32), edge)
    out_ref[0, :unit, HEAD_AT:] = as_low(edge)
    width = out_ref.shape[2]
    start = unit + skip_ref.shape[0]
    out_ref[0, unit:start] = as_low(skip_ref[...])
    for j in range(attend_ref.shape[1] // width):
        here = slice(start + j * unit, start + (j + 1) * unit)
        out_ref[0, here] = as_low(attend_ref[:, j * width : (j + 1) * width])
    for z in range(1, out_ref.shape[0]):
        out_ref[z] = out_ref[0]


def prepare(facts, turned, table, head, gains, skip, attend, deep, frames, at_mel, at_count):
    vmem = pl.BlockSpec(memory_space=pltpu.VMEM)
    width = skip.shape[1]
    rows = turned.shape[0] + skip.shape[0] + attend.size // width
    return pl.pallas_call(
        partial(prepare_kernel, at_mel, at_count, frames),
        in_specs=[pl.BlockSpec(memory_space=pltpu.SMEM)] + [vmem] * 6,
        out_specs=vmem,
        out_shape=jax.ShapeDtypeStruct((deep, rows, width), jnp.bfloat16),
        compiler_params=params(),
        name="prepare",
    )(facts, turned, table, head, gains, skip, attend)


def shards(
    grid,
    fast,
    clean_mel,
    gauss_noise,
    flow_time,
    phone_ids,
    lengths,
    span_start,
    span_end,
    speaker,
    skip_states,
    w_input,
    phone_table,
    w_skip,
    w_attend,
    w_output,
    w_expand,
    w_reduce,
    w_head,
    norm_gains,
    moment_input,
    moment_table,
    moment_skip,
    moment_attend,
    moment_output,
    moment_expand,
    moment_reduce,
    moment_head,
    moment_gains,
    square_input,
    square_table,
    square_skip,
    square_attend,
    square_output,
    square_expand,
    square_reduce,
    square_head,
    square_gains,
):
    masters = (w_input, phone_table, w_skip, w_attend, w_output, w_expand, w_reduce, w_head, norm_gains)
    moments = (
        moment_input, moment_table, moment_skip, moment_attend, moment_output,
        moment_expand, moment_reduce, moment_head, moment_gains,
    )
    squares = (
        square_input, square_table, square_skip, square_attend, square_output,
        square_expand, square_reduce, square_head, square_gains,
    )
    frames, mel_bins = clean_mel.shape
    width = w_skip.shape[1]
    heads = width // HD
    devices = grid.total
    unit = width // devices
    inputs = w_input.shape[0]
    phones = phone_table.shape[0]
    phone_wide = phone_table.shape[1]
    phone_width = phone_wide * devices
    mel_lanes = TABLE_AT - phone_width
    at_gain = HEAD_AT + mel_bins
    at_count = at_gain + 3
    position = jnp.arange(frames)
    frame_valid = (position < lengths[0]).astype(jnp.float32)
    frame_inside = ((position >= span_start[0]) & (position < span_end[0])).astype(
        jnp.float32
    ) * frame_valid
    speaker_hot = (speaker[0] == jnp.arange(SPK)).astype(jnp.float32)
    count = jnp.sum(frame_inside)
    count_high = jnp.floor(count / 16.0)
    tally = jnp.stack([speaker[0].astype(jnp.float32), count_high, count - 16.0 * count_high])

    low_input = as_low(w_input)
    small = jnp.concatenate(
        [
            low_input[2 * mel_bins :].T,
            low_input[: 2 * mel_bins].T,
            jnp.zeros((unit, TABLE_AT - inputs), jnp.bfloat16),
            jnp.pad(as_low(phone_table).T, ((0, unit - phone_wide), (0, 0))),
            as_low(w_head),
            as_low(norm_gains).T,
            jnp.broadcast_to(as_low(tally)[None, :], (unit, 3)),
            jnp.zeros((unit, width - at_count - 3), jnp.bfloat16),
        ],
        1,
    )

    def blocks(x):
        return [as_low(x[:, j : j + width]) for j in range(0, x.shape[1], width)]

    attend_blocks, expand_blocks = blocks(w_attend), blocks(w_expand)
    packs, wides = len(attend_blocks), len(expand_blocks)
    stages = [
        [("small", None, small), ("skip", None, as_low(w_skip))]
        + [("attend", j, w) for j, w in enumerate(attend_blocks)],
        [("output", None, as_low(w_output))] + [("expand", j, w) for j, w in enumerate(expand_blocks)],
        [("reduce", None, as_low(w_reduce))],
    ]
    if fast:
        own, other = grid.owners(0, -1), grid.owners(1, -1)
        own_turned, other_turned = grid.owners(0, -1, True), grid.owners(1, -1, True)
        mine, theirs = grid.owners(0, 1), grid.owners(1, 1)

    def load(stage):
        return jnp.concatenate([w for _, _, w in stage], 0)

    def sibling(x):
        return shift(grid, x, "core", 1)

    def along(x, role, *after):
        return spread(grid, tied(x, *after) if after else x, role)

    def deepen(x, *after):
        return swap_deep(grid, tied(x, *after) if after else x)

    def hop_far(pieces):
        return [shift(grid, p, "far", f) for f in range(1, grid.size("far")) for p in pieces]

    def gather_whole(stage):
        rows = lax.all_gather(load(stage), AXES, axis=0, tiled=False)
        parts, start = [], 0
        for name, _, w in stage:
            part = rows[:, start : start + w.shape[0]]
            start += w.shape[0]
            if name == "small":
                table = part[:, :phone_wide, TABLE_AT:HEAD_AT].reshape(BANDS, -1, phones)
                table = jnp.pad(table, ((0, 0), (0, width // BANDS - table.shape[1]), (0, 0)))
                part = part.reshape(BANDS, -1, width)
                part = jnp.concatenate([part[..., :TABLE_AT], table, part[..., HEAD_AT:]], 2)
            parts.append(part.reshape(BANDS, -1, width))
        rows = jnp.concatenate(parts, 1)
        return [rows[: BANDS // 2], rows[BANDS // 2 :]]

    flow = flow_time[0]
    noisy_mel = (1.0 - (1.0 - SIGMA) * flow) * gauss_noise + flow * clean_mel
    context = clean_mel * (frame_valid - frame_inside)[:, None]
    target = clean_mel - (1.0 - SIGMA) * gauss_noise
    mel = jnp.concatenate([as_low(noisy_mel), as_low(context)], 1)
    mel = jnp.pad(mel, ((0, 0), (0, mel_lanes - mel.shape[1])))
    phone_hot = as_low(phone_ids[:, None] == jnp.arange(phones)[None, :])
    slopes = head_slopes(heads)
    times = time_features(flow, width)[None, :]
    inside = frame_inside[:, None]
    states_turned = skip_states.T
    loads = [load(stage) for stage in stages]
    if fast:
        first = prepare(
            jnp.stack([speaker[0], span_start[0], span_end[0], lengths[0]]), w_input.T, phone_table.T,
            w_head, norm_gains, w_skip, w_attend, grid.size("z"), frames, 2 * mel_bins, at_count,
        )
        pair_1 = stack(along(loads[1], "near"), grid.size("z"))
        load_2 = stack([loads[2]], grid.size("z"))[:, 0]
        deep_0, pair_1, load_2 = join(deepen(first), pair_1, load_2)
        deep_1 = deepen(pair_1)
        near_0 = along(deep_0, "near")
        near_0 = [tied(near_0[0], near_0[-1])] + near_0[1:]
        (
            near_0, far_0, core_0, deep_1, own, other, own_turned, other_turned, mine, theirs,
            target, mel, phone_hot, slopes, times, inside, states_turned,
        ) = join(
            near_0, hop_far(near_0), [sibling(p) for p in near_0], deep_1,
            own, other, own_turned, other_turned, mine, theirs,
            target, mel, phone_hot, slopes, times, inside, states_turned,
        )
        pieces_0 = near_0 + far_0 + core_0 + [sibling(p) for p in far_0]
        near_1 = deep_1.reshape((-1,) + deep_1.shape[2:])
        far_1 = along(near_1, "far")[1]
        core_1 = sibling(near_1)
        deep_2 = deepen(load_2, near_1)
    else:
        own, other = jnp.arange(BANDS // 2), jnp.arange(BANDS // 2, BANDS)
        own_turned, other_turned = own, other
        pieces_0 = gather_whole(stages[0])
    small_full, skip_full, embedded, stream, joined_turned, attn_in, attn_turned, edges, share = front(
        speaker, own, other, pieces_0, skip_states, states_turned, phone_hot, mel, times, phone_width, mel_bins, at_count, unit
    )
    attend_full, packed = pack(own, other, pieces_0, attn_in, packs)
    if fast:
        near_2 = along(tied(deep_2, packed), "near")
    mixed, lse = attend(lengths, slopes, packed)
    if fast:
        far_1, near_2, core_1, stream, packed, mixed, lse, joined_turned, edges, share = join(
            far_1, near_2, core_1, stream, packed, mixed, lse, joined_turned, edges, share
        )
        pieces_1 = [near_1, far_1, core_1, sibling(far_1)]
        far_2 = hop_far(near_2)
        core_2 = [sibling(p) for p in near_2]
    else:
        pieces_1 = gather_whole(stages[1])
    output_full, stream_mid, ffn_in, ffn_turned, mixed_turned = mid_step(
        own_turned, other_turned, pieces_1, mixed, stream, edges, mel_bins + 1
    )
    expand_full, activated, act_turned, gelu_slope = expand(
        own_turned, other_turned, pieces_1, ffn_in, wides
    )
    if fast:
        far_2, core_2, stream_mid, ffn_turned, mixed_turned, activated, act_turned, gelu_slope = join(
            far_2, core_2, stream_mid, ffn_turned, mixed_turned, activated, act_turned, gelu_slope
        )
        pieces_2 = near_2 + far_2 + core_2 + [sibling(p) for p in far_2]
    else:
        pieces_2 = gather_whole(stages[2])
    reduce_full, d_stream_out, d_branch, grad_head, grad_gain_three, error_sum = head_step(
        share, own, other, pieces_2, activated, stream_mid, edges, target, inside, mel_bins + 2
    )
    far, near, deep = (grid.size(r) for r in ("far", "near", "z"))

    def both(*arrays):
        return [y for x in arrays for y in (x, sibling(x))]

    def sums(plan, arrays, *others, **options):
        first = [tied(arrays[0], *others)] if others else arrays[:1]
        return grads(plan, first + arrays[1:], mine, frames, unit, width, far, **options)

    def hops(legs, role, *others):
        sent = [tied(leg, *others) if others else leg for leg in legs[1:]]
        return [shift(grid, leg, role, j + 1) for j, leg in enumerate(sent)]

    def dense(pairs):
        parts = []
        for turned, right, stride, offset in pairs:
            if right is None:
                part = turned.reshape(devices, unit, width)
            else:
                turned = turned.reshape(devices, stride, frames)[:, offset : offset + unit]
                part = dot_nn(turned.reshape(width, frames), right).reshape(devices, unit, width)
            parts.append(part)
        return lax.psum_scatter(jnp.concatenate(parts, 1), AXES, scatter_dimension=0)

    offsets = [j * unit for j in range(wides)]
    if fast:
        plan = [((0, 1), (2, 3), wides * unit, o) for o in offsets]
        legs_0 = sums(plan, both(tied(act_turned, *pieces_2), d_branch))
        moved_0 = hops(legs_0, "far")
        d_branch_next = tied(d_branch, legs_0[0])
    else:
        share_reduce = dense([(act_turned, d_branch, wides * unit, o) for o in offsets])
        d_branch_next = d_branch
    d_stream_mid, d_out, grad_gain_two, *d_hidden = ffn_back(
        d_branch_next, d_stream_out, reduce_full, gelu_slope, expand_full, stream_mid, edges, mel_bins + 1
    )
    if fast:
        turned = both(ffn_turned)
        d_hiddens = both(*d_hidden)
        moved_0, turned, d_hiddens, d_stream_mid, d_out = join(
            moved_0, turned, d_hiddens, d_stream_mid, d_out
        )
        legs_0 = fold([legs_0[0]] + moved_0, near)
        moved_0 = hops(legs_0, "near")
        plan = [((0, 1), (2 + 2 * j, 3 + 2 * j), unit, 0) for j in range(wides)]
        legs_1 = sums(plan, turned + d_hiddens, legs_0[0])
        turned = both(tied(mixed_turned, legs_0[0]), attn_turned, d_out)
        moved_0, legs_1, turned, d_out = join(moved_0, legs_1, turned, d_out)
        (sums_0,) = fold([legs_0[0]] + moved_0, 1)
        d_out = tied(d_out, sums_0)
        moved_1 = hops(legs_1, "far", sums_0)
        sums_0 = swap_deep(grid, sums_0)
    else:
        share_expand = dense([(ffn_turned, d, unit, 0) for d in d_hidden])
    d_packed = attend_back(lengths, slopes, packed, d_out, output_full, lse)
    d_joined_in, grad_gain_one = pack_back(
        d_packed, attend_full, d_stream_mid, stream, edges, mel_bins
    )
    if fast:
        d_packs = both(*d_packed)
        moved_1, sums_0, d_packs, d_joined_in = join(moved_1, sums_0, d_packs, d_joined_in)
        legs_1 = fold([legs_1[0]] + moved_1, near)
        moved_1 = hops(legs_1, "near")
        plan = [((0, 1), (4, 5), unit, 0)]
        plan = plan + [((2, 3), (6 + 2 * j, 7 + 2 * j), unit, 0) for j in range(packs)]
        legs_2 = sums(plan, turned + d_packs, legs_1[0])
        joined = both(tied(joined_turned, legs_1[0]), tied(d_joined_in, legs_1[0]))
        moved_1, legs_2, joined, d_joined_in = join(moved_1, legs_2, joined, d_joined_in)
        (sums_1,) = fold([legs_1[0]] + moved_1, 1)
        d_joined_in = tied(d_joined_in, sums_1)
        moved_2 = hops(legs_2, "far", sums_1)
        sums_1 = swap_deep(grid, sums_1)
    else:
        share_attend = dense(
            [(mixed_turned, d_out, unit, 0)] + [(attn_turned, d, unit, 0) for d in d_packed]
        )
    tallies = edges[at_count - HEAD_AT : at_count - HEAD_AT + 3].reshape(3, devices, unit)
    tallies = tallies[:, :, 0].astype(jnp.float32)
    counts = jnp.sum(
        (tallies[0][:, None] == jnp.arange(SPK, dtype=jnp.float32)[None, :])
        * (16.0 * tallies[1] + tallies[2])[:, None],
        0,
    )
    gain_grads = [grad_gain_one, grad_gain_two, grad_gain_three]
    small_grads = tail(
        d_joined_in, skip_full, small_full, embedded, mel, phone_hot, grad_head, gain_grads, mel_bins
    )
    if fast:
        small_grads = list(small_grads)
        (sent,) = grads([((0, 1, 2), None, 0, 0)], small_grads, theirs, frames, unit, width, 1)
        plan = [((0, 1), (2, 3), 2 * unit, o) for o in offsets[:2]] + [((4, 5, 6), None, 0, 0)]
        legs_3 = sums(plan, joined + small_grads, sent, came=sibling(sent))
        moved_2, legs_3 = join(moved_2, legs_3)
        legs_2 = fold([legs_2[0]] + moved_2, near)
        moved_3 = hops(legs_3, "far", legs_2[0])
        moved_2, sums_1, counts = join(hops(legs_2, "near"), sums_1, counts)
        (sums_2,) = fold([legs_2[0]] + moved_2, 1)
        moved_3 = [tied(moved_3[0], sums_2)] + moved_3[1:]
        legs_3 = fold([legs_3[0]] + moved_3, near)
        moved_3, sums_2 = join(hops(legs_3, "near"), swap_deep(grid, sums_2))
        (sums_3,) = fold([legs_3[0]] + moved_3, 1)
        sums_3 = swap_deep(grid, sums_3)
        share_reduce, share_expand, share_attend, share_last = [
            jnp.sum(x.astype(jnp.float32), 0) for x in (sums_0, sums_1, sums_2, sums_3)
        ]
    else:
        main, table, edge = small_grads
        table = table.reshape(devices, phone_wide, phones)
        table = jnp.pad(table, ((0, 0), (0, unit - phone_wide), (0, 0))).reshape(width, phones)
        small_grads = jnp.concatenate([main, table, edge], 1).astype(jnp.float32)
        share_last = dense(
            [(joined_turned, d_joined_in, 2 * unit, o) for o in offsets[:2]]
            + [(small_grads, None, 0, 0)]
        )

    shares = (share_last, share_attend, share_expand, share_reduce)
    local_square = sum((jnp.sum(g * g) for g in shares))
    totals = all_sum(grid, jnp.concatenate([speaker_hot * error_sum[0, 0], local_square[None]]))
    sums, total_square = totals[:SPK], totals[SPK]
    loss_value = jnp.mean(sums / jnp.maximum(counts, 1.0))
    grad_norm = jnp.sqrt(total_square)
    clip = jnp.minimum(1.0, 1.0 / (grad_norm + 1e-06))
    at = (phone_wide, phone_width, inputs, mel_bins)
    results = adam(clip[None], shares, masters, moments, squares, at)
    return (loss_value, grad_norm, *results)


def solution(mesh):
    grid = Grid(mesh)
    in_specs = (
        P(("wide", "narrow"), None),
        P(("wide", "narrow"), None),
        P(("wide", "narrow")),
        P(("wide", "narrow")),
        P(("wide", "narrow")),
        P(("wide", "narrow")),
        P(("wide", "narrow")),
        P(("wide", "narrow")),
        P(("wide", "narrow"), None),
        P(None, ("wide", "narrow")),
        P(None, ("wide", "narrow")),
        P(("wide", "narrow"), None),
        P(("wide", "narrow"), None),
        P(("wide", "narrow"), None),
        P(("wide", "narrow"), None),
        P(("wide", "narrow"), None),
        P(("wide", "narrow"), None),
        P(None, ("wide", "narrow")),
        P(None, ("wide", "narrow")),
        P(None, ("wide", "narrow")),
        P(("wide", "narrow"), None),
        P(("wide", "narrow"), None),
        P(("wide", "narrow"), None),
        P(("wide", "narrow"), None),
        P(("wide", "narrow"), None),
        P(("wide", "narrow"), None),
        P(None, ("wide", "narrow")),
        P(None, ("wide", "narrow")),
        P(None, ("wide", "narrow")),
        P(("wide", "narrow"), None),
        P(("wide", "narrow"), None),
        P(("wide", "narrow"), None),
        P(("wide", "narrow"), None),
        P(("wide", "narrow"), None),
        P(("wide", "narrow"), None),
        P(None, ("wide", "narrow")),
    )
    out_specs = (
        P(),
        P(),
        P(None, ("wide", "narrow")),
        P(None, ("wide", "narrow")),
        P(("wide", "narrow"), None),
        P(("wide", "narrow"), None),
        P(("wide", "narrow"), None),
        P(("wide", "narrow"), None),
        P(("wide", "narrow"), None),
        P(("wide", "narrow"), None),
        P(None, ("wide", "narrow")),
        P(None, ("wide", "narrow")),
        P(None, ("wide", "narrow")),
        P(("wide", "narrow"), None),
        P(("wide", "narrow"), None),
        P(("wide", "narrow"), None),
        P(("wide", "narrow"), None),
        P(("wide", "narrow"), None),
        P(("wide", "narrow"), None),
        P(None, ("wide", "narrow")),
        P(None, ("wide", "narrow")),
        P(None, ("wide", "narrow")),
        P(("wide", "narrow"), None),
        P(("wide", "narrow"), None),
        P(("wide", "narrow"), None),
        P(("wide", "narrow"), None),
        P(("wide", "narrow"), None),
        P(("wide", "narrow"), None),
        P(None, ("wide", "narrow")),
    )

    def body(*args):
        unit = args[11].shape[1] // grid.total
        return shards(grid, unit % 32 == 0, *args)

    return jax.shard_map(body, mesh=mesh, in_specs=in_specs, out_specs=out_specs, check_vma=False)
```

```python
from functools import partial
import math

import jax
import jax.numpy as jnp
from jax import lax
from jax.experimental import pallas as pl
from jax.experimental.pallas import tpu as pltpu
from jax.sharding import PartitionSpec as P

HD = 64
SPK = 16
STEP = 10


SIGMA = 1e-05
NORM_EPS = 1e-05
LEARN_RATE = 0.01
GAIN_RATE = 0.3
BETA_ONE = 0.5
BETA_TWO = 0.5
DECAY = 0.01
ADAM_EPS = 1e-08
FAR_AWAY = -1e30
VMEM = 64 * 1024 * 1024
TABLE_AT = 768
HEAD_AT = 896
BANDS = 32
HEADS_AT_ONCE = 8


def as_low(x):
    return x.astype(jnp.bfloat16)


def contract_rows(left, right):
    return lax.dot_general(
        left, right, (((0,), (0,)), ((), ())), preferred_element_type=jnp.float32
    )


def time_features(flow, width):
    half = width // 2
    freqs = jnp.exp(-math.log(10000.0) * jnp.arange(half, dtype=jnp.float32) / half)
    angle = 1000.0 * flow * freqs
    return jnp.concatenate([jnp.sin(angle), jnp.cos(angle)])


def normalize(x):
    centered = x - jnp.mean(x, -1, keepdims=True)
    inverse = lax.rsqrt(jnp.mean(centered * centered, -1, keepdims=True) + NORM_EPS)
    return (centered * inverse, inverse)


def normalize_back(grad, normed, inverse):
    return inverse * (
        grad
        - jnp.mean(grad, -1, keepdims=True)
        - normed * jnp.mean(grad * normed, -1, keepdims=True)
    )


def head_slopes(heads):
    return 2.0 ** (-8.0 * (jnp.arange(heads, dtype=jnp.float32) + 1.0) / heads)


def adam_step(master, grad, moment, square, rate):
    moment = BETA_ONE * moment + (1.0 - BETA_ONE) * grad
    square = BETA_TWO * square + (1.0 - BETA_TWO) * grad * grad
    moment_hat = moment / (1.0 - BETA_ONE**STEP)
    square_hat = square / (1.0 - BETA_TWO**STEP)
    master = master - rate * (moment_hat / (jnp.sqrt(square_hat) + ADAM_EPS) + DECAY * master)
    return (master, moment, square)


AXES = ("wide", "narrow")


def grid_sizes(wide, narrow):
    low = 1
    while (2 * low) * (2 * low) <= wide:
        low *= 2
    return (wide // low, low, narrow // 2, 2)


class Grid:
    def __init__(self, mesh):
        self.sizes = grid_sizes(mesh.shape["wide"], mesh.shape["narrow"])
        self.total = mesh.shape["wide"] * mesh.shape["narrow"]

    def coords(self, index):
        out = []
        for size in reversed(self.sizes):
            out.append(index % size)
            index = index // size
        return out[::-1]

    def index(self, coords):
        index = 0
        for size, value in zip(self.sizes, coords):
            index = index * size + value
        return index

    def mixed(self):
        return self.sizes[1] == self.sizes[2]

    def axis(self, role, core):
        if role == "z":
            return 0
        if role == "core":
            return 3
        if self.mixed():
            return (2, 1)[core] if role == "far" else (1, 2)[core]
        return 2 if role == "far" else 1

    def size(self, role):
        return self.sizes[self.axis(role, 0)]

    def pairs(self, role, step):
        out = []
        for source in range(self.total):
            coords = self.coords(source)
            axis = self.axis(role, coords[3])
            coords[axis] = (coords[axis] + step) % self.sizes[axis]
            out.append((source, self.index(coords)))
        return out

    def lines(self):
        deep = self.total // self.sizes[0]
        return [[z * deep + rest for z in range(self.sizes[0])] for rest in range(deep)]

    def owners(self, core_step, direction, deep_first=False):
        me = self.coords(lax.axis_index(AXES))
        core = (me[3] + core_step) % 2
        far, near, deep = (self.size(r) for r in ("far", "near", "z"))
        f, n, z = jnp.meshgrid(jnp.arange(far), jnp.arange(near), jnp.arange(deep), indexing="ij")
        if deep_first:
            f, n, z = (t.swapaxes(1, 2) for t in (f, n, z))
        if self.mixed():
            y = jnp.where(core == 0, me[1] + direction * n, me[1] + direction * f) % self.sizes[1]
            x = jnp.where(core == 0, me[2] + direction * f, me[2] + direction * n) % self.sizes[2]
        else:
            y = (me[1] + direction * n) % self.sizes[1]
            x = (me[2] + direction * f) % self.sizes[2]
        return self.index((z, y, x, core)).reshape(-1).astype(jnp.int32)


def shift(grid, x, role, step):
    return lax.ppermute(x, AXES, grid.pairs(role, step))


def tied(x, *others):
    return lax.optimization_barrier((x,) + others)[0]


def swap_deep(grid, x):
    return lax.all_to_all(x, AXES, 0, 0, axis_index_groups=grid.lines())


def join(*xs):
    return lax.optimization_barrier(xs)


def spread(grid, x, role):
    return [x] + [shift(grid, x, role, step) for step in range(1, grid.size(role))]


def all_sum(grid, x):
    return jnp.sum(lax.all_to_all(jnp.broadcast_to(x[None], (grid.total,) + x.shape), AXES, 0, 0), 0)


def dot_nn(a, b):
    return lax.dot_general(a, b, (((1,), (0,)), ((), ())), preferred_element_type=jnp.float32)


def dot_nt(a, b):
    return lax.dot_general(a, b, (((1,), (1,)), ((), ())), preferred_element_type=jnp.float32)


def dot_tn(a, b):
    return lax.dot_general(a, b, (((0,), (0,)), ((), ())), preferred_element_type=jnp.float32)


def params():
    return pltpu.CompilerParams(vmem_limit_bytes=VMEM)


def key_bias(length, frames):
    key = lax.broadcasted_iota(jnp.int32, (frames, frames), 0)
    query = lax.broadcasted_iota(jnp.int32, (frames, frames), 1)
    dist = -jnp.abs(key - query).astype(jnp.float32)
    return jnp.where(key < length, dist, FAR_AWAY)


def attend_kernel(length_ref, slope_ref, packed_ref, mixed_ref, lse_ref, bias_ref):
    step = pl.program_id(0)
    q_ref, k_ref, v_ref = (packed_ref.at[j] for j in range(3))
    frames, lanes_here = mixed_ref.shape
    here = lanes_here // HD

    @pl.when(step == 0)
    def _():
        bias_ref[...] = key_bias(length_ref[0], frames)

    parts = []
    for h in range(here):
        lanes = slice(h * HD, (h + 1) * HD)
        scores = dot_nt(k_ref[:, lanes], q_ref[:, lanes] * jnp.bfloat16(HD**-0.5))
        scores = scores + slope_ref[here * step + h] * bias_ref[...]
        top = jnp.max(scores, 0, keepdims=True)
        expo = jnp.exp(scores - top)
        total = jnp.sum(expo, 0, keepdims=True)
        lse_ref[0, h : h + 1] = top + jnp.log(total)
        probs = as_low(expo * (1.0 / total))
        parts.append(dot_tn(v_ref[:, lanes], probs))
    mixed_ref[...] = as_low(jnp.concatenate(parts, 0).T)


def attend(length, slopes, packed):
    _, frames, width = packed.shape
    steps = width // (HEADS_AT_ONCE * HD)
    block = pl.BlockSpec((frames, HEADS_AT_ONCE * HD), lambda i: (0, i))
    return pl.pallas_call(
        attend_kernel,
        grid=(steps,),
        in_specs=[pl.BlockSpec(memory_space=pltpu.SMEM)] * 2
        + [pl.BlockSpec((3, frames, HEADS_AT_ONCE * HD), lambda i: (0, 0, i))],
        out_specs=[block, pl.BlockSpec((1, HEADS_AT_ONCE, frames), lambda i: (i, 0, 0))],
        out_shape=[
            jax.ShapeDtypeStruct((frames, width), jnp.bfloat16),
            jax.ShapeDtypeStruct((steps, HEADS_AT_ONCE, frames), jnp.float32),
        ],
        scratch_shapes=[pltpu.VMEM((frames, frames), jnp.float32)],
        compiler_params=params(),
        name="attend",
    )(length, slopes, packed)


def attend_back_kernel(
    length_ref, slope_ref, packed_ref, d_out_ref, w_ref, lse_ref, dq_ref, dk_ref, dv_ref, bias_ref
):
    step = pl.program_id(0)
    q_ref, k_ref, v_ref = (packed_ref.at[j] for j in range(3))
    frames, lanes_here = dq_ref.shape
    here = lanes_here // HD

    @pl.when(step == 0)
    def _():
        bias_ref[...] = key_bias(length_ref[0], frames)

    d_mixed_here = as_low(dot_nt(d_out_ref[...], w_ref[...]))
    d_query, d_keys, d_values = [], [], []
    for h in range(here):
        lanes = slice(h * HD, (h + 1) * HD)
        query = q_ref[:, lanes] * jnp.bfloat16(HD**-0.5)
        keys, values, d_mixed = k_ref[:, lanes], v_ref[:, lanes], d_mixed_here[:, lanes]
        scores = dot_nt(keys, query) + slope_ref[here * step + h] * bias_ref[...]
        probs = jnp.exp(scores - lse_ref[0, h : h + 1])
        d_probs = dot_nt(values, d_mixed)
        row_dot = jnp.sum(d_probs * probs, 0, keepdims=True)
        d_scores = as_low(probs * (d_probs - row_dot))
        d_values.append(dot_nn(as_low(probs), d_mixed))
        d_keys.append(dot_nn(d_scores, query))
        d_query.append(dot_tn(keys, d_scores))
    dq_ref[...] = as_low((jnp.concatenate(d_query, 0) * HD**-0.5).T)
    dk_ref[...] = as_low(jnp.concatenate(d_keys, 1))
    dv_ref[...] = as_low(jnp.concatenate(d_values, 1))


def attend_back(length, slopes, packed, d_out, w, lse):
    _, frames, width = packed.shape
    wide = HEADS_AT_ONCE * HD
    block = pl.BlockSpec((frames, wide), lambda i: (0, i))
    return pl.pallas_call(
        attend_back_kernel,
        grid=(width // wide,),
        in_specs=[pl.BlockSpec(memory_space=pltpu.SMEM)] * 2
        + [
            pl.BlockSpec((3, frames, wide), lambda i: (0, 0, i)),
            pl.BlockSpec((frames, width), lambda i: (0, 0)),
            pl.BlockSpec((wide, width), lambda i: (i, 0)),
            pl.BlockSpec((1, HEADS_AT_ONCE, frames), lambda i: (i, 0, 0)),
        ],
        out_specs=[block] * 3,
        out_shape=[jax.ShapeDtypeStruct((frames, width), jnp.bfloat16)] * 3,
        scratch_shapes=[pltpu.VMEM((frames, frames), jnp.float32)],
        compiler_params=params(),
        name="attend_back",
    )(length, slopes, packed, d_out, w, lse)


def gelu_both(x):
    z = jnp.abs(x) * (0.5**0.5)
    bell = jnp.exp(-z * z)
    t = 1.0 / (1.0 + 0.3275911 * z)
    poly = t * (0.254829592 + t * (-0.284496736 + t * (1.421413741 + t * (-1.453152027 + t * 1.061405429))))
    tail = 0.5 * poly * bell
    share = jnp.where(x >= 0, 1.0 - tail, tail)
    return x * share, share + x * bell * (0.5 / math.pi) ** 0.5


def expand_kernel(count, blocks, own_ref, other_ref, *refs):
    sources = refs[:count]
    x_ref, w_out, act_ref, turned_ref, slope_ref, w_ref, sems, out_sems = refs[count:]
    step = pl.program_id(0)
    width = x_ref.shape[1]
    unit = width // sum(source.shape[0] for source in sources)

    def copies(j):
        entry = (w_ref.at[j], (j + 1) * unit, unit, None, sems.at[j])
        return landing((own_ref, other_ref), sources, [entry])

    def kept(j):
        return pltpu.make_async_copy(w_ref.at[j], w_out.at[j], out_sems.at[j])

    def chunk(j):
        if j == 0:
            for n in range(blocks):
                begin(copies(n))
        finish(copies(j))
        kept(j).start()
        hidden = dot_nn(x_ref[...], w_ref[j])
        act, slope = gelu_both(hidden)
        act = as_low(act)
        act_ref[...] = act
        turned_ref[...] = act.T
        slope_ref[...] = as_low(slope)
        if j == blocks - 1:
            for n in range(blocks):
                kept(n).wait()

    for j in range(blocks):
        pl.when(step == j)(partial(chunk, j))


def expand(own, other, pieces, x, blocks):
    frames, width = x.shape
    total = blocks * width
    return pl.pallas_call(
        partial(expand_kernel, len(pieces), blocks),
        grid=(blocks,),
        in_specs=piece_specs(pieces) + [pl.BlockSpec((frames, width), lambda i: (0, 0))],
        out_specs=[
            pl.BlockSpec(memory_space=pl.ANY),
            pl.BlockSpec((frames, width), lambda i: (0, i)),
            pl.BlockSpec((width, frames), lambda i: (i, 0)),
            pl.BlockSpec((frames, width), lambda i: (0, i)),
        ],
        out_shape=[
            jax.ShapeDtypeStruct((blocks, width, width), jnp.bfloat16),
            jax.ShapeDtypeStruct((frames, total), jnp.bfloat16),
            jax.ShapeDtypeStruct((total, frames), jnp.bfloat16),
            jax.ShapeDtypeStruct((frames, total), jnp.bfloat16),
        ],
        scratch_shapes=[
            pltpu.VMEM((blocks, width, width), jnp.bfloat16),
            pltpu.SemaphoreType.DMA((blocks,)),
            pltpu.SemaphoreType.DMA((blocks,)),
        ],
        compiler_params=params(),
        name="expand",
    )(own, other, *pieces, x)


def landing(idx_refs, sources, entries):
    half = len(sources) // 2
    copies = []
    for s, source in enumerate(sources):
        idx_ref = idx_refs[s // half]
        count = source.shape[0]
        for i in range(count):
            band = idx_ref[(s % half) * count + i]
            for goal, start, rows, lane, sem in entries:
                part = source.at[i, pl.ds(start, rows)]
                if lane is not None:
                    part = source.at[i, pl.ds(start, rows), pl.ds(lane, goal.shape[-1])]
                place = goal.at[pl.ds(pl.multiple_of(band * rows, rows), rows)]
                copies.append(pltpu.make_async_copy(part, place, sem(band) if callable(sem) else sem))
    return copies


def begin(copies):
    for copy in copies:
        copy.start()


def finish(copies):
    for copy in copies:
        copy.wait()


def piece_specs(pieces):
    smem = pl.BlockSpec(memory_space=pltpu.SMEM)
    return [smem, smem] + [pl.BlockSpec(memory_space=pl.ANY)] * len(pieces)


def gain_row(edge_ref, at):
    return edge_ref[at : at + 1].astype(jnp.float32)


def front_kernel(
    at_gain, at_count, spacing, count, phone_rows, speaker_ref, own_ref, other_ref, *refs
):
    sources = refs[:count]
    states_ref, states_turned_ref, hot_ref, mel_ref, time_ref = refs[count : count + 5]
    (
        small_out, skip_out, embed_ref, stream_ref, joined_ref, normed_ref, turned_ref, edge_ref, share_ref,
        small_ref, skip_ref, table_ref, sems, out_sems,
    ) = refs[count + 5 :]
    width = stream_ref.shape[1]
    bands = sum(source.shape[0] for source in sources)
    unit = width // bands
    idx = (own_ref, other_ref)
    first = landing(
        idx, sources,
        [(small_ref, 0, unit, None, sems.at[0]), (table_ref, 0, phone_rows, TABLE_AT, sems.at[0])],
    )
    second = landing(idx, sources, [(skip_ref, unit, 2 * unit, None, sems.at[1])])
    begin(first)
    begin(second)
    phones = embed_ref.shape[1]
    joined_ref[width:] = states_turned_ref[...]
    finish(first)
    small_copy = pltpu.make_async_copy(small_ref, small_out, out_sems.at[0])
    small_copy.start()
    edge_ref[...] = small_ref[:, HEAD_AT:].T
    facts = edge_ref[at_count - HEAD_AT : at_count - HEAD_AT + 3].astype(jnp.float32)
    lane = lax.broadcasted_iota(jnp.int32, (1, width), 1)
    hit = (facts[:1] == speaker_ref[0].astype(jnp.float32)) & (lax.rem(lane, spacing) == 0)
    masked = jnp.sum(jnp.where(hit, 16.0 * facts[1:2] + facts[2:3], 0.0), 1, keepdims=True)
    share_ref[...] = (1.0 / SPK) / jnp.maximum(masked, 1.0)
    embedded = as_low(dot_nt(hot_ref[...], table_ref[...]))
    embed_ref[...] = embedded
    start = dot_nt(embedded, small_ref[:, :phones])
    start = start + dot_nt(mel_ref[...], small_ref[:, phones:TABLE_AT]) + time_ref[...]
    start = as_low(start)
    joined_ref[:width] = start.T
    finish(second)
    skip_copy = pltpu.make_async_copy(skip_ref, skip_out, out_sems.at[1])
    skip_copy.start()
    stream = dot_nn(start, skip_ref[:width]) + dot_nn(states_ref[...], skip_ref[width:])
    stream_ref[...] = stream
    normed = as_low(normalize(stream)[0] * gain_row(edge_ref, at_gain))
    normed_ref[...] = normed
    turned_ref[...] = normed.T
    small_copy.wait()
    skip_copy.wait()


def front(speaker, own, other, pieces, states, states_turned, hot, mel, time, phones, at_gain, at_count, spacing):
    frames, width = states.shape
    f32, low = jnp.float32, jnp.bfloat16
    bands = sum(p.shape[0] for p in pieces)
    vmem, anywhere = pl.BlockSpec(memory_space=pltpu.VMEM), pl.BlockSpec(memory_space=pl.ANY)
    return pl.pallas_call(
        partial(front_kernel, at_gain, at_count, spacing, len(pieces), phones // bands),
        in_specs=[pl.BlockSpec(memory_space=pltpu.SMEM)] + piece_specs(pieces) + [vmem] * 5,
        out_specs=[anywhere] * 2 + [vmem] * 7,
        out_shape=[
            jax.ShapeDtypeStruct((width, width), low),
            jax.ShapeDtypeStruct((2 * width, width), low),
            jax.ShapeDtypeStruct((frames, phones), low),
            jax.ShapeDtypeStruct((frames, width), f32),
            jax.ShapeDtypeStruct((2 * width, frames), low),
            jax.ShapeDtypeStruct((frames, width), low),
            jax.ShapeDtypeStruct((width, frames), low),
            jax.ShapeDtypeStruct((width - HEAD_AT, width), low),
            jax.ShapeDtypeStruct((1, 1), f32),
        ],
        scratch_shapes=[
            pltpu.VMEM((width, width), low),
            pltpu.VMEM((2 * width, width), low),
            pltpu.VMEM((phones, hot.shape[1]), low),
            pltpu.SemaphoreType.DMA((2,)),
            pltpu.SemaphoreType.DMA((2,)),
        ],
        compiler_params=params(),
        name="front",
    )(speaker, own, other, *pieces, states, states_turned, hot, mel, time)


def pack_kernel(count, blocks, own_ref, other_ref, *refs):
    sources = refs[:count]
    x_ref, w_out, out_ref, w_ref, sems, out_sems = refs[count:]
    step = pl.program_id(0)
    width = x_ref.shape[1]
    unit = width // sum(source.shape[0] for source in sources)

    def copies(j):
        entry = (w_ref.at[j], (3 + j) * unit, unit, None, sems.at[j])
        return landing((own_ref, other_ref), sources, [entry])

    def kept(j):
        return pltpu.make_async_copy(w_ref.at[j], w_out.at[j], out_sems.at[j])

    def chunk(j):
        if j == 0:
            for n in range(blocks):
                begin(copies(n))
        finish(copies(j))
        kept(j).start()
        out_ref[0] = as_low(dot_nn(x_ref[...], w_ref[j]))
        if j == blocks - 1:
            for n in range(blocks):
                kept(n).wait()

    for j in range(blocks):
        pl.when(step == j)(partial(chunk, j))


def pack(own, other, pieces, x, blocks):
    frames, width = x.shape
    return pl.pallas_call(
        partial(pack_kernel, len(pieces), blocks),
        grid=(blocks,),
        in_specs=piece_specs(pieces) + [pl.BlockSpec((frames, width), lambda i: (0, 0))],
        out_specs=[
            pl.BlockSpec(memory_space=pl.ANY),
            pl.BlockSpec((1, frames, width), lambda i: (i, 0, 0)),
        ],
        out_shape=[
            jax.ShapeDtypeStruct((blocks, width, width), jnp.bfloat16),
            jax.ShapeDtypeStruct((blocks, frames, width), jnp.bfloat16),
        ],
        scratch_shapes=[
            pltpu.VMEM((blocks, width, width), jnp.bfloat16),
            pltpu.SemaphoreType.DMA((blocks,)),
            pltpu.SemaphoreType.DMA((blocks,)),
        ],
        compiler_params=params(),
        name="pack",
    )(own, other, *pieces, x)


def mid_kernel(at_gain, count, own_ref, other_ref, *refs):
    sources = refs[:count]
    (
        mixed_ref, stream_ref, edge_ref, w_out, mid_ref, in_ref, turned_ref, mixed_turned_ref,
        w_ref, sem, out_sem,
    ) = refs[count:]
    width = stream_ref.shape[1]
    unit = width // sum(source.shape[0] for source in sources)
    copies = landing((own_ref, other_ref), sources, [(w_ref, 0, unit, None, sem)])
    begin(copies)
    mixed = mixed_ref[...]
    mixed_turned_ref[...] = mixed.T
    finish(copies)
    kept = pltpu.make_async_copy(w_ref, w_out, out_sem)
    kept.start()
    mid = stream_ref[...] + dot_nn(mixed, w_ref[...])
    mid_ref[...] = mid
    normed = as_low(normalize(mid)[0] * gain_row(edge_ref, at_gain))
    in_ref[...] = normed
    turned_ref[...] = normed.T
    kept.wait()


def mid_step(own, other, pieces, mixed, stream, edge, at_gain):
    frames, width = stream.shape
    low = jnp.bfloat16
    vmem = pl.BlockSpec(memory_space=pltpu.VMEM)
    return pl.pallas_call(
        partial(mid_kernel, at_gain, len(pieces)),
        in_specs=piece_specs(pieces) + [vmem] * 3,
        out_specs=[pl.BlockSpec(memory_space=pl.ANY)] + [vmem] * 4,
        out_shape=[
            jax.ShapeDtypeStruct((width, width), low),
            jax.ShapeDtypeStruct((frames, width), jnp.float32),
            jax.ShapeDtypeStruct((frames, width), low),
            jax.ShapeDtypeStruct((width, frames), low),
            jax.ShapeDtypeStruct((width, frames), low),
        ],
        scratch_shapes=[
            pltpu.VMEM((width, width), low),
            pltpu.SemaphoreType.DMA,
            pltpu.SemaphoreType.DMA,
        ],
        compiler_params=params(),
        name="mid",
    )(own, other, *pieces, mixed, stream, edge)


def head_kernel(at_gain, count, share_ref, own_ref, other_ref, *refs):
    sources = refs[:count]
    (
        act_ref, mid_ref, edge_ref, target_ref, inside_ref,
        w_out, d_ref, low_ref, grad_ref, gain_grad_ref, error_ref,
        total_ref, w_ref, sem, out_sem,
    ) = refs[count:]
    step = pl.program_id(0)
    tile = act_ref.shape[1]
    rows = w_ref.shape[0] // sum(source.shape[0] for source in sources)
    kept = pltpu.make_async_copy(w_ref, w_out, out_sem)
    each = tile // rows

    @pl.when(step == 0)
    def _():
        by_step = lambda band: sem.at[lax.div(band, each)]
        begin(landing((own_ref, other_ref), sources, [(w_ref, 0, rows, None, by_step)]))

    for _ in range(each):
        pltpu.make_async_copy(sources[0].at[0, pl.ds(0, rows)], w_ref.at[pl.ds(0, rows)], sem.at[step]).wait()

    @pl.when(step == pl.num_programs(0) - 1)
    def _():
        kept.start()

    part = dot_nn(act_ref[...], w_ref[pl.ds(pl.multiple_of(step * tile, tile), tile)])

    @pl.when(step == 0)
    def _():
        total_ref[...] = mid_ref[...] + part

    @pl.when(step > 0)
    def _():
        total_ref[...] += part

    @pl.when(step == pl.num_programs(0) - 1)
    def _():
        bins = target_ref.shape[1]
        normed, inverse = normalize(total_ref[...])
        gain = gain_row(edge_ref, at_gain)
        head_in = as_low(normed * gain)
        head = edge_ref[:bins]
        inside = inside_ref[...]
        error = dot_nt(head_in, head) - target_ref[...]
        error_ref[...] = jnp.sum(jnp.sum(error * error, 1, keepdims=True) * inside, 0, keepdims=True)
        d_prediction = as_low((2.0 * share_ref[...]) * error * inside)
        grad_ref[...] = dot_tn(head_in, d_prediction)
        d_head_in = dot_nn(d_prediction, head)
        gain_grad_ref[...] = jnp.sum(d_head_in * normed, 0, keepdims=True)
        d_stream = normalize_back(d_head_in * gain, normed, inverse)
        d_ref[...] = d_stream
        low_ref[...] = as_low(d_stream)
        kept.wait()


def head_step(share, own, other, pieces, act, mid, edge, target, inside, at_gain, tile=1024):
    frames, width = mid.shape
    bins = target.shape[1]
    total = act.shape[1]
    whole = lambda *shape: pl.BlockSpec(shape, lambda i: (0,) * len(shape))
    return pl.pallas_call(
        partial(head_kernel, at_gain, len(pieces)),
        grid=(total // tile,),
        in_specs=[whole(1, 1)]
        + piece_specs(pieces)
        + [
            pl.BlockSpec((frames, tile), lambda i: (0, i)),
            whole(frames, width), whole(*edge.shape), whole(frames, bins), whole(frames, 1),
        ],
        out_specs=[
            pl.BlockSpec(memory_space=pl.ANY),
            whole(frames, width), whole(frames, width), whole(width, bins), whole(1, width), whole(1, 1),
        ],
        out_shape=[
            jax.ShapeDtypeStruct((total, width), jnp.bfloat16),
            jax.ShapeDtypeStruct((frames, width), jnp.float32),
            jax.ShapeDtypeStruct((frames, width), jnp.bfloat16),
            jax.ShapeDtypeStruct((width, bins), jnp.float32),
            jax.ShapeDtypeStruct((1, width), jnp.float32),
            jax.ShapeDtypeStruct((1, 1), jnp.float32),
        ],
        scratch_shapes=[
            pltpu.VMEM((frames, width), jnp.float32),
            pltpu.VMEM((total, width), jnp.bfloat16),
            pltpu.SemaphoreType.DMA((total // tile,)),
            pltpu.SemaphoreType.DMA,
        ],
        compiler_params=params(),
        name="head",
    )(share, own, other, *pieces, act, mid, edge, target, inside)


def ffn_back_kernel(
    at_gain, low_ref, d_ref, down_ref, slope_ref, up_ref, mid_ref, edge_ref,
    out_ref, out_low_ref, gain_grad_ref, *refs,
):
    hidden_refs, total_ref = refs[:-1], refs[-1]
    step = pl.program_id(0)
    d_hidden = as_low(dot_nt(low_ref[...], down_ref[...]) * slope_ref[...].astype(jnp.float32))
    for j, ref in enumerate(hidden_refs):

        @pl.when(step == j)
        def _(ref=ref):
            ref[...] = d_hidden

    part = dot_nt(d_hidden, up_ref[0])

    @pl.when(step == 0)
    def _():
        total_ref[...] = part

    @pl.when(step > 0)
    def _():
        total_ref[...] += part

    @pl.when(step == pl.num_programs(0) - 1)
    def _():
        normed, inverse = normalize(mid_ref[...])
        grad = total_ref[...]
        gain_grad_ref[...] = jnp.sum(grad * normed, 0, keepdims=True)
        out = d_ref[...] + normalize_back(grad * gain_row(edge_ref, at_gain), normed, inverse)
        out_ref[...] = out
        out_low_ref[...] = as_low(out)


def ffn_back(low, d, down, slope, up, mid, edge, at_gain):
    frames, width = mid.shape
    count = up.shape[0]
    whole = lambda *shape: pl.BlockSpec(shape, lambda i: (0,) * len(shape))
    return pl.pallas_call(
        partial(ffn_back_kernel, at_gain),
        grid=(count,),
        in_specs=[
            whole(frames, width), whole(frames, width),
            pl.BlockSpec((width, width), lambda i: (i, 0)),
            pl.BlockSpec((frames, width), lambda i: (0, i)),
            pl.BlockSpec((1, width, width), lambda i: (i, 0, 0)),
            whole(frames, width), whole(*edge.shape),
        ],
        out_specs=[whole(frames, width), whole(frames, width), whole(1, width)]
        + [whole(frames, width)] * count,
        out_shape=[
            jax.ShapeDtypeStruct((frames, width), jnp.float32),
            jax.ShapeDtypeStruct((frames, width), jnp.bfloat16),
            jax.ShapeDtypeStruct((1, width), jnp.float32),
        ]
        + [jax.ShapeDtypeStruct((frames, width), jnp.bfloat16)] * count,
        scratch_shapes=[pltpu.VMEM((frames, width), jnp.float32)],
        compiler_params=params(),
        name="ffn_back",
    )(low, d, down, slope, up, mid, edge)


def pack_back_kernel(at_gain, blocks, *refs):
    w_ref, d_ref, stream_ref, edge_ref, low_ref, gain_grad_ref, total_ref = refs[blocks:]
    step = pl.program_id(0)

    def chunk(j):
        part = dot_nt(refs[j][...], w_ref[0])
        total_ref[...] = part if j == 0 else total_ref[...] + part

    for j in range(blocks):
        pl.when(step == j)(partial(chunk, j))

    @pl.when(step == pl.num_programs(0) - 1)
    def _():
        grad = total_ref[...]
        normed, inverse = normalize(stream_ref[...])
        gain_grad_ref[...] = jnp.sum(grad * normed, 0, keepdims=True)
        gain = gain_row(edge_ref, at_gain)
        low_ref[...] = as_low(d_ref[...] + normalize_back(grad * gain, normed, inverse))


def pack_back(packed, w, d, stream, edge, at_gain):
    frames, width = stream.shape
    whole = lambda *shape: pl.BlockSpec(shape, lambda i: (0,) * len(shape))
    return pl.pallas_call(
        partial(pack_back_kernel, at_gain, w.shape[0]),
        grid=(w.shape[0],),
        in_specs=[whole(frames, width)] * w.shape[0]
        + [
            pl.BlockSpec((1, width, width), lambda i: (i, 0, 0)),
            whole(frames, width), whole(frames, width), whole(*edge.shape),
        ],
        out_specs=[whole(frames, width), whole(1, width)],
        out_shape=[
            jax.ShapeDtypeStruct((frames, width), jnp.bfloat16),
            jax.ShapeDtypeStruct((1, width), jnp.float32),
        ],
        scratch_shapes=[pltpu.VMEM((frames, width), jnp.float32)],
        compiler_params=params(),
        name="pack_back",
    )(*packed, w, d, stream, edge)


def tail_kernel(
    at_gain, d_ref, skip_ref, small_ref, embed_ref, mel_ref, hot_ref, head_ref, one_ref, two_ref, three_ref,
    main_ref, table_ref, edge_ref,
):
    phones = embed_ref.shape[1]
    d_start = as_low(dot_nt(d_ref[...], skip_ref[...]))
    d_phones = as_low(dot_nn(d_start, small_ref[:, :phones]))
    main_ref[:, :phones] = as_low(dot_tn(d_start, embed_ref[...]))
    main_ref[:, phones:] = as_low(dot_tn(d_start, mel_ref[...]))
    table_ref[...] = as_low(dot_tn(d_phones, hot_ref[...]))
    edge = head_ref[...]
    lanes = edge.shape[1]
    edge = jnp.pad(edge, ((0, 0), (0, edge_ref.shape[1] - lanes)))
    lane = lax.broadcasted_iota(jnp.int32, edge.shape, 1)
    for j, ref in enumerate((one_ref, two_ref, three_ref)):
        column = jnp.broadcast_to(ref[...], (8, edge.shape[0])).T[:, :1]
        edge = jnp.where(lane == at_gain + j, column, edge)
    edge_ref[...] = as_low(edge)


def tail(d, skip, small, embed, mel, hot, head, gains, at_gain):
    width = d.shape[1]
    phones = embed.shape[1]
    whole = lambda x: pl.BlockSpec(x.shape, lambda i: (0, 0))
    arrays = (small, embed, mel, hot, head, *gains)
    shapes = [(width, TABLE_AT), (phones, hot.shape[1]), (width, width - HEAD_AT)]
    return pl.pallas_call(
        partial(tail_kernel, at_gain),
        grid=(1,),
        in_specs=[whole(d), pl.BlockSpec((width, width), lambda i: (0, 0))] + [whole(x) for x in arrays],
        out_specs=[pl.BlockSpec(s, lambda i: (0, 0)) for s in shapes],
        out_shape=[jax.ShapeDtypeStruct(s, jnp.bfloat16) for s in shapes],
        compiler_params=params(),
        name="tail",
    )(d, skip, *arrays)


def grads_kernel(plan, count, rows, legs, came_too, idx_ref, *refs):
    refs, picked_ref, right_ref, sems = refs[:-3], refs[-3], refs[-2], refs[-1]
    frames = right_ref.shape[1] // 2
    outs = refs[len(refs) - legs :]
    came_ref = refs[len(refs) - legs - 1] if came_too else None
    step = pl.program_id(0)
    each = count // legs

    def copies(c):
        lefts, rights, stride, offset = plan[c]
        if rights is None:
            return []
        slot = c % 2
        return [
            pltpu.make_async_copy(
                refs[left].at[pl.ds(pl.multiple_of(idx_ref[i] * stride + offset, rows), rows)],
                picked_ref.at[slot, pl.ds(i * rows, rows), pl.ds(side * frames, frames)],
                sems.at[slot],
            )
            for side, left in enumerate(lefts)
            for i in range(count)
        ] + [
            pltpu.make_async_copy(refs[right], right_ref.at[slot, pl.ds(side * frames, frames)], sems.at[slot])
            for side, right in enumerate(rights)
        ]

    def chunk(c):
        lefts, rights, _, _ = plan[c]
        if c == 0:
            for copy in copies(0):
                copy.start()
        if c + 1 < len(plan):
            for copy in copies(c + 1):
                copy.start()
        for copy in copies(c):
            copy.wait()
        if rights is None:
            main, table, edge = (refs[r] for r in lefts)
            thick = table.shape[0] // (main.shape[0] // rows)
            blocks = []
            for i in range(count):
                start = pl.multiple_of(idx_ref[i] * rows, rows)
                short = pl.multiple_of(idx_ref[i] * thick, thick)
                lead = table[pl.ds(short, thick)]
                rest = jnp.zeros((rows - thick, lead.shape[1]), lead.dtype)
                middle = jnp.concatenate([lead, rest], 0) if thick < rows else lead
                block = [main[pl.ds(start, rows)], middle, edge[pl.ds(start, rows)]]
                blocks.append(jnp.concatenate(block, 1).astype(jnp.float32))
            total = jnp.stack(blocks)
            if came_too:
                total = total + came_ref[...].astype(jnp.float32)
        else:
            wide = outs[0].shape[2]
            total = dot_nn(picked_ref[c % 2], right_ref[c % 2])
            total = total.reshape(count, rows, wide)
        for f in range(legs):
            outs[f][...] = as_low(total[f * each : (f + 1) * each])

    for c in range(len(plan)):
        pl.when(step == c)(partial(chunk, c))


def grads(plan, arrays, idx, frames, rows, width, legs, came=None):
    count = idx.shape[0]
    copied = [j for entry in plan if entry[1] is not None for j in entry[0] + entry[1]]

    def spec(j, x):
        if j in copied:
            return pl.BlockSpec(memory_space=pltpu.HBM)
        return pl.BlockSpec(x.shape, lambda i, n=len(x.shape): (0,) * n)

    specs = [spec(j, x) for j, x in enumerate(arrays)]
    if came is not None:
        specs.append(pl.BlockSpec((count, rows, width), lambda i: (0, 0, 0)))
        arrays = list(arrays) + [came]
    return pl.pallas_call(
        partial(grads_kernel, plan, count, rows, legs, came is not None),
        grid=(len(plan),),
        in_specs=[pl.BlockSpec(memory_space=pltpu.SMEM)] + specs,
        out_specs=[pl.BlockSpec((count // legs, rows, width), lambda i: (0, i, 0))] * legs,
        out_shape=[jax.ShapeDtypeStruct((count // legs, rows * len(plan), width), jnp.bfloat16)] * legs,
        scratch_shapes=[
            pltpu.VMEM((2, count * rows, 2 * frames), jnp.bfloat16),
            pltpu.VMEM((2, 2 * frames, width), jnp.bfloat16),
            pltpu.SemaphoreType.DMA((2,)),
        ],
        compiler_params=params(),
        name="grads",
    )(idx, *arrays)


def fold_kernel(legs, *refs):
    ins, outs = refs[:-legs], refs[-legs:]
    took = len(ins) // legs
    for j in range(legs):
        total = ins[j * took][...].astype(jnp.float32)
        for ref in ins[j * took + 1 : (j + 1) * took]:
            total = total + ref[...].astype(jnp.float32)
        outs[j][...] = as_low(total)


def fold(parts, legs):
    count, rows, width = parts[0].shape
    each = count // legs
    tile = rows // 2
    return pl.pallas_call(
        partial(fold_kernel, legs),
        grid=(rows // tile,),
        in_specs=[
            pl.BlockSpec((each, tile, width), lambda i, j=j: (j, i, 0)) for j in range(legs) for _ in parts
        ],
        out_specs=[pl.BlockSpec((each, tile, width), lambda i: (0, i, 0))] * legs,
        out_shape=[jax.ShapeDtypeStruct((each, rows, width), jnp.bfloat16)] * legs,
        compiler_params=params(),
        name="fold",
    )(*[p for _ in range(legs) for p in parts])


def stack_kernel(*refs):
    ins, out, sem = refs[:-2], refs[-2], refs[-1]
    copies = [
        pltpu.make_async_copy(ref, out.at[n, i], sem) for n in range(out.shape[0]) for i, ref in enumerate(ins)
    ]
    for copy in copies:
        copy.start()
    for copy in copies:
        copy.wait()


def stack(parts, times):
    return pl.pallas_call(
        stack_kernel,
        in_specs=[pl.BlockSpec(memory_space=pl.ANY)] * len(parts),
        out_specs=pl.BlockSpec(memory_space=pltpu.VMEM),
        out_shape=jax.ShapeDtypeStruct((times, len(parts)) + parts[0].shape, parts[0].dtype),
        scratch_shapes=[pltpu.SemaphoreType.DMA],
        compiler_params=params(),
        name="stack",
    )(*parts)


def update(grad, rate, master_ref, moment_ref, square_ref, clip):
    return adam_step(master_ref[...], grad * clip, moment_ref[...], square_ref[...], rate)


def adam_kernel(at, clip_ref, *refs):
    phone_rows, phone_width, inputs, at_gain = at
    last, attend, expand, reduce = refs[:4]
    masters, moments, squares = refs[4:13], refs[13:22], refs[22:31]
    outs = refs[31:]
    unit = last.shape[0] // 3
    small = last[2 * unit :]
    clip = clip_ref[0]
    mel_lanes = inputs - phone_width
    lanes = [small[:, phone_width : phone_width + mel_lanes], small[:, :phone_width]]
    edge = small[:, HEAD_AT:]
    turned_edge = edge.T
    bins = masters[7].shape[1]

    def columns(ref, first):
        blocks = [ref[j : j + unit] for j in range(first, ref.shape[0], unit)]
        return jnp.concatenate(blocks, 1)

    grads_of = [
        jnp.concatenate(lanes, 1),
        small[:phone_rows, TABLE_AT:HEAD_AT],
        last[: 2 * unit],
        columns(attend, unit),
        attend[:unit],
        columns(expand, 0),
        reduce[...],
        edge[:, :bins],
        turned_edge[at_gain : at_gain + 3],
    ]
    for j, grad in enumerate(grads_of):
        rate = GAIN_RATE if j in (1, 8) else LEARN_RATE
        after = update(grad, rate, masters[j], moments[j], squares[j], clip)
        for n, value in enumerate(after):
            outs[9 * n + j][...] = value


def adam(clip, shares, masters, moments, squares, at):
    turned = lambda group: [x.T if j < 2 else x for j, x in enumerate(group)]
    masters, moments, squares = turned(masters), turned(moments), turned(squares)
    vmem = pl.BlockSpec(memory_space=pltpu.VMEM)
    arrays = [*shares, *masters, *moments, *squares]
    results = pl.pallas_call(
        partial(adam_kernel, at),
        in_specs=[pl.BlockSpec(memory_space=pltpu.SMEM)] + [vmem] * len(arrays),
        out_specs=[vmem] * 27,
        out_shape=[jax.ShapeDtypeStruct(x.shape, jnp.float32) for x in (*masters, *moments, *squares)],
        compiler_params=params(),
        name="adam",
    )(clip, *arrays)
    return [y for n in range(3) for y in turned(results[9 * n : 9 * n + 9])]


def prepare_kernel(
    at_mel, at_count, frames,
    facts_ref, input_ref, table_ref, head_ref, gains_ref, skip_ref, attend_ref, out_ref,
):
    unit, inputs = input_ref.shape
    phones = inputs - at_mel
    turned = as_low(input_ref[...])
    out_ref[0, :unit, :phones] = turned[:, at_mel:]
    out_ref[0, :unit, phones:TABLE_AT] = jnp.pad(turned[:, :at_mel], ((0, 0), (0, TABLE_AT - inputs)))
    table = as_low(table_ref[...])
    rest = jnp.zeros((unit - table.shape[0], table.shape[1]), jnp.bfloat16)
    out_ref[0, :unit, TABLE_AT:HEAD_AT] = jnp.concatenate([table, rest], 0)
    bins = head_ref.shape[1]
    edge = jnp.pad(head_ref[...], ((0, 0), (0, out_ref.shape[2] - HEAD_AT - bins)))
    lane = lax.broadcasted_iota(jnp.int32, edge.shape, 1)
    spot = (gains_ref.shape[0], edge.shape[1])
    row = lax.broadcasted_iota(jnp.int32, spot, 0)
    here = lax.broadcasted_iota(jnp.int32, spot, 1) == row + bins
    edge = as_low(edge).astype(jnp.float32) + dot_tn(as_low(gains_ref[...]), as_low(here))
    end = jnp.minimum(jnp.minimum(facts_ref[2], facts_ref[3]), frames)
    count = jnp.maximum(end - jnp.maximum(facts_ref[1], 0), 0)
    for j, fact in enumerate((facts_ref[0], lax.div(count, 16), lax.rem(count, 16))):
        edge = jnp.where(lane == at_count - HEAD_AT + j, fact.astype(jnp.float32), edge)
    out_ref[0, :unit, HEAD_AT:] = as_low(edge)
    width = out_ref.shape[2]
    start = unit + skip_ref.shape[0]
    out_ref[0, unit:start] = as_low(skip_ref[...])
    for j in range(attend_ref.shape[1] // width):
        here = slice(start + j * unit, start + (j + 1) * unit)
        out_ref[0, here] = as_low(attend_ref[:, j * width : (j + 1) * width])
    for z in range(1, out_ref.shape[0]):
        out_ref[z] = out_ref[0]


def prepare(facts, turned, table, head, gains, skip, attend, deep, frames, at_mel, at_count):
    vmem = pl.BlockSpec(memory_space=pltpu.VMEM)
    width = skip.shape[1]
    rows = turned.shape[0] + skip.shape[0] + attend.size // width
    return pl.pallas_call(
        partial(prepare_kernel, at_mel, at_count, frames),
        in_specs=[pl.BlockSpec(memory_space=pltpu.SMEM)] + [vmem] * 6,
        out_specs=vmem,
        out_shape=jax.ShapeDtypeStruct((deep, rows, width), jnp.bfloat16),
        compiler_params=params(),
        name="prepare",
    )(facts, turned, table, head, gains, skip, attend)


def shards(
    grid,
    fast,
    clean_mel,
    gauss_noise,
    flow_time,
    phone_ids,
    lengths,
    span_start,
    span_end,
    speaker,
    skip_states,
    w_input,
    phone_table,
    w_skip,
    w_attend,
    w_output,
    w_expand,
    w_reduce,
    w_head,
    norm_gains,
    moment_input,
    moment_table,
    moment_skip,
    moment_attend,
    moment_output,
    moment_expand,
    moment_reduce,
    moment_head,
    moment_gains,
    square_input,
    square_table,
    square_skip,
    square_attend,
    square_output,
    square_expand,
    square_reduce,
    square_head,
    square_gains,
):
    masters = (w_input, phone_table, w_skip, w_attend, w_output, w_expand, w_reduce, w_head, norm_gains)
    moments = (
        moment_input, moment_table, moment_skip, moment_attend, moment_output,
        moment_expand, moment_reduce, moment_head, moment_gains,
    )
    squares = (
        square_input, square_table, square_skip, square_attend, square_output,
        square_expand, square_reduce, square_head, square_gains,
    )
    frames, mel_bins = clean_mel.shape
    width = w_skip.shape[1]
    heads = width // HD
    devices = grid.total
    unit = width // devices
    inputs = w_input.shape[0]
    phones = phone_table.shape[0]
    phone_wide = phone_table.shape[1]
    phone_width = phone_wide * devices
    mel_lanes = TABLE_AT - phone_width
    at_gain = HEAD_AT + mel_bins
    at_count = at_gain + 3
    position = jnp.arange(frames)
    frame_valid = (position < lengths[0]).astype(jnp.float32)
    frame_inside = ((position >= span_start[0]) & (position < span_end[0])).astype(
        jnp.float32
    ) * frame_valid
    speaker_hot = (speaker[0] == jnp.arange(SPK)).astype(jnp.float32)
    count = jnp.sum(frame_inside)
    count_high = jnp.floor(count / 16.0)
    tally = jnp.stack([speaker[0].astype(jnp.float32), count_high, count - 16.0 * count_high])

    low_input = as_low(w_input)
    small = jnp.concatenate(
        [
            low_input[2 * mel_bins :].T,
            low_input[: 2 * mel_bins].T,
            jnp.zeros((unit, TABLE_AT - inputs), jnp.bfloat16),
            jnp.pad(as_low(phone_table).T, ((0, unit - phone_wide), (0, 0))),
            as_low(w_head),
            as_low(norm_gains).T,
            jnp.broadcast_to(as_low(tally)[None, :], (unit, 3)),
            jnp.zeros((unit, width - at_count - 3), jnp.bfloat16),
        ],
        1,
    )

    def blocks(x):
        return [as_low(x[:, j : j + width]) for j in range(0, x.shape[1], width)]

    attend_blocks, expand_blocks = blocks(w_attend), blocks(w_expand)
    packs, wides = len(attend_blocks), len(expand_blocks)
    stages = [
        [("small", None, small), ("skip", None, as_low(w_skip))]
        + [("attend", j, w) for j, w in enumerate(attend_blocks)],
        [("output", None, as_low(w_output))] + [("expand", j, w) for j, w in enumerate(expand_blocks)],
        [("reduce", None, as_low(w_reduce))],
    ]
    if fast:
        own, other = grid.owners(0, -1), grid.owners(1, -1)
        own_turned, other_turned = grid.owners(0, -1, True), grid.owners(1, -1, True)
        mine, theirs = grid.owners(0, 1), grid.owners(1, 1)

    def load(stage):
        return jnp.concatenate([w for _, _, w in stage], 0)

    def sibling(x):
        return shift(grid, x, "core", 1)

    def along(x, role, *after):
        return spread(grid, tied(x, *after) if after else x, role)

    def deepen(x, *after):
        return swap_deep(grid, tied(x, *after) if after else x)

    def hop_far(pieces):
        return [shift(grid, p, "far", f) for f in range(1, grid.size("far")) for p in pieces]

    def gather_whole(stage):
        rows = lax.all_gather(load(stage), AXES, axis=0, tiled=False)
        parts, start = [], 0
        for name, _, w in stage:
            part = rows[:, start : start + w.shape[0]]
            start += w.shape[0]
            if name == "small":
                table = part[:, :phone_wide, TABLE_AT:HEAD_AT].reshape(BANDS, -1, phones)
                table = jnp.pad(table, ((0, 0), (0, width // BANDS - table.shape[1]), (0, 0)))
                part = part.reshape(BANDS, -1, width)
                part = jnp.concatenate([part[..., :TABLE_AT], table, part[..., HEAD_AT:]], 2)
            parts.append(part.reshape(BANDS, -1, width))
        rows = jnp.concatenate(parts, 1)
        return [rows[: BANDS // 2], rows[BANDS // 2 :]]

    flow = flow_time[0]
    noisy_mel = (1.0 - (1.0 - SIGMA) * flow) * gauss_noise + flow * clean_mel
    context = clean_mel * (frame_valid - frame_inside)[:, None]
    target = clean_mel - (1.0 - SIGMA) * gauss_noise
    mel = jnp.concatenate([as_low(noisy_mel), as_low(context)], 1)
    mel = jnp.pad(mel, ((0, 0), (0, mel_lanes - mel.shape[1])))
    phone_hot = as_low(phone_ids[:, None] == jnp.arange(phones)[None, :])
    slopes = head_slopes(heads)
    times = time_features(flow, width)[None, :]
    inside = frame_inside[:, None]
    states_turned = skip_states.T
    loads = [load(stage) for stage in stages]
    if fast:
        first = prepare(
            jnp.stack([speaker[0], span_start[0], span_end[0], lengths[0]]), w_input.T, phone_table.T,
            w_head, norm_gains, w_skip, w_attend, grid.size("z"), frames, 2 * mel_bins, at_count,
        )
        pair_1 = stack(along(loads[1], "near"), grid.size("z"))
        load_2 = stack([loads[2]], grid.size("z"))[:, 0]
        deep_0, pair_1, load_2 = join(deepen(first), pair_1, load_2)
        deep_1 = deepen(pair_1)
        near_0 = along(deep_0, "near")
        near_0 = [tied(near_0[0], near_0[-1])] + near_0[1:]
        (
            near_0, far_0, core_0, deep_1, own, other, own_turned, other_turned, mine, theirs,
            target, mel, phone_hot, slopes, times, inside, states_turned,
        ) = join(
            near_0, hop_far(near_0), [sibling(p) for p in near_0], deep_1,
            own, other, own_turned, other_turned, mine, theirs,
            target, mel, phone_hot, slopes, times, inside, states_turned,
        )
        pieces_0 = near_0 + far_0 + core_0 + [sibling(p) for p in far_0]
        near_1 = deep_1.reshape((-1,) + deep_1.shape[2:])
        far_1 = along(near_1, "far")[1]
        core_1 = sibling(near_1)
        deep_2 = deepen(load_2, near_1)
    else:
        own, other = jnp.arange(BANDS // 2), jnp.arange(BANDS // 2, BANDS)
        own_turned, other_turned = own, other
        pieces_0 = gather_whole(stages[0])
    small_full, skip_full, embedded, stream, joined_turned, attn_in, attn_turned, edges, share = front(
        speaker, own, other, pieces_0, skip_states, states_turned, phone_hot, mel, times, phone_width, mel_bins, at_count, unit
    )
    attend_full, packed = pack(own, other, pieces_0, attn_in, packs)
    if fast:
        near_2 = along(tied(deep_2, packed), "near")
    mixed, lse = attend(lengths, slopes, packed)
    if fast:
        far_1, near_2, core_1, stream, packed, mixed, lse, joined_turned, edges, share = join(
            far_1, near_2, core_1, stream, packed, mixed, lse, joined_turned, edges, share
        )
        pieces_1 = [near_1, far_1, core_1, sibling(far_1)]
        far_2 = hop_far(near_2)
        core_2 = [sibling(p) for p in near_2]
    else:
        pieces_1 = gather_whole(stages[1])
    output_full, stream_mid, ffn_in, ffn_turned, mixed_turned = mid_step(
        own_turned, other_turned, pieces_1, mixed, stream, edges, mel_bins + 1
    )
    expand_full, activated, act_turned, gelu_slope = expand(
        own_turned, other_turned, pieces_1, ffn_in, wides
    )
    if fast:
        far_2, core_2, stream_mid, ffn_turned, mixed_turned, activated, act_turned, gelu_slope = join(
            far_2, core_2, stream_mid, ffn_turned, mixed_turned, activated, act_turned, gelu_slope
        )
        pieces_2 = near_2 + far_2 + core_2 + [sibling(p) for p in far_2]
    else:
        pieces_2 = gather_whole(stages[2])
    reduce_full, d_stream_out, d_branch, grad_head, grad_gain_three, error_sum = head_step(
        share, own, other, pieces_2, activated, stream_mid, edges, target, inside, mel_bins + 2
    )
    far, near, deep = (grid.size(r) for r in ("far", "near", "z"))

    def both(*arrays):
        return [y for x in arrays for y in (x, sibling(x))]

    def sums(plan, arrays, *others, **options):
        first = [tied(arrays[0], *others)] if others else arrays[:1]
        return grads(plan, first + arrays[1:], mine, frames, unit, width, far, **options)

    def hops(legs, role, *others):
        sent = [tied(leg, *others) if others else leg for leg in legs[1:]]
        return [shift(grid, leg, role, j + 1) for j, leg in enumerate(sent)]

    def dense(pairs):
        parts = []
        for turned, right, stride, offset in pairs:
            if right is None:
                part = turned.reshape(devices, unit, width)
            else:
                turned = turned.reshape(devices, stride, frames)[:, offset : offset + unit]
                part = dot_nn(turned.reshape(width, frames), right).reshape(devices, unit, width)
            parts.append(part)
        return lax.psum_scatter(jnp.concatenate(parts, 1), AXES, scatter_dimension=0)

    offsets = [j * unit for j in range(wides)]
    if fast:
        plan = [((0, 1), (2, 3), wides * unit, o) for o in offsets]
        legs_0 = sums(plan, both(tied(act_turned, *pieces_2), d_branch))
        moved_0 = hops(legs_0, "far")
        d_branch_next = tied(d_branch, legs_0[0])
    else:
        share_reduce = dense([(act_turned, d_branch, wides * unit, o) for o in offsets])
        d_branch_next = d_branch
    d_stream_mid, d_out, grad_gain_two, *d_hidden = ffn_back(
        d_branch_next, d_stream_out, reduce_full, gelu_slope, expand_full, stream_mid, edges, mel_bins + 1
    )
    if fast:
        turned = both(ffn_turned)
        d_hiddens = both(*d_hidden)
        moved_0, turned, d_hiddens[:4], d_stream_mid, d_out = join(
            moved_0, turned, d_hiddens[:4], d_stream_mid, d_out
        )
        legs_0 = fold([legs_0[0]] + moved_0, near)
        moved_0 = hops(legs_0, "near")
        plan = [((0, 1), (2 + 2 * j, 3 + 2 * j), unit, 0) for j in range(wides)]
        legs_1 = sums(plan, turned + d_hiddens, legs_0[0])
        turned = both(tied(mixed_turned, legs_0[0]), attn_turned, d_out)
        moved_0, legs_1, turned, d_out = join(moved_0, legs_1, turned, d_out)
        (sums_0,) = fold([legs_0[0]] + moved_0, 1)
        d_out = tied(d_out, sums_0)
        moved_1 = hops(legs_1, "far", sums_0)
        sums_0 = swap_deep(grid, sums_0)
    else:
        share_expand = dense([(ffn_turned, d, unit, 0) for d in d_hidden])
    d_packed = attend_back(lengths, slopes, packed, d_out, output_full, lse)
    d_joined_in, grad_gain_one = pack_back(
        d_packed, attend_full, d_stream_mid, stream, edges, mel_bins
    )
    if fast:
        d_packs = both(*d_packed)
        moved_1, sums_0, d_packs, d_joined_in = join(moved_1, sums_0, d_packs, d_joined_in)
        legs_1 = fold([legs_1[0]] + moved_1, near)
        moved_1 = hops(legs_1, "near")
        plan = [((0, 1), (4, 5), unit, 0)]
        plan = plan + [((2, 3), (6 + 2 * j, 7 + 2 * j), unit, 0) for j in range(packs)]
        legs_2 = sums(plan, turned + d_packs, legs_1[0])
        joined = both(tied(joined_turned, legs_1[0]), tied(d_joined_in, legs_1[0]))
        moved_1, legs_2, joined, d_joined_in = join(moved_1, legs_2, joined, d_joined_in)
        (sums_1,) = fold([legs_1[0]] + moved_1, 1)
        d_joined_in = tied(d_joined_in, sums_1)
        moved_2 = hops(legs_2, "far", sums_1)
        sums_1 = swap_deep(grid, sums_1)
    else:
        share_attend = dense(
            [(mixed_turned, d_out, unit, 0)] + [(attn_turned, d, unit, 0) for d in d_packed]
        )
    tallies = edges[at_count - HEAD_AT : at_count - HEAD_AT + 3].reshape(3, devices, unit)
    tallies = tallies[:, :, 0].astype(jnp.float32)
    counts = jnp.sum(
        (tallies[0][:, None] == jnp.arange(SPK, dtype=jnp.float32)[None, :])
        * (16.0 * tallies[1] + tallies[2])[:, None],
        0,
    )
    gain_grads = [grad_gain_one, grad_gain_two, grad_gain_three]
    small_grads = tail(
        d_joined_in, skip_full, small_full, embedded, mel, phone_hot, grad_head, gain_grads, mel_bins
    )
    if fast:
        small_grads = list(small_grads)
        (sent,) = grads([((0, 1, 2), None, 0, 0)], small_grads, theirs, frames, unit, width, 1)
        plan = [((0, 1), (2, 3), 2 * unit, o) for o in offsets[:2]] + [((4, 5, 6), None, 0, 0)]
        legs_3 = sums(plan, joined + small_grads, sent, came=sibling(sent))
        moved_2, legs_3 = join(moved_2, legs_3)
        legs_2 = fold([legs_2[0]] + moved_2, near)
        moved_3 = hops(legs_3, "far", legs_2[0])
        moved_2, sums_1, counts = join(hops(legs_2, "near"), sums_1, counts)
        (sums_2,) = fold([legs_2[0]] + moved_2, 1)
        moved_3 = [tied(moved_3[0], sums_2)] + moved_3[1:]
        legs_3 = fold([legs_3[0]] + moved_3, near)
        moved_3, sums_2 = join(hops(legs_3, "near"), swap_deep(grid, sums_2))
        (sums_3,) = fold([legs_3[0]] + moved_3, 1)
        sums_3 = swap_deep(grid, sums_3)
        share_reduce, share_expand, share_attend, share_last = [
            jnp.sum(x.astype(jnp.float32), 0) for x in (sums_0, sums_1, sums_2, sums_3)
        ]
    else:
        main, table, edge = small_grads
        table = table.reshape(devices, phone_wide, phones)
        table = jnp.pad(table, ((0, 0), (0, unit - phone_wide), (0, 0))).reshape(width, phones)
        small_grads = jnp.concatenate([main, table, edge], 1).astype(jnp.float32)
        share_last = dense(
            [(joined_turned, d_joined_in, 2 * unit, o) for o in offsets[:2]]
            + [(small_grads, None, 0, 0)]
        )

    shares = (share_last, share_attend, share_expand, share_reduce)
    local_square = sum((jnp.sum(g * g) for g in shares))
    totals = all_sum(grid, jnp.concatenate([speaker_hot * error_sum[0, 0], local_square[None]]))
    sums, total_square = totals[:SPK], totals[SPK]
    loss_value = jnp.mean(sums / jnp.maximum(counts, 1.0))
    grad_norm = jnp.sqrt(total_square)
    clip = jnp.minimum(1.0, 1.0 / (grad_norm + 1e-06))
    at = (phone_wide, phone_width, inputs, mel_bins)
    results = adam(clip[None], shares, masters, moments, squares, at)
    return (loss_value, grad_norm, *results)


def solution(mesh):
    grid = Grid(mesh)
    in_specs = (
        P(("wide", "narrow"), None),
        P(("wide", "narrow"), None),
        P(("wide", "narrow")),
        P(("wide", "narrow")),
        P(("wide", "narrow")),
        P(("wide", "narrow")),
        P(("wide", "narrow")),
        P(("wide", "narrow")),
        P(("wide", "narrow"), None),
        P(None, ("wide", "narrow")),
        P(None, ("wide", "narrow")),
        P(("wide", "narrow"), None),
        P(("wide", "narrow"), None),
        P(("wide", "narrow"), None),
        P(("wide", "narrow"), None),
        P(("wide", "narrow"), None),
        P(("wide", "narrow"), None),
        P(None, ("wide", "narrow")),
        P(None, ("wide", "narrow")),
        P(None, ("wide", "narrow")),
        P(("wide", "narrow"), None),
        P(("wide", "narrow"), None),
        P(("wide", "narrow"), None),
        P(("wide", "narrow"), None),
        P(("wide", "narrow"), None),
        P(("wide", "narrow"), None),
        P(None, ("wide", "narrow")),
        P(None, ("wide", "narrow")),
        P(None, ("wide", "narrow")),
        P(("wide", "narrow"), None),
        P(("wide", "narrow"), None),
        P(("wide", "narrow"), None),
        P(("wide", "narrow"), None),
        P(("wide", "narrow"), None),
        P(("wide", "narrow"), None),
        P(None, ("wide", "narrow")),
    )
    out_specs = (
        P(),
        P(),
        P(None, ("wide", "narrow")),
        P(None, ("wide", "narrow")),
        P(("wide", "narrow"), None),
        P(("wide", "narrow"), None),
        P(("wide", "narrow"), None),
        P(("wide", "narrow"), None),
        P(("wide", "narrow"), None),
        P(("wide", "narrow"), None),
        P(None, ("wide", "narrow")),
        P(None, ("wide", "narrow")),
        P(None, ("wide", "narrow")),
        P(("wide", "narrow"), None),
        P(("wide", "narrow"), None),
        P(("wide", "narrow"), None),
        P(("wide", "narrow"), None),
        P(("wide", "narrow"), None),
        P(("wide", "narrow"), None),
        P(None, ("wide", "narrow")),
        P(None, ("wide", "narrow")),
        P(None, ("wide", "narrow")),
        P(("wide", "narrow"), None),
        P(("wide", "narrow"), None),
        P(("wide", "narrow"), None),
        P(("wide", "narrow"), None),
        P(("wide", "narrow"), None),
        P(("wide", "narrow"), None),
        P(None, ("wide", "narrow")),
    )

    def body(*args):
        unit = args[11].shape[1] // grid.total
        return shards(grid, unit % 32 == 0, *args)

    return jax.shard_map(body, mesh=mesh, in_specs=in_specs, out_specs=out_specs, check_vma=False)
```

```python
from functools import partial
import math

import jax
import jax.numpy as jnp
from jax import lax
from jax.experimental import pallas as pl
from jax.experimental.pallas import tpu as pltpu
from jax.sharding import PartitionSpec as P

HD = 64
SPK = 16
STEP = 10


SIGMA = 1e-05
NORM_EPS = 1e-05
LEARN_RATE = 0.01
GAIN_RATE = 0.3
BETA_ONE = 0.5
BETA_TWO = 0.5
DECAY = 0.01
ADAM_EPS = 1e-08
FAR_AWAY = -1e30
VMEM = 64 * 1024 * 1024
TABLE_AT = 768
HEAD_AT = 896
BANDS = 32
HEADS_AT_ONCE = 8


def as_low(x):
    return x.astype(jnp.bfloat16)


def contract_rows(left, right):
    return lax.dot_general(
        left, right, (((0,), (0,)), ((), ())), preferred_element_type=jnp.float32
    )


def time_features(flow, width):
    half = width // 2
    freqs = jnp.exp(-math.log(10000.0) * jnp.arange(half, dtype=jnp.float32) / half)
    angle = 1000.0 * flow * freqs
    return jnp.concatenate([jnp.sin(angle), jnp.cos(angle)])


def normalize(x):
    centered = x - jnp.mean(x, -1, keepdims=True)
    inverse = lax.rsqrt(jnp.mean(centered * centered, -1, keepdims=True) + NORM_EPS)
    return (centered * inverse, inverse)


def normalize_back(grad, normed, inverse):
    return inverse * (
        grad
        - jnp.mean(grad, -1, keepdims=True)
        - normed * jnp.mean(grad * normed, -1, keepdims=True)
    )


def head_slopes(heads):
    return 2.0 ** (-8.0 * (jnp.arange(heads, dtype=jnp.float32) + 1.0) / heads)


def adam_step(master, grad, moment, square, rate):
    moment = BETA_ONE * moment + (1.0 - BETA_ONE) * grad
    square = BETA_TWO * square + (1.0 - BETA_TWO) * grad * grad
    moment_hat = moment / (1.0 - BETA_ONE**STEP)
    square_hat = square / (1.0 - BETA_TWO**STEP)
    master = master - rate * (moment_hat / (jnp.sqrt(square_hat) + ADAM_EPS) + DECAY * master)
    return (master, moment, square)


AXES = ("wide", "narrow")


def grid_sizes(wide, narrow):
    low = 1
    while (2 * low) * (2 * low) <= wide:
        low *= 2
    return (wide // low, low, narrow // 2, 2)


class Grid:
    def __init__(self, mesh):
        self.sizes = grid_sizes(mesh.shape["wide"], mesh.shape["narrow"])
        self.total = mesh.shape["wide"] * mesh.shape["narrow"]

    def coords(self, index):
        out = []
        for size in reversed(self.sizes):
            out.append(index % size)
            index = index // size
        return out[::-1]

    def index(self, coords):
        index = 0
        for size, value in zip(self.sizes, coords):
            index = index * size + value
        return index

    def mixed(self):
        return self.sizes[1] == self.sizes[2]

    def axis(self, role, core):
        if role == "z":
            return 0
        if role == "core":
            return 3
        if self.mixed():
            return (2, 1)[core] if role == "far" else (1, 2)[core]
        return 2 if role == "far" else 1

    def size(self, role):
        return self.sizes[self.axis(role, 0)]

    def pairs(self, role, step):
        out = []
        for source in range(self.total):
            coords = self.coords(source)
            axis = self.axis(role, coords[3])
            coords[axis] = (coords[axis] + step) % self.sizes[axis]
            out.append((source, self.index(coords)))
        return out

    def lines(self):
        deep = self.total // self.sizes[0]
        return [[z * deep + rest for z in range(self.sizes[0])] for rest in range(deep)]

    def owners(self, core_step, direction, deep_first=False):
        me = self.coords(lax.axis_index(AXES))
        core = (me[3] + core_step) % 2
        far, near, deep = (self.size(r) for r in ("far", "near", "z"))
        f, n, z = jnp.meshgrid(jnp.arange(far), jnp.arange(near), jnp.arange(deep), indexing="ij")
        if deep_first:
            f, n, z = (t.swapaxes(1, 2) for t in (f, n, z))
        if self.mixed():
            y = jnp.where(core == 0, me[1] + direction * n, me[1] + direction * f) % self.sizes[1]
            x = jnp.where(core == 0, me[2] + direction * f, me[2] + direction * n) % self.sizes[2]
        else:
            y = (me[1] + direction * n) % self.sizes[1]
            x = (me[2] + direction * f) % self.sizes[2]
        return self.index((z, y, x, core)).reshape(-1).astype(jnp.int32)


def shift(grid, x, role, step):
    return lax.ppermute(x, AXES, grid.pairs(role, step))


def tied(x, *others):
    return lax.optimization_barrier((x,) + others)[0]


def swap_deep(grid, x):
    return lax.all_to_all(x, AXES, 0, 0, axis_index_groups=grid.lines())


def join(*xs):
    return lax.optimization_barrier(xs)


def spread(grid, x, role):
    return [x] + [shift(grid, x, role, step) for step in range(1, grid.size(role))]


def all_sum(grid, x):
    return jnp.sum(lax.all_to_all(jnp.broadcast_to(x[None], (grid.total,) + x.shape), AXES, 0, 0), 0)


def dot_nn(a, b):
    return lax.dot_general(a, b, (((1,), (0,)), ((), ())), preferred_element_type=jnp.float32)


def dot_nt(a, b):
    return lax.dot_general(a, b, (((1,), (1,)), ((), ())), preferred_element_type=jnp.float32)


def dot_tn(a, b):
    return lax.dot_general(a, b, (((0,), (0,)), ((), ())), preferred_element_type=jnp.float32)


def params():
    return pltpu.CompilerParams(vmem_limit_bytes=VMEM)


def key_bias(length, frames):
    key = lax.broadcasted_iota(jnp.int32, (frames, frames), 0)
    query = lax.broadcasted_iota(jnp.int32, (frames, frames), 1)
    dist = -jnp.abs(key - query).astype(jnp.float32)
    return jnp.where(key < length, dist, FAR_AWAY)


def attend_kernel(length_ref, slope_ref, packed_ref, mixed_ref, lse_ref, bias_ref):
    step = pl.program_id(0)
    q_ref, k_ref, v_ref = (packed_ref.at[j] for j in range(3))
    frames, lanes_here = mixed_ref.shape
    here = lanes_here // HD

    @pl.when(step == 0)
    def _():
        bias_ref[...] = key_bias(length_ref[0], frames)

    parts = []
    for h in range(here):
        lanes = slice(h * HD, (h + 1) * HD)
        scores = dot_nt(k_ref[:, lanes], q_ref[:, lanes] * jnp.bfloat16(HD**-0.5))
        scores = scores + slope_ref[here * step + h] * bias_ref[...]
        top = jnp.max(scores, 0, keepdims=True)
        expo = jnp.exp(scores - top)
        total = jnp.sum(expo, 0, keepdims=True)
        lse_ref[0, h : h + 1] = top + jnp.log(total)
        probs = as_low(expo * (1.0 / total))
        parts.append(dot_tn(v_ref[:, lanes], probs))
    mixed_ref[...] = as_low(jnp.concatenate(parts, 0).T)


def attend(length, slopes, packed):
    _, frames, width = packed.shape
    steps = width // (HEADS_AT_ONCE * HD)
    block = pl.BlockSpec((frames, HEADS_AT_ONCE * HD), lambda i: (0, i))
    return pl.pallas_call(
        attend_kernel,
        grid=(steps,),
        in_specs=[pl.BlockSpec(memory_space=pltpu.SMEM)] * 2
        + [pl.BlockSpec((3, frames, HEADS_AT_ONCE * HD), lambda i: (0, 0, i))],
        out_specs=[block, pl.BlockSpec((1, HEADS_AT_ONCE, frames), lambda i: (i, 0, 0))],
        out_shape=[
            jax.ShapeDtypeStruct((frames, width), jnp.bfloat16),
            jax.ShapeDtypeStruct((steps, HEADS_AT_ONCE, frames), jnp.float32),
        ],
        scratch_shapes=[pltpu.VMEM((frames, frames), jnp.float32)],
        compiler_params=params(),
        name="attend",
    )(length, slopes, packed)


def attend_back_kernel(
    length_ref, slope_ref, packed_ref, d_out_ref, w_ref, lse_ref, dq_ref, dk_ref, dv_ref, bias_ref
):
    step = pl.program_id(0)
    q_ref, k_ref, v_ref = (packed_ref.at[j] for j in range(3))
    frames, lanes_here = dq_ref.shape
    here = lanes_here // HD

    @pl.when(step == 0)
    def _():
        bias_ref[...] = key_bias(length_ref[0], frames)

    d_mixed_here = as_low(dot_nt(d_out_ref[...], w_ref[...]))
    d_query, d_keys, d_values = [], [], []
    for h in range(here):
        lanes = slice(h * HD, (h + 1) * HD)
        query = q_ref[:, lanes] * jnp.bfloat16(HD**-0.5)
        keys, values, d_mixed = k_ref[:, lanes], v_ref[:, lanes], d_mixed_here[:, lanes]
        scores = dot_nt(keys, query) + slope_ref[here * step + h] * bias_ref[...]
        probs = jnp.exp(scores - lse_ref[0, h : h + 1])
        d_probs = dot_nt(values, d_mixed)
        row_dot = jnp.sum(d_probs * probs, 0, keepdims=True)
        d_scores = as_low(probs * (d_probs - row_dot))
        d_values.append(dot_nn(as_low(probs), d_mixed))
        d_keys.append(dot_nn(d_scores, query))
        d_query.append(dot_tn(keys, d_scores))
    dq_ref[...] = as_low((jnp.concatenate(d_query, 0) * HD**-0.5).T)
    dk_ref[...] = as_low(jnp.concatenate(d_keys, 1))
    dv_ref[...] = as_low(jnp.concatenate(d_values, 1))


def attend_back(length, slopes, packed, d_out, w, lse):
    _, frames, width = packed.shape
    wide = HEADS_AT_ONCE * HD
    block = pl.BlockSpec((frames, wide), lambda i: (0, i))
    return pl.pallas_call(
        attend_back_kernel,
        grid=(width // wide,),
        in_specs=[pl.BlockSpec(memory_space=pltpu.SMEM)] * 2
        + [
            pl.BlockSpec((3, frames, wide), lambda i: (0, 0, i)),
            pl.BlockSpec((frames, width), lambda i: (0, 0)),
            pl.BlockSpec((wide, width), lambda i: (i, 0)),
            pl.BlockSpec((1, HEADS_AT_ONCE, frames), lambda i: (i, 0, 0)),
        ],
        out_specs=[block] * 3,
        out_shape=[jax.ShapeDtypeStruct((frames, width), jnp.bfloat16)] * 3,
        scratch_shapes=[pltpu.VMEM((frames, frames), jnp.float32)],
        compiler_params=params(),
        name="attend_back",
    )(length, slopes, packed, d_out, w, lse)


def gelu_both(x):
    z = jnp.abs(x) * (0.5**0.5)
    bell = jnp.exp(-z * z)
    t = 1.0 / (1.0 + 0.3275911 * z)
    poly = t * (0.254829592 + t * (-0.284496736 + t * (1.421413741 + t * (-1.453152027 + t * 1.061405429))))
    tail = 0.5 * poly * bell
    share = jnp.where(x >= 0, 1.0 - tail, tail)
    return x * share, share + x * bell * (0.5 / math.pi) ** 0.5


def expand_kernel(count, blocks, own_ref, other_ref, *refs):
    sources = refs[:count]
    x_ref, w_out, act_ref, turned_ref, slope_ref, w_ref, sems, out_sems = refs[count:]
    step = pl.program_id(0)
    width = x_ref.shape[1]
    unit = width // sum(source.shape[0] for source in sources)

    def copies(j):
        entry = (w_ref.at[j], (j + 1) * unit, unit, None, sems.at[j])
        return landing((own_ref, other_ref), sources, [entry])

    def kept(j):
        return pltpu.make_async_copy(w_ref.at[j], w_out.at[j], out_sems.at[j])

    def chunk(j):
        if j == 0:
            for n in range(blocks):
                begin(copies(n))
        finish(copies(j))
        kept(j).start()
        hidden = dot_nn(x_ref[...], w_ref[j])
        act, slope = gelu_both(hidden)
        act = as_low(act)
        act_ref[...] = act
        turned_ref[...] = act.T
        slope_ref[...] = as_low(slope)
        if j == blocks - 1:
            for n in range(blocks):
                kept(n).wait()

    for j in range(blocks):
        pl.when(step == j)(partial(chunk, j))


def expand(own, other, pieces, x, blocks):
    frames, width = x.shape
    total = blocks * width
    return pl.pallas_call(
        partial(expand_kernel, len(pieces), blocks),
        grid=(blocks,),
        in_specs=piece_specs(pieces) + [pl.BlockSpec((frames, width), lambda i: (0, 0))],
        out_specs=[
            pl.BlockSpec(memory_space=pl.ANY),
            pl.BlockSpec((frames, width), lambda i: (0, i)),
            pl.BlockSpec((width, frames), lambda i: (i, 0)),
            pl.BlockSpec((frames, width), lambda i: (0, i)),
        ],
        out_shape=[
            jax.ShapeDtypeStruct((blocks, width, width), jnp.bfloat16),
            jax.ShapeDtypeStruct((frames, total), jnp.bfloat16),
            jax.ShapeDtypeStruct((total, frames), jnp.bfloat16),
            jax.ShapeDtypeStruct((frames, total), jnp.bfloat16),
        ],
        scratch_shapes=[
            pltpu.VMEM((blocks, width, width), jnp.bfloat16),
            pltpu.SemaphoreType.DMA((blocks,)),
            pltpu.SemaphoreType.DMA((blocks,)),
        ],
        compiler_params=params(),
        name="expand",
    )(own, other, *pieces, x)


def landing(idx_refs, sources, entries):
    half = len(sources) // 2
    copies = []
    for s, source in enumerate(sources):
        idx_ref = idx_refs[s // half]
        count = source.shape[0]
        for i in range(count):
            band = idx_ref[(s % half) * count + i]
            for goal, start, rows, lane, sem in entries:
                part = source.at[i, pl.ds(start, rows)]
                if lane is not None:
                    part = source.at[i, pl.ds(start, rows), pl.ds(lane, goal.shape[-1])]
                place = goal.at[pl.ds(pl.multiple_of(band * rows, rows), rows)]
                copies.append(pltpu.make_async_copy(part, place, sem(band) if callable(sem) else sem))
    return copies


def begin(copies):
    for copy in copies:
        copy.start()


def finish(copies):
    for copy in copies:
        copy.wait()


def piece_specs(pieces):
    smem = pl.BlockSpec(memory_space=pltpu.SMEM)
    return [smem, smem] + [pl.BlockSpec(memory_space=pl.ANY)] * len(pieces)


def gain_row(edge_ref, at):
    return edge_ref[at : at + 1].astype(jnp.float32)


def front_kernel(
    at_gain, at_count, spacing, count, phone_rows, speaker_ref, own_ref, other_ref, *refs
):
    sources = refs[:count]
    states_ref, states_turned_ref, hot_ref, mel_ref, time_ref = refs[count : count + 5]
    (
        small_out, skip_out, embed_ref, stream_ref, joined_ref, normed_ref, turned_ref, edge_ref, share_ref,
        small_ref, skip_ref, table_ref, sems, out_sems,
    ) = refs[count + 5 :]
    width = stream_ref.shape[1]
    bands = sum(source.shape[0] for source in sources)
    unit = width // bands
    idx = (own_ref, other_ref)
    first = landing(
        idx, sources,
        [(small_ref, 0, unit, None, sems.at[0]), (table_ref, 0, phone_rows, TABLE_AT, sems.at[0])],
    )
    second = landing(idx, sources, [(skip_ref, unit, 2 * unit, None, sems.at[1])])
    begin(first)
    begin(second)
    phones = embed_ref.shape[1]
    joined_ref[width:] = states_turned_ref[...]
    finish(first)
    small_copy = pltpu.make_async_copy(small_ref, small_out, out_sems.at[0])
    small_copy.start()
    edge_ref[...] = small_ref[:, HEAD_AT:].T
    facts = edge_ref[at_count - HEAD_AT : at_count - HEAD_AT + 3].astype(jnp.float32)
    lane = lax.broadcasted_iota(jnp.int32, (1, width), 1)
    hit = (facts[:1] == speaker_ref[0].astype(jnp.float32)) & (lax.rem(lane, spacing) == 0)
    masked = jnp.sum(jnp.where(hit, 16.0 * facts[1:2] + facts[2:3], 0.0), 1, keepdims=True)
    share_ref[...] = (1.0 / SPK) / jnp.maximum(masked, 1.0)
    embedded = as_low(dot_nt(hot_ref[...], table_ref[...]))
    embed_ref[...] = embedded
    start = dot_nt(embedded, small_ref[:, :phones])
    start = start + dot_nt(mel_ref[...], small_ref[:, phones:TABLE_AT]) + time_ref[...]
    start = as_low(start)
    joined_ref[:width] = start.T
    finish(second)
    skip_copy = pltpu.make_async_copy(skip_ref, skip_out, out_sems.at[1])
    skip_copy.start()
    stream = dot_nn(start, skip_ref[:width]) + dot_nn(states_ref[...], skip_ref[width:])
    stream_ref[...] = stream
    normed = as_low(normalize(stream)[0] * gain_row(edge_ref, at_gain))
    normed_ref[...] = normed
    turned_ref[...] = normed.T
    small_copy.wait()
    skip_copy.wait()


def front(speaker, own, other, pieces, states, states_turned, hot, mel, time, phones, at_gain, at_count, spacing):
    frames, width = states.shape
    f32, low = jnp.float32, jnp.bfloat16
    bands = sum(p.shape[0] for p in pieces)
    vmem, anywhere = pl.BlockSpec(memory_space=pltpu.VMEM), pl.BlockSpec(memory_space=pl.ANY)
    return pl.pallas_call(
        partial(front_kernel, at_gain, at_count, spacing, len(pieces), phones // bands),
        in_specs=[pl.BlockSpec(memory_space=pltpu.SMEM)] + piece_specs(pieces) + [vmem] * 5,
        out_specs=[anywhere] * 2 + [vmem] * 7,
        out_shape=[
            jax.ShapeDtypeStruct((width, width), low),
            jax.ShapeDtypeStruct((2 * width, width), low),
            jax.ShapeDtypeStruct((frames, phones), low),
            jax.ShapeDtypeStruct((frames, width), f32),
            jax.ShapeDtypeStruct((2 * width, frames), low),
            jax.ShapeDtypeStruct((frames, width), low),
            jax.ShapeDtypeStruct((width, frames), low),
            jax.ShapeDtypeStruct((width - HEAD_AT, width), low),
            jax.ShapeDtypeStruct((1, 1), f32),
        ],
        scratch_shapes=[
            pltpu.VMEM((width, width), low),
            pltpu.VMEM((2 * width, width), low),
            pltpu.VMEM((phones, hot.shape[1]), low),
            pltpu.SemaphoreType.DMA((2,)),
            pltpu.SemaphoreType.DMA((2,)),
        ],
        compiler_params=params(),
        name="front",
    )(speaker, own, other, *pieces, states, states_turned, hot, mel, time)


def pack_kernel(count, blocks, own_ref, other_ref, *refs):
    sources = refs[:count]
    x_ref, w_out, out_ref, w_ref, sems, out_sems = refs[count:]
    step = pl.program_id(0)
    width = x_ref.shape[1]
    unit = width // sum(source.shape[0] for source in sources)

    def copies(j):
        entry = (w_ref.at[j], (3 + j) * unit, unit, None, sems.at[j])
        return landing((own_ref, other_ref), sources, [entry])

    def kept(j):
        return pltpu.make_async_copy(w_ref.at[j], w_out.at[j], out_sems.at[j])

    def chunk(j):
        if j == 0:
            for n in range(blocks):
                begin(copies(n))
        finish(copies(j))
        kept(j).start()
        out_ref[0] = as_low(dot_nn(x_ref[...], w_ref[j]))
        if j == blocks - 1:
            for n in range(blocks):
                kept(n).wait()

    for j in range(blocks):
        pl.when(step == j)(partial(chunk, j))


def pack(own, other, pieces, x, blocks):
    frames, width = x.shape
    return pl.pallas_call(
        partial(pack_kernel, len(pieces), blocks),
        grid=(blocks,),
        in_specs=piece_specs(pieces) + [pl.BlockSpec((frames, width), lambda i: (0, 0))],
        out_specs=[
            pl.BlockSpec(memory_space=pl.ANY),
            pl.BlockSpec((1, frames, width), lambda i: (i, 0, 0)),
        ],
        out_shape=[
            jax.ShapeDtypeStruct((blocks, width, width), jnp.bfloat16),
            jax.ShapeDtypeStruct((blocks, frames, width), jnp.bfloat16),
        ],
        scratch_shapes=[
            pltpu.VMEM((blocks, width, width), jnp.bfloat16),
            pltpu.SemaphoreType.DMA((blocks,)),
            pltpu.SemaphoreType.DMA((blocks,)),
        ],
        compiler_params=params(),
        name="pack",
    )(own, other, *pieces, x)


def mid_kernel(at_gain, count, own_ref, other_ref, *refs):
    sources = refs[:count]
    (
        mixed_ref, stream_ref, edge_ref, w_out, mid_ref, in_ref, turned_ref, mixed_turned_ref,
        w_ref, sem, out_sem,
    ) = refs[count:]
    width = stream_ref.shape[1]
    unit = width // sum(source.shape[0] for source in sources)
    copies = landing((own_ref, other_ref), sources, [(w_ref, 0, unit, None, sem)])
    begin(copies)
    mixed = mixed_ref[...]
    mixed_turned_ref[...] = mixed.T
    finish(copies)
    kept = pltpu.make_async_copy(w_ref, w_out, out_sem)
    kept.start()
    mid = stream_ref[...] + dot_nn(mixed, w_ref[...])
    mid_ref[...] = mid
    normed = as_low(normalize(mid)[0] * gain_row(edge_ref, at_gain))
    in_ref[...] = normed
    turned_ref[...] = normed.T
    kept.wait()


def mid_step(own, other, pieces, mixed, stream, edge, at_gain):
    frames, width = stream.shape
    low = jnp.bfloat16
    vmem = pl.BlockSpec(memory_space=pltpu.VMEM)
    return pl.pallas_call(
        partial(mid_kernel, at_gain, len(pieces)),
        in_specs=piece_specs(pieces) + [vmem] * 3,
        out_specs=[pl.BlockSpec(memory_space=pl.ANY)] + [vmem] * 4,
        out_shape=[
            jax.ShapeDtypeStruct((width, width), low),
            jax.ShapeDtypeStruct((frames, width), jnp.float32),
            jax.ShapeDtypeStruct((frames, width), low),
            jax.ShapeDtypeStruct((width, frames), low),
            jax.ShapeDtypeStruct((width, frames), low),
        ],
        scratch_shapes=[
            pltpu.VMEM((width, width), low),
            pltpu.SemaphoreType.DMA,
            pltpu.SemaphoreType.DMA,
        ],
        compiler_params=params(),
        name="mid",
    )(own, other, *pieces, mixed, stream, edge)


def head_kernel(at_gain, count, share_ref, own_ref, other_ref, *refs):
    sources = refs[:count]
    (
        act_ref, mid_ref, edge_ref, target_ref, inside_ref,
        w_out, d_ref, low_ref, grad_ref, gain_grad_ref, error_ref,
        total_ref, w_ref, sem, out_sem,
    ) = refs[count:]
    step = pl.program_id(0)
    tile = act_ref.shape[1]
    rows = w_ref.shape[0] // sum(source.shape[0] for source in sources)
    kept = pltpu.make_async_copy(w_ref, w_out, out_sem)
    each = tile // rows

    @pl.when(step == 0)
    def _():
        by_step = lambda band: sem.at[lax.div(band, each)]
        begin(landing((own_ref, other_ref), sources, [(w_ref, 0, rows, None, by_step)]))

    for _ in range(each):
        pltpu.make_async_copy(sources[0].at[0, pl.ds(0, rows)], w_ref.at[pl.ds(0, rows)], sem.at[step]).wait()

    @pl.when(step == pl.num_programs(0) - 1)
    def _():
        kept.start()

    part = dot_nn(act_ref[...], w_ref[pl.ds(pl.multiple_of(step * tile, tile), tile)])

    @pl.when(step == 0)
    def _():
        total_ref[...] = mid_ref[...] + part

    @pl.when(step > 0)
    def _():
        total_ref[...] += part

    @pl.when(step == pl.num_programs(0) - 1)
    def _():
        bins = target_ref.shape[1]
        normed, inverse = normalize(total_ref[...])
        gain = gain_row(edge_ref, at_gain)
        head_in = as_low(normed * gain)
        head = edge_ref[:bins]
        inside = inside_ref[...]
        error = dot_nt(head_in, head) - target_ref[...]
        error_ref[...] = jnp.sum(jnp.sum(error * error, 1, keepdims=True) * inside, 0, keepdims=True)
        d_prediction = as_low((2.0 * share_ref[...]) * error * inside)
        grad_ref[...] = dot_tn(head_in, d_prediction)
        d_head_in = dot_nn(d_prediction, head)
        gain_grad_ref[...] = jnp.sum(d_head_in * normed, 0, keepdims=True)
        d_stream = normalize_back(d_head_in * gain, normed, inverse)
        d_ref[...] = d_stream
        low_ref[...] = as_low(d_stream)
        kept.wait()


def head_step(share, own, other, pieces, act, mid, edge, target, inside, at_gain, tile=1024):
    frames, width = mid.shape
    bins = target.shape[1]
    total = act.shape[1]
    whole = lambda *shape: pl.BlockSpec(shape, lambda i: (0,) * len(shape))
    return pl.pallas_call(
        partial(head_kernel, at_gain, len(pieces)),
        grid=(total // tile,),
        in_specs=[whole(1, 1)]
        + piece_specs(pieces)
        + [
            pl.BlockSpec((frames, tile), lambda i: (0, i)),
            whole(frames, width), whole(*edge.shape), whole(frames, bins), whole(frames, 1),
        ],
        out_specs=[
            pl.BlockSpec(memory_space=pl.ANY),
            whole(frames, width), whole(frames, width), whole(width, bins), whole(1, width), whole(1, 1),
        ],
        out_shape=[
            jax.ShapeDtypeStruct((total, width), jnp.bfloat16),
            jax.ShapeDtypeStruct((frames, width), jnp.float32),
            jax.ShapeDtypeStruct((frames, width), jnp.bfloat16),
            jax.ShapeDtypeStruct((width, bins), jnp.float32),
            jax.ShapeDtypeStruct((1, width), jnp.float32),
            jax.ShapeDtypeStruct((1, 1), jnp.float32),
        ],
        scratch_shapes=[
            pltpu.VMEM((frames, width), jnp.float32),
            pltpu.VMEM((total, width), jnp.bfloat16),
            pltpu.SemaphoreType.DMA((total // tile,)),
            pltpu.SemaphoreType.DMA,
        ],
        compiler_params=params(),
        name="head",
    )(share, own, other, *pieces, act, mid, edge, target, inside)


def ffn_back_kernel(
    at_gain, low_ref, d_ref, down_ref, slope_ref, up_ref, mid_ref, edge_ref,
    out_ref, out_low_ref, gain_grad_ref, *refs,
):
    hidden_refs, total_ref = refs[:-1], refs[-1]
    step = pl.program_id(0)
    d_hidden = as_low(dot_nt(low_ref[...], down_ref[...]) * slope_ref[...].astype(jnp.float32))
    for j, ref in enumerate(hidden_refs):

        @pl.when(step == j)
        def _(ref=ref):
            ref[...] = d_hidden

    part = dot_nt(d_hidden, up_ref[0])

    @pl.when(step == 0)
    def _():
        total_ref[...] = part

    @pl.when(step > 0)
    def _():
        total_ref[...] += part

    @pl.when(step == pl.num_programs(0) - 1)
    def _():
        normed, inverse = normalize(mid_ref[...])
        grad = total_ref[...]
        gain_grad_ref[...] = jnp.sum(grad * normed, 0, keepdims=True)
        out = d_ref[...] + normalize_back(grad * gain_row(edge_ref, at_gain), normed, inverse)
        out_ref[...] = out
        out_low_ref[...] = as_low(out)


def ffn_back(low, d, down, slope, up, mid, edge, at_gain):
    frames, width = mid.shape
    count = up.shape[0]
    whole = lambda *shape: pl.BlockSpec(shape, lambda i: (0,) * len(shape))
    return pl.pallas_call(
        partial(ffn_back_kernel, at_gain),
        grid=(count,),
        in_specs=[
            whole(frames, width), whole(frames, width),
            pl.BlockSpec((width, width), lambda i: (i, 0)),
            pl.BlockSpec((frames, width), lambda i: (0, i)),
            pl.BlockSpec((1, width, width), lambda i: (i, 0, 0)),
            whole(frames, width), whole(*edge.shape),
        ],
        out_specs=[whole(frames, width), whole(frames, width), whole(1, width)]
        + [whole(frames, width)] * count,
        out_shape=[
            jax.ShapeDtypeStruct((frames, width), jnp.float32),
            jax.ShapeDtypeStruct((frames, width), jnp.bfloat16),
            jax.ShapeDtypeStruct((1, width), jnp.float32),
        ]
        + [jax.ShapeDtypeStruct((frames, width), jnp.bfloat16)] * count,
        scratch_shapes=[pltpu.VMEM((frames, width), jnp.float32)],
        compiler_params=params(),
        name="ffn_back",
    )(low, d, down, slope, up, mid, edge)


def pack_back_kernel(at_gain, blocks, *refs):
    w_ref, d_ref, stream_ref, edge_ref, low_ref, gain_grad_ref, total_ref = refs[blocks:]
    step = pl.program_id(0)

    def chunk(j):
        part = dot_nt(refs[j][...], w_ref[0])
        total_ref[...] = part if j == 0 else total_ref[...] + part

    for j in range(blocks):
        pl.when(step == j)(partial(chunk, j))

    @pl.when(step == pl.num_programs(0) - 1)
    def _():
        grad = total_ref[...]
        normed, inverse = normalize(stream_ref[...])
        gain_grad_ref[...] = jnp.sum(grad * normed, 0, keepdims=True)
        gain = gain_row(edge_ref, at_gain)
        low_ref[...] = as_low(d_ref[...] + normalize_back(grad * gain, normed, inverse))


def pack_back(packed, w, d, stream, edge, at_gain):
    frames, width = stream.shape
    whole = lambda *shape: pl.BlockSpec(shape, lambda i: (0,) * len(shape))
    return pl.pallas_call(
        partial(pack_back_kernel, at_gain, w.shape[0]),
        grid=(w.shape[0],),
        in_specs=[whole(frames, width)] * w.shape[0]
        + [
            pl.BlockSpec((1, width, width), lambda i: (i, 0, 0)),
            whole(frames, width), whole(frames, width), whole(*edge.shape),
        ],
        out_specs=[whole(frames, width), whole(1, width)],
        out_shape=[
            jax.ShapeDtypeStruct((frames, width), jnp.bfloat16),
            jax.ShapeDtypeStruct((1, width), jnp.float32),
        ],
        scratch_shapes=[pltpu.VMEM((frames, width), jnp.float32)],
        compiler_params=params(),
        name="pack_back",
    )(*packed, w, d, stream, edge)


def tail_kernel(
    at_gain, d_ref, skip_ref, small_ref, embed_ref, mel_ref, hot_ref, head_ref, one_ref, two_ref, three_ref,
    main_ref, table_ref, edge_ref,
):
    phones = embed_ref.shape[1]
    d_start = as_low(dot_nt(d_ref[...], skip_ref[...]))
    d_phones = as_low(dot_nn(d_start, small_ref[:, :phones]))
    main_ref[:, :phones] = as_low(dot_tn(d_start, embed_ref[...]))
    main_ref[:, phones:] = as_low(dot_tn(d_start, mel_ref[...]))
    table_ref[...] = as_low(dot_tn(d_phones, hot_ref[...]))
    edge = head_ref[...]
    lanes = edge.shape[1]
    edge = jnp.pad(edge, ((0, 0), (0, edge_ref.shape[1] - lanes)))
    lane = lax.broadcasted_iota(jnp.int32, edge.shape, 1)
    for j, ref in enumerate((one_ref, two_ref, three_ref)):
        column = jnp.broadcast_to(ref[...], (8, edge.shape[0])).T[:, :1]
        edge = jnp.where(lane == at_gain + j, column, edge)
    edge_ref[...] = as_low(edge)


def tail(d, skip, small, embed, mel, hot, head, gains, at_gain):
    width = d.shape[1]
    phones = embed.shape[1]
    whole = lambda x: pl.BlockSpec(x.shape, lambda i: (0, 0))
    arrays = (small, embed, mel, hot, head, *gains)
    shapes = [(width, TABLE_AT), (phones, hot.shape[1]), (width, width - HEAD_AT)]
    return pl.pallas_call(
        partial(tail_kernel, at_gain),
        grid=(1,),
        in_specs=[whole(d), pl.BlockSpec((width, width), lambda i: (0, 0))] + [whole(x) for x in arrays],
        out_specs=[pl.BlockSpec(s, lambda i: (0, 0)) for s in shapes],
        out_shape=[jax.ShapeDtypeStruct(s, jnp.bfloat16) for s in shapes],
        compiler_params=params(),
        name="tail",
    )(d, skip, *arrays)


def grads_kernel(plan, count, rows, legs, came_too, idx_ref, *refs):
    refs, picked_ref, right_ref, sems = refs[:-3], refs[-3], refs[-2], refs[-1]
    frames = right_ref.shape[1] // 2
    outs = refs[len(refs) - legs :]
    came_ref = refs[len(refs) - legs - 1] if came_too else None
    step = pl.program_id(0)
    each = count // legs

    def copies(c):
        lefts, rights, stride, offset = plan[c]
        if rights is None:
            return []
        slot = c % 2
        return [
            pltpu.make_async_copy(
                refs[left].at[pl.ds(pl.multiple_of(idx_ref[i] * stride + offset, rows), rows)],
                picked_ref.at[slot, pl.ds(i * rows, rows), pl.ds(side * frames, frames)],
                sems.at[slot],
            )
            for side, left in enumerate(lefts)
            for i in range(count)
        ] + [
            pltpu.make_async_copy(refs[right], right_ref.at[slot, pl.ds(side * frames, frames)], sems.at[slot])
            for side, right in enumerate(rights)
        ]

    def chunk(c):
        lefts, rights, _, _ = plan[c]
        if c == 0:
            for copy in copies(0):
                copy.start()
        if c + 1 < len(plan):
            for copy in copies(c + 1):
                copy.start()
        for copy in copies(c):
            copy.wait()
        if rights is None:
            main, table, edge = (refs[r] for r in lefts)
            thick = table.shape[0] // (main.shape[0] // rows)
            blocks = []
            for i in range(count):
                start = pl.multiple_of(idx_ref[i] * rows, rows)
                short = pl.multiple_of(idx_ref[i] * thick, thick)
                lead = table[pl.ds(short, thick)]
                rest = jnp.zeros((rows - thick, lead.shape[1]), lead.dtype)
                middle = jnp.concatenate([lead, rest], 0) if thick < rows else lead
                block = [main[pl.ds(start, rows)], middle, edge[pl.ds(start, rows)]]
                blocks.append(jnp.concatenate(block, 1).astype(jnp.float32))
            total = jnp.stack(blocks)
            if came_too:
                total = total + came_ref[...].astype(jnp.float32)
        else:
            wide = outs[0].shape[2]
            total = dot_nn(picked_ref[c % 2], right_ref[c % 2])
            total = total.reshape(count, rows, wide)
        for f in range(legs):
            outs[f][...] = as_low(total[f * each : (f + 1) * each])

    for c in range(len(plan)):
        pl.when(step == c)(partial(chunk, c))


def grads(plan, arrays, idx, frames, rows, width, legs, came=None):
    count = idx.shape[0]
    copied = [j for entry in plan if entry[1] is not None for j in entry[0] + entry[1]]

    def spec(j, x):
        if j in copied:
            return pl.BlockSpec(memory_space=pltpu.HBM)
        return pl.BlockSpec(x.shape, lambda i, n=len(x.shape): (0,) * n)

    specs = [spec(j, x) for j, x in enumerate(arrays)]
    if came is not None:
        specs.append(pl.BlockSpec((count, rows, width), lambda i: (0, 0, 0)))
        arrays = list(arrays) + [came]
    return pl.pallas_call(
        partial(grads_kernel, plan, count, rows, legs, came is not None),
        grid=(len(plan),),
        in_specs=[pl.BlockSpec(memory_space=pltpu.SMEM)] + specs,
        out_specs=[pl.BlockSpec((count // legs, rows, width), lambda i: (0, i, 0))] * legs,
        out_shape=[jax.ShapeDtypeStruct((count // legs, rows * len(plan), width), jnp.bfloat16)] * legs,
        scratch_shapes=[
            pltpu.VMEM((2, count * rows, 2 * frames), jnp.bfloat16),
            pltpu.VMEM((2, 2 * frames, width), jnp.bfloat16),
            pltpu.SemaphoreType.DMA((2,)),
        ],
        compiler_params=params(),
        name="grads",
    )(idx, *arrays)


def fold_kernel(legs, *refs):
    ins, outs = refs[:-legs], refs[-legs:]
    took = len(ins) // legs
    for j in range(legs):
        total = ins[j * took][...].astype(jnp.float32)
        for ref in ins[j * took + 1 : (j + 1) * took]:
            total = total + ref[...].astype(jnp.float32)
        outs[j][...] = as_low(total)


def fold(parts, legs):
    count, rows, width = parts[0].shape
    each = count // legs
    tile = rows // 2
    return pl.pallas_call(
        partial(fold_kernel, legs),
        grid=(rows // tile,),
        in_specs=[
            pl.BlockSpec((each, tile, width), lambda i, j=j: (j, i, 0)) for j in range(legs) for _ in parts
        ],
        out_specs=[pl.BlockSpec((each, tile, width), lambda i: (0, i, 0))] * legs,
        out_shape=[jax.ShapeDtypeStruct((each, rows, width), jnp.bfloat16)] * legs,
        compiler_params=params(),
        name="fold",
    )(*[p for _ in range(legs) for p in parts])


def stack_kernel(*refs):
    ins, out, sem = refs[:-2], refs[-2], refs[-1]
    copies = [
        pltpu.make_async_copy(ref, out.at[n, i], sem) for n in range(out.shape[0]) for i, ref in enumerate(ins)
    ]
    for copy in copies:
        copy.start()
    for copy in copies:
        copy.wait()


def stack(parts, times):
    return pl.pallas_call(
        stack_kernel,
        in_specs=[pl.BlockSpec(memory_space=pl.ANY)] * len(parts),
        out_specs=pl.BlockSpec(memory_space=pltpu.VMEM),
        out_shape=jax.ShapeDtypeStruct((times, len(parts)) + parts[0].shape, parts[0].dtype),
        scratch_shapes=[pltpu.SemaphoreType.DMA],
        compiler_params=params(),
        name="stack",
    )(*parts)


def update(grad, rate, master_ref, moment_ref, square_ref, clip):
    return adam_step(master_ref[...], grad * clip, moment_ref[...], square_ref[...], rate)


def adam_kernel(at, clip_ref, *refs):
    phone_rows, phone_width, inputs, at_gain = at
    last, attend, expand, reduce = refs[:4]
    masters, moments, squares = refs[4:13], refs[13:22], refs[22:31]
    outs = refs[31:]
    unit = last.shape[0] // 3
    small = last[2 * unit :]
    clip = clip_ref[0]
    mel_lanes = inputs - phone_width
    lanes = [small[:, phone_width : phone_width + mel_lanes], small[:, :phone_width]]
    edge = small[:, HEAD_AT:]
    turned_edge = edge.T
    bins = masters[7].shape[1]

    def columns(ref, first):
        blocks = [ref[j : j + unit] for j in range(first, ref.shape[0], unit)]
        return jnp.concatenate(blocks, 1)

    grads_of = [
        jnp.concatenate(lanes, 1),
        small[:phone_rows, TABLE_AT:HEAD_AT],
        last[: 2 * unit],
        columns(attend, unit),
        attend[:unit],
        columns(expand, 0),
        reduce[...],
        edge[:, :bins],
        turned_edge[at_gain : at_gain + 3],
    ]
    for j, grad in enumerate(grads_of):
        rate = GAIN_RATE if j in (1, 8) else LEARN_RATE
        after = update(grad, rate, masters[j], moments[j], squares[j], clip)
        for n, value in enumerate(after):
            outs[9 * n + j][...] = value


def adam(clip, shares, masters, moments, squares, at):
    turned = lambda group: [x.T if j < 2 else x for j, x in enumerate(group)]
    masters, moments, squares = turned(masters), turned(moments), turned(squares)
    vmem = pl.BlockSpec(memory_space=pltpu.VMEM)
    arrays = [*shares, *masters, *moments, *squares]
    results = pl.pallas_call(
        partial(adam_kernel, at),
        in_specs=[pl.BlockSpec(memory_space=pltpu.SMEM)] + [vmem] * len(arrays),
        out_specs=[vmem] * 27,
        out_shape=[jax.ShapeDtypeStruct(x.shape, jnp.float32) for x in (*masters, *moments, *squares)],
        compiler_params=params(),
        name="adam",
    )(clip, *arrays)
    return [y for n in range(3) for y in turned(results[9 * n : 9 * n + 9])]


def prepare_kernel(
    at_mel, at_count, frames,
    facts_ref, input_ref, table_ref, head_ref, gains_ref, skip_ref, attend_ref, out_ref,
):
    unit, inputs = input_ref.shape
    phones = inputs - at_mel
    turned = as_low(input_ref[...])
    out_ref[0, :unit, :phones] = turned[:, at_mel:]
    out_ref[0, :unit, phones:TABLE_AT] = jnp.pad(turned[:, :at_mel], ((0, 0), (0, TABLE_AT - inputs)))
    table = as_low(table_ref[...])
    rest = jnp.zeros((unit - table.shape[0], table.shape[1]), jnp.bfloat16)
    out_ref[0, :unit, TABLE_AT:HEAD_AT] = jnp.concatenate([table, rest], 0)
    bins = head_ref.shape[1]
    edge = jnp.pad(head_ref[...], ((0, 0), (0, out_ref.shape[2] - HEAD_AT - bins)))
    lane = lax.broadcasted_iota(jnp.int32, edge.shape, 1)
    spot = (gains_ref.shape[0], edge.shape[1])
    row = lax.broadcasted_iota(jnp.int32, spot, 0)
    here = lax.broadcasted_iota(jnp.int32, spot, 1) == row + bins
    edge = as_low(edge).astype(jnp.float32) + dot_tn(as_low(gains_ref[...]), as_low(here))
    end = jnp.minimum(jnp.minimum(facts_ref[2], facts_ref[3]), frames)
    count = jnp.maximum(end - jnp.maximum(facts_ref[1], 0), 0)
    for j, fact in enumerate((facts_ref[0], lax.div(count, 16), lax.rem(count, 16))):
        edge = jnp.where(lane == at_count - HEAD_AT + j, fact.astype(jnp.float32), edge)
    out_ref[0, :unit, HEAD_AT:] = as_low(edge)
    width = out_ref.shape[2]
    start = unit + skip_ref.shape[0]
    out_ref[0, unit:start] = as_low(skip_ref[...])
    for j in range(attend_ref.shape[1] // width):
        here = slice(start + j * unit, start + (j + 1) * unit)
        out_ref[0, here] = as_low(attend_ref[:, j * width : (j + 1) * width])
    for z in range(1, out_ref.shape[0]):
        out_ref[z] = out_ref[0]


def prepare(facts, turned, table, head, gains, skip, attend, deep, frames, at_mel, at_count):
    vmem = pl.BlockSpec(memory_space=pltpu.VMEM)
    width = skip.shape[1]
    rows = turned.shape[0] + skip.shape[0] + attend.size // width
    return pl.pallas_call(
        partial(prepare_kernel, at_mel, at_count, frames),
        in_specs=[pl.BlockSpec(memory_space=pltpu.SMEM)] + [vmem] * 6,
        out_specs=vmem,
        out_shape=jax.ShapeDtypeStruct((deep, rows, width), jnp.bfloat16),
        compiler_params=params(),
        name="prepare",
    )(facts, turned, table, head, gains, skip, attend)


def shards(
    grid,
    fast,
    clean_mel,
    gauss_noise,
    flow_time,
    phone_ids,
    lengths,
    span_start,
    span_end,
    speaker,
    skip_states,
    w_input,
    phone_table,
    w_skip,
    w_attend,
    w_output,
    w_expand,
    w_reduce,
    w_head,
    norm_gains,
    moment_input,
    moment_table,
    moment_skip,
    moment_attend,
    moment_output,
    moment_expand,
    moment_reduce,
    moment_head,
    moment_gains,
    square_input,
    square_table,
    square_skip,
    square_attend,
    square_output,
    square_expand,
    square_reduce,
    square_head,
    square_gains,
):
    masters = (w_input, phone_table, w_skip, w_attend, w_output, w_expand, w_reduce, w_head, norm_gains)
    moments = (
        moment_input, moment_table, moment_skip, moment_attend, moment_output,
        moment_expand, moment_reduce, moment_head, moment_gains,
    )
    squares = (
        square_input, square_table, square_skip, square_attend, square_output,
        square_expand, square_reduce, square_head, square_gains,
    )
    frames, mel_bins = clean_mel.shape
    width = w_skip.shape[1]
    heads = width // HD
    devices = grid.total
    unit = width // devices
    inputs = w_input.shape[0]
    phones = phone_table.shape[0]
    phone_wide = phone_table.shape[1]
    phone_width = phone_wide * devices
    mel_lanes = TABLE_AT - phone_width
    at_gain = HEAD_AT + mel_bins
    at_count = at_gain + 3
    position = jnp.arange(frames)
    frame_valid = (position < lengths[0]).astype(jnp.float32)
    frame_inside = ((position >= span_start[0]) & (position < span_end[0])).astype(
        jnp.float32
    ) * frame_valid
    speaker_hot = (speaker[0] == jnp.arange(SPK)).astype(jnp.float32)
    count = jnp.sum(frame_inside)
    count_high = jnp.floor(count / 16.0)
    tally = jnp.stack([speaker[0].astype(jnp.float32), count_high, count - 16.0 * count_high])

    low_input = as_low(w_input)
    small = jnp.concatenate(
        [
            low_input[2 * mel_bins :].T,
            low_input[: 2 * mel_bins].T,
            jnp.zeros((unit, TABLE_AT - inputs), jnp.bfloat16),
            jnp.pad(as_low(phone_table).T, ((0, unit - phone_wide), (0, 0))),
            as_low(w_head),
            as_low(norm_gains).T,
            jnp.broadcast_to(as_low(tally)[None, :], (unit, 3)),
            jnp.zeros((unit, width - at_count - 3), jnp.bfloat16),
        ],
        1,
    )

    def blocks(x):
        return [as_low(x[:, j : j + width]) for j in range(0, x.shape[1], width)]

    attend_blocks, expand_blocks = blocks(w_attend), blocks(w_expand)
    packs, wides = len(attend_blocks), len(expand_blocks)
    stages = [
        [("small", None, small), ("skip", None, as_low(w_skip))]
        + [("attend", j, w) for j, w in enumerate(attend_blocks)],
        [("output", None, as_low(w_output))] + [("expand", j, w) for j, w in enumerate(expand_blocks)],
        [("reduce", None, as_low(w_reduce))],
    ]
    if fast:
        own, other = grid.owners(0, -1), grid.owners(1, -1)
        own_turned, other_turned = grid.owners(0, -1, True), grid.owners(1, -1, True)
        mine, theirs = grid.owners(0, 1), grid.owners(1, 1)

    def load(stage):
        return jnp.concatenate([w for _, _, w in stage], 0)

    def sibling(x):
        return shift(grid, x, "core", 1)

    def along(x, role, *after):
        return spread(grid, tied(x, *after) if after else x, role)

    def deepen(x, *after):
        return swap_deep(grid, tied(x, *after) if after else x)

    def hop_far(pieces):
        return [shift(grid, p, "far", f) for f in range(1, grid.size("far")) for p in pieces]

    def gather_whole(stage):
        rows = lax.all_gather(load(stage), AXES, axis=0, tiled=False)
        parts, start = [], 0
        for name, _, w in stage:
            part = rows[:, start : start + w.shape[0]]
            start += w.shape[0]
            if name == "small":
                table = part[:, :phone_wide, TABLE_AT:HEAD_AT].reshape(BANDS, -1, phones)
                table = jnp.pad(table, ((0, 0), (0, width // BANDS - table.shape[1]), (0, 0)))
                part = part.reshape(BANDS, -1, width)
                part = jnp.concatenate([part[..., :TABLE_AT], table, part[..., HEAD_AT:]], 2)
            parts.append(part.reshape(BANDS, -1, width))
        rows = jnp.concatenate(parts, 1)
        return [rows[: BANDS // 2], rows[BANDS // 2 :]]

    flow = flow_time[0]
    noisy_mel = (1.0 - (1.0 - SIGMA) * flow) * gauss_noise + flow * clean_mel
    context = clean_mel * (frame_valid - frame_inside)[:, None]
    target = clean_mel - (1.0 - SIGMA) * gauss_noise
    mel = jnp.concatenate([as_low(noisy_mel), as_low(context)], 1)
    mel = jnp.pad(mel, ((0, 0), (0, mel_lanes - mel.shape[1])))
    phone_hot = as_low(phone_ids[:, None] == jnp.arange(phones)[None, :])
    slopes = head_slopes(heads)
    times = time_features(flow, width)[None, :]
    inside = frame_inside[:, None]
    states_turned = skip_states.T
    loads = [load(stage) for stage in stages]
    if fast:
        first = prepare(
            jnp.stack([speaker[0], span_start[0], span_end[0], lengths[0]]), w_input.T, phone_table.T,
            w_head, norm_gains, w_skip, w_attend, grid.size("z"), frames, 2 * mel_bins, at_count,
        )
        pair_1 = stack(along(loads[1], "near"), grid.size("z"))
        load_2 = stack([loads[2]], grid.size("z"))[:, 0]
        deep_0, pair_1, load_2 = join(deepen(first), pair_1, load_2)
        deep_1 = deepen(pair_1)
        near_0 = along(deep_0, "near")
        near_0 = [tied(near_0[0], near_0[-1])] + near_0[1:]
        (
            near_0, far_0, core_0, deep_1, own, other, own_turned, other_turned, mine, theirs,
            target, mel, phone_hot, slopes, times, inside, states_turned,
        ) = join(
            near_0, hop_far(near_0), [sibling(p) for p in near_0], deep_1,
            own, other, own_turned, other_turned, mine, theirs,
            target, mel, phone_hot, slopes, times, inside, states_turned,
        )
        pieces_0 = near_0 + far_0 + core_0 + [sibling(p) for p in far_0]
        near_1 = deep_1.reshape((-1,) + deep_1.shape[2:])
        far_1 = along(near_1, "far")[1]
        core_1 = sibling(near_1)
        deep_2 = deepen(load_2, near_1)
    else:
        own, other = jnp.arange(BANDS // 2), jnp.arange(BANDS // 2, BANDS)
        own_turned, other_turned = own, other
        pieces_0 = gather_whole(stages[0])
    small_full, skip_full, embedded, stream, joined_turned, attn_in, attn_turned, edges, share = front(
        speaker, own, other, pieces_0, skip_states, states_turned, phone_hot, mel, times, phone_width, mel_bins, at_count, unit
    )
    attend_full, packed = pack(own, other, pieces_0, attn_in, packs)
    if fast:
        near_2 = along(tied(deep_2, packed), "near")
    mixed, lse = attend(lengths, slopes, packed)
    if fast:
        far_1, near_2, core_1, stream, packed, mixed, lse, joined_turned, edges, share = join(
            far_1, near_2, core_1, stream, packed, mixed, lse, joined_turned, edges, share
        )
        pieces_1 = [near_1, far_1, core_1, sibling(far_1)]
        far_2 = hop_far(near_2)
        core_2 = [sibling(p) for p in near_2]
    else:
        pieces_1 = gather_whole(stages[1])
    output_full, stream_mid, ffn_in, ffn_turned, mixed_turned = mid_step(
        own_turned, other_turned, pieces_1, mixed, stream, edges, mel_bins + 1
    )
    expand_full, activated, act_turned, gelu_slope = expand(
        own_turned, other_turned, pieces_1, ffn_in, wides
    )
    if fast:
        far_2, core_2, stream_mid, ffn_turned, mixed_turned, activated, act_turned, gelu_slope = join(
            far_2, core_2, stream_mid, ffn_turned, mixed_turned, activated, act_turned, gelu_slope
        )
        pieces_2 = near_2 + far_2 + core_2 + [sibling(p) for p in far_2]
    else:
        pieces_2 = gather_whole(stages[2])
    reduce_full, d_stream_out, d_branch, grad_head, grad_gain_three, error_sum = head_step(
        share, own, other, pieces_2, activated, stream_mid, edges, target, inside, mel_bins + 2
    )
    far, near, deep = (grid.size(r) for r in ("far", "near", "z"))

    def both(*arrays):
        return [y for x in arrays for y in (x, sibling(x))]

    def sums(plan, arrays, *others, **options):
        first = [tied(arrays[0], *others)] if others else arrays[:1]
        return grads(plan, first + arrays[1:], mine, frames, unit, width, far, **options)

    def hops(legs, role, *others):
        sent = [tied(leg, *others) if others else leg for leg in legs[1:]]
        return [shift(grid, leg, role, j + 1) for j, leg in enumerate(sent)]

    def dense(pairs):
        parts = []
        for turned, right, stride, offset in pairs:
            if right is None:
                part = turned.reshape(devices, unit, width)
            else:
                turned = turned.reshape(devices, stride, frames)[:, offset : offset + unit]
                part = dot_nn(turned.reshape(width, frames), right).reshape(devices, unit, width)
            parts.append(part)
        return lax.psum_scatter(jnp.concatenate(parts, 1), AXES, scatter_dimension=0)

    offsets = [j * unit for j in range(wides)]
    if fast:
        plan = [((0, 1), (2, 3), wides * unit, o) for o in offsets]
        legs_0 = sums(plan, both(tied(act_turned, *pieces_2), d_branch))
        moved_0 = hops(legs_0, "far")
        d_branch_next = tied(d_branch, legs_0[0])
    else:
        share_reduce = dense([(act_turned, d_branch, wides * unit, o) for o in offsets])
        d_branch_next = d_branch
    d_stream_mid, d_out, grad_gain_two, *d_hidden = ffn_back(
        d_branch_next, d_stream_out, reduce_full, gelu_slope, expand_full, stream_mid, edges, mel_bins + 1
    )
    if fast:
        turned = both(ffn_turned)
        d_hiddens = both(*d_hidden)
        moved_0, turned, d_hiddens[:2], d_stream_mid, d_out = join(
            moved_0, turned, d_hiddens[:2], d_stream_mid, d_out
        )
        legs_0 = fold([legs_0[0]] + moved_0, near)
        moved_0 = hops(legs_0, "near")
        plan = [((0, 1), (2 + 2 * j, 3 + 2 * j), unit, 0) for j in range(wides)]
        legs_1 = sums(plan, turned + d_hiddens, legs_0[0])
        turned = both(tied(mixed_turned, legs_0[0]), attn_turned, d_out)
        moved_0, legs_1, turned, d_out = join(moved_0, legs_1, turned, d_out)
        (sums_0,) = fold([legs_0[0]] + moved_0, 1)
        d_out = tied(d_out, sums_0)
        moved_1 = hops(legs_1, "far", sums_0)
        sums_0 = swap_deep(grid, sums_0)
    else:
        share_expand = dense([(ffn_turned, d, unit, 0) for d in d_hidden])
    d_packed = attend_back(lengths, slopes, packed, d_out, output_full, lse)
    d_joined_in, grad_gain_one = pack_back(
        d_packed, attend_full, d_stream_mid, stream, edges, mel_bins
    )
    if fast:
        d_packs = both(*d_packed)
        moved_1, sums_0, d_packs, d_joined_in = join(moved_1, sums_0, d_packs, d_joined_in)
        legs_1 = fold([legs_1[0]] + moved_1, near)
        moved_1 = hops(legs_1, "near")
        plan = [((0, 1), (4, 5), unit, 0)]
        plan = plan + [((2, 3), (6 + 2 * j, 7 + 2 * j), unit, 0) for j in range(packs)]
        legs_2 = sums(plan, turned + d_packs, legs_1[0])
        joined = both(tied(joined_turned, legs_1[0]), tied(d_joined_in, legs_1[0]))
        moved_1, legs_2, joined, d_joined_in = join(moved_1, legs_2, joined, d_joined_in)
        (sums_1,) = fold([legs_1[0]] + moved_1, 1)
        d_joined_in = tied(d_joined_in, sums_1)
        moved_2 = hops(legs_2, "far", sums_1)
        sums_1 = swap_deep(grid, sums_1)
    else:
        share_attend = dense(
            [(mixed_turned, d_out, unit, 0)] + [(attn_turned, d, unit, 0) for d in d_packed]
        )
    tallies = edges[at_count - HEAD_AT : at_count - HEAD_AT + 3].reshape(3, devices, unit)
    tallies = tallies[:, :, 0].astype(jnp.float32)
    counts = jnp.sum(
        (tallies[0][:, None] == jnp.arange(SPK, dtype=jnp.float32)[None, :])
        * (16.0 * tallies[1] + tallies[2])[:, None],
        0,
    )
    gain_grads = [grad_gain_one, grad_gain_two, grad_gain_three]
    small_grads = tail(
        d_joined_in, skip_full, small_full, embedded, mel, phone_hot, grad_head, gain_grads, mel_bins
    )
    if fast:
        small_grads = list(small_grads)
        (sent,) = grads([((0, 1, 2), None, 0, 0)], small_grads, theirs, frames, unit, width, 1)
        plan = [((0, 1), (2, 3), 2 * unit, o) for o in offsets[:2]] + [((4, 5, 6), None, 0, 0)]
        legs_3 = sums(plan, joined + small_grads, sent, came=sibling(sent))
        moved_2, legs_3 = join(moved_2, legs_3)
        legs_2 = fold([legs_2[0]] + moved_2, near)
        moved_3 = hops(legs_3, "far", legs_2[0])
        moved_2, sums_1, counts = join(hops(legs_2, "near"), sums_1, counts)
        (sums_2,) = fold([legs_2[0]] + moved_2, 1)
        moved_3 = [tied(moved_3[0], sums_2)] + moved_3[1:]
        legs_3 = fold([legs_3[0]] + moved_3, near)
        moved_3, sums_2 = join(hops(legs_3, "near"), swap_deep(grid, sums_2))
        (sums_3,) = fold([legs_3[0]] + moved_3, 1)
        sums_3 = swap_deep(grid, sums_3)
        share_reduce, share_expand, share_attend, share_last = [
            jnp.sum(x.astype(jnp.float32), 0) for x in (sums_0, sums_1, sums_2, sums_3)
        ]
    else:
        main, table, edge = small_grads
        table = table.reshape(devices, phone_wide, phones)
        table = jnp.pad(table, ((0, 0), (0, unit - phone_wide), (0, 0))).reshape(width, phones)
        small_grads = jnp.concatenate([main, table, edge], 1).astype(jnp.float32)
        share_last = dense(
            [(joined_turned, d_joined_in, 2 * unit, o) for o in offsets[:2]]
            + [(small_grads, None, 0, 0)]
        )

    shares = (share_last, share_attend, share_expand, share_reduce)
    local_square = sum((jnp.sum(g * g) for g in shares))
    totals = all_sum(grid, jnp.concatenate([speaker_hot * error_sum[0, 0], local_square[None]]))
    sums, total_square = totals[:SPK], totals[SPK]
    loss_value = jnp.mean(sums / jnp.maximum(counts, 1.0))
    grad_norm = jnp.sqrt(total_square)
    clip = jnp.minimum(1.0, 1.0 / (grad_norm + 1e-06))
    at = (phone_wide, phone_width, inputs, mel_bins)
    results = adam(clip[None], shares, masters, moments, squares, at)
    return (loss_value, grad_norm, *results)


def solution(mesh):
    grid = Grid(mesh)
    in_specs = (
        P(("wide", "narrow"), None),
        P(("wide", "narrow"), None),
        P(("wide", "narrow")),
        P(("wide", "narrow")),
        P(("wide", "narrow")),
        P(("wide", "narrow")),
        P(("wide", "narrow")),
        P(("wide", "narrow")),
        P(("wide", "narrow"), None),
        P(None, ("wide", "narrow")),
        P(None, ("wide", "narrow")),
        P(("wide", "narrow"), None),
        P(("wide", "narrow"), None),
        P(("wide", "narrow"), None),
        P(("wide", "narrow"), None),
        P(("wide", "narrow"), None),
        P(("wide", "narrow"), None),
        P(None, ("wide", "narrow")),
        P(None, ("wide", "narrow")),
        P(None, ("wide", "narrow")),
        P(("wide", "narrow"), None),
        P(("wide", "narrow"), None),
        P(("wide", "narrow"), None),
        P(("wide", "narrow"), None),
        P(("wide", "narrow"), None),
        P(("wide", "narrow"), None),
        P(None, ("wide", "narrow")),
        P(None, ("wide", "narrow")),
        P(None, ("wide", "narrow")),
        P(("wide", "narrow"), None),
        P(("wide", "narrow"), None),
        P(("wide", "narrow"), None),
        P(("wide", "narrow"), None),
        P(("wide", "narrow"), None),
        P(("wide", "narrow"), None),
        P(None, ("wide", "narrow")),
    )
    out_specs = (
        P(),
        P(),
        P(None, ("wide", "narrow")),
        P(None, ("wide", "narrow")),
        P(("wide", "narrow"), None),
        P(("wide", "narrow"), None),
        P(("wide", "narrow"), None),
        P(("wide", "narrow"), None),
        P(("wide", "narrow"), None),
        P(("wide", "narrow"), None),
        P(None, ("wide", "narrow")),
        P(None, ("wide", "narrow")),
        P(None, ("wide", "narrow")),
        P(("wide", "narrow"), None),
        P(("wide", "narrow"), None),
        P(("wide", "narrow"), None),
        P(("wide", "narrow"), None),
        P(("wide", "narrow"), None),
        P(("wide", "narrow"), None),
        P(None, ("wide", "narrow")),
        P(None, ("wide", "narrow")),
        P(None, ("wide", "narrow")),
        P(("wide", "narrow"), None),
        P(("wide", "narrow"), None),
        P(("wide", "narrow"), None),
        P(("wide", "narrow"), None),
        P(("wide", "narrow"), None),
        P(("wide", "narrow"), None),
        P(None, ("wide", "narrow")),
    )

    def body(*args):
        unit = args[11].shape[1] // grid.total
        return shards(grid, unit % 32 == 0, *args)

    return jax.shard_map(body, mesh=mesh, in_specs=in_specs, out_specs=out_specs, check_vma=False)
```
